32 devices in a mesh: img: 4 (over y, core), seq: 8 (over z, x).
Axes of the slice: x: 2, y: 2, z: 4, core: 2. Of those that a mesh axis runs over, the one named last changes fastest.
Arguments:
- llm_grads: bfloat16 [4, 256, 8192], P('img', 'seq'), may hold values from -6 to 6
- token_target: int32 [4, 256], P('img', 'seq'), may hold values from 0 to 255, as said below
- patches: bfloat16 [4, 1024, 1280], P('img', 'seq'), may hold values from -150 to 150
- gain: float32 [1280], replicated, may hold values from 0.5 to 1.5
- w_down: bfloat16 [5120, 8192], P(None, 'img'), may hold values from -0.078125 to 0.078125
- queries: bfloat16 [4, 1024, 1280], P('img', 'seq'), may hold values from -40 to 40
- keys: bfloat16 [4, 1024, 1280], P('img', 'seq'), may hold values from -5 to 5
- values: bfloat16 [4, 1024, 1280], P('img', 'seq'), may hold values from -5 to 5
- window_ids: int32 [4, 8, 32], P('img', 'seq'), may hold values from 0 to 3, never falling along the last dimension, each value on 1 to 16 neighbouring positions
Outputs:
- grad_q: bfloat16 [4, 1024, 1280], P('img', 'seq')
- grad_k: bfloat16 [4, 1024, 1280], P('img', 'seq')
- grad_v: bfloat16 [4, 1024, 1280], P('img', 'seq')
- gain_grad: float32 [1280], replicated
- bias_grad: float32 [8192], replicated
The draws below stay inside these ranges and needn't reach their ends.
Inputs may be any that keep to these rules, and one draw needn't show every extreme that they name: In each group i, token_target[i] is a permutation: position s * 32 + j (held by index s of seq) holds merged token d * 32 + m (held by index d of seq). At most 8 position of one seq index holds a merged token of any one seq index, and in every group some pair of seq indices has exactly 8.
All inputs are finite; a program needn't handle non-finite values.
Results may differ from the reference program's by a relative error of at most 0.024.
Values may be sent and summed in bfloat16 or wider, within the bound.
No kernel may reach another device: no remote copies, remote signals or barrier semaphores. Data moves between devices by JAX's collectives and lax.ppermute only.
A program may use at most 64 MiB of HBM per device.

```python
import math
import jax
import jax.numpy as jnp
import numpy as np
from jax import lax

HEADS = 16
HEAD_DIM = 80
D = 1280
MERGE_IN = 5120
OUT = 8192
M_DEV = 32
P_DEV = 128
TOK_GROUP = 256
PATCH_GROUP = 1024
CAP = 8
WIN = 16
N_IMG = 4
N_SEQ = 8


def group_tables(group_key):
    subkeys = jax.random.split(group_key, 4 + CAP)
    sigma_perm = jax.random.permutation(subkeys[0], N_SEQ).astype(jnp.int32)
    shuffle_dest = jax.random.permutation(subkeys[1], N_SEQ).astype(jnp.int32)
    window_len = M_DEV // CAP
    counts = jnp.zeros((N_SEQ, N_SEQ), jnp.int32)
    for offset in range(CAP):
        others = jax.random.permutation(subkeys[4 + offset], N_SEQ - 1).astype(jnp.int32) + 1
        mapping = jnp.concatenate([jnp.zeros((1,), jnp.int32), others])
        shifted = sigma_perm[mapping]
        counts = counts + (jnp.mod(shuffle_dest[None, :] - shifted[:, None], N_SEQ) < window_len).astype(jnp.int32)
    bounds = jnp.cumsum(counts, axis=1)
    row_ids = jnp.arange(M_DEV, dtype=jnp.int32)
    sorted_dest = jnp.sum((bounds[:, None, :] <= row_ids[None, :, None]).astype(jnp.int32), axis=2)
    row_perms = jax.vmap(lambda random_key: jax.random.permutation(random_key, M_DEV))(jax.random.split(subkeys[2], N_SEQ)).astype(jnp.int32)
    dest_of = jnp.take_along_axis(sorted_dest, row_perms, axis=1)
    flat_dest = dest_of.reshape(-1)
    ordering = jnp.argsort(flat_dest, stable=True).astype(jnp.int32)
    dest_sorted = flat_dest[ordering]
    rank_in_dest = jnp.arange(N_SEQ * M_DEV, dtype=jnp.int32) - dest_sorted * M_DEV
    slot_perms = jax.vmap(lambda random_key: jax.random.permutation(random_key, M_DEV))(jax.random.split(subkeys[3], N_SEQ)).astype(jnp.int32)
    merged_row = slot_perms[dest_sorted, rank_in_dest]
    merged_index = dest_sorted * M_DEV + merged_row
    targets = jnp.zeros((N_SEQ * M_DEV,), jnp.int32).at[ordering].set(merged_index)
    return targets


def draw_token_target(key, part):
    base_key = jax.random.fold_in(key, 4242)
    group_keys = jax.random.split(base_key, N_IMG)
    return jax.vmap(group_tables)(group_keys)


def draw_patches(key, part):
    subkeys = jax.random.split(jax.random.fold_in(key, 11), 3)
    shape = (N_IMG, PATCH_GROUP, D)
    column_scale = jnp.exp(jax.random.uniform(subkeys[2], (D,), jnp.float32, math.log(0.3), math.log(3.0)))
    base_values = jnp.clip(jax.random.normal(subkeys[0], shape, jnp.float32), -5.0, 5.0)
    row_scale = jnp.exp(jax.random.uniform(subkeys[1], (N_IMG, PATCH_GROUP, 1), jnp.float32, 0.0, math.log(10.0)))
    return (base_values * row_scale * column_scale[None, None, :]).astype(jnp.bfloat16)


def attention_pair(key):
    subkeys = jax.random.split(jax.random.fold_in(key, 23), 2)
    shape = (N_IMG, PATCH_GROUP, D)
    key_rows = jnp.clip(jax.random.normal(subkeys[0], shape, jnp.float32), -5.0, 5.0)
    query_rows = jnp.clip(jax.random.normal(subkeys[1], shape, jnp.float32), -5.0, 5.0)
    return (query_rows, key_rows)


def draw_queries(key, part):
    return attention_pair(key)[0].astype(jnp.bfloat16)


def draw_keys(key, part):
    return attention_pair(key)[1].astype(jnp.bfloat16)


def shard_levels(stream_key, shape, cuts, low, largest):
    level = 1.0
    for axis_at, parts in cuts:
        draws = jax.random.uniform(jax.random.fold_in(jax.random.fold_in(stream_key, 6), axis_at), (parts,), jnp.float32, low / len(cuts), largest / len(cuts))
        level = level * jnp.repeat(jnp.exp(draws), shape[axis_at] // parts).reshape((-1,) + (1,) * (len(shape) - 1 - axis_at))
    return level


def length_profile(count, total, limit, lean):
    loads = [(1 << 20) // math.isqrt(rank ** lean) + 1 for rank in range(2, count + 1)]
    spare, given = total - limit - (count - 1), [1] * (count - 1)
    while spare > 0:
        free = [i for i in range(count - 1) if given[i] < limit]
        whole, left = sum([loads[i] for i in free]), spare
        for i in free:
            addition = min(limit - given[i], max(1, left * loads[i] // whole), spare)
            given[i] = given[i] + addition
            spare = spare - addition
    return np.array([limit] + given)


def uneven_parts(key, count, total, most, skew):
    if count == 2:
        one = jax.random.randint(key, (), max(1, total - most), min(most, total - 1) + 1)
        return jnp.stack([one, total - one])
    sizes = jnp.asarray(length_profile(count, total, most, skew), jnp.int32)
    twos = (count - 1) // 2
    donor, taker = sizes[1:1 + 2 * twos:2], sizes[2:2 + 2 * twos:2]
    slack = jnp.minimum(donor - 1, most - taker)
    moved = jax.random.randint(jax.random.fold_in(key, 1), (twos,), 0, 1 << 20) % (slack + 1)
    sizes = sizes.at[1:1 + 2 * twos:2].set(donor - moved).at[2:2 + 2 * twos:2].set(taker + moved)
    return sizes[jax.random.permutation(jax.random.fold_in(key, 2), count)]


def centred(rng, shape, spread, reach, shards=(), held_as=jnp.bfloat16):
    array = jax.random.normal(rng, shape, jnp.float32) * spread
    if len(shards) > 0:
        array = shard_levels(rng, shape, shards, -0.22, 0.18) * array
    return jnp.clip(array, min=-reach, max=reach).astype(held_as)


def setup_inputs(seed: int = 0) -> dict:
    splits = jax.random.split(jax.random.key(seed), 10)
    llm_grads = centred(splits[0], (N_IMG, TOK_GROUP, OUT), 1.0, 6.0, ((0, 4), (1, 8)))
    token_target = draw_token_target(jax.random.fold_in(splits[9], 71), 0)
    patches = draw_patches(jax.random.fold_in(splits[9], 71), 0)
    gain = jnp.clip(1.0 + 0.1 * jax.random.normal(splits[3], (D,), jnp.float32), 0.5, 1.5)
    w_down = centred(splits[4], (MERGE_IN, OUT), MERGE_IN ** -0.5, 0.078125, ((1, 4),))
    queries = draw_queries(jax.random.fold_in(splits[9], 71), 0)
    keys = draw_keys(jax.random.fold_in(splits[9], 71), 0)
    values = centred(splits[7], (N_IMG, PATCH_GROUP, D), 1.0, 5.0, ((0, 4), (1, 8)))
    window_ids = jax.vmap(lambda own: jnp.searchsorted(jnp.cumsum(uneven_parts(own, M_DEV // 8, M_DEV, WIN, 2)), jnp.arange(M_DEV), side="right"))(jax.random.split(splits[8], N_IMG * N_SEQ)).reshape((N_IMG, N_SEQ, M_DEV)).astype(jnp.int32)
    return dict(llm_grads=llm_grads, token_target=token_target, patches=patches, gain=gain, w_down=w_down, queries=queries, keys=keys, values=values, window_ids=window_ids)


def group_products(grad_rows, w_down):
    block_width = OUT // N_IMG
    total = jnp.zeros((TOK_GROUP, MERGE_IN), jnp.float32)
    for block_index in range(N_IMG):
        column_block = grad_rows[:, block_index * block_width:(block_index + 1) * block_width]
        weight_block = w_down[:, block_index * block_width:(block_index + 1) * block_width]
        partial_term = jnp.dot(column_block, weight_block.T, preferred_element_type=jnp.float32)
        rounded = lax.optimization_barrier(partial_term.astype(jnp.bfloat16))
        total = total + rounded.astype(jnp.float32)
    return total.astype(jnp.bfloat16)

def norm_backward(token_rows, patch_rows, gain):
    patch_grads = token_rows.reshape(PATCH_GROUP, D).astype(jnp.float32)
    inputs = patch_rows.astype(jnp.float32)
    inverse_rms = lax.rsqrt(lax.optimization_barrier(jnp.mean(inputs * inputs, axis=1, keepdims=True)) + 1e-06)
    normed = inputs * inverse_rms
    gain_part = lax.optimization_barrier(jnp.sum(patch_grads * normed, axis=0))
    scaled = gain[None, :] * patch_grads
    out_grads = inverse_rms * (scaled - normed * lax.optimization_barrier(jnp.mean(scaled * normed, axis=1, keepdims=True)))
    return (out_grads.astype(jnp.bfloat16), gain_part)

def window_backward(operands):
    query_rows, key_rows, value_rows, grad_rows, window_labels = operands
    score_scale = 1.0 / math.sqrt(HEAD_DIM)
    labels = jnp.repeat(window_labels, 4)
    allowed = labels[:, None] == labels[None, :]
    query_heads = query_rows.reshape(P_DEV, HEADS, HEAD_DIM).astype(jnp.float32)
    key_heads = key_rows.reshape(P_DEV, HEADS, HEAD_DIM).astype(jnp.float32)
    value_heads = value_rows.reshape(P_DEV, HEADS, HEAD_DIM).astype(jnp.float32)
    grad_heads = grad_rows.reshape(P_DEV, HEADS, HEAD_DIM).astype(jnp.float32)
    scores = jnp.einsum('phd,qhd->hpq', query_heads, key_heads) * score_scale
    scores = jnp.where(allowed[None, :, :], scores, -jnp.inf)
    peak = lax.optimization_barrier(jnp.max(scores, axis=2, keepdims=True))
    raw_weights = jnp.exp(scores - peak)
    probs = raw_weights / lax.optimization_barrier(jnp.sum(raw_weights, axis=2, keepdims=True))
    probs_bf = probs.astype(jnp.bfloat16).astype(jnp.float32)
    attended = jnp.einsum('hpq,qhd->phd', probs_bf, value_heads)
    row_delta = lax.optimization_barrier(jnp.sum(grad_heads * attended, axis=2))
    prob_grads = jnp.einsum('phd,qhd->hpq', grad_heads, value_heads)
    score_bf = (probs * (prob_grads - jnp.transpose(row_delta)[:, :, None])).astype(jnp.bfloat16).astype(jnp.float32)
    grad_query = jnp.einsum('hpq,qhd->phd', score_bf, key_heads) * score_scale
    grad_key = jnp.einsum('hpq,phd->qhd', score_bf, query_heads) * score_scale
    grad_value = jnp.einsum('hpq,phd->qhd', probs_bf, grad_heads)
    return (grad_query.reshape(P_DEV, D).astype(jnp.bfloat16), grad_key.reshape(P_DEV, D).astype(jnp.bfloat16), grad_value.reshape(P_DEV, D).astype(jnp.bfloat16))

def place_rows(product_rows, target_rows):
    empty = jnp.zeros(product_rows.shape, product_rows.dtype)
    return empty.at[target_rows.astype(jnp.int32)].set(product_rows)

def reference(llm_grads, token_target, patches, gain, w_down, queries, keys, values, window_ids):
    products = lax.map(lambda grad_rows: group_products(grad_rows, w_down), llm_grads)
    merged = jax.vmap(place_rows)(products, token_target)
    out_grads, gain_parts = lax.map(lambda pair: norm_backward(pair[0], pair[1], gain), (merged, patches))
    gain_grad = lax.optimization_barrier(jnp.sum(gain_parts, axis=0)) / math.sqrt(N_IMG * PATCH_GROUP)
    bias_parts = lax.map(lambda grad_rows: lax.optimization_barrier(jnp.sum(grad_rows.astype(jnp.float32), axis=0)), llm_grads)
    bias_grad = lax.optimization_barrier(jnp.sum(bias_parts, axis=0)) / math.sqrt(N_IMG * TOK_GROUP)
    block_count = N_IMG * N_SEQ
    grad_query, grad_key, grad_value = lax.map(window_backward, (queries.reshape(block_count, P_DEV, D), keys.reshape(block_count, P_DEV, D), values.reshape(block_count, P_DEV, D), out_grads.reshape(block_count, P_DEV, D), window_ids.reshape(block_count, M_DEV)))
    return (grad_query.reshape(N_IMG, PATCH_GROUP, D), grad_key.reshape(N_IMG, PATCH_GROUP, D), grad_value.reshape(N_IMG, PATCH_GROUP, D), gain_grad, bias_grad)
```

```python
import functools
import math

import jax
import jax.numpy as jnp
from jax import lax
from jax.experimental import pallas as pl
from jax.experimental.pallas import tpu as pltpu
from jax.sharding import PartitionSpec as P

HEADS = 16
HEAD_DIM = 80
LANES = 128
CHUNKS = (2, 2)
DIRECT = 8
VMEM_BYTES = 40 * 1024 * 1024

F32 = jnp.float32
BF16 = jnp.bfloat16


def iota(shape, axis):
    return lax.broadcasted_iota(jnp.int32, shape, axis)


def dot(a, b, over):
    return lax.dot_general(a, b, ((over[:1], over[1:]), ((), ())), preferred_element_type=F32)


def vmem(count):
    return [pl.BlockSpec(memory_space=pltpu.VMEM)] * count


def swap(x, axis, mask):
    n = lax.axis_size(axis)
    return lax.ppermute(x, axis, [(i, i ^ mask) for i in range(n)])


def tree_sum(terms):
    while len(terms) > 1:
        terms = [terms[i] + terms[i + 1] for i in range(0, len(terms), 2)]
    return terms[0]


def sum_over(x, axis):
    n = lax.axis_size(axis)
    if n > DIRECT:
        return lax.psum(x, axis)
    return tree_sum([x] + [swap(x, axis, mask) for mask in range(1, n)])


def head_windows():
    windows = []
    for head in range(HEADS):
        low, high = head * HEAD_DIM, (head + 1) * HEAD_DIM
        start = low // LANES * LANES
        windows.append((low, high, start, -(-high // LANES) * LANES))
    return windows


def lane_mask(low, high, start, stop):
    at = iota((1, stop - start), 1) + start
    return jnp.logical_and(at >= low, at < high)


def masked(x, low, high, start, stop):
    return jnp.where(lane_mask(low, high, start, stop), x, jnp.zeros_like(x))


def project_kernel(blocks, first, tile, tiles, with_sum, *refs):
    x_refs, w_ref = refs[:blocks], refs[blocks]
    outs = refs[blocks + 1 : 2 * blocks + 1]
    w_tiles, sems = refs[-2:]
    copies = [
        pltpu.make_async_copy(w_ref.at[pl.ds(first + t * tile, tile)], w_tiles.at[t], sems.at[t])
        for t in range(tiles)
    ]
    for copy in copies:
        copy.start()
    x = jnp.concatenate([ref[...] for ref in x_refs], axis=0)
    rows = x_refs[0].shape[0]
    if with_sum:
        ones = jnp.ones((16, x.shape[0]), BF16)
        refs[2 * blocks + 1][...] = dot(ones, x, (1, 0))[:1]
    for t in range(tiles):
        copies[t].wait()
        product = dot(x, w_tiles[t], (1, 1)).astype(BF16)
        for j in range(blocks):
            outs[j][:, t * tile : (t + 1) * tile] = product[j * rows : (j + 1) * rows]


def project(x_blocks, w_down, first, width, with_sum):
    blocks, (rows, depth) = len(x_blocks), x_blocks[0].shape
    tile = 256
    tiles = width // tile
    out_shape = [jax.ShapeDtypeStruct((rows, width), BF16)] * blocks
    if with_sum:
        out_shape = out_shape + [jax.ShapeDtypeStruct((1, depth), F32)]
    out = pl.pallas_call(
        functools.partial(project_kernel, blocks, first, tile, tiles, with_sum),
        out_shape=out_shape,
        in_specs=vmem(blocks) + [pl.BlockSpec(memory_space=pl.ANY)],
        out_specs=vmem(len(out_shape)),
        scratch_shapes=[
            pltpu.VMEM((tiles, tile, depth), BF16),
            pltpu.SemaphoreType.DMA((tiles,)),
        ],
        compiler_params=pltpu.CompilerParams(vmem_limit_bytes=VMEM_BYTES),
        cost_estimate=pl.CostEstimate(
            flops=2 * blocks * rows * depth * width,
            bytes_accessed=2 * width * depth,
            transcendentals=0,
        ),
        name="project",
    )(*x_blocks, w_down)
    return out[:blocks], (out[blocks] if with_sum else None)


def pack_kernel(peers, capacity, direct, labelled, blocks, me_ref, targets_ref, *refs):
    terms, outs = refs[:blocks], refs[blocks:]
    targets = targets_ref[...]
    rows = targets.shape[1]
    dest = targets // rows
    local = targets - dest * rows
    dest_column = jnp.sum(
        jnp.where(iota((rows, rows), 0) == iota((rows, rows), 1), dest, 0), axis=1, keepdims=True
    )
    same_before = jnp.logical_and(dest_column == dest, iota((rows, rows), 0) < iota((rows, rows), 1))
    rank = jnp.sum(same_before.astype(jnp.int32), axis=0, keepdims=True)
    slots = peers * capacity
    slot = iota((slots, rows), 0)
    holder = slot // capacity
    if direct:
        holder = holder ^ me_ref[0]
    chosen = jnp.logical_and(dest == holder, rank == slot % capacity)
    total = terms[0][...].astype(F32)
    for term in terms[1:]:
        total = total + term[...].astype(F32)
    width = total.shape[1]
    packed = dot(chosen.astype(F32).astype(BF16), total.astype(BF16), (1, 0))
    if labelled:
        label = jnp.sum(jnp.where(chosen, local + 1, 0), axis=1, keepdims=True) - 1
        packed = jnp.concatenate(
            [packed, jnp.broadcast_to(label.astype(F32), (slots, LANES))], axis=1
        )
    if not direct:
        outs[0][...] = packed.astype(BF16)
        return
    for m in range(peers):
        outs[m][...] = packed[m * capacity : (m + 1) * capacity].astype(BF16)


def pack(terms, targets, me, peers, capacity, direct, labelled):
    rows, width = terms[0].shape
    width = width + (LANES if labelled else 0)
    if direct:
        out_shape = [jax.ShapeDtypeStruct((capacity, width), BF16)] * peers
    else:
        out_shape = [jax.ShapeDtypeStruct((peers * capacity, width), BF16)]
    return pl.pallas_call(
        functools.partial(pack_kernel, peers, capacity, direct, labelled, len(terms)),
        out_shape=out_shape,
        in_specs=[pl.BlockSpec(memory_space=pltpu.SMEM)] + vmem(1 + len(terms)),
        out_specs=vmem(len(out_shape)),
        compiler_params=pltpu.CompilerParams(vmem_limit_bytes=VMEM_BYTES),
        cost_estimate=pl.CostEstimate(
            flops=2 * rows * peers * capacity * width,
            bytes_accessed=2 * (len(terms) * rows + peers * capacity) * width,
            transcendentals=0,
        ),
        name="pack",
    )(me, targets, *terms)


def route(packed, peers, capacity, direct):
    if direct:
        return [packed[0]] + [swap(packed[m], "seq", m) for m in range(1, peers)]
    width = packed[0].shape[1]
    sent = packed[0].reshape(peers, capacity, width)
    got = lax.all_to_all(sent, "seq", split_axis=0, concat_axis=0, tiled=True)
    return [got.reshape(peers * capacity, width)]


def probs_kernel(q_ref, k_ref, ids_ref, probs_ref, probs_t_ref):
    patches = q_ref.shape[0]
    ids = ids_ref[...]
    per_token = patches // ids.shape[1]
    token = iota((patches, ids.shape[1]), 0) // per_token
    column = jnp.sum(
        jnp.where(token == iota((patches, ids.shape[1]), 1), ids, 0), axis=1, keepdims=True
    )
    square = (patches, patches)
    row = jnp.sum(
        jnp.where(iota(square, 0) == iota(square, 1), column, 0), axis=0, keepdims=True
    )
    allowed = column == row
    scale = 1.0 / math.sqrt(HEAD_DIM)
    for head, (low, high, start, stop) in enumerate(head_windows()):
        q = masked(q_ref[:, start:stop], low, high, start, stop)
        k = k_ref[:, start:stop]
        for out, scores, axis in (
            (probs_ref, dot(q, k, (1, 1)), 1),
            (probs_t_ref, dot(k, q, (1, 1)), 0),
        ):
            scores = jnp.where(allowed, scores * scale, -jnp.inf)
            weights = jnp.exp(scores - jnp.max(scores, axis=axis, keepdims=True))
            out[head] = weights / jnp.sum(weights, axis=axis, keepdims=True)


def window_probs(queries, keys, ids):
    patches = queries.shape[0]
    shape = jax.ShapeDtypeStruct((HEADS, patches, patches), F32)
    return pl.pallas_call(
        probs_kernel,
        out_shape=[shape, shape],
        in_specs=vmem(3),
        out_specs=vmem(2),
        compiler_params=pltpu.CompilerParams(vmem_limit_bytes=VMEM_BYTES),
        cost_estimate=pl.CostEstimate(
            flops=8 * HEADS * patches * patches * LANES,
            bytes_accessed=8 * HEADS * patches * patches,
            transcendentals=2 * HEADS * patches * patches,
        ),
        name="probs",
    )(queries, keys, ids)


def norm_kernel(counts, parts, slots, patches_ref, gain_ref, *refs):
    chunks, at = [], 0
    for count in counts:
        chunks.append([ref[...].astype(F32) for ref in refs[at : at + count]])
        at += count
    out_ref, gain_grad_ref = refs[at:]
    patches, width = patches_ref.shape
    chunks = [jnp.concatenate(chunk, axis=0) for chunk in chunks]
    labels = chunks[0][:, parts[0] * width :][:, :1]
    columns = []
    for chunk, count in zip(chunks, parts):
        columns += [chunk[:, c * width : (c + 1) * width] for c in range(count)]
    held = jnp.concatenate(columns, axis=0).astype(BF16)
    lanes = len(columns) * slots
    lane = iota((slots, lanes), 1)
    row_of_lane = jnp.sum(
        jnp.where(lane % slots == iota((slots, lanes), 0), labels, 0.0), axis=0, keepdims=True
    ).astype(jnp.int32)
    patch_of_lane = row_of_lane * len(columns) + iota((1, lanes), 1) // slots
    patch_of_lane = jnp.where(row_of_lane < 0, -1, patch_of_lane)
    chosen = patch_of_lane == iota((patches, lanes), 0)
    patch_grads = dot(chosen.astype(F32).astype(BF16), held, (1, 0))
    inputs = patches_ref[...].astype(F32)
    inverse_rms = lax.rsqrt(jnp.mean(inputs * inputs, axis=1, keepdims=True) + 1e-06)
    normed = inputs * inverse_rms
    gain_grad_ref[...] = jnp.sum(patch_grads * normed, axis=0, keepdims=True)
    scaled = gain_ref[...] * patch_grads
    out_ref[...] = (
        inverse_rms * (scaled - normed * jnp.mean(scaled * normed, axis=1, keepdims=True))
    ).astype(BF16)


def norm_backward(received, parts, slots, patches, gain):
    counts = [len(chunk) for chunk in received]
    flat = [x for chunk in received for x in chunk]
    count, width = patches.shape
    return pl.pallas_call(
        functools.partial(norm_kernel, counts, parts, slots),
        out_shape=[
            jax.ShapeDtypeStruct((count, width), BF16),
            jax.ShapeDtypeStruct((1, width), F32),
        ],
        in_specs=vmem(2 + len(flat)),
        out_specs=vmem(2),
        compiler_params=pltpu.CompilerParams(vmem_limit_bytes=VMEM_BYTES),
        cost_estimate=pl.CostEstimate(
            flops=2 * count * width * slots * sum(parts),
            bytes_accessed=2 * width * (2 * count + slots * sum(parts)),
            transcendentals=0,
        ),
        name="norm",
    )(patches, gain, *flat)


def window_kernel(g_ref, q_ref, k_ref, v_ref, probs_ref, probs_t_ref, dq_ref, dk_ref, dv_ref):
    width = g_ref.shape[1]
    windows = head_windows()
    scores, scores_t, probs_t = [], [], []
    for head, (low, high, start, stop) in enumerate(windows):
        g = masked(g_ref[:, start:stop], low, high, start, stop)
        v = v_ref[:, start:stop]
        found = []
        for ref, grads, axis in (
            (probs_ref, dot(g, v, (1, 1)), 1),
            (probs_t_ref, dot(v, g, (1, 1)), 0),
        ):
            probs = ref[head]
            rounded = probs.astype(BF16)
            delta = jnp.sum(rounded.astype(F32) * grads, axis=axis, keepdims=True)
            found.append(((probs * (grads - delta)).astype(BF16), rounded))
        scores.append(found[0][0])
        scores_t.append(found[1][0])
        probs_t.append(found[1][1])
    scale = 1.0 / math.sqrt(HEAD_DIM)
    for start in range(0, width, LANES):
        stop = start + LANES
        heads = [h for h, (low, high, _, _) in enumerate(windows) if low < stop and high > start]
        for out, left, right_ref, factor in (
            (dq_ref, scores, k_ref, scale),
            (dk_ref, scores_t, q_ref, scale),
            (dv_ref, probs_t, g_ref, 1.0),
        ):
            right = right_ref[:, start:stop]
            rows = [masked(right, windows[h][0], windows[h][1], start, stop) for h in heads]
            product = dot(
                jnp.concatenate([left[h] for h in heads], axis=1),
                jnp.concatenate(rows, axis=0),
                (1, 0),
            )
            out[:, start:stop] = (product * factor).astype(BF16)


def window_backward(out_grads, queries, keys, values, probs, probs_t):
    patches, width = queries.shape
    shape = jax.ShapeDtypeStruct((patches, width), BF16)
    return pl.pallas_call(
        window_kernel,
        out_shape=[shape] * 3,
        in_specs=vmem(6),
        out_specs=vmem(3),
        compiler_params=pltpu.CompilerParams(vmem_limit_bytes=VMEM_BYTES),
        cost_estimate=pl.CostEstimate(
            flops=10 * HEADS * patches * patches * LANES,
            bytes_accessed=8 * HEADS * patches * patches + 14 * patches * width,
            transcendentals=0,
        ),
        name="window",
    )(out_grads, queries, keys, values, probs, probs_t)


def body(llm_grads, token_target, patches, gain, w_down, queries, keys, values, window_ids):
    grad_rows = llm_grads[0]
    rows = grad_rows.shape[0]
    images, peers = lax.axis_size("img"), lax.axis_size("seq")
    image, me = lax.axis_index("img"), lax.axis_index("seq")
    capacity = max(1, 2 * rows // peers)
    slots = peers * capacity
    direct = peers <= DIRECT
    block = w_down.shape[1]
    width = patches.shape[2]

    def column_block(index):
        return lax.dynamic_slice(grad_rows, (0, index * block), (rows, block))

    x_blocks = [column_block(image)]
    x_blocks += [swap(column_block(image ^ j), "img", j) for j in range(1, images)]
    probs, probs_t = window_probs(queries[0], keys[0], window_ids[0])

    received, first = [], 0
    for index, count in enumerate(CHUNKS):
        terms, sums = project(x_blocks, w_down, first, count * width, index == 0)
        first += count * width
        if index == 0:
            bias_part = sums
        terms = [terms[0]] + [swap(terms[j], "img", j) for j in range(1, images)]
        packed = pack(terms, token_target, me.reshape(1), peers, capacity, direct, index == 0)
        received.append(route(packed, peers, capacity, direct))

    bias_block = sum_over(bias_part, "seq")
    bias_blocks = [bias_block] + [swap(bias_block, "img", j) for j in range(1, images)]
    bias_total = jnp.zeros((images, 1, block), F32)
    for j in range(images):
        bias_total = lax.dynamic_update_slice(bias_total, bias_blocks[j][None], (image ^ j, 0, 0))
    bias_total = bias_total.reshape(-1)

    out_grads, gain_part = norm_backward(received, CHUNKS, slots, patches[0], gain[None])
    gain_total = sum_over(sum_over(gain_part, "seq"), "img")[0]
    grads = window_backward(out_grads, queries[0], keys[0], values[0], probs, probs_t)
    devices = images * peers
    gain_grad = gain_total / math.sqrt(devices * patches.shape[1])
    bias_grad = bias_total / math.sqrt(devices * rows)
    return (grads[0][None], grads[1][None], grads[2][None], gain_grad, bias_grad)


def solution(mesh):
    return jax.shard_map(
        body,
        mesh=mesh,
        in_specs=(
            P("img", "seq", None),
            P("img", "seq"),
            P("img", "seq", None),
            P(),
            P(None, "img"),
            P("img", "seq", None),
            P("img", "seq", None),
            P("img", "seq", None),
            P("img", "seq", None),
        ),
        out_specs=(P("img", "seq", None), P("img", "seq", None), P("img", "seq", None), P(), P()),
        check_vma=False,
    )
```

```python
import functools
import math

import jax
import jax.numpy as jnp
from jax import lax
from jax.experimental import pallas as pl
from jax.experimental.pallas import tpu as pltpu
from jax.sharding import PartitionSpec as P

HEADS = 16
HEAD_DIM = 80
LANES = 128
CHUNKS = (2, 2)
VMEM_BYTES = 40 * 1024 * 1024

F32 = jnp.float32
BF16 = jnp.bfloat16


def iota(shape, axis):
    return lax.broadcasted_iota(jnp.int32, shape, axis)


def dot(a, b, over):
    return lax.dot_general(a, b, ((over[:1], over[1:]), ((), ())), preferred_element_type=F32)


def vmem(count):
    return [pl.BlockSpec(memory_space=pltpu.VMEM)] * count


def head_windows():
    windows = []
    for head in range(HEADS):
        low, high = head * HEAD_DIM, (head + 1) * HEAD_DIM
        start = low // LANES * LANES
        windows.append((low, high, start, -(-high // LANES) * LANES))
    return windows


def lane_mask(low, high, start, stop):
    at = iota((1, stop - start), 1) + start
    return jnp.logical_and(at >= low, at < high)


def masked(x, low, high, start, stop):
    return jnp.where(lane_mask(low, high, start, stop), x, jnp.zeros_like(x))


def project_kernel(first, tile, tiles, with_sum, x_ref, w_ref, *refs):
    out_ref, (w_tiles, sems) = refs[0], refs[-2:]
    copies = [
        pltpu.make_async_copy(w_ref.at[pl.ds(first + t * tile, tile)], w_tiles.at[t], sems.at[t])
        for t in range(tiles)
    ]
    for copy in copies:
        copy.start()
    x = x_ref[...]
    if with_sum:
        refs[1][...] = dot(jnp.ones((16, x.shape[0]), BF16), x, (1, 0))[:1]
    x = x.T
    for t in range(tiles):
        copies[t].wait()
        product = dot(w_tiles[t], x, (1, 0))
        out_ref[:, t * tile : (t + 1) * tile] = product.T.astype(BF16)


def project(x, w_down, first, width, with_sum):
    rows, depth = x.shape
    tile = 512
    while width % tile:
        tile //= 2
    tiles = width // tile
    out_shape = [jax.ShapeDtypeStruct((rows, width), BF16)]
    if with_sum:
        out_shape = out_shape + [jax.ShapeDtypeStruct((1, depth), F32)]
    return pl.pallas_call(
        functools.partial(project_kernel, first, tile, tiles, with_sum),
        out_shape=out_shape,
        in_specs=vmem(1) + [pl.BlockSpec(memory_space=pl.ANY)],
        out_specs=vmem(len(out_shape)),
        scratch_shapes=[
            pltpu.VMEM((tiles, tile, depth), BF16),
            pltpu.SemaphoreType.DMA((tiles,)),
        ],
        compiler_params=pltpu.CompilerParams(vmem_limit_bytes=VMEM_BYTES),
        cost_estimate=pl.CostEstimate(
            flops=2 * rows * depth * width,
            bytes_accessed=2 * width * depth,
            transcendentals=0,
        ),
        name="project",
    )(x, w_down)


def pack_kernel(peers, capacity, first, carries, targets_ref, terms_ref, *refs):
    out_ref = refs[-1]
    targets = targets_ref[...]
    rows = targets.shape[1]
    dest = targets // rows
    local = targets - dest * rows
    dest_column = jnp.sum(
        jnp.where(iota((rows, rows), 0) == iota((rows, rows), 1), dest, 0), axis=1, keepdims=True
    )
    same_before = jnp.logical_and(dest_column == dest, iota((rows, rows), 0) < iota((rows, rows), 1))
    rank = jnp.sum(same_before.astype(jnp.int32), axis=0, keepdims=True)
    slots = peers * capacity
    slot = iota((slots, rows), 0)
    chosen = jnp.logical_and(dest == slot // capacity, rank == slot % capacity)
    total = terms_ref[0].astype(F32)
    for term in range(1, terms_ref.shape[0]):
        total = total + terms_ref[term].astype(F32)
    packed = dot(chosen.astype(F32).astype(BF16), total.astype(BF16), (1, 0))
    if first:
        label = jnp.sum(jnp.where(chosen, local + 1, 0), axis=1, keepdims=True) - 1
        packed = jnp.concatenate(
            [packed, jnp.broadcast_to(label.astype(F32), (slots, LANES))], axis=1
        )
    if carries:
        sums = refs[0][...]
        high = sums.astype(BF16).astype(F32)
        middle = (sums - high).astype(BF16).astype(F32)
        low = (sums - high - middle).astype(BF16).astype(F32)
        extra = jnp.zeros((slots, LANES), F32)
        row = iota((slots, LANES), 0)
        pieces = sums.shape[1] // peers // LANES
        for peer in range(peers):
            for level, values in enumerate((high, middle, low)):
                for piece in range(pieces):
                    at = (peer * pieces + piece) * LANES
                    line = jnp.broadcast_to(values[:, at : at + LANES], (slots, LANES))
                    extra = jnp.where(row == peer * capacity + level * pieces + piece, line, extra)
        packed = jnp.concatenate([packed, extra], axis=1)
    out_ref[...] = packed.astype(BF16)


def pack(terms, targets, sums, peers, capacity, first, carries):
    _, rows, width = terms.shape
    width = width + (LANES if first else 0) + (LANES if carries else 0)
    return pl.pallas_call(
        functools.partial(pack_kernel, peers, capacity, first, carries),
        out_shape=jax.ShapeDtypeStruct((peers * capacity, width), BF16),
        in_specs=vmem(3 if carries else 2),
        out_specs=pl.BlockSpec(memory_space=pltpu.VMEM),
        compiler_params=pltpu.CompilerParams(vmem_limit_bytes=VMEM_BYTES),
        cost_estimate=pl.CostEstimate(
            flops=2 * rows * peers * capacity * width,
            bytes_accessed=2 * (terms.shape[0] * rows + peers * capacity) * width,
            transcendentals=0,
        ),
        name="pack",
    )(*((targets, terms, sums) if carries else (targets, terms)))


def exchange(x, axis, pieces):
    shape = x.shape
    if x.ndim == 2:
        x = x.reshape(pieces, -1, shape[1])
    return lax.all_to_all(x, axis, split_axis=0, concat_axis=0, tiled=True).reshape(shape)


def probs_kernel(q_ref, k_ref, ids_ref, probs_ref, probs_t_ref):
    patches = q_ref.shape[0]
    ids = ids_ref[...]
    per_token = patches // ids.shape[1]
    token = iota((patches, ids.shape[1]), 0) // per_token
    column = jnp.sum(
        jnp.where(token == iota((patches, ids.shape[1]), 1), ids, 0), axis=1, keepdims=True
    )
    square = (patches, patches)
    row = jnp.sum(
        jnp.where(iota(square, 0) == iota(square, 1), column, 0), axis=0, keepdims=True
    )
    allowed = column == row
    scale = 1.0 / math.sqrt(HEAD_DIM)
    for head, (low, high, start, stop) in enumerate(head_windows()):
        q = masked(q_ref[:, start:stop], low, high, start, stop)
        k = k_ref[:, start:stop]
        for out, scores, axis in (
            (probs_ref, dot(q, k, (1, 1)), 1),
            (probs_t_ref, dot(k, q, (1, 1)), 0),
        ):
            scores = jnp.where(allowed, scores * scale, -jnp.inf)
            weights = jnp.exp(scores - jnp.max(scores, axis=axis, keepdims=True))
            out[head] = weights / jnp.sum(weights, axis=axis, keepdims=True)


def window_probs(queries, keys, ids):
    patches = queries.shape[0]
    shape = jax.ShapeDtypeStruct((HEADS, patches, patches), F32)
    return pl.pallas_call(
        probs_kernel,
        out_shape=[shape, shape],
        in_specs=vmem(3),
        out_specs=vmem(2),
        compiler_params=pltpu.CompilerParams(vmem_limit_bytes=VMEM_BYTES),
        cost_estimate=pl.CostEstimate(
            flops=8 * HEADS * patches * patches * LANES,
            bytes_accessed=8 * HEADS * patches * patches,
            transcendentals=2 * HEADS * patches * patches,
        ),
        name="probs",
    )(queries, keys, ids)


def norm_kernel(parts, peers, copies, patches_ref, gain_ref, *refs):
    chunk_refs, (out_ref, share_ref) = refs[:-2], refs[-2:]
    patches, width = patches_ref.shape
    slots = chunk_refs[0].shape[0]
    first, count = chunk_refs[0], parts[0]
    labels = first[:, count * width : count * width + LANES].astype(F32)[:, :1]
    columns = []
    for ref, count in zip(chunk_refs, parts):
        columns += [ref[:, c * width : (c + 1) * width].astype(F32) for c in range(count)]
    held = jnp.concatenate(columns, axis=0).astype(BF16)
    lanes = len(columns) * slots
    lane = iota((slots, lanes), 1)
    row_of_lane = jnp.sum(
        jnp.where(lane % slots == iota((slots, lanes), 0), labels, 0.0), axis=0, keepdims=True
    ).astype(jnp.int32)
    patch_of_lane = row_of_lane * len(columns) + iota((1, lanes), 1) // slots
    patch_of_lane = jnp.where(row_of_lane < 0, -1, patch_of_lane)
    chosen = patch_of_lane == iota((patches, lanes), 0)
    patch_grads = dot(chosen.astype(F32).astype(BF16), held, (1, 0))
    inputs = patches_ref[...].astype(F32)
    inverse_rms = lax.rsqrt(jnp.mean(inputs * inputs, axis=1, keepdims=True) + 1e-06)
    normed = inputs * inverse_rms
    gain_part = jnp.sum(patch_grads * normed, axis=0, keepdims=True)
    if copies:
        rows = [gain_part[:, at : at + LANES] for at in range(0, width, LANES)]
        carried = first[:, parts[0] * width + LANES :].astype(F32)
        capacity = slots // peers
        pieces = share_ref.shape[1] - len(rows)
        for piece in range(pieces):
            kept = iota((slots, LANES), 0) % capacity % pieces == piece
            kept = jnp.logical_and(kept, iota((slots, LANES), 0) % capacity < 3 * pieces)
            rows.append(jnp.sum(jnp.where(kept, carried, 0.0), axis=0, keepdims=True))
        for at, row in enumerate(rows):
            share_ref[:, at : at + 1, :] = jnp.broadcast_to(row[None], (copies, 1, LANES))
    else:
        share_ref[...] = gain_part
    scaled = gain_ref[...] * patch_grads
    out_ref[...] = (
        inverse_rms * (scaled - normed * jnp.mean(scaled * normed, axis=1, keepdims=True))
    ).astype(BF16)


def norm_backward(received, parts, peers, patches, gain, share):
    count, width = patches.shape
    slots = received[0].shape[0]
    return pl.pallas_call(
        functools.partial(norm_kernel, parts, peers, share[0] if len(share) == 3 else 0),
        out_shape=[jax.ShapeDtypeStruct((count, width), BF16), jax.ShapeDtypeStruct(share, F32)],
        in_specs=vmem(2 + len(received)),
        out_specs=vmem(2),
        compiler_params=pltpu.CompilerParams(vmem_limit_bytes=VMEM_BYTES),
        cost_estimate=pl.CostEstimate(
            flops=2 * count * width * slots * sum(parts),
            bytes_accessed=2 * width * (2 * count + slots * sum(parts)),
            transcendentals=0,
        ),
        name="norm",
    )(patches, gain, *received)


def window_kernel(g_ref, q_ref, k_ref, v_ref, probs_ref, probs_t_ref, dq_ref, dk_ref, dv_ref):
    width = g_ref.shape[1]
    windows = head_windows()
    scores, scores_t, probs_t = [], [], []
    for head, (low, high, start, stop) in enumerate(windows):
        g = masked(g_ref[:, start:stop], low, high, start, stop)
        v = v_ref[:, start:stop]
        found = []
        for ref, grads, axis in (
            (probs_ref, dot(g, v, (1, 1)), 1),
            (probs_t_ref, dot(v, g, (1, 1)), 0),
        ):
            probs = ref[head]
            rounded = probs.astype(BF16)
            delta = jnp.sum(rounded.astype(F32) * grads, axis=axis, keepdims=True)
            found.append(((probs * (grads - delta)).astype(BF16), rounded))
        scores.append(found[0][0])
        scores_t.append(found[1][0])
        probs_t.append(found[1][1])
    scale = 1.0 / math.sqrt(HEAD_DIM)
    for start in range(0, width, LANES):
        stop = start + LANES
        heads = [h for h, (low, high, _, _) in enumerate(windows) if low < stop and high > start]
        for out, left, right_ref, factor in (
            (dq_ref, scores, k_ref, scale),
            (dk_ref, scores_t, q_ref, scale),
            (dv_ref, probs_t, g_ref, 1.0),
        ):
            right = right_ref[:, start:stop]
            rows = [masked(right, windows[h][0], windows[h][1], start, stop) for h in heads]
            product = dot(
                jnp.concatenate([left[h] for h in heads], axis=1),
                jnp.concatenate(rows, axis=0),
                (1, 0),
            )
            out[:, start:stop] = (product * factor).astype(BF16)


def window_backward(out_grads, queries, keys, values, probs, probs_t):
    patches, width = queries.shape
    shape = jax.ShapeDtypeStruct((patches, width), BF16)
    return pl.pallas_call(
        window_kernel,
        out_shape=[shape] * 3,
        in_specs=vmem(6),
        out_specs=vmem(3),
        compiler_params=pltpu.CompilerParams(vmem_limit_bytes=VMEM_BYTES),
        cost_estimate=pl.CostEstimate(
            flops=10 * HEADS * patches * patches * LANES,
            bytes_accessed=8 * HEADS * patches * patches + 14 * patches * width,
            transcendentals=0,
        ),
        name="window",
    )(out_grads, queries, keys, values, probs, probs_t)


def body(llm_grads, token_target, patches, gain, w_down, queries, keys, values, window_ids):
    grad_rows = llm_grads[0]
    rows = grad_rows.shape[0]
    images, peers = lax.axis_size("img"), lax.axis_size("seq")
    devices = images * peers
    capacity = max(1, 2 * rows // peers)
    block = w_down.shape[1]
    width = patches.shape[2]
    pieces = block // peers // LANES
    carries = pieces > 0 and 3 * pieces <= capacity

    columns = grad_rows.reshape(rows, images, block).transpose(1, 0, 2)
    x = exchange(columns, "img", images).reshape(images * rows, block)
    probs, probs_t = window_probs(queries[0], keys[0], window_ids[0])

    received, first = [], 0
    for index, count in enumerate(CHUNKS):
        partial = project(x, w_down, first, count * width, index == 0)
        first += count * width
        if index == 0:
            bias_part = partial[1]
        terms = exchange(partial[0].reshape(images, rows, -1), "img", images)
        begins = index == 0
        packed = pack(
            terms, token_target, bias_part, peers, capacity, begins, begins and carries
        )
        received.append(exchange(packed, "seq", peers))

    gain_rows = width // LANES
    share = (devices, gain_rows + pieces, LANES) if carries else (1, width)
    out_grads, shared = norm_backward(received, CHUNKS, peers, patches[0], gain[None], share)
    if carries:
        shared = exchange(shared, ("img", "seq"), devices)
        gain_total = jnp.sum(shared[:, :gain_rows], axis=0).reshape(-1)
        bias_total = shared[:, gain_rows:].reshape(-1)
    else:
        gain_total = lax.psum(shared[0], ("img", "seq"))
        bias_total = lax.all_gather(lax.psum(bias_part[0], "seq"), "img", tiled=True)
    grads = window_backward(out_grads, queries[0], keys[0], values[0], probs, probs_t)
    gain_grad = gain_total / math.sqrt(devices * patches.shape[1])
    bias_grad = bias_total / math.sqrt(devices * rows)
    return (grads[0][None], grads[1][None], grads[2][None], gain_grad, bias_grad)


def solution(mesh):
    return jax.shard_map(
        body,
        mesh=mesh,
        in_specs=(
            P("img", "seq", None),
            P("img", "seq"),
            P("img", "seq", None),
            P(),
            P(None, "img"),
            P("img", "seq", None),
            P("img", "seq", None),
            P("img", "seq", None),
            P("img", "seq", None),
        ),
        out_specs=(P("img", "seq", None), P("img", "seq", None), P("img", "seq", None), P(), P()),
        check_vma=False,
    )
```

```python
import functools
import math

import jax
import jax.numpy as jnp
from jax import lax
from jax.experimental import pallas as pl
from jax.experimental.pallas import tpu as pltpu
from jax.sharding import PartitionSpec as P

HEADS = 16
HEAD_DIM = 80
LANES = 128
CHUNKS = (2, 2)
VMEM_BYTES = 24 * 1024 * 1024

F32 = jnp.float32
BF16 = jnp.bfloat16


def iota(shape, axis):
    return lax.broadcasted_iota(jnp.int32, shape, axis)


def dot(a, b, over):
    return lax.dot_general(a, b, ((over[:1], over[1:]), ((), ())), preferred_element_type=F32)


def vmem(count):
    return [pl.BlockSpec(memory_space=pltpu.VMEM)] * count


def head_windows():
    windows = []
    for head in range(HEADS):
        low, high = head * HEAD_DIM, (head + 1) * HEAD_DIM
        start = low // LANES * LANES
        windows.append((low, high, start, -(-high // LANES) * LANES))
    return windows


def lane_mask(low, high, start, stop):
    at = iota((1, stop - start), 1) + start
    return jnp.logical_and(at >= low, at < high)


def masked(x, low, high, start, stop):
    return jnp.where(lane_mask(low, high, start, stop), x, jnp.zeros_like(x))


def project_kernel(blocks, tile, with_sum, *refs):
    x_refs, w_ref = refs[:blocks], refs[blocks]
    keep_ref, send_ref = refs[blocks + 1 : blocks + 3]
    x = jnp.concatenate([ref[...] for ref in x_refs], axis=0)
    if with_sum:
        refs[blocks + 3][...] = dot(jnp.ones((16, x.shape[0]), BF16), x, (1, 0))[:1]
    x = x.T
    half = keep_ref.shape[0]
    for t in range(0, w_ref.shape[0], tile):
        product = dot(w_ref[t : t + tile], x, (1, 0)).T.astype(BF16)
        keep_ref[:, t : t + tile] = product[:half]
        send_ref[:, t : t + tile] = product[half:]


def project(x_blocks, w_rows, with_sum):
    blocks, (rows, depth) = len(x_blocks), x_blocks[0].shape
    width = w_rows.shape[0]
    tile = 512
    while width % tile:
        tile //= 2
    out_shape = [jax.ShapeDtypeStruct((blocks * rows // 2, width), BF16)] * 2
    if with_sum:
        out_shape = out_shape + [jax.ShapeDtypeStruct((1, depth), F32)]
    return pl.pallas_call(
        functools.partial(project_kernel, blocks, tile, with_sum),
        out_shape=out_shape,
        in_specs=vmem(blocks + 1),
        out_specs=vmem(len(out_shape)),
        compiler_params=pltpu.CompilerParams(vmem_limit_bytes=VMEM_BYTES),
        cost_estimate=pl.CostEstimate(
            flops=2 * blocks * rows * depth * width,
            bytes_accessed=2 * width * depth,
            transcendentals=0,
        ),
        name="project",
    )(*x_blocks, w_rows)


def halve_kernel(kept_ref, got_ref, keep_ref, send_ref):
    half = keep_ref.shape[0]
    keep_ref[...] = kept_ref[:half].astype(F32) + got_ref[:half].astype(F32)
    send_ref[...] = (kept_ref[half:].astype(F32) + got_ref[half:].astype(F32)).astype(BF16)


def halve(kept, got):
    rows, width = kept.shape
    return pl.pallas_call(
        halve_kernel,
        out_shape=[
            jax.ShapeDtypeStruct((rows // 2, width), F32),
            jax.ShapeDtypeStruct((rows // 2, width), BF16),
        ],
        in_specs=vmem(2),
        out_specs=vmem(2),
        compiler_params=pltpu.CompilerParams(vmem_limit_bytes=VMEM_BYTES),
        cost_estimate=pl.CostEstimate(
            flops=rows * width, bytes_accessed=7 * rows * width, transcendentals=0
        ),
        name="halve",
    )(kept, got)


def pack_kernel(peers, capacity, chunks, carries, targets_ref, *refs):
    terms, out_ref = refs[: 2 * chunks], refs[-1]
    targets = targets_ref[...]
    rows = targets.shape[1]
    dest = targets // rows
    local = targets - dest * rows
    dest_column = jnp.sum(
        jnp.where(iota((rows, rows), 0) == iota((rows, rows), 1), dest, 0), axis=1, keepdims=True
    )
    same_before = jnp.logical_and(dest_column == dest, iota((rows, rows), 0) < iota((rows, rows), 1))
    rank = jnp.sum(same_before.astype(jnp.int32), axis=0, keepdims=True)
    slots = peers * capacity
    slot = iota((slots, rows), 0)
    chosen = jnp.logical_and(dest == slot // capacity, rank == slot % capacity)
    selector = chosen.astype(F32).astype(BF16)
    at = 0
    for chunk in range(chunks):
        kept, got = terms[2 * chunk], terms[2 * chunk + 1]
        total = (kept[...].astype(F32) + got[...].astype(F32)).astype(BF16)
        width = total.shape[1]
        out_ref[:, at : at + width] = dot(selector, total, (1, 0)).astype(BF16)
        at += width
    label = jnp.sum(jnp.where(chosen, local + 1, 0), axis=1, keepdims=True) - 1
    out_ref[:, at : at + LANES] = jnp.broadcast_to(label.astype(F32), (slots, LANES)).astype(BF16)
    if carries:
        sums = refs[2 * chunks][...]
        high = sums.astype(BF16).astype(F32)
        middle = (sums - high).astype(BF16).astype(F32)
        low = (sums - high - middle).astype(BF16).astype(F32)
        extra = jnp.zeros((slots, LANES), F32)
        row = iota((slots, LANES), 0)
        pieces = sums.shape[1] // peers // LANES
        for peer in range(peers):
            for level, values in enumerate((high, middle, low)):
                for piece in range(pieces):
                    start = (peer * pieces + piece) * LANES
                    line = jnp.broadcast_to(values[:, start : start + LANES], (slots, LANES))
                    extra = jnp.where(row == peer * capacity + level * pieces + piece, line, extra)
        out_ref[:, at + LANES : at + 2 * LANES] = extra.astype(BF16)


def pack(terms, targets, sums, peers, capacity, carries):
    rows = targets.shape[1]
    width = sum(kept.shape[1] for kept, _ in terms) + (2 * LANES if carries else LANES)
    operands = [targets] + [x for pair in terms for x in pair] + ([sums] if carries else [])
    return pl.pallas_call(
        functools.partial(pack_kernel, peers, capacity, len(terms), carries),
        out_shape=jax.ShapeDtypeStruct((peers * capacity, width), BF16),
        in_specs=vmem(len(operands)),
        out_specs=pl.BlockSpec(memory_space=pltpu.VMEM),
        compiler_params=pltpu.CompilerParams(vmem_limit_bytes=VMEM_BYTES),
        cost_estimate=pl.CostEstimate(
            flops=2 * rows * peers * capacity * width,
            bytes_accessed=(6 * rows + 2 * peers * capacity) * width,
            transcendentals=0,
        ),
        name="pack",
    )(*operands)


def swap(x, axis, mask):
    n = lax.axis_size(axis)
    return lax.ppermute(x, axis, [(i, i ^ mask) for i in range(n)])


def exchange(x, axis, pieces):
    shape = x.shape
    if x.ndim == 2:
        x = x.reshape(pieces, -1, shape[1])
    return lax.all_to_all(x, axis, split_axis=0, concat_axis=0, tiled=True).reshape(shape)


def probs_kernel(q_ref, k_ref, ids_ref, probs_ref, probs_t_ref):
    patches = q_ref.shape[0]
    ids = ids_ref[...]
    per_token = patches // ids.shape[1]
    token = iota((patches, ids.shape[1]), 0) // per_token
    column = jnp.sum(
        jnp.where(token == iota((patches, ids.shape[1]), 1), ids, 0), axis=1, keepdims=True
    )
    square = (patches, patches)
    row = jnp.sum(
        jnp.where(iota(square, 0) == iota(square, 1), column, 0), axis=0, keepdims=True
    )
    allowed = column == row
    scale = 1.0 / math.sqrt(HEAD_DIM)
    for head, (low, high, start, stop) in enumerate(head_windows()):
        q = masked(q_ref[:, start:stop], low, high, start, stop)
        k = k_ref[:, start:stop]
        for out, scores, axis in (
            (probs_ref, dot(q, k, (1, 1)), 1),
            (probs_t_ref, dot(k, q, (1, 1)), 0),
        ):
            scores = jnp.where(allowed, scores * scale, -jnp.inf)
            weights = jnp.exp(scores - jnp.max(scores, axis=axis, keepdims=True))
            out[head] = weights / jnp.sum(weights, axis=axis, keepdims=True)


def window_probs(queries, keys, ids):
    patches = queries.shape[0]
    shape = jax.ShapeDtypeStruct((HEADS, patches, patches), F32)
    return pl.pallas_call(
        probs_kernel,
        out_shape=[shape, shape],
        in_specs=vmem(3),
        out_specs=vmem(2),
        compiler_params=pltpu.CompilerParams(vmem_limit_bytes=VMEM_BYTES),
        cost_estimate=pl.CostEstimate(
            flops=8 * HEADS * patches * patches * LANES,
            bytes_accessed=8 * HEADS * patches * patches,
            transcendentals=2 * HEADS * patches * patches,
        ),
        name="probs",
    )(queries, keys, ids)


def norm_kernel(peers, copies, patches_ref, gain_ref, routed_ref, out_ref, share_ref):
    patches, width = patches_ref.shape
    slots = routed_ref.shape[0]
    per_token = routed_ref.shape[1] // width
    labels = routed_ref[:, per_token * width : per_token * width + LANES].astype(F32)[:, :1]
    columns = [routed_ref[:, c * width : (c + 1) * width].astype(F32) for c in range(per_token)]
    held = jnp.concatenate(columns, axis=0).astype(BF16)
    lanes = len(columns) * slots
    lane = iota((slots, lanes), 1)
    row_of_lane = jnp.sum(
        jnp.where(lane % slots == iota((slots, lanes), 0), labels, 0.0), axis=0, keepdims=True
    ).astype(jnp.int32)
    patch_of_lane = row_of_lane * len(columns) + iota((1, lanes), 1) // slots
    patch_of_lane = jnp.where(row_of_lane < 0, -1, patch_of_lane)
    chosen = patch_of_lane == iota((patches, lanes), 0)
    patch_grads = dot(chosen.astype(F32).astype(BF16), held, (1, 0))
    inputs = patches_ref[...].astype(F32)
    inverse_rms = lax.rsqrt(jnp.mean(inputs * inputs, axis=1, keepdims=True) + 1e-06)
    normed = inputs * inverse_rms
    gain_part = jnp.sum(patch_grads * normed, axis=0, keepdims=True)
    if copies:
        rows = [gain_part[:, at : at + LANES] for at in range(0, width, LANES)]
        carried = routed_ref[:, per_token * width + LANES :].astype(F32)
        capacity = slots // peers
        pieces = share_ref.shape[1] - len(rows)
        for piece in range(pieces):
            kept = iota((slots, LANES), 0) % capacity % pieces == piece
            kept = jnp.logical_and(kept, iota((slots, LANES), 0) % capacity < 3 * pieces)
            rows.append(jnp.sum(jnp.where(kept, carried, 0.0), axis=0, keepdims=True))
        for at, row in enumerate(rows):
            share_ref[:, at : at + 1, :] = jnp.broadcast_to(row[None], (copies, 1, LANES))
    else:
        share_ref[...] = gain_part
    scaled = gain_ref[...] * patch_grads
    out_ref[...] = (
        inverse_rms * (scaled - normed * jnp.mean(scaled * normed, axis=1, keepdims=True))
    ).astype(BF16)


def norm_backward(routed, peers, patches, gain, share):
    count, width = patches.shape
    return pl.pallas_call(
        functools.partial(norm_kernel, peers, share[0] if len(share) == 3 else 0),
        out_shape=[jax.ShapeDtypeStruct((count, width), BF16), jax.ShapeDtypeStruct(share, F32)],
        in_specs=vmem(3),
        out_specs=vmem(2),
        compiler_params=pltpu.CompilerParams(vmem_limit_bytes=VMEM_BYTES),
        cost_estimate=pl.CostEstimate(
            flops=2 * count * routed.size,
            bytes_accessed=4 * count * width + 2 * routed.size,
            transcendentals=0,
        ),
        name="norm",
    )(patches, gain, routed)


def window_kernel(g_ref, q_ref, k_ref, v_ref, probs_ref, probs_t_ref, dq_ref, dk_ref, dv_ref):
    width = g_ref.shape[1]
    windows = head_windows()
    scores, scores_t, probs_t = [], [], []
    for head, (low, high, start, stop) in enumerate(windows):
        g = masked(g_ref[:, start:stop], low, high, start, stop)
        v = v_ref[:, start:stop]
        found = []
        for ref, grads, axis in (
            (probs_ref, dot(g, v, (1, 1)), 1),
            (probs_t_ref, dot(v, g, (1, 1)), 0),
        ):
            probs = ref[head]
            rounded = probs.astype(BF16)
            delta = jnp.sum(rounded.astype(F32) * grads, axis=axis, keepdims=True)
            found.append(((probs * (grads - delta)).astype(BF16), rounded))
        scores.append(found[0][0])
        scores_t.append(found[1][0])
        probs_t.append(found[1][1])
    scale = 1.0 / math.sqrt(HEAD_DIM)
    for start in range(0, width, LANES):
        stop = start + LANES
        heads = [h for h, (low, high, _, _) in enumerate(windows) if low < stop and high > start]
        for out, left, right_ref, factor in (
            (dq_ref, scores, k_ref, scale),
            (dk_ref, scores_t, q_ref, scale),
            (dv_ref, probs_t, g_ref, 1.0),
        ):
            right = right_ref[:, start:stop]
            rows = [masked(right, windows[h][0], windows[h][1], start, stop) for h in heads]
            product = dot(
                jnp.concatenate([left[h] for h in heads], axis=1),
                jnp.concatenate(rows, axis=0),
                (1, 0),
            )
            out[:, start:stop] = (product * factor).astype(BF16)


def window_backward(out_grads, queries, keys, values, probs, probs_t):
    patches, width = queries.shape
    shape = jax.ShapeDtypeStruct((patches, width), BF16)
    return pl.pallas_call(
        window_kernel,
        out_shape=[shape] * 3,
        in_specs=vmem(6),
        out_specs=vmem(3),
        compiler_params=pltpu.CompilerParams(vmem_limit_bytes=VMEM_BYTES),
        cost_estimate=pl.CostEstimate(
            flops=10 * HEADS * patches * patches * LANES,
            bytes_accessed=8 * HEADS * patches * patches + 14 * patches * width,
            transcendentals=0,
        ),
        name="window",
    )(out_grads, queries, keys, values, probs, probs_t)


def body(llm_grads, token_target, patches, gain, w_down, queries, keys, values, window_ids):
    grad_rows = llm_grads[0]
    rows = grad_rows.shape[0]
    images, peers = lax.axis_size("img"), lax.axis_size("seq")
    devices = images * peers
    capacity = max(1, 2 * rows // peers)
    block = w_down.shape[1]
    width = patches.shape[2]
    pieces = block // peers // LANES
    carries = pieces > 0 and 3 * pieces <= capacity

    order = [0]
    while len(order) < images:
        order = [2 * j for j in order] + [2 * j + 1 for j in order]
    image = lax.axis_index("img")

    def columns(j):
        return lax.dynamic_slice(grad_rows, (0, (image ^ j) * block), (rows, block))

    x_blocks = [columns(0)] + [swap(columns(j), "img", j) for j in range(1, images)]
    x_blocks = [x_blocks[j] for j in order]
    probs, probs_t = window_probs(queries[0], keys[0], window_ids[0])

    terms, first = [], 0
    for index, count in enumerate(CHUNKS):
        w_rows = lax.slice_in_dim(w_down, first, first + count * width)
        w_rows = pltpu.with_memory_space_constraint(w_rows, pltpu.VMEM)
        first += count * width
        kept, sent, *sums = project(x_blocks, w_rows, index == 0)
        if index == 0:
            bias_part = sums[0]
        mask = 1
        while 2 * mask < images:
            kept, sent = halve(kept, swap(sent, "img", mask))
            mask *= 2
        terms.append((kept, swap(sent, "img", mask)))
    packed = pack(terms, token_target, bias_part, peers, capacity, carries)
    routed = exchange(packed, "seq", peers)

    gain_rows = width // LANES
    share = (devices, gain_rows + pieces, LANES) if carries else (1, width)
    out_grads, shared = norm_backward(routed, peers, patches[0], gain[None], share)
    if carries:
        shared = exchange(shared, ("img", "seq"), devices)
        gain_total = jnp.sum(shared[:, :gain_rows], axis=0).reshape(-1)
        bias_total = shared[:, gain_rows:].reshape(-1)
    else:
        gain_total = lax.psum(shared[0], ("img", "seq"))
        bias_total = lax.all_gather(lax.psum(bias_part[0], "seq"), "img", tiled=True)
    grads = window_backward(out_grads, queries[0], keys[0], values[0], probs, probs_t)
    gain_grad = gain_total / math.sqrt(devices * patches.shape[1])
    bias_grad = bias_total / math.sqrt(devices * rows)
    return (grads[0][None], grads[1][None], grads[2][None], gain_grad, bias_grad)


def solution(mesh):
    return jax.shard_map(
        body,
        mesh=mesh,
        in_specs=(
            P("img", "seq", None),
            P("img", "seq"),
            P("img", "seq", None),
            P(),
            P(None, "img"),
            P("img", "seq", None),
            P("img", "seq", None),
            P("img", "seq", None),
            P("img", "seq", None),
        ),
        out_specs=(P("img", "seq", None), P("img", "seq", None), P("img", "seq", None), P(), P()),
        check_vma=False,
    )
```

```python
import functools
import math

import jax
import jax.numpy as jnp
from jax import lax
from jax.experimental import pallas as pl
from jax.experimental.pallas import tpu as pltpu
from jax.sharding import PartitionSpec as P

HEADS = 16
HEAD_DIM = 80
LANES = 128
CHUNKS = (2, 2)
DIRECT = 8
VMEM_BYTES = 32 * 1024 * 1024

F32 = jnp.float32
BF16 = jnp.bfloat16


def iota(shape, axis):
    return lax.broadcasted_iota(jnp.int32, shape, axis)


def dot(a, b, over):
    return lax.dot_general(a, b, ((over[:1], over[1:]), ((), ())), preferred_element_type=F32)


def vmem(count):
    return [pl.BlockSpec(memory_space=pltpu.VMEM)] * count


def head_windows():
    windows = []
    for head in range(HEADS):
        low, high = head * HEAD_DIM, (head + 1) * HEAD_DIM
        start = low // LANES * LANES
        windows.append((low, high, start, -(-high // LANES) * LANES))
    return windows


def lane_mask(low, high, start, stop):
    at = iota((1, stop - start), 1) + start
    return jnp.logical_and(at >= low, at < high)


def masked(x, low, high, start, stop):
    return jnp.where(lane_mask(low, high, start, stop), x, jnp.zeros_like(x))


def project_kernel(blocks, first, tile, tiles, with_sum, *refs):
    x_refs, w_ref = refs[:blocks], refs[blocks]
    keep_ref, send_ref = refs[blocks + 1 : blocks + 3]
    w_tiles, sems = refs[-2:]
    copies = [
        pltpu.make_async_copy(w_ref.at[pl.ds(first + t * tile, tile)], w_tiles.at[t], sems.at[t])
        for t in range(tiles)
    ]
    for t, copy in enumerate(copies):
        copy.start(priority=t % 2)
    x = jnp.concatenate([ref[...] for ref in x_refs], axis=0)
    if with_sum:
        refs[blocks + 3][...] = dot(jnp.ones((16, x.shape[0]), BF16), x, (1, 0))[:1]
    x = x.T
    half = keep_ref.shape[0]
    for t in range(tiles):
        copies[t].wait()
        product = dot(w_tiles[t], x, (1, 0)).T.astype(BF16)
        keep_ref[:, t * tile : (t + 1) * tile] = product[:half]
        send_ref[:, t * tile : (t + 1) * tile] = product[half:]


def project(x_blocks, w_down, first, width, with_sum):
    blocks, (rows, depth) = len(x_blocks), x_blocks[0].shape
    tile = 256
    tiles = width // tile
    out_shape = [jax.ShapeDtypeStruct((blocks * rows // 2, width), BF16)] * 2
    if with_sum:
        out_shape = out_shape + [jax.ShapeDtypeStruct((1, depth), F32)]
    return pl.pallas_call(
        functools.partial(project_kernel, blocks, first, tile, tiles, with_sum),
        out_shape=out_shape,
        in_specs=vmem(blocks) + [pl.BlockSpec(memory_space=pl.ANY)],
        out_specs=vmem(len(out_shape)),
        scratch_shapes=[
            pltpu.VMEM((tiles, tile, depth), BF16),
            pltpu.SemaphoreType.DMA((tiles,)),
        ],
        compiler_params=pltpu.CompilerParams(vmem_limit_bytes=VMEM_BYTES),
        cost_estimate=pl.CostEstimate(
            flops=2 * blocks * rows * depth * width,
            bytes_accessed=2 * width * depth,
            transcendentals=0,
        ),
        name="project",
    )(*x_blocks, w_down)


def halve_kernel(kept_ref, got_ref, keep_ref, send_ref):
    half = keep_ref.shape[0]
    keep_ref[...] = kept_ref[:half].astype(F32) + got_ref[:half].astype(F32)
    send_ref[...] = (kept_ref[half:].astype(F32) + got_ref[half:].astype(F32)).astype(BF16)


def halve(kept, got):
    rows, width = kept.shape
    return pl.pallas_call(
        halve_kernel,
        out_shape=[
            jax.ShapeDtypeStruct((rows // 2, width), F32),
            jax.ShapeDtypeStruct((rows // 2, width), BF16),
        ],
        in_specs=vmem(2),
        out_specs=vmem(2),
        compiler_params=pltpu.CompilerParams(vmem_limit_bytes=VMEM_BYTES),
        cost_estimate=pl.CostEstimate(
            flops=rows * width, bytes_accessed=7 * rows * width, transcendentals=0
        ),
        name="halve",
    )(kept, got)


def pack_kernel(peers, capacity, chunks, targets_ref, *refs):
    terms, out_ref = refs[: 2 * chunks], refs[-1]
    targets = targets_ref[...]
    rows = targets.shape[1]
    dest = targets // rows
    dest_column = jnp.sum(
        jnp.where(iota((rows, rows), 0) == iota((rows, rows), 1), dest, 0), axis=1, keepdims=True
    )
    same_before = jnp.logical_and(dest_column == dest, iota((rows, rows), 0) < iota((rows, rows), 1))
    rank = jnp.sum(same_before.astype(jnp.int32), axis=0, keepdims=True)
    slots = peers * capacity
    slot = iota((slots, rows), 0)
    chosen = jnp.logical_and(dest == slot // capacity, rank == slot % capacity)
    selector = chosen.astype(F32).astype(BF16)
    at = 0
    for chunk in range(chunks):
        kept, got = terms[2 * chunk], terms[2 * chunk + 1]
        total = (kept[...].astype(F32) + got[...].astype(F32)).astype(BF16)
        width = total.shape[1]
        out_ref[:, at : at + width] = dot(selector, total, (1, 0)).astype(BF16)
        at += width


def pack(terms, targets, peers, capacity):
    rows = targets.shape[1]
    width = sum(kept.shape[1] for kept, _ in terms)
    operands = [targets] + [x for pair in terms for x in pair]
    return pl.pallas_call(
        functools.partial(pack_kernel, peers, capacity, len(terms)),
        out_shape=jax.ShapeDtypeStruct((peers * capacity, width), BF16),
        in_specs=vmem(len(operands)),
        out_specs=pl.BlockSpec(memory_space=pltpu.VMEM),
        compiler_params=pltpu.CompilerParams(vmem_limit_bytes=VMEM_BYTES),
        cost_estimate=pl.CostEstimate(
            flops=2 * rows * peers * capacity * width,
            bytes_accessed=(6 * rows + 2 * peers * capacity) * width,
            transcendentals=0,
        ),
        name="pack",
    )(*operands)


def spread_kernel(capacity, me_ref, targets_ref, patches_ref, out_ref, labels_ref):
    targets = targets_ref[:, 0, :]
    peers, rows = targets.shape
    dest = targets // rows
    local = (targets - dest * rows).astype(F32).astype(BF16)
    mine = (dest == me_ref[0]).astype(F32).astype(BF16)
    earlier = (iota((rows, rows), 0) < iota((rows, rows), 1)).astype(F32).astype(BF16)
    rank = dot(mine, earlier, (1, 0)).astype(BF16)
    slots = peers * capacity
    holder = (iota((slots, peers), 0) // capacity == iota((slots, peers), 1)).astype(F32).astype(BF16)
    mine, rank, local = (dot(holder, x, (1, 0)) for x in (mine, rank, local))
    place = (iota((slots, rows), 0) % capacity).astype(F32)
    chosen = jnp.logical_and(mine == 1.0, rank == place)
    label = jnp.sum(jnp.where(chosen, local + 1.0, 0.0), axis=1, keepdims=True) - 1.0
    labels_ref[...] = jnp.broadcast_to(label, (slots, LANES))
    patches, width = patches_ref.shape
    per_token = patches // rows
    label = label.astype(jnp.int32)
    held = patches_ref[...]
    for c in range(per_token):
        wanted = jnp.where(label < 0, -1, label * per_token + c)
        selector = (wanted == iota((slots, patches), 1)).astype(F32).astype(BF16)
        out_ref[:, c * width : (c + 1) * width] = dot(selector, held, (1, 0)).astype(BF16)


def spread(me, targets, patches, capacity):
    peers, _, rows = targets.shape
    count, width = patches.shape
    slots, wide = peers * capacity, count // rows * width
    return pl.pallas_call(
        functools.partial(spread_kernel, capacity),
        out_shape=[
            jax.ShapeDtypeStruct((slots, wide), BF16),
            jax.ShapeDtypeStruct((slots, LANES), F32),
        ],
        in_specs=[pl.BlockSpec(memory_space=pltpu.SMEM)] + vmem(2),
        out_specs=vmem(2),
        compiler_params=pltpu.CompilerParams(vmem_limit_bytes=VMEM_BYTES),
        cost_estimate=pl.CostEstimate(
            flops=2 * count * slots * wide,
            bytes_accessed=2 * (count * width + slots * wide),
            transcendentals=0,
        ),
        name="spread",
    )(me, targets, patches)


def share_kernel(width, packed_ref, patches_ref, sums_ref, out_ref):
    total = jnp.zeros((1, width), F32)
    for at in range(0, packed_ref.shape[1], width):
        inputs = patches_ref[:, at : at + width].astype(F32)
        inverse_rms = lax.rsqrt(jnp.mean(inputs * inputs, axis=1, keepdims=True) + 1e-06)
        terms = packed_ref[:, at : at + width].astype(F32) * (inputs * inverse_rms)
        total = total + jnp.sum(terms, axis=0, keepdims=True)
    out_ref[:, :width] = total
    out_ref[:, width:] = sums_ref[...]


def gain_and_bias_share(packed, patches, sums, width):
    return pl.pallas_call(
        functools.partial(share_kernel, width),
        out_shape=jax.ShapeDtypeStruct((1, width + sums.shape[1]), F32),
        in_specs=vmem(3),
        out_specs=pl.BlockSpec(memory_space=pltpu.VMEM),
        compiler_params=pltpu.CompilerParams(vmem_limit_bytes=VMEM_BYTES),
        cost_estimate=pl.CostEstimate(
            flops=6 * packed.size, bytes_accessed=4 * packed.size, transcendentals=0
        ),
        name="share",
    )(packed, patches, sums)


def swap(x, axis, mask):
    n = lax.axis_size(axis)
    return lax.ppermute(x, axis, [(i, i ^ mask) for i in range(n)])


def exchange(x, axis, pieces):
    shape = x.shape
    if x.ndim == 2:
        x = x.reshape(pieces, -1, shape[1])
    return lax.all_to_all(x, axis, split_axis=0, concat_axis=0, tiled=True).reshape(shape)


def probs_kernel(q_ref, k_ref, ids_ref, probs_ref, probs_t_ref):
    patches = q_ref.shape[0]
    ids = ids_ref[...]
    per_token = patches // ids.shape[1]
    token = iota((patches, ids.shape[1]), 0) // per_token
    column = jnp.sum(
        jnp.where(token == iota((patches, ids.shape[1]), 1), ids, 0), axis=1, keepdims=True
    )
    square = (patches, patches)
    row = jnp.sum(
        jnp.where(iota(square, 0) == iota(square, 1), column, 0), axis=0, keepdims=True
    )
    allowed = column == row
    scale = 1.0 / math.sqrt(HEAD_DIM)
    for head, (low, high, start, stop) in enumerate(head_windows()):
        q = masked(q_ref[:, start:stop], low, high, start, stop)
        k = k_ref[:, start:stop]
        for out, scores, axis in (
            (probs_ref, dot(q, k, (1, 1)), 1),
            (probs_t_ref, dot(k, q, (1, 1)), 0),
        ):
            scores = jnp.where(allowed, scores * scale, -jnp.inf)
            weights = jnp.exp(scores - jnp.max(scores, axis=axis, keepdims=True))
            out[head] = weights / jnp.sum(weights, axis=axis, keepdims=True)


def window_probs(queries, keys, ids):
    patches = queries.shape[0]
    shape = jax.ShapeDtypeStruct((HEADS, patches, patches), F32)
    return pl.pallas_call(
        probs_kernel,
        out_shape=[shape, shape],
        in_specs=vmem(3),
        out_specs=vmem(2),
        compiler_params=pltpu.CompilerParams(vmem_limit_bytes=VMEM_BYTES),
        cost_estimate=pl.CostEstimate(
            flops=8 * HEADS * patches * patches * LANES,
            bytes_accessed=8 * HEADS * patches * patches,
            transcendentals=2 * HEADS * patches * patches,
        ),
        name="probs",
    )(queries, keys, ids)


def norm_kernel(patches_ref, gain_ref, labels_ref, routed_ref, out_ref):
    patches, width = patches_ref.shape
    slots = routed_ref.shape[0]
    per_token = routed_ref.shape[1] // width
    columns = [routed_ref[:, c * width : (c + 1) * width].astype(F32) for c in range(per_token)]
    held = jnp.concatenate(columns, axis=0).astype(BF16)
    lanes = per_token * slots
    lane = iota((slots, lanes), 1)
    row_of_lane = jnp.sum(
        jnp.where(lane % slots == iota((slots, lanes), 0), labels_ref[:, :1], 0.0),
        axis=0,
        keepdims=True,
    ).astype(jnp.int32)
    patch_of_lane = row_of_lane * per_token + iota((1, lanes), 1) // slots
    patch_of_lane = jnp.where(row_of_lane < 0, -1, patch_of_lane)
    chosen = patch_of_lane == iota((patches, lanes), 0)
    patch_grads = dot(chosen.astype(F32).astype(BF16), held, (1, 0))
    inputs = patches_ref[...].astype(F32)
    inverse_rms = lax.rsqrt(jnp.mean(inputs * inputs, axis=1, keepdims=True) + 1e-06)
    normed = inputs * inverse_rms
    scaled = gain_ref[...] * patch_grads
    out_ref[...] = (
        inverse_rms * (scaled - normed * jnp.mean(scaled * normed, axis=1, keepdims=True))
    ).astype(BF16)


def norm_backward(routed, labels, patches, gain):
    count, width = patches.shape
    return pl.pallas_call(
        norm_kernel,
        out_shape=jax.ShapeDtypeStruct((count, width), BF16),
        in_specs=vmem(4),
        out_specs=pl.BlockSpec(memory_space=pltpu.VMEM),
        compiler_params=pltpu.CompilerParams(vmem_limit_bytes=VMEM_BYTES),
        cost_estimate=pl.CostEstimate(
            flops=2 * count * routed.size,
            bytes_accessed=4 * count * width + 2 * routed.size,
            transcendentals=0,
        ),
        name="norm",
    )(patches, gain, labels, routed)


def window_kernel(g_ref, q_ref, k_ref, v_ref, probs_ref, probs_t_ref, dq_ref, dk_ref, dv_ref):
    width = g_ref.shape[1]
    windows = head_windows()
    scores, scores_t, probs_t = [], [], []
    for head, (low, high, start, stop) in enumerate(windows):
        g = masked(g_ref[:, start:stop], low, high, start, stop)
        v = v_ref[:, start:stop]
        found = []
        for ref, grads, axis in (
            (probs_ref, dot(g, v, (1, 1)), 1),
            (probs_t_ref, dot(v, g, (1, 1)), 0),
        ):
            probs = ref[head]
            rounded = probs.astype(BF16)
            delta = jnp.sum(rounded.astype(F32) * grads, axis=axis, keepdims=True)
            found.append(((probs * (grads - delta)).astype(BF16), rounded))
        scores.append(found[0][0])
        scores_t.append(found[1][0])
        probs_t.append(found[1][1])
    scale = 1.0 / math.sqrt(HEAD_DIM)
    for start in range(0, width, LANES):
        stop = start + LANES
        heads = [h for h, (low, high, _, _) in enumerate(windows) if low < stop and high > start]
        for out, left, right_ref, factor in (
            (dq_ref, scores, k_ref, scale),
            (dk_ref, scores_t, q_ref, scale),
            (dv_ref, probs_t, g_ref, 1.0),
        ):
            right = right_ref[:, start:stop]
            rows = [masked(right, windows[h][0], windows[h][1], start, stop) for h in heads]
            product = dot(
                jnp.concatenate([left[h] for h in heads], axis=1),
                jnp.concatenate(rows, axis=0),
                (1, 0),
            )
            out[:, start:stop] = (product * factor).astype(BF16)


def window_backward(out_grads, queries, keys, values, probs, probs_t):
    patches, width = queries.shape
    shape = jax.ShapeDtypeStruct((patches, width), BF16)
    return pl.pallas_call(
        window_kernel,
        out_shape=[shape] * 3,
        in_specs=vmem(6),
        out_specs=vmem(3),
        compiler_params=pltpu.CompilerParams(vmem_limit_bytes=VMEM_BYTES),
        cost_estimate=pl.CostEstimate(
            flops=10 * HEADS * patches * patches * LANES,
            bytes_accessed=8 * HEADS * patches * patches + 14 * patches * width,
            transcendentals=0,
        ),
        name="window",
    )(out_grads, queries, keys, values, probs, probs_t)


def finish_kernel(blocks, width, image_ref, *refs):
    shares, (gain_ref, bias_ref) = refs[:blocks], refs[blocks:]
    gains = [ref[:, :width] for ref in shares]
    while len(gains) > 1:
        gains = [gains[i] + gains[i + 1] for i in range(0, len(gains), 2)]
    gain_ref[...] = gains[0]
    for j in range(blocks):
        bias_ref[pl.ds(image_ref[0] ^ j, 1), :] = shares[j][:, width:]


def sum_shares(share, width):
    images, peers = lax.axis_size("img"), lax.axis_size("seq")
    block = share.shape[1] - width
    if max(images, peers) > DIRECT:
        gain = lax.psum(share[0, :width], ("img", "seq"))
        bias = lax.all_gather(lax.psum(share[0, width:], "seq"), "img", tiled=True)
        return gain, bias
    mask = 1
    while mask < peers:
        share = share + swap(share, "seq", mask)
        mask *= 2
    shares = [share] + [swap(share, "img", j) for j in range(1, images)]
    gain, bias = pl.pallas_call(
        functools.partial(finish_kernel, images, width),
        out_shape=[
            jax.ShapeDtypeStruct((1, width), F32),
            jax.ShapeDtypeStruct((images, block), F32),
        ],
        in_specs=[pl.BlockSpec(memory_space=pltpu.SMEM)] + vmem(images),
        out_specs=vmem(2),
        name="finish",
    )(lax.axis_index("img").reshape(1), *shares)
    return gain[0], bias.reshape(-1)


def body(llm_grads, token_target, patches, gain, w_down, queries, keys, values, window_ids):
    grad_rows = llm_grads[0]
    rows = grad_rows.shape[0]
    images, peers = lax.axis_size("img"), lax.axis_size("seq")
    image, me = lax.axis_index("img"), lax.axis_index("seq")
    capacity = max(1, 2 * rows // peers)
    block = w_down.shape[1]
    width = patches.shape[2]

    order = [0]
    while len(order) < images:
        order = [2 * j for j in order] + [2 * j + 1 for j in order]

    def columns(j):
        return lax.dynamic_slice(grad_rows, (0, (image ^ j) * block), (rows, block))

    x_blocks = [columns(0)] + [swap(columns(j), "img", j) for j in range(1, images)]

    targets = exchange(jnp.broadcast_to(token_target[None], (peers, 1, rows)), "seq", peers)
    spread_patches, labels = spread(me.reshape(1), targets, patches[0], capacity)
    slot_patches = exchange(spread_patches, "seq", peers)
    probs, probs_t = window_probs(queries[0], keys[0], window_ids[0])
    x_blocks, spread_patches = lax.optimization_barrier((x_blocks, spread_patches))

    terms, first = [], 0
    for index, count in enumerate(CHUNKS):
        kept, sent, *sums = project(
            [x_blocks[j] for j in order], w_down, first, count * width, index == 0
        )
        first += count * width
        if index == 0:
            bias_part = sums[0]
        mask = 1
        while 2 * mask < images:
            kept, sent = halve(kept, swap(sent, "img", mask))
            mask *= 2
        terms.append((kept, swap(sent, "img", mask)))
    packed = pack(terms, token_target, peers, capacity)
    routed = exchange(packed, "seq", peers)

    share = gain_and_bias_share(packed, slot_patches, bias_part, width)
    gain_total, bias_total = sum_shares(share, width)
    out_grads = norm_backward(routed, labels, patches[0], gain[None])
    grads = window_backward(out_grads, queries[0], keys[0], values[0], probs, probs_t)
    gain_grad = gain_total / math.sqrt(images * peers * patches.shape[1])
    bias_grad = bias_total / math.sqrt(images * peers * rows)
    return (grads[0][None], grads[1][None], grads[2][None], gain_grad, bias_grad)


def solution(mesh):
    return jax.shard_map(
        body,
        mesh=mesh,
        in_specs=(
            P("img", "seq", None),
            P("img", "seq"),
            P("img", "seq", None),
            P(),
            P(None, "img"),
            P("img", "seq", None),
            P("img", "seq", None),
            P("img", "seq", None),
            P("img", "seq", None),
        ),
        out_specs=(P("img", "seq", None), P("img", "seq", None), P("img", "seq", None), P(), P()),
        check_vma=False,
    )
```

```python
import functools
import math

import jax
import jax.numpy as jnp
from jax import lax
from jax.experimental import pallas as pl
from jax.experimental.pallas import tpu as pltpu
from jax.sharding import PartitionSpec as P

HEADS = 16
HEAD_DIM = 80
LANES = 128
CHUNKS = (2, 2)
DIRECT = 8
VMEM_BYTES = 24 * 1024 * 1024

F32 = jnp.float32
BF16 = jnp.bfloat16


def iota(shape, axis):
    return lax.broadcasted_iota(jnp.int32, shape, axis)


def dot(a, b, over):
    return lax.dot_general(a, b, ((over[:1], over[1:]), ((), ())), preferred_element_type=F32)


def vmem(count):
    return [pl.BlockSpec(memory_space=pltpu.VMEM)] * count


def head_windows():
    windows = []
    for head in range(HEADS):
        low, high = head * HEAD_DIM, (head + 1) * HEAD_DIM
        start = low // LANES * LANES
        windows.append((low, high, start, -(-high // LANES) * LANES))
    return windows


def lane_mask(low, high, start, stop):
    at = iota((1, stop - start), 1) + start
    return jnp.logical_and(at >= low, at < high)


def masked(x, low, high, start, stop):
    return jnp.where(lane_mask(low, high, start, stop), x, jnp.zeros_like(x))


def project_kernel(blocks, tile, with_sum, *refs):
    x_refs, w_ref = refs[:blocks], refs[blocks]
    keep_ref, send_ref = refs[blocks + 1 : blocks + 3]
    x = jnp.concatenate([ref[...] for ref in x_refs], axis=0)
    if with_sum:
        refs[blocks + 3][...] = dot(jnp.ones((16, x.shape[0]), BF16), x, (1, 0))[:1]
    x = x.T
    half = keep_ref.shape[0]
    for t in range(0, w_ref.shape[0], tile):
        product = dot(w_ref[t : t + tile], x, (1, 0)).T.astype(BF16)
        keep_ref[:, t : t + tile] = product[:half]
        send_ref[:, t : t + tile] = product[half:]


def project(x_blocks, w_rows, with_sum):
    blocks, (rows, depth) = len(x_blocks), x_blocks[0].shape
    width = w_rows.shape[0]
    tile = 512
    while width % tile:
        tile //= 2
    out_shape = [jax.ShapeDtypeStruct((blocks * rows // 2, width), BF16)] * 2
    if with_sum:
        out_shape = out_shape + [jax.ShapeDtypeStruct((1, depth), F32)]
    return pl.pallas_call(
        functools.partial(project_kernel, blocks, tile, with_sum),
        out_shape=out_shape,
        in_specs=vmem(blocks + 1),
        out_specs=vmem(len(out_shape)),
        compiler_params=pltpu.CompilerParams(vmem_limit_bytes=VMEM_BYTES),
        cost_estimate=pl.CostEstimate(
            flops=2 * blocks * rows * depth * width,
            bytes_accessed=2 * width * depth,
            transcendentals=0,
        ),
        name="project",
    )(*x_blocks, w_rows)


def halve_kernel(kept_ref, got_ref, keep_ref, send_ref):
    half = keep_ref.shape[0]
    keep_ref[...] = kept_ref[:half].astype(F32) + got_ref[:half].astype(F32)
    send_ref[...] = (kept_ref[half:].astype(F32) + got_ref[half:].astype(F32)).astype(BF16)


def halve(kept, got):
    rows, width = kept.shape
    return pl.pallas_call(
        halve_kernel,
        out_shape=[
            jax.ShapeDtypeStruct((rows // 2, width), F32),
            jax.ShapeDtypeStruct((rows // 2, width), BF16),
        ],
        in_specs=vmem(2),
        out_specs=vmem(2),
        compiler_params=pltpu.CompilerParams(vmem_limit_bytes=VMEM_BYTES),
        cost_estimate=pl.CostEstimate(
            flops=rows * width, bytes_accessed=7 * rows * width, transcendentals=0
        ),
        name="halve",
    )(kept, got)


def pack_kernel(peers, capacity, direct, labelled, carries, me_ref, targets_ref, kept_ref, got_ref, *refs):
    outs = refs[1:] if carries else refs
    targets = targets_ref[...]
    rows = targets.shape[1]
    dest = targets // rows
    local = targets - dest * rows
    dest_column = jnp.sum(
        jnp.where(iota((rows, rows), 0) == iota((rows, rows), 1), dest, 0), axis=1, keepdims=True
    )
    same_before = jnp.logical_and(dest_column == dest, iota((rows, rows), 0) < iota((rows, rows), 1))
    rank = jnp.sum(same_before.astype(jnp.int32), axis=0, keepdims=True)
    slots = peers * capacity
    slot = iota((slots, rows), 0)
    holder = slot // capacity
    if direct:
        holder = holder ^ me_ref[0]
    chosen = jnp.logical_and(dest == holder, rank == slot % capacity)
    total = (kept_ref[...].astype(F32) + got_ref[...].astype(F32)).astype(BF16)
    parts = [dot(chosen.astype(F32).astype(BF16), total, (1, 0))]
    if labelled:
        label = jnp.sum(jnp.where(chosen, local + 1, 0), axis=1, keepdims=True) - 1
        parts.append(jnp.broadcast_to(label.astype(F32), (slots, LANES)))
    if carries:
        sums = refs[0][...]
        high = sums.astype(BF16).astype(F32)
        middle = (sums - high).astype(BF16).astype(F32)
        low = (sums - high - middle).astype(BF16).astype(F32)
        extra = jnp.zeros((slots, LANES), F32)
        row = iota((slots, LANES), 0) % capacity
        peer = iota((slots, LANES), 0) // capacity
        if direct:
            peer = peer ^ me_ref[0]
        pieces = sums.shape[1] // peers // LANES
        for p in range(peers):
            for level, values in enumerate((high, middle, low)):
                for piece in range(pieces):
                    start = (p * pieces + piece) * LANES
                    line = jnp.broadcast_to(values[:, start : start + LANES], (slots, LANES))
                    here = jnp.logical_and(peer == p, row == level * pieces + piece)
                    extra = jnp.where(here, line, extra)
        parts.append(extra)
    packed = jnp.concatenate(parts, axis=1) if len(parts) > 1 else parts[0]
    if not direct:
        outs[0][...] = packed.astype(BF16)
        return
    for m in range(peers):
        outs[m][...] = packed[m * capacity : (m + 1) * capacity].astype(BF16)


def pack(kept, got, targets, me, sums, peers, capacity, direct, labelled):
    rows, width = kept.shape
    width = width + (LANES if labelled else 0) + (0 if sums is None else LANES)
    operands = [me, targets, kept, got] + ([] if sums is None else [sums])
    if direct:
        out_shape = [jax.ShapeDtypeStruct((capacity, width), BF16)] * peers
    else:
        out_shape = [jax.ShapeDtypeStruct((peers * capacity, width), BF16)]
    return pl.pallas_call(
        functools.partial(pack_kernel, peers, capacity, direct, labelled, sums is not None),
        out_shape=out_shape,
        in_specs=[pl.BlockSpec(memory_space=pltpu.SMEM)] + vmem(len(operands) - 1),
        out_specs=vmem(len(out_shape)),
        compiler_params=pltpu.CompilerParams(vmem_limit_bytes=VMEM_BYTES),
        cost_estimate=pl.CostEstimate(
            flops=2 * rows * peers * capacity * width,
            bytes_accessed=(6 * rows + 2 * peers * capacity) * width,
            transcendentals=0,
        ),
        name="pack",
    )(*operands)


def route(packed, peers, direct):
    if not direct:
        return [exchange(packed[0], "seq", peers)]
    routed = {0: packed[0]}
    half = peers // 2
    for near in range(half):
        for m in (half + near, near):
            if m:
                routed[m] = swap(packed[m], "seq", m)
    return [routed[m] for m in range(peers)]


def swap(x, axis, mask):
    n = lax.axis_size(axis)
    return lax.ppermute(x, axis, [(i, i ^ mask) for i in range(n)])


def exchange(x, axis, pieces):
    shape = x.shape
    if x.ndim == 2:
        x = x.reshape(pieces, -1, shape[1])
    return lax.all_to_all(x, axis, split_axis=0, concat_axis=0, tiled=True).reshape(shape)


def probs_kernel(q_ref, k_ref, ids_ref, probs_ref, probs_t_ref):
    patches = q_ref.shape[0]
    ids = ids_ref[...]
    per_token = patches // ids.shape[1]
    token = iota((patches, ids.shape[1]), 0) // per_token
    column = jnp.sum(
        jnp.where(token == iota((patches, ids.shape[1]), 1), ids, 0), axis=1, keepdims=True
    )
    square = (patches, patches)
    row = jnp.sum(
        jnp.where(iota(square, 0) == iota(square, 1), column, 0), axis=0, keepdims=True
    )
    allowed = column == row
    scale = 1.0 / math.sqrt(HEAD_DIM)
    for head, (low, high, start, stop) in enumerate(head_windows()):
        q = masked(q_ref[:, start:stop], low, high, start, stop)
        k = k_ref[:, start:stop]
        for out, scores, axis in (
            (probs_ref, dot(q, k, (1, 1)), 1),
            (probs_t_ref, dot(k, q, (1, 1)), 0),
        ):
            scores = jnp.where(allowed, scores * scale, -jnp.inf)
            weights = jnp.exp(scores - jnp.max(scores, axis=axis, keepdims=True))
            out[head] = weights / jnp.sum(weights, axis=axis, keepdims=True)


def window_probs(queries, keys, ids):
    patches = queries.shape[0]
    shape = jax.ShapeDtypeStruct((HEADS, patches, patches), F32)
    return pl.pallas_call(
        probs_kernel,
        out_shape=[shape, shape],
        in_specs=vmem(3),
        out_specs=vmem(2),
        compiler_params=pltpu.CompilerParams(vmem_limit_bytes=VMEM_BYTES),
        cost_estimate=pl.CostEstimate(
            flops=8 * HEADS * patches * patches * LANES,
            bytes_accessed=8 * HEADS * patches * patches,
            transcendentals=2 * HEADS * patches * patches,
        ),
        name="probs",
    )(queries, keys, ids)


def norm_kernel(counts, parts, capacity, share, patches_ref, gain_ref, *refs):
    chunks, at = [], 0
    for count in counts:
        pieces = [ref[...].astype(F32) for ref in refs[at : at + count]]
        chunks.append(jnp.concatenate(pieces, axis=0) if count > 1 else pieces[0])
        at += count
    out_ref, share_ref = refs[at:]
    patches, width = patches_ref.shape
    slots = chunks[0].shape[0]
    columns = []
    for chunk, count in zip(chunks, parts):
        columns += [chunk[:, c * width : (c + 1) * width] for c in range(count)]
    per_token = len(columns)
    held = jnp.concatenate(columns, axis=0).astype(BF16)
    labels = chunks[0][:, parts[0] * width : parts[0] * width + 1]
    lanes = per_token * slots
    lane = iota((slots, lanes), 1)
    row_of_lane = jnp.sum(
        jnp.where(lane % slots == iota((slots, lanes), 0), labels, 0.0), axis=0, keepdims=True
    ).astype(jnp.int32)
    patch_of_lane = row_of_lane * per_token + iota((1, lanes), 1) // slots
    patch_of_lane = jnp.where(row_of_lane < 0, -1, patch_of_lane)
    chosen = patch_of_lane == iota((patches, lanes), 0)
    patch_grads = dot(chosen.astype(F32).astype(BF16), held, (1, 0))
    inputs = patches_ref[...].astype(F32)
    inverse_rms = lax.rsqrt(jnp.mean(inputs * inputs, axis=1, keepdims=True) + 1e-06)
    normed = inputs * inverse_rms
    gain_part = jnp.sum(patch_grads * normed, axis=0, keepdims=True)
    copies = share_ref.shape[0]
    share_ref[:, :, :width] = jnp.broadcast_to(gain_part[None], (copies, 1, width))
    if share:
        carried = chunks[0][:, parts[0] * width + LANES :]
        row = iota((slots, LANES), 0) % capacity
        for piece in range(share):
            kept = jnp.logical_and(row % share == piece, row < 3 * share)
            line = jnp.sum(jnp.where(kept, carried, 0.0), axis=0, keepdims=True)
            share_ref[:, :, width + piece * LANES : width + (piece + 1) * LANES] = jnp.broadcast_to(
                line[None], (copies, 1, LANES)
            )
    scaled = gain_ref[...] * patch_grads
    out_ref[...] = (
        inverse_rms * (scaled - normed * jnp.mean(scaled * normed, axis=1, keepdims=True))
    ).astype(BF16)


def norm_backward(received, parts, capacity, patches, gain, copies, share):
    counts = [len(chunk) for chunk in received]
    flat = [x for chunk in received for x in chunk]
    count, width = patches.shape
    routed = sum(x.size for x in flat)
    return pl.pallas_call(
        functools.partial(norm_kernel, counts, parts, capacity, share),
        out_shape=[
            jax.ShapeDtypeStruct((count, width), BF16),
            jax.ShapeDtypeStruct((copies, 1, width + share * LANES), F32),
        ],
        in_specs=vmem(2 + len(flat)),
        out_specs=vmem(2),
        compiler_params=pltpu.CompilerParams(vmem_limit_bytes=VMEM_BYTES),
        cost_estimate=pl.CostEstimate(
            flops=2 * count * routed,
            bytes_accessed=4 * count * width + 2 * routed,
            transcendentals=0,
        ),
        name="norm",
    )(patches, gain, *flat)


def gather_kernel(width, shared_ref, out_ref):
    copies, _, wide = shared_ref.shape
    total = shared_ref[0, :, :width]
    for copy in range(1, copies):
        total = total + shared_ref[copy, :, :width]
    out_ref[:, :width] = total
    piece = wide - width
    for copy in range(copies):
        at = width + copy * piece
        out_ref[:, at : at + piece] = shared_ref[copy, :, width:]


def finish_kernel(blocks, width, gain_scale, bias_scale, image_ref, *refs):
    shares, (gain_ref, bias_ref) = refs[:blocks], refs[blocks:]
    gains = [ref[:, :width] for ref in shares]
    while len(gains) > 1:
        gains = [gains[i] + gains[i + 1] for i in range(0, len(gains), 2)]
    gain_ref[...] = gains[0] * gain_scale
    for j in range(blocks):
        bias_ref[pl.ds(image_ref[0] ^ j, 1), :] = shares[j][:, width:] * bias_scale


def sum_shares(shared, width, gain_scale, bias_scale):
    images, peers = lax.axis_size("img"), lax.axis_size("seq")
    shared = exchange(shared, "seq", peers)
    piece = shared.shape[2] - width
    share = pl.pallas_call(
        functools.partial(gather_kernel, width),
        out_shape=jax.ShapeDtypeStruct((1, width + peers * piece), F32),
        in_specs=vmem(1),
        out_specs=pl.BlockSpec(memory_space=pltpu.VMEM),
        name="gather",
    )(shared)
    shares = [share] + [swap(share, "img", j) for j in range(1, images)]
    gain, bias = pl.pallas_call(
        functools.partial(finish_kernel, images, width, gain_scale, bias_scale),
        out_shape=[
            jax.ShapeDtypeStruct((1, width), F32),
            jax.ShapeDtypeStruct((images, peers * piece), F32),
        ],
        in_specs=[pl.BlockSpec(memory_space=pltpu.SMEM)] + vmem(images),
        out_specs=vmem(2),
        name="finish",
    )(lax.axis_index("img").reshape(1), *shares)
    return gain[0], bias.reshape(-1)


def window_kernel(g_ref, q_ref, k_ref, v_ref, probs_ref, probs_t_ref, dq_ref, dk_ref, dv_ref):
    width = g_ref.shape[1]
    windows = head_windows()
    scores, scores_t, probs_t = [], [], []
    for head, (low, high, start, stop) in enumerate(windows):
        g = masked(g_ref[:, start:stop], low, high, start, stop)
        v = v_ref[:, start:stop]
        found = []
        for ref, grads, axis in (
            (probs_ref, dot(g, v, (1, 1)), 1),
            (probs_t_ref, dot(v, g, (1, 1)), 0),
        ):
            probs = ref[head]
            rounded = probs.astype(BF16)
            delta = jnp.sum(rounded.astype(F32) * grads, axis=axis, keepdims=True)
            found.append(((probs * (grads - delta)).astype(BF16), rounded))
        scores.append(found[0][0])
        scores_t.append(found[1][0])
        probs_t.append(found[1][1])
    scale = 1.0 / math.sqrt(HEAD_DIM)
    for start in range(0, width, LANES):
        stop = start + LANES
        heads = [h for h, (low, high, _, _) in enumerate(windows) if low < stop and high > start]
        for out, left, right_ref, factor in (
            (dq_ref, scores, k_ref, scale),
            (dk_ref, scores_t, q_ref, scale),
            (dv_ref, probs_t, g_ref, 1.0),
        ):
            right = right_ref[:, start:stop]
            rows = [masked(right, windows[h][0], windows[h][1], start, stop) for h in heads]
            product = dot(
                jnp.concatenate([left[h] for h in heads], axis=1),
                jnp.concatenate(rows, axis=0),
                (1, 0),
            )
            out[:, start:stop] = (product * factor).astype(BF16)


def window_backward(out_grads, queries, keys, values, probs, probs_t):
    patches, width = queries.shape
    shape = jax.ShapeDtypeStruct((patches, width), BF16)
    return pl.pallas_call(
        window_kernel,
        out_shape=[shape] * 3,
        in_specs=vmem(6),
        out_specs=vmem(3),
        compiler_params=pltpu.CompilerParams(vmem_limit_bytes=VMEM_BYTES),
        cost_estimate=pl.CostEstimate(
            flops=10 * HEADS * patches * patches * LANES,
            bytes_accessed=8 * HEADS * patches * patches + 14 * patches * width,
            transcendentals=0,
        ),
        name="window",
    )(out_grads, queries, keys, values, probs, probs_t)


def body(llm_grads, token_target, patches, gain, w_down, queries, keys, values, window_ids):
    grad_rows = llm_grads[0]
    rows = grad_rows.shape[0]
    images, peers = lax.axis_size("img"), lax.axis_size("seq")
    capacity = max(1, 2 * rows // peers)
    block = w_down.shape[1]
    width = patches.shape[2]
    pieces = block // peers // LANES
    direct = max(images, peers) <= DIRECT and pieces > 0 and 3 * pieces <= capacity

    order = [0]
    while len(order) < images:
        order = [2 * j for j in order] + [2 * j + 1 for j in order]
    image, me = lax.axis_index("img"), lax.axis_index("seq")

    def columns(j):
        return lax.dynamic_slice(grad_rows, (0, (image ^ j) * block), (rows, block))

    x_blocks = [columns(0)] + [swap(columns(j), "img", j) for j in range(1, images)]
    x_blocks = [x_blocks[j] for j in order]
    probs, probs_t = window_probs(queries[0], keys[0], window_ids[0])
    token_target, probs, probs_t = lax.optimization_barrier((token_target, probs, probs_t))

    received, first = [], 0
    for index, count in enumerate(CHUNKS):
        w_rows = lax.slice_in_dim(w_down, first, first + count * width)
        w_rows = pltpu.with_memory_space_constraint(w_rows, pltpu.VMEM)
        first += count * width
        kept, sent, *sums = project(x_blocks, w_rows, index == 0)
        if index == 0:
            bias_part = sums[0]
        mask = 1
        while 2 * mask < images:
            kept, sent = halve(kept, swap(sent, "img", mask))
            mask *= 2
        got = swap(sent, "img", mask)
        carried = bias_part if index == 0 and direct else None
        packed = pack(
            kept, got, token_target, me.reshape(1), carried, peers, capacity, direct, index == 0
        )
        received.append(route(packed, peers, direct))

    gain_scale = 1.0 / math.sqrt(images * peers * patches.shape[1])
    bias_scale = 1.0 / math.sqrt(images * peers * rows)
    share, copies = (pieces, peers) if direct else (0, 1)
    out_grads, shared = norm_backward(
        received, CHUNKS, capacity, patches[0], gain[None], copies, share
    )
    if direct:
        gain_grad, bias_grad = sum_shares(shared, width, gain_scale, bias_scale)
    else:
        gain_grad = lax.psum(shared[0, 0], ("img", "seq")) * gain_scale
        bias_grad = lax.all_gather(lax.psum(bias_part[0], "seq"), "img", tiled=True) * bias_scale
    grads = window_backward(out_grads, queries[0], keys[0], values[0], probs, probs_t)
    return (grads[0][None], grads[1][None], grads[2][None], gain_grad, bias_grad)


def solution(mesh):
    return jax.shard_map(
        body,
        mesh=mesh,
        in_specs=(
            P("img", "seq", None),
            P("img", "seq"),
            P("img", "seq", None),
            P(),
            P(None, "img"),
            P("img", "seq", None),
            P("img", "seq", None),
            P("img", "seq", None),
            P("img", "seq", None),
        ),
        out_specs=(P("img", "seq", None), P("img", "seq", None), P("img", "seq", None), P(), P()),
        check_vma=False,
    )
```

```python
import functools
import math

import jax
import jax.numpy as jnp
from jax import lax
from jax.experimental import pallas as pl
from jax.experimental.pallas import tpu as pltpu
from jax.sharding import PartitionSpec as P

HEADS = 16
HEAD_DIM = 80
LANES = 128
CHUNKS = (2, 2)
DIRECT = 8
VMEM_BYTES = 24 * 1024 * 1024

F32 = jnp.float32
BF16 = jnp.bfloat16


def iota(shape, axis):
    return lax.broadcasted_iota(jnp.int32, shape, axis)


def dot(a, b, over):
    return lax.dot_general(a, b, ((over[:1], over[1:]), ((), ())), preferred_element_type=F32)


def vmem(count):
    return [pl.BlockSpec(memory_space=pltpu.VMEM)] * count


def head_windows():
    windows = []
    for head in range(HEADS):
        low, high = head * HEAD_DIM, (head + 1) * HEAD_DIM
        start = low // LANES * LANES
        windows.append((low, high, start, -(-high // LANES) * LANES))
    return windows


def lane_mask(low, high, start, stop):
    at = iota((1, stop - start), 1) + start
    return jnp.logical_and(at >= low, at < high)


def masked(x, low, high, start, stop):
    return jnp.where(lane_mask(low, high, start, stop), x, jnp.zeros_like(x))


def project_kernel(blocks, tile, with_sum, *refs):
    x_refs, w_ref = refs[:blocks], refs[blocks]
    keep_ref, send_ref = refs[blocks + 1 : blocks + 3]
    x = jnp.concatenate([ref[...] for ref in x_refs], axis=0)
    if with_sum:
        refs[blocks + 3][...] = dot(jnp.ones((16, x.shape[0]), BF16), x, (1, 0))[:1]
    x = x.T
    half = keep_ref.shape[0]
    for t in range(0, w_ref.shape[0], tile):
        product = dot(w_ref[t : t + tile], x, (1, 0)).T.astype(BF16)
        keep_ref[:, t : t + tile] = product[:half]
        send_ref[:, t : t + tile] = product[half:]


def project(x_blocks, w_rows, with_sum):
    blocks, (rows, depth) = len(x_blocks), x_blocks[0].shape
    width = w_rows.shape[0]
    tile = 512
    while width % tile:
        tile //= 2
    out_shape = [jax.ShapeDtypeStruct((blocks * rows // 2, width), BF16)] * 2
    if with_sum:
        out_shape = out_shape + [jax.ShapeDtypeStruct((1, depth), F32)]
    return pl.pallas_call(
        functools.partial(project_kernel, blocks, tile, with_sum),
        out_shape=out_shape,
        in_specs=vmem(blocks + 1),
        out_specs=vmem(len(out_shape)),
        compiler_params=pltpu.CompilerParams(vmem_limit_bytes=VMEM_BYTES),
        cost_estimate=pl.CostEstimate(
            flops=2 * blocks * rows * depth * width,
            bytes_accessed=2 * width * depth,
            transcendentals=0,
        ),
        name="project",
    )(*x_blocks, w_rows)


def halve_kernel(kept_ref, got_ref, keep_ref, send_ref):
    half = keep_ref.shape[0]
    keep_ref[...] = kept_ref[:half].astype(F32) + got_ref[:half].astype(F32)
    send_ref[...] = (kept_ref[half:].astype(F32) + got_ref[half:].astype(F32)).astype(BF16)


def halve(kept, got):
    rows, width = kept.shape
    return pl.pallas_call(
        halve_kernel,
        out_shape=[
            jax.ShapeDtypeStruct((rows // 2, width), F32),
            jax.ShapeDtypeStruct((rows // 2, width), BF16),
        ],
        in_specs=vmem(2),
        out_specs=vmem(2),
        compiler_params=pltpu.CompilerParams(vmem_limit_bytes=VMEM_BYTES),
        cost_estimate=pl.CostEstimate(
            flops=rows * width, bytes_accessed=7 * rows * width, transcendentals=0
        ),
        name="halve",
    )(kept, got)


def pack_kernel(peers, capacity, direct, chunks, me_ref, targets_ref, *refs):
    terms, outs = refs[: 2 * chunks], refs[2 * chunks :]
    targets = targets_ref[...]
    rows = targets.shape[1]
    dest = targets // rows
    local = targets - dest * rows
    dest_column = jnp.sum(
        jnp.where(iota((rows, rows), 0) == iota((rows, rows), 1), dest, 0), axis=1, keepdims=True
    )
    same_before = jnp.logical_and(dest_column == dest, iota((rows, rows), 0) < iota((rows, rows), 1))
    rank = jnp.sum(same_before.astype(jnp.int32), axis=0, keepdims=True)
    slots = peers * capacity
    slot = iota((slots, rows), 0)
    holder = slot // capacity
    if direct:
        holder = holder ^ me_ref[0]
    chosen = jnp.logical_and(dest == holder, rank == slot % capacity)
    selector = chosen.astype(F32).astype(BF16)
    label = jnp.sum(jnp.where(chosen, local + 1, 0), axis=1, keepdims=True) - 1
    parts = []
    for chunk in range(chunks):
        total = (terms[2 * chunk][...].astype(F32) + terms[2 * chunk + 1][...].astype(F32)).astype(BF16)
        parts.append(dot(selector, total, (1, 0)))
    parts.append(jnp.broadcast_to(label.astype(F32), (slots, LANES)))
    at = 0
    for part in parts:
        width = part.shape[1]
        if direct:
            for m in range(peers):
                outs[m][:, at : at + width] = part[m * capacity : (m + 1) * capacity].astype(BF16)
        else:
            outs[0][:, at : at + width] = part.astype(BF16)
        at += width


def pack(terms, targets, me, peers, capacity, direct):
    rows = targets.shape[1]
    width = sum(kept.shape[1] for kept, _ in terms) + LANES
    operands = [me, targets] + [x for pair in terms for x in pair]
    if direct:
        out_shape = [jax.ShapeDtypeStruct((capacity, width), BF16)] * peers
    else:
        out_shape = [jax.ShapeDtypeStruct((peers * capacity, width), BF16)]
    return pl.pallas_call(
        functools.partial(pack_kernel, peers, capacity, direct, len(terms)),
        out_shape=out_shape,
        in_specs=[pl.BlockSpec(memory_space=pltpu.SMEM)] + vmem(len(operands) - 1),
        out_specs=vmem(len(out_shape)),
        compiler_params=pltpu.CompilerParams(vmem_limit_bytes=VMEM_BYTES),
        cost_estimate=pl.CostEstimate(
            flops=2 * rows * peers * capacity * width,
            bytes_accessed=(6 * rows + 2 * peers * capacity) * width,
            transcendentals=0,
        ),
        name="pack",
    )(*operands)


def route(packed, peers, direct):
    if not direct:
        return [exchange(packed[0], "seq", peers)]
    routed = {0: packed[0]}
    half = peers // 2
    for near in range(half):
        for m in (half + near, near):
            if m:
                routed[m] = swap(packed[m], "seq", m)
    return [routed[m] for m in range(peers)]


def swap(x, axis, mask):
    n = lax.axis_size(axis)
    return lax.ppermute(x, axis, [(i, i ^ mask) for i in range(n)])


def exchange(x, axis, pieces):
    shape = x.shape
    if x.ndim == 2:
        x = x.reshape(pieces, -1, shape[1])
    return lax.all_to_all(x, axis, split_axis=0, concat_axis=0, tiled=True).reshape(shape)


def probs_kernel(q_ref, k_ref, ids_ref, probs_ref, probs_t_ref):
    patches = q_ref.shape[0]
    ids = ids_ref[...]
    per_token = patches // ids.shape[1]
    token = iota((patches, ids.shape[1]), 0) // per_token
    column = jnp.sum(
        jnp.where(token == iota((patches, ids.shape[1]), 1), ids, 0), axis=1, keepdims=True
    )
    square = (patches, patches)
    row = jnp.sum(
        jnp.where(iota(square, 0) == iota(square, 1), column, 0), axis=0, keepdims=True
    )
    allowed = column == row
    scale = 1.0 / math.sqrt(HEAD_DIM)
    for head, (low, high, start, stop) in enumerate(head_windows()):
        q = masked(q_ref[:, start:stop], low, high, start, stop)
        k = k_ref[:, start:stop]
        for out, scores, axis in (
            (probs_ref, dot(q, k, (1, 1)), 1),
            (probs_t_ref, dot(k, q, (1, 1)), 0),
        ):
            scores = jnp.where(allowed, scores * scale, -jnp.inf)
            weights = jnp.exp(scores - jnp.max(scores, axis=axis, keepdims=True))
            out[head] = weights / jnp.sum(weights, axis=axis, keepdims=True)


def window_probs(queries, keys, ids):
    patches = queries.shape[0]
    shape = jax.ShapeDtypeStruct((HEADS, patches, patches), F32)
    return pl.pallas_call(
        probs_kernel,
        out_shape=[shape, shape],
        in_specs=vmem(3),
        out_specs=vmem(2),
        compiler_params=pltpu.CompilerParams(vmem_limit_bytes=VMEM_BYTES),
        cost_estimate=pl.CostEstimate(
            flops=8 * HEADS * patches * patches * LANES,
            bytes_accessed=8 * HEADS * patches * patches,
            transcendentals=2 * HEADS * patches * patches,
        ),
        name="probs",
    )(queries, keys, ids)


def norm_kernel(patches_ref, gain_ref, *refs):
    pieces, (out_ref, gain_grad_ref) = refs[:-2], refs[-2:]
    patches, width = patches_ref.shape
    pieces = [ref[...].astype(F32) for ref in pieces]
    routed = jnp.concatenate(pieces, axis=0) if len(pieces) > 1 else pieces[0]
    slots, wide = routed.shape
    per_token = wide // width
    columns = [routed[:, c * width : (c + 1) * width] for c in range(per_token)]
    held = jnp.concatenate(columns, axis=0).astype(BF16)
    labels = routed[:, per_token * width : per_token * width + 1]
    lanes = per_token * slots
    lane = iota((slots, lanes), 1)
    row_of_lane = jnp.sum(
        jnp.where(lane % slots == iota((slots, lanes), 0), labels, 0.0), axis=0, keepdims=True
    ).astype(jnp.int32)
    patch_of_lane = row_of_lane * per_token + iota((1, lanes), 1) // slots
    patch_of_lane = jnp.where(row_of_lane < 0, -1, patch_of_lane)
    chosen = patch_of_lane == iota((patches, lanes), 0)
    patch_grads = dot(chosen.astype(F32).astype(BF16), held, (1, 0))
    inputs = patches_ref[...].astype(F32)
    inverse_rms = lax.rsqrt(jnp.mean(inputs * inputs, axis=1, keepdims=True) + 1e-06)
    normed = inputs * inverse_rms
    gain_grad_ref[...] = jnp.sum(patch_grads * normed, axis=0, keepdims=True)
    scaled = gain_ref[...] * patch_grads
    out_ref[...] = (
        inverse_rms * (scaled - normed * jnp.mean(scaled * normed, axis=1, keepdims=True))
    ).astype(BF16)


def norm_backward(received, patches, gain):
    count, width = patches.shape
    routed = sum(x.size for x in received)
    return pl.pallas_call(
        norm_kernel,
        out_shape=[
            jax.ShapeDtypeStruct((count, width), BF16),
            jax.ShapeDtypeStruct((1, width), F32),
        ],
        in_specs=vmem(2 + len(received)),
        out_specs=vmem(2),
        compiler_params=pltpu.CompilerParams(vmem_limit_bytes=VMEM_BYTES),
        cost_estimate=pl.CostEstimate(
            flops=2 * count * routed,
            bytes_accessed=4 * count * width + 2 * routed,
            transcendentals=0,
        ),
        name="norm",
    )(patches, gain, *received)


def sum_over(x, axis):
    n = lax.axis_size(axis)
    if n > DIRECT:
        return lax.psum(x, axis)
    mask = 1
    while mask < n:
        x = x + swap(x, axis, mask)
        mask *= 2
    return x


def side_by_side(x, axis):
    n = lax.axis_size(axis)
    if n > DIRECT:
        return lax.all_gather(x[0], axis, tiled=True)[None]
    place = lax.axis_index(axis)
    mask = 1
    while mask < n:
        other = swap(x, axis, mask)
        first = place & mask == 0
        x = jnp.concatenate([jnp.where(first, x, other), jnp.where(first, other, x)], axis=1)
        mask *= 2
    return x


def window_kernel(g_ref, q_ref, k_ref, v_ref, probs_ref, probs_t_ref, dq_ref, dk_ref, dv_ref):
    width = g_ref.shape[1]
    windows = head_windows()
    scores, scores_t, probs_t = [], [], []
    for head, (low, high, start, stop) in enumerate(windows):
        g = masked(g_ref[:, start:stop], low, high, start, stop)
        v = v_ref[:, start:stop]
        found = []
        for ref, grads, axis in (
            (probs_ref, dot(g, v, (1, 1)), 1),
            (probs_t_ref, dot(v, g, (1, 1)), 0),
        ):
            probs = ref[head]
            rounded = probs.astype(BF16)
            delta = jnp.sum(rounded.astype(F32) * grads, axis=axis, keepdims=True)
            found.append(((probs * (grads - delta)).astype(BF16), rounded))
        scores.append(found[0][0])
        scores_t.append(found[1][0])
        probs_t.append(found[1][1])
    scale = 1.0 / math.sqrt(HEAD_DIM)
    for start in range(0, width, LANES):
        stop = start + LANES
        heads = [h for h, (low, high, _, _) in enumerate(windows) if low < stop and high > start]
        for out, left, right_ref, factor in (
            (dq_ref, scores, k_ref, scale),
            (dk_ref, scores_t, q_ref, scale),
            (dv_ref, probs_t, g_ref, 1.0),
        ):
            right = right_ref[:, start:stop]
            rows = [masked(right, windows[h][0], windows[h][1], start, stop) for h in heads]
            product = dot(
                jnp.concatenate([left[h] for h in heads], axis=1),
                jnp.concatenate(rows, axis=0),
                (1, 0),
            )
            out[:, start:stop] = (product * factor).astype(BF16)


def window_backward(out_grads, queries, keys, values, probs, probs_t):
    patches, width = queries.shape
    shape = jax.ShapeDtypeStruct((patches, width), BF16)
    return pl.pallas_call(
        window_kernel,
        out_shape=[shape] * 3,
        in_specs=vmem(6),
        out_specs=vmem(3),
        compiler_params=pltpu.CompilerParams(vmem_limit_bytes=VMEM_BYTES),
        cost_estimate=pl.CostEstimate(
            flops=10 * HEADS * patches * patches * LANES,
            bytes_accessed=8 * HEADS * patches * patches + 14 * patches * width,
            transcendentals=0,
        ),
        name="window",
    )(out_grads, queries, keys, values, probs, probs_t)


def body(llm_grads, token_target, patches, gain, w_down, queries, keys, values, window_ids):
    grad_rows = llm_grads[0]
    rows = grad_rows.shape[0]
    images, peers = lax.axis_size("img"), lax.axis_size("seq")
    capacity = max(1, 2 * rows // peers)
    block = w_down.shape[1]
    width = patches.shape[2]
    direct = peers <= DIRECT

    order = [0]
    while len(order) < images:
        order = [2 * j for j in order] + [2 * j + 1 for j in order]
    image, me = lax.axis_index("img"), lax.axis_index("seq")

    def columns(j):
        return lax.dynamic_slice(grad_rows, (0, (image ^ j) * block), (rows, block))

    x_blocks = [columns(0)] + [swap(columns(j), "img", j) for j in range(1, images)]
    x_blocks = [x_blocks[j] for j in order]
    probs, probs_t = window_probs(queries[0], keys[0], window_ids[0])
    token_target, probs, probs_t = lax.optimization_barrier((token_target, probs, probs_t))

    terms, first = [], 0
    for index, count in enumerate(CHUNKS):
        w_rows = lax.slice_in_dim(w_down, first, first + count * width)
        w_rows = pltpu.with_memory_space_constraint(w_rows, pltpu.VMEM)
        first += count * width
        kept, sent, *sums = project(x_blocks, w_rows, index == 0)
        if index == 0:
            bias_part = sums[0]
        mask = 1
        while 2 * mask < images:
            kept, sent = halve(kept, swap(sent, "img", mask))
            mask *= 2
        terms.append((kept, swap(sent, "img", mask)))
    packed = pack(terms, token_target, me.reshape(1), peers, capacity, direct)
    received = route(packed, peers, direct)

    bias_total = side_by_side(sum_over(bias_part, "seq"), "img")[0]
    out_grads, gain_part = norm_backward(received, patches[0], gain[None])
    gain_total = sum_over(sum_over(gain_part, "img"), "seq")[0]
    gain_grad = gain_total / math.sqrt(images * peers * patches.shape[1])
    bias_grad = bias_total / math.sqrt(images * peers * rows)
    grads = window_backward(out_grads, queries[0], keys[0], values[0], probs, probs_t)
    return (grads[0][None], grads[1][None], grads[2][None], gain_grad, bias_grad)


def solution(mesh):
    return jax.shard_map(
        body,
        mesh=mesh,
        in_specs=(
            P("img", "seq", None),
            P("img", "seq"),
            P("img", "seq", None),
            P(),
            P(None, "img"),
            P("img", "seq", None),
            P("img", "seq", None),
            P("img", "seq", None),
            P("img", "seq", None),
        ),
        out_specs=(P("img", "seq", None), P("img", "seq", None), P("img", "seq", None), P(), P()),
        check_vma=False,
    )
```

```python
import functools
import math

import jax
import jax.numpy as jnp
from jax import lax
from jax.experimental import pallas as pl
from jax.experimental.pallas import tpu as pltpu
from jax.sharding import PartitionSpec as P

HEADS = 16
HEAD_DIM = 80
LANES = 128
CHUNKS = (2, 2)
VMEM_BYTES = 16 * 1024 * 1024

F32 = jnp.float32
BF16 = jnp.bfloat16


def iota(shape, axis):
    return lax.broadcasted_iota(jnp.int32, shape, axis)


def dot(a, b, over):
    return lax.dot_general(a, b, ((over[:1], over[1:]), ((), ())), preferred_element_type=F32)


def vmem(count):
    return [pl.BlockSpec(memory_space=pltpu.VMEM)] * count


def head_windows():
    windows = []
    for head in range(HEADS):
        low, high = head * HEAD_DIM, (head + 1) * HEAD_DIM
        start = low // LANES * LANES
        windows.append((low, high, start, -(-high // LANES) * LANES))
    return windows


def lane_mask(low, high, start, stop):
    at = iota((1, stop - start), 1) + start
    return jnp.logical_and(at >= low, at < high)


def masked(x, low, high, start, stop):
    return jnp.where(lane_mask(low, high, start, stop), x, jnp.zeros_like(x))


def project_kernel(blocks, first, tile, with_sum, *refs):
    x_refs, w_ref = refs[:blocks], refs[blocks]
    keep_ref, send_ref = refs[blocks + 1 : blocks + 3]
    x = jnp.concatenate([ref[...] for ref in x_refs], axis=0)
    if with_sum:
        refs[blocks + 3][...] = dot(jnp.ones((16, x.shape[0]), BF16), x, (1, 0))[:1]
    x = x.T
    half = keep_ref.shape[0]
    for t in range(0, keep_ref.shape[1], tile):
        product = dot(w_ref[first + t : first + t + tile], x, (1, 0)).T.astype(BF16)
        keep_ref[:, t : t + tile] = product[:half]
        send_ref[:, t : t + tile] = product[half:]


def project(x_blocks, w_down, first, width, with_sum):
    blocks, (rows, depth) = len(x_blocks), x_blocks[0].shape
    tile = 512
    while width % tile:
        tile //= 2
    out_shape = [jax.ShapeDtypeStruct((blocks * rows // 2, width), BF16)] * 2
    if with_sum:
        out_shape = out_shape + [jax.ShapeDtypeStruct((1, depth), F32)]
    return pl.pallas_call(
        functools.partial(project_kernel, blocks, first, tile, with_sum),
        out_shape=out_shape,
        in_specs=vmem(blocks + 1),
        out_specs=vmem(len(out_shape)),
        compiler_params=pltpu.CompilerParams(vmem_limit_bytes=VMEM_BYTES),
        cost_estimate=pl.CostEstimate(
            flops=2 * blocks * rows * depth * width,
            bytes_accessed=2 * width * depth,
            transcendentals=0,
        ),
        name="project",
    )(*x_blocks, pltpu.with_memory_space_constraint(w_down, pltpu.VMEM))


def hold_kernel(w_ref, out_ref):
    del w_ref, out_ref


def hold(w_down):
    return pl.pallas_call(
        hold_kernel,
        out_shape=jax.ShapeDtypeStruct(w_down.shape, w_down.dtype),
        in_specs=[pl.BlockSpec(memory_space=pl.ANY)],
        out_specs=pl.BlockSpec(memory_space=pl.ANY),
        input_output_aliases={0: 0},
        name="hold",
    )(w_down)


def halve_kernel(kept_ref, got_ref, keep_ref, send_ref):
    half = keep_ref.shape[0]
    keep_ref[...] = kept_ref[:half].astype(F32) + got_ref[:half].astype(F32)
    send_ref[...] = (kept_ref[half:].astype(F32) + got_ref[half:].astype(F32)).astype(BF16)


def halve(kept, got):
    rows, width = kept.shape
    return pl.pallas_call(
        halve_kernel,
        out_shape=[
            jax.ShapeDtypeStruct((rows // 2, width), F32),
            jax.ShapeDtypeStruct((rows // 2, width), BF16),
        ],
        in_specs=vmem(2),
        out_specs=vmem(2),
        compiler_params=pltpu.CompilerParams(vmem_limit_bytes=VMEM_BYTES),
        cost_estimate=pl.CostEstimate(
            flops=rows * width, bytes_accessed=7 * rows * width, transcendentals=0
        ),
        name="halve",
    )(kept, got)


def pack_kernel(peers, capacity, chunks, carries, targets_ref, *refs):
    terms, out_ref = refs[: 2 * chunks], refs[-1]
    targets = targets_ref[...]
    rows = targets.shape[1]
    dest = targets // rows
    local = targets - dest * rows
    dest_column = jnp.sum(
        jnp.where(iota((rows, rows), 0) == iota((rows, rows), 1), dest, 0), axis=1, keepdims=True
    )
    same_before = jnp.logical_and(dest_column == dest, iota((rows, rows), 0) < iota((rows, rows), 1))
    rank = jnp.sum(same_before.astype(jnp.int32), axis=0, keepdims=True)
    slots = peers * capacity
    slot = iota((slots, rows), 0)
    chosen = jnp.logical_and(dest == slot // capacity, rank == slot % capacity)
    selector = chosen.astype(F32).astype(BF16)
    at = 0
    for chunk in range(chunks):
        kept, got = terms[2 * chunk], terms[2 * chunk + 1]
        total = (kept[...].astype(F32) + got[...].astype(F32)).astype(BF16)
        width = total.shape[1]
        out_ref[:, at : at + width] = dot(selector, total, (1, 0)).astype(BF16)
        at += width
    label = jnp.sum(jnp.where(chosen, local + 1, 0), axis=1, keepdims=True) - 1
    out_ref[:, at : at + LANES] = jnp.broadcast_to(label.astype(F32), (slots, LANES)).astype(BF16)
    if carries:
        sums = refs[2 * chunks][...]
        high = sums.astype(BF16).astype(F32)
        middle = (sums - high).astype(BF16).astype(F32)
        low = (sums - high - middle).astype(BF16).astype(F32)
        extra = jnp.zeros((slots, LANES), F32)
        row = iota((slots, LANES), 0)
        pieces = sums.shape[1] // peers // LANES
        for peer in range(peers):
            for level, values in enumerate((high, middle, low)):
                for piece in range(pieces):
                    start = (peer * pieces + piece) * LANES
                    line = jnp.broadcast_to(values[:, start : start + LANES], (slots, LANES))
                    extra = jnp.where(row == peer * capacity + level * pieces + piece, line, extra)
        out_ref[:, at + LANES : at + 2 * LANES] = extra.astype(BF16)


def pack(terms, targets, sums, peers, capacity, carries):
    rows = targets.shape[1]
    width = sum(kept.shape[1] for kept, _ in terms) + (2 * LANES if carries else LANES)
    operands = [targets] + [x for pair in terms for x in pair] + ([sums] if carries else [])
    return pl.pallas_call(
        functools.partial(pack_kernel, peers, capacity, len(terms), carries),
        out_shape=jax.ShapeDtypeStruct((peers * capacity, width), BF16),
        in_specs=vmem(len(operands)),
        out_specs=pl.BlockSpec(memory_space=pltpu.VMEM),
        compiler_params=pltpu.CompilerParams(vmem_limit_bytes=VMEM_BYTES),
        cost_estimate=pl.CostEstimate(
            flops=2 * rows * peers * capacity * width,
            bytes_accessed=(6 * rows + 2 * peers * capacity) * width,
            transcendentals=0,
        ),
        name="pack",
    )(*operands)


def swap(x, axis, mask):
    n = lax.axis_size(axis)
    return lax.ppermute(x, axis, [(i, i ^ mask) for i in range(n)])


def exchange(x, axis, pieces):
    shape = x.shape
    if x.ndim == 2:
        x = x.reshape(pieces, -1, shape[1])
    return lax.all_to_all(x, axis, split_axis=0, concat_axis=0, tiled=True).reshape(shape)


def probs_kernel(q_ref, k_ref, ids_ref, probs_ref, probs_t_ref):
    patches = q_ref.shape[0]
    ids = ids_ref[...]
    per_token = patches // ids.shape[1]
    token = iota((patches, ids.shape[1]), 0) // per_token
    column = jnp.sum(
        jnp.where(token == iota((patches, ids.shape[1]), 1), ids, 0), axis=1, keepdims=True
    )
    square = (patches, patches)
    row = jnp.sum(
        jnp.where(iota(square, 0) == iota(square, 1), column, 0), axis=0, keepdims=True
    )
    allowed = column == row
    scale = 1.0 / math.sqrt(HEAD_DIM)
    for head, (low, high, start, stop) in enumerate(head_windows()):
        q = masked(q_ref[:, start:stop], low, high, start, stop)
        k = k_ref[:, start:stop]
        for out, scores, axis in (
            (probs_ref, dot(q, k, (1, 1)), 1),
            (probs_t_ref, dot(k, q, (1, 1)), 0),
        ):
            scores = jnp.where(allowed, scores * scale, -jnp.inf)
            weights = jnp.exp(scores - jnp.max(scores, axis=axis, keepdims=True))
            out[head] = weights / jnp.sum(weights, axis=axis, keepdims=True)


def window_probs(queries, keys, ids):
    patches = queries.shape[0]
    shape = jax.ShapeDtypeStruct((HEADS, patches, patches), F32)
    return pl.pallas_call(
        probs_kernel,
        out_shape=[shape, shape],
        in_specs=vmem(3),
        out_specs=vmem(2),
        compiler_params=pltpu.CompilerParams(vmem_limit_bytes=VMEM_BYTES),
        cost_estimate=pl.CostEstimate(
            flops=8 * HEADS * patches * patches * LANES,
            bytes_accessed=8 * HEADS * patches * patches,
            transcendentals=2 * HEADS * patches * patches,
        ),
        name="probs",
    )(queries, keys, ids)


def norm_kernel(peers, carries, patches_ref, gain_ref, routed_ref, out_ref, share_ref):
    patches, width = patches_ref.shape
    slots = routed_ref.shape[0]
    per_token = routed_ref.shape[1] // width
    labels = routed_ref[:, per_token * width : per_token * width + LANES].astype(F32)[:, :1]
    columns = [routed_ref[:, c * width : (c + 1) * width].astype(F32) for c in range(per_token)]
    held = jnp.concatenate(columns, axis=0).astype(BF16)
    lanes = len(columns) * slots
    lane = iota((slots, lanes), 1)
    row_of_lane = jnp.sum(
        jnp.where(lane % slots == iota((slots, lanes), 0), labels, 0.0), axis=0, keepdims=True
    ).astype(jnp.int32)
    patch_of_lane = row_of_lane * len(columns) + iota((1, lanes), 1) // slots
    patch_of_lane = jnp.where(row_of_lane < 0, -1, patch_of_lane)
    chosen = patch_of_lane == iota((patches, lanes), 0)
    patch_grads = dot(chosen.astype(F32).astype(BF16), held, (1, 0))
    inputs = patches_ref[...].astype(F32)
    inverse_rms = lax.rsqrt(jnp.mean(inputs * inputs, axis=1, keepdims=True) + 1e-06)
    normed = inputs * inverse_rms
    gain_part = jnp.sum(patch_grads * normed, axis=0, keepdims=True)
    share_ref[:, :, :width] = jnp.broadcast_to(gain_part[None], (share_ref.shape[0], 1, width))
    if carries:
        carried = routed_ref[:, per_token * width + LANES :].astype(F32)
        capacity = slots // peers
        pieces = (share_ref.shape[2] - width) // LANES
        row = iota((slots, LANES), 0) % capacity
        for piece in range(pieces):
            kept = jnp.logical_and(row % pieces == piece, row < 3 * pieces)
            line = jnp.sum(jnp.where(kept, carried, 0.0), axis=0, keepdims=True)
            at = width + piece * LANES
            share_ref[:, :, at : at + LANES] = jnp.broadcast_to(
                line[None], (share_ref.shape[0], 1, LANES)
            )
    scaled = gain_ref[...] * patch_grads
    out_ref[...] = (
        inverse_rms * (scaled - normed * jnp.mean(scaled * normed, axis=1, keepdims=True))
    ).astype(BF16)


def norm_backward(routed, peers, patches, gain, share):
    count, width = patches.shape
    return pl.pallas_call(
        functools.partial(norm_kernel, peers, share[2] > width),
        out_shape=[jax.ShapeDtypeStruct((count, width), BF16), jax.ShapeDtypeStruct(share, F32)],
        in_specs=vmem(3),
        out_specs=vmem(2),
        compiler_params=pltpu.CompilerParams(vmem_limit_bytes=VMEM_BYTES),
        cost_estimate=pl.CostEstimate(
            flops=2 * count * routed.size,
            bytes_accessed=4 * count * width + 2 * routed.size,
            transcendentals=0,
        ),
        name="norm",
    )(patches, gain, routed)


def window_kernel(g_ref, q_ref, k_ref, v_ref, probs_ref, probs_t_ref, dq_ref, dk_ref, dv_ref):
    width = g_ref.shape[1]
    windows = head_windows()
    scores, scores_t, probs_t = [], [], []
    for head, (low, high, start, stop) in enumerate(windows):
        g = masked(g_ref[:, start:stop], low, high, start, stop)
        v = v_ref[:, start:stop]
        found = []
        for ref, grads, axis in (
            (probs_ref, dot(g, v, (1, 1)), 1),
            (probs_t_ref, dot(v, g, (1, 1)), 0),
        ):
            probs = ref[head]
            rounded = probs.astype(BF16)
            delta = jnp.sum(rounded.astype(F32) * grads, axis=axis, keepdims=True)
            found.append(((probs * (grads - delta)).astype(BF16), rounded))
        scores.append(found[0][0])
        scores_t.append(found[1][0])
        probs_t.append(found[1][1])
    scale = 1.0 / math.sqrt(HEAD_DIM)
    for start in range(0, width, LANES):
        stop = start + LANES
        heads = [h for h, (low, high, _, _) in enumerate(windows) if low < stop and high > start]
        for out, left, right_ref, factor in (
            (dq_ref, scores, k_ref, scale),
            (dk_ref, scores_t, q_ref, scale),
            (dv_ref, probs_t, g_ref, 1.0),
        ):
            right = right_ref[:, start:stop]
            rows = [masked(right, windows[h][0], windows[h][1], start, stop) for h in heads]
            product = dot(
                jnp.concatenate([left[h] for h in heads], axis=1),
                jnp.concatenate(rows, axis=0),
                (1, 0),
            )
            out[:, start:stop] = (product * factor).astype(BF16)


def window_backward(out_grads, queries, keys, values, probs, probs_t):
    patches, width = queries.shape
    shape = jax.ShapeDtypeStruct((patches, width), BF16)
    return pl.pallas_call(
        window_kernel,
        out_shape=[shape] * 3,
        in_specs=vmem(6),
        out_specs=vmem(3),
        compiler_params=pltpu.CompilerParams(vmem_limit_bytes=VMEM_BYTES),
        cost_estimate=pl.CostEstimate(
            flops=10 * HEADS * patches * patches * LANES,
            bytes_accessed=8 * HEADS * patches * patches + 14 * patches * width,
            transcendentals=0,
        ),
        name="window",
    )(out_grads, queries, keys, values, probs, probs_t)


def body(llm_grads, token_target, patches, gain, w_down, queries, keys, values, window_ids):
    grad_rows = llm_grads[0]
    rows = grad_rows.shape[0]
    images, peers = lax.axis_size("img"), lax.axis_size("seq")
    devices = images * peers
    capacity = max(1, 2 * rows // peers)
    block = w_down.shape[1]
    width = patches.shape[2]
    pieces = block // peers // LANES
    carries = pieces > 0 and 3 * pieces <= capacity

    order = [0]
    while len(order) < images:
        order = [2 * j for j in order] + [2 * j + 1 for j in order]
    image = lax.axis_index("img")

    def columns(j):
        return lax.dynamic_slice(grad_rows, (0, (image ^ j) * block), (rows, block))

    x_blocks = [columns(0)] + [swap(columns(j), "img", j) for j in range(1, images)]
    x_blocks = [x_blocks[j] for j in order]
    probs, probs_t = window_probs(queries[0], keys[0], window_ids[0])

    w_down = hold(w_down)
    terms, first = [], 0
    for index, count in enumerate(CHUNKS):
        kept, sent, *sums = project(x_blocks, w_down, first, count * width, index == 0)
        first += count * width
        if index == 0:
            bias_part = sums[0]
        mask = 1
        while 2 * mask < images:
            kept, sent = halve(kept, swap(sent, "img", mask))
            mask *= 2
        terms.append((kept, swap(sent, "img", mask)))
    packed = pack(terms, token_target, bias_part, peers, capacity, carries)
    routed = exchange(packed, "seq", peers)

    share = (devices, 1, width + pieces * LANES) if carries else (1, 1, width)
    out_grads, shared = norm_backward(routed, peers, patches[0], gain[None], share)
    if carries:
        shared = exchange(shared, ("img", "seq"), devices)
        gain_total = jnp.sum(shared[:, 0, :width], axis=0)
        bias_total = shared[:, 0, width:].reshape(-1)
    else:
        gain_total = lax.psum(shared[0, 0], ("img", "seq"))
        bias_total = lax.all_gather(lax.psum(bias_part[0], "seq"), "img", tiled=True)
    grads = window_backward(out_grads, queries[0], keys[0], values[0], probs, probs_t)
    gain_grad = gain_total / math.sqrt(devices * patches.shape[1])
    bias_grad = bias_total / math.sqrt(devices * rows)
    return (grads[0][None], grads[1][None], grads[2][None], gain_grad, bias_grad)


def solution(mesh):
    return jax.shard_map(
        body,
        mesh=mesh,
        in_specs=(
            P("img", "seq", None),
            P("img", "seq"),
            P("img", "seq", None),
            P(),
            P(None, "img"),
            P("img", "seq", None),
            P("img", "seq", None),
            P("img", "seq", None),
            P("img", "seq", None),
        ),
        out_specs=(P("img", "seq", None), P("img", "seq", None), P("img", "seq", None), P(), P()),
        check_vma=False,
    )
```

```python
import functools
import math

import jax
import jax.numpy as jnp
from jax import lax
from jax.experimental import pallas as pl
from jax.experimental.pallas import tpu as pltpu
from jax.sharding import PartitionSpec as P

HEADS = 16
HEAD_DIM = 80
LANES = 128
CHUNKS = (2, 2)
VMEM_BYTES = 24 * 1024 * 1024
PROJECT_VMEM_BYTES = 40 * 1024 * 1024

F32 = jnp.float32
BF16 = jnp.bfloat16


def iota(shape, axis):
    return lax.broadcasted_iota(jnp.int32, shape, axis)


def dot(a, b, over):
    return lax.dot_general(a, b, ((over[:1], over[1:]), ((), ())), preferred_element_type=F32)


def vmem(count):
    return [pl.BlockSpec(memory_space=pltpu.VMEM)] * count


def head_windows():
    windows = []
    for head in range(HEADS):
        low, high = head * HEAD_DIM, (head + 1) * HEAD_DIM
        start = low // LANES * LANES
        windows.append((low, high, start, -(-high // LANES) * LANES))
    return windows


def lane_mask(low, high, start, stop):
    at = iota((1, stop - start), 1) + start
    return jnp.logical_and(at >= low, at < high)


def masked(x, low, high, start, stop):
    return jnp.where(lane_mask(low, high, start, stop), x, jnp.zeros_like(x))


def project_kernel(blocks, tile, last, with_sum, *refs):
    x_refs, w_ref, w_hbm = refs[:blocks], refs[blocks], refs[blocks + 1]
    keep_ref, send_ref = refs[blocks + 2 : blocks + 4]
    w_last, sem = refs[-2:]
    copy = pltpu.make_async_copy(w_hbm.at[pl.ds(last, w_last.shape[0])], w_last, sem)
    copy.start()
    x = jnp.concatenate([ref[...] for ref in x_refs], axis=0)
    if with_sum:
        refs[blocks + 4][...] = dot(jnp.ones((16, x.shape[0]), BF16), x, (1, 0))[:1]
    x = x.T
    half = keep_ref.shape[0]

    def store(w_rows, at):
        product = dot(w_rows, x, (1, 0)).T.astype(BF16)
        keep_ref[:, at : at + tile] = product[:half]
        send_ref[:, at : at + tile] = product[half:]

    for t in range(0, w_ref.shape[0], tile):
        store(w_ref[t : t + tile], t)
    copy.wait()
    for t in range(0, w_last.shape[0], tile):
        store(w_last[t : t + tile], w_ref.shape[0] + t)


def project(x_blocks, w_down, first, width, with_sum):
    blocks, (rows, depth) = len(x_blocks), x_blocks[0].shape
    streamed = width // 4
    tile = 640
    while streamed % tile:
        tile //= 2
    last = first + width - streamed
    w_rows = pltpu.with_memory_space_constraint(
        lax.slice_in_dim(w_down, first, last), pltpu.VMEM
    )
    out_shape = [jax.ShapeDtypeStruct((blocks * rows // 2, width), BF16)] * 2
    if with_sum:
        out_shape = out_shape + [jax.ShapeDtypeStruct((1, depth), F32)]
    return pl.pallas_call(
        functools.partial(project_kernel, blocks, tile, last, with_sum),
        out_shape=out_shape,
        in_specs=vmem(blocks + 1) + [pl.BlockSpec(memory_space=pl.ANY)],
        out_specs=vmem(len(out_shape)),
        scratch_shapes=[pltpu.VMEM((streamed, depth), BF16), pltpu.SemaphoreType.DMA],
        compiler_params=pltpu.CompilerParams(vmem_limit_bytes=PROJECT_VMEM_BYTES),
        cost_estimate=pl.CostEstimate(
            flops=2 * blocks * rows * depth * width,
            bytes_accessed=2 * width * depth,
            transcendentals=0,
        ),
        name="project",
    )(*x_blocks, w_rows, w_down)


def halve_kernel(kept_ref, got_ref, keep_ref, send_ref):
    half = keep_ref.shape[0]
    keep_ref[...] = kept_ref[:half].astype(F32) + got_ref[:half].astype(F32)
    send_ref[...] = (kept_ref[half:].astype(F32) + got_ref[half:].astype(F32)).astype(BF16)


def halve(kept, got):
    rows, width = kept.shape
    return pl.pallas_call(
        halve_kernel,
        out_shape=[
            jax.ShapeDtypeStruct((rows // 2, width), F32),
            jax.ShapeDtypeStruct((rows // 2, width), BF16),
        ],
        in_specs=vmem(2),
        out_specs=vmem(2),
        compiler_params=pltpu.CompilerParams(vmem_limit_bytes=VMEM_BYTES),
        cost_estimate=pl.CostEstimate(
            flops=rows * width, bytes_accessed=7 * rows * width, transcendentals=0
        ),
        name="halve",
    )(kept, got)


def pack_kernel(peers, capacity, chunks, carries, targets_ref, *refs):
    terms, out_ref = refs[: 2 * chunks], refs[-1]
    targets = targets_ref[...]
    rows = targets.shape[1]
    dest = targets // rows
    local = targets - dest * rows
    dest_column = jnp.sum(
        jnp.where(iota((rows, rows), 0) == iota((rows, rows), 1), dest, 0), axis=1, keepdims=True
    )
    same_before = jnp.logical_and(dest_column == dest, iota((rows, rows), 0) < iota((rows, rows), 1))
    rank = jnp.sum(same_before.astype(jnp.int32), axis=0, keepdims=True)
    slots = peers * capacity
    slot = iota((slots, rows), 0)
    chosen = jnp.logical_and(dest == slot // capacity, rank == slot % capacity)
    selector = chosen.astype(F32).astype(BF16)
    at = 0
    for chunk in range(chunks):
        kept, got = terms[2 * chunk], terms[2 * chunk + 1]
        total = (kept[...].astype(F32) + got[...].astype(F32)).astype(BF16)
        width = total.shape[1]
        out_ref[:, at : at + width] = dot(selector, total, (1, 0)).astype(BF16)
        at += width
    label = jnp.sum(jnp.where(chosen, local + 1, 0), axis=1, keepdims=True) - 1
    out_ref[:, at : at + LANES] = jnp.broadcast_to(label.astype(F32), (slots, LANES)).astype(BF16)
    if carries:
        sums = refs[2 * chunks][...]
        high = sums.astype(BF16).astype(F32)
        middle = (sums - high).astype(BF16).astype(F32)
        low = (sums - high - middle).astype(BF16).astype(F32)
        extra = jnp.zeros((slots, LANES), F32)
        row = iota((slots, LANES), 0)
        pieces = sums.shape[1] // peers // LANES
        for peer in range(peers):
            for level, values in enumerate((high, middle, low)):
                for piece in range(pieces):
                    start = (peer * pieces + piece) * LANES
                    line = jnp.broadcast_to(values[:, start : start + LANES], (slots, LANES))
                    extra = jnp.where(row == peer * capacity + level * pieces + piece, line, extra)
        out_ref[:, at + LANES : at + 2 * LANES] = extra.astype(BF16)


def pack(terms, targets, sums, peers, capacity, carries):
    rows = targets.shape[1]
    width = sum(kept.shape[1] for kept, _ in terms) + (2 * LANES if carries else LANES)
    operands = [targets] + [x for pair in terms for x in pair] + ([sums] if carries else [])
    return pl.pallas_call(
        functools.partial(pack_kernel, peers, capacity, len(terms), carries),
        out_shape=jax.ShapeDtypeStruct((peers * capacity, width), BF16),
        in_specs=vmem(len(operands)),
        out_specs=pl.BlockSpec(memory_space=pltpu.VMEM),
        compiler_params=pltpu.CompilerParams(vmem_limit_bytes=VMEM_BYTES),
        cost_estimate=pl.CostEstimate(
            flops=2 * rows * peers * capacity * width,
            bytes_accessed=(6 * rows + 2 * peers * capacity) * width,
            transcendentals=0,
        ),
        name="pack",
    )(*operands)


def swap(x, axis, mask):
    n = lax.axis_size(axis)
    return lax.ppermute(x, axis, [(i, i ^ mask) for i in range(n)])


def exchange(x, axis, pieces):
    shape = x.shape
    if x.ndim == 2:
        x = x.reshape(pieces, -1, shape[1])
    return lax.all_to_all(x, axis, split_axis=0, concat_axis=0, tiled=True).reshape(shape)


def probs_kernel(q_ref, k_ref, ids_ref, probs_ref, probs_t_ref):
    patches = q_ref.shape[0]
    ids = ids_ref[...]
    per_token = patches // ids.shape[1]
    token = iota((patches, ids.shape[1]), 0) // per_token
    column = jnp.sum(
        jnp.where(token == iota((patches, ids.shape[1]), 1), ids, 0), axis=1, keepdims=True
    )
    square = (patches, patches)
    row = jnp.sum(
        jnp.where(iota(square, 0) == iota(square, 1), column, 0), axis=0, keepdims=True
    )
    allowed = column == row
    scale = 1.0 / math.sqrt(HEAD_DIM)
    for head, (low, high, start, stop) in enumerate(head_windows()):
        q = masked(q_ref[:, start:stop], low, high, start, stop)
        k = k_ref[:, start:stop]
        for out, scores, axis in (
            (probs_ref, dot(q, k, (1, 1)), 1),
            (probs_t_ref, dot(k, q, (1, 1)), 0),
        ):
            scores = jnp.where(allowed, scores * scale, -jnp.inf)
            weights = jnp.exp(scores - jnp.max(scores, axis=axis, keepdims=True))
            out[head] = weights / jnp.sum(weights, axis=axis, keepdims=True)


def window_probs(queries, keys, ids):
    patches = queries.shape[0]
    shape = jax.ShapeDtypeStruct((HEADS, patches, patches), F32)
    return pl.pallas_call(
        probs_kernel,
        out_shape=[shape, shape],
        in_specs=vmem(3),
        out_specs=vmem(2),
        compiler_params=pltpu.CompilerParams(vmem_limit_bytes=VMEM_BYTES),
        cost_estimate=pl.CostEstimate(
            flops=8 * HEADS * patches * patches * LANES,
            bytes_accessed=8 * HEADS * patches * patches,
            transcendentals=2 * HEADS * patches * patches,
        ),
        name="probs",
    )(queries, keys, ids)


def norm_kernel(peers, carries, patches_ref, gain_ref, routed_ref, out_ref, share_ref):
    patches, width = patches_ref.shape
    slots = routed_ref.shape[0]
    per_token = routed_ref.shape[1] // width
    labels = routed_ref[:, per_token * width : per_token * width + LANES].astype(F32)[:, :1]
    columns = [routed_ref[:, c * width : (c + 1) * width].astype(F32) for c in range(per_token)]
    held = jnp.concatenate(columns, axis=0).astype(BF16)
    lanes = len(columns) * slots
    lane = iota((slots, lanes), 1)
    row_of_lane = jnp.sum(
        jnp.where(lane % slots == iota((slots, lanes), 0), labels, 0.0), axis=0, keepdims=True
    ).astype(jnp.int32)
    patch_of_lane = row_of_lane * len(columns) + iota((1, lanes), 1) // slots
    patch_of_lane = jnp.where(row_of_lane < 0, -1, patch_of_lane)
    chosen = patch_of_lane == iota((patches, lanes), 0)
    patch_grads = dot(chosen.astype(F32).astype(BF16), held, (1, 0))
    inputs = patches_ref[...].astype(F32)
    inverse_rms = lax.rsqrt(jnp.mean(inputs * inputs, axis=1, keepdims=True) + 1e-06)
    normed = inputs * inverse_rms
    gain_part = jnp.sum(patch_grads * normed, axis=0, keepdims=True)
    share_ref[:, :, :width] = jnp.broadcast_to(gain_part[None], (share_ref.shape[0], 1, width))
    if carries:
        carried = routed_ref[:, per_token * width + LANES :].astype(F32)
        capacity = slots // peers
        pieces = (share_ref.shape[2] - width) // LANES
        row = iota((slots, LANES), 0) % capacity
        for piece in range(pieces):
            kept = jnp.logical_and(row % pieces == piece, row < 3 * pieces)
            line = jnp.sum(jnp.where(kept, carried, 0.0), axis=0, keepdims=True)
            at = width + piece * LANES
            share_ref[:, :, at : at + LANES] = jnp.broadcast_to(
                line[None], (share_ref.shape[0], 1, LANES)
            )
    scaled = gain_ref[...] * patch_grads
    out_ref[...] = (
        inverse_rms * (scaled - normed * jnp.mean(scaled * normed, axis=1, keepdims=True))
    ).astype(BF16)


def norm_backward(routed, peers, patches, gain, share):
    count, width = patches.shape
    return pl.pallas_call(
        functools.partial(norm_kernel, peers, share[2] > width),
        out_shape=[jax.ShapeDtypeStruct((count, width), BF16), jax.ShapeDtypeStruct(share, F32)],
        in_specs=vmem(3),
        out_specs=vmem(2),
        compiler_params=pltpu.CompilerParams(vmem_limit_bytes=VMEM_BYTES),
        cost_estimate=pl.CostEstimate(
            flops=2 * count * routed.size,
            bytes_accessed=4 * count * width + 2 * routed.size,
            transcendentals=0,
        ),
        name="norm",
    )(patches, gain, routed)


def window_kernel(g_ref, q_ref, k_ref, v_ref, probs_ref, probs_t_ref, dq_ref, dk_ref, dv_ref):
    width = g_ref.shape[1]
    windows = head_windows()
    scores, scores_t, probs_t = [], [], []
    for head, (low, high, start, stop) in enumerate(windows):
        g = masked(g_ref[:, start:stop], low, high, start, stop)
        v = v_ref[:, start:stop]
        found = []
        for ref, grads, axis in (
            (probs_ref, dot(g, v, (1, 1)), 1),
            (probs_t_ref, dot(v, g, (1, 1)), 0),
        ):
            probs = ref[head]
            rounded = probs.astype(BF16)
            delta = jnp.sum(rounded.astype(F32) * grads, axis=axis, keepdims=True)
            found.append(((probs * (grads - delta)).astype(BF16), rounded))
        scores.append(found[0][0])
        scores_t.append(found[1][0])
        probs_t.append(found[1][1])
    scale = 1.0 / math.sqrt(HEAD_DIM)
    for start in range(0, width, LANES):
        stop = start + LANES
        heads = [h for h, (low, high, _, _) in enumerate(windows) if low < stop and high > start]
        for out, left, right_ref, factor in (
            (dq_ref, scores, k_ref, scale),
            (dk_ref, scores_t, q_ref, scale),
            (dv_ref, probs_t, g_ref, 1.0),
        ):
            right = right_ref[:, start:stop]
            rows = [masked(right, windows[h][0], windows[h][1], start, stop) for h in heads]
            product = dot(
                jnp.concatenate([left[h] for h in heads], axis=1),
                jnp.concatenate(rows, axis=0),
                (1, 0),
            )
            out[:, start:stop] = (product * factor).astype(BF16)


def window_backward(out_grads, queries, keys, values, probs, probs_t):
    patches, width = queries.shape
    shape = jax.ShapeDtypeStruct((patches, width), BF16)
    return pl.pallas_call(
        window_kernel,
        out_shape=[shape] * 3,
        in_specs=vmem(6),
        out_specs=vmem(3),
        compiler_params=pltpu.CompilerParams(vmem_limit_bytes=VMEM_BYTES),
        cost_estimate=pl.CostEstimate(
            flops=10 * HEADS * patches * patches * LANES,
            bytes_accessed=8 * HEADS * patches * patches + 14 * patches * width,
            transcendentals=0,
        ),
        name="window",
    )(out_grads, queries, keys, values, probs, probs_t)


def body(llm_grads, token_target, patches, gain, w_down, queries, keys, values, window_ids):
    grad_rows = llm_grads[0]
    rows = grad_rows.shape[0]
    images, peers = lax.axis_size("img"), lax.axis_size("seq")
    devices = images * peers
    capacity = max(1, 2 * rows // peers)
    block = w_down.shape[1]
    width = patches.shape[2]
    pieces = block // peers // LANES
    carries = pieces > 0 and 3 * pieces <= capacity

    order = [0]
    while len(order) < images:
        order = [2 * j for j in order] + [2 * j + 1 for j in order]
    image = lax.axis_index("img")

    def columns(j):
        return lax.dynamic_slice(grad_rows, (0, (image ^ j) * block), (rows, block))

    x_blocks = [columns(0)] + [swap(columns(j), "img", j) for j in range(1, images)]
    x_blocks = [x_blocks[j] for j in order]
    probs, probs_t = window_probs(queries[0], keys[0], window_ids[0])

    terms, first = [], 0
    for index, count in enumerate(CHUNKS):
        kept, sent, *sums = project(x_blocks, w_down, first, count * width, index == 0)
        first += count * width
        if index == 0:
            bias_part = sums[0]
        mask = 1
        while 2 * mask < images:
            kept, sent = halve(kept, swap(sent, "img", mask))
            mask *= 2
        terms.append((kept, swap(sent, "img", mask)))
    packed = pack(terms, token_target, bias_part, peers, capacity, carries)
    routed = exchange(packed, "seq", peers)

    share = (devices, 1, width + pieces * LANES) if carries else (1, 1, width)
    out_grads, shared = norm_backward(routed, peers, patches[0], gain[None], share)
    if carries:
        shared = exchange(shared, ("img", "seq"), devices)
        gain_total = jnp.sum(shared[:, 0, :width], axis=0)
        bias_total = shared[:, 0, width:].reshape(-1)
    else:
        gain_total = lax.psum(shared[0, 0], ("img", "seq"))
        bias_total = lax.all_gather(lax.psum(bias_part[0], "seq"), "img", tiled=True)
    grads = window_backward(out_grads, queries[0], keys[0], values[0], probs, probs_t)
    gain_grad = gain_total / math.sqrt(devices * patches.shape[1])
    bias_grad = bias_total / math.sqrt(devices * rows)
    return (grads[0][None], grads[1][None], grads[2][None], gain_grad, bias_grad)


def solution(mesh):
    return jax.shard_map(
        body,
        mesh=mesh,
        in_specs=(
            P("img", "seq", None),
            P("img", "seq"),
            P("img", "seq", None),
            P(),
            P(None, "img"),
            P("img", "seq", None),
            P("img", "seq", None),
            P("img", "seq", None),
            P("img", "seq", None),
        ),
        out_specs=(P("img", "seq", None), P("img", "seq", None), P("img", "seq", None), P(), P()),
        check_vma=False,
    )
```

```python
import functools
import math

import jax
import jax.numpy as jnp
from jax import lax
from jax.experimental import pallas as pl
from jax.experimental.pallas import tpu as pltpu
from jax.sharding import PartitionSpec as P

HEADS = 16
HEAD_DIM = 80
LANES = 128
CHUNKS = (2, 2)
VMEM_BYTES = 16 * 1024 * 1024

F32 = jnp.float32
BF16 = jnp.bfloat16


def iota(shape, axis):
    return lax.broadcasted_iota(jnp.int32, shape, axis)


def dot(a, b, over):
    return lax.dot_general(a, b, ((over[:1], over[1:]), ((), ())), preferred_element_type=F32)


def vmem(count):
    return [pl.BlockSpec(memory_space=pltpu.VMEM)] * count


def head_windows():
    windows = []
    for head in range(HEADS):
        low, high = head * HEAD_DIM, (head + 1) * HEAD_DIM
        start = low // LANES * LANES
        windows.append((low, high, start, -(-high // LANES) * LANES))
    return windows


def lane_mask(low, high, start, stop):
    at = iota((1, stop - start), 1) + start
    return jnp.logical_and(at >= low, at < high)


def masked(x, low, high, start, stop):
    return jnp.where(lane_mask(low, high, start, stop), x, jnp.zeros_like(x))


def project_kernel(blocks, first, tile, with_sum, *refs):
    x_refs, w_ref = refs[:blocks], refs[blocks]
    keep_ref, send_ref = refs[blocks + 2 : blocks + 4]
    x = jnp.concatenate([ref[...] for ref in x_refs], axis=0)
    if with_sum:
        refs[blocks + 4][...] = dot(jnp.ones((16, x.shape[0]), BF16), x, (1, 0))[:1]
    x = x.T
    half = keep_ref.shape[0]
    for t in range(0, keep_ref.shape[1], tile):
        product = dot(w_ref[first + t : first + t + tile], x, (1, 0)).T.astype(BF16)
        keep_ref[:, t : t + tile] = product[:half]
        send_ref[:, t : t + tile] = product[half:]


def project(x_blocks, w_down, touched, first, width, with_sum):
    blocks, (rows, depth) = len(x_blocks), x_blocks[0].shape
    tile = 512
    while width % tile:
        tile //= 2
    out_shape = [jax.ShapeDtypeStruct((blocks * rows // 2, width), BF16)] * 2
    if with_sum:
        out_shape = out_shape + [jax.ShapeDtypeStruct((1, depth), F32)]
    return pl.pallas_call(
        functools.partial(project_kernel, blocks, first, tile, with_sum),
        out_shape=out_shape,
        in_specs=vmem(blocks + 1) + [pl.BlockSpec(memory_space=pl.ANY)],
        out_specs=vmem(len(out_shape)),
        compiler_params=pltpu.CompilerParams(vmem_limit_bytes=VMEM_BYTES),
        cost_estimate=pl.CostEstimate(
            flops=2 * blocks * rows * depth * width,
            bytes_accessed=2 * width * depth,
            transcendentals=0,
        ),
        name="project",
    )(*x_blocks, pltpu.with_memory_space_constraint(w_down, pltpu.VMEM), touched)


def touch_kernel(w_ref, out_ref):
    out_ref[...] = w_ref[: out_ref.shape[0], : out_ref.shape[1]]


def touch(w_down):
    return pl.pallas_call(
        touch_kernel,
        out_shape=jax.ShapeDtypeStruct((16, LANES), w_down.dtype),
        in_specs=vmem(1),
        out_specs=pl.BlockSpec(memory_space=pltpu.VMEM),
        compiler_params=pltpu.CompilerParams(vmem_limit_bytes=VMEM_BYTES),
        cost_estimate=pl.CostEstimate(
            flops=0, bytes_accessed=2 * w_down.size, transcendentals=0
        ),
        name="touch",
    )(pltpu.with_memory_space_constraint(w_down, pltpu.VMEM))


def halve_kernel(kept_ref, got_ref, keep_ref, send_ref):
    half = keep_ref.shape[0]
    keep_ref[...] = kept_ref[:half].astype(F32) + got_ref[:half].astype(F32)
    send_ref[...] = (kept_ref[half:].astype(F32) + got_ref[half:].astype(F32)).astype(BF16)


def halve(kept, got):
    rows, width = kept.shape
    return pl.pallas_call(
        halve_kernel,
        out_shape=[
            jax.ShapeDtypeStruct((rows // 2, width), F32),
            jax.ShapeDtypeStruct((rows // 2, width), BF16),
        ],
        in_specs=vmem(2),
        out_specs=vmem(2),
        compiler_params=pltpu.CompilerParams(vmem_limit_bytes=VMEM_BYTES),
        cost_estimate=pl.CostEstimate(
            flops=rows * width, bytes_accessed=7 * rows * width, transcendentals=0
        ),
        name="halve",
    )(kept, got)


def pack_kernel(peers, capacity, at, first, carries, targets_ref, kept_ref, got_ref, *refs):
    out_ref = refs[-1]
    targets = targets_ref[...]
    rows = targets.shape[1]
    dest = targets // rows
    local = targets - dest * rows
    dest_column = jnp.sum(
        jnp.where(iota((rows, rows), 0) == iota((rows, rows), 1), dest, 0), axis=1, keepdims=True
    )
    same_before = jnp.logical_and(dest_column == dest, iota((rows, rows), 0) < iota((rows, rows), 1))
    rank = jnp.sum(same_before.astype(jnp.int32), axis=0, keepdims=True)
    slots = peers * capacity
    slot = iota((slots, rows), 0)
    chosen = jnp.logical_and(dest == slot // capacity, rank == slot % capacity)
    selector = chosen.astype(F32).astype(BF16)
    total = (kept_ref[...].astype(F32) + got_ref[...].astype(F32)).astype(BF16)
    end = at + total.shape[1]
    out_ref[:, at:end] = dot(selector, total, (1, 0)).astype(BF16)
    if not first:
        out_ref[:, :at] = refs[0][:, :at]
        out_ref[:, end:] = refs[0][:, end:]
        return
    wide = out_ref.shape[1] - (2 * LANES if carries else LANES)
    label = jnp.sum(jnp.where(chosen, local + 1, 0), axis=1, keepdims=True) - 1
    out_ref[:, wide : wide + LANES] = jnp.broadcast_to(label.astype(F32), (slots, LANES)).astype(BF16)
    if carries:
        sums = refs[0][...]
        high = sums.astype(BF16).astype(F32)
        middle = (sums - high).astype(BF16).astype(F32)
        low = (sums - high - middle).astype(BF16).astype(F32)
        extra = jnp.zeros((slots, LANES), F32)
        row = iota((slots, LANES), 0)
        pieces = sums.shape[1] // peers // LANES
        for peer in range(peers):
            for level, values in enumerate((high, middle, low)):
                for piece in range(pieces):
                    start = (peer * pieces + piece) * LANES
                    line = jnp.broadcast_to(values[:, start : start + LANES], (slots, LANES))
                    extra = jnp.where(row == peer * capacity + level * pieces + piece, line, extra)
        out_ref[:, wide + LANES :] = extra.astype(BF16)


def pack(packed, kept, got, targets, sums, peers, capacity, at, wide, carries):
    rows, width = kept.shape
    first = packed is None
    operands = [targets, kept, got] + ([sums] if first and carries else [])
    if not first:
        operands.append(packed)
    return pl.pallas_call(
        functools.partial(pack_kernel, peers, capacity, at, first, carries),
        out_shape=jax.ShapeDtypeStruct((peers * capacity, wide), BF16),
        in_specs=vmem(len(operands)),
        out_specs=pl.BlockSpec(memory_space=pltpu.VMEM),
        compiler_params=pltpu.CompilerParams(vmem_limit_bytes=VMEM_BYTES),
        cost_estimate=pl.CostEstimate(
            flops=2 * rows * peers * capacity * width,
            bytes_accessed=(6 * rows + 2 * peers * capacity) * width,
            transcendentals=0,
        ),
        name="pack",
    )(*operands)


def swap(x, axis, mask):
    n = lax.axis_size(axis)
    return lax.ppermute(x, axis, [(i, i ^ mask) for i in range(n)])


def exchange(x, axis, pieces):
    shape = x.shape
    if x.ndim == 2:
        x = x.reshape(pieces, -1, shape[1])
    return lax.all_to_all(x, axis, split_axis=0, concat_axis=0, tiled=True).reshape(shape)


def probs_kernel(q_ref, k_ref, ids_ref, probs_ref, probs_t_ref):
    patches = q_ref.shape[0]
    ids = ids_ref[...]
    per_token = patches // ids.shape[1]
    token = iota((patches, ids.shape[1]), 0) // per_token
    column = jnp.sum(
        jnp.where(token == iota((patches, ids.shape[1]), 1), ids, 0), axis=1, keepdims=True
    )
    square = (patches, patches)
    row = jnp.sum(
        jnp.where(iota(square, 0) == iota(square, 1), column, 0), axis=0, keepdims=True
    )
    allowed = column == row
    scale = 1.0 / math.sqrt(HEAD_DIM)
    for head, (low, high, start, stop) in enumerate(head_windows()):
        q = masked(q_ref[:, start:stop], low, high, start, stop)
        k = k_ref[:, start:stop]
        for out, scores, axis in (
            (probs_ref, dot(q, k, (1, 1)), 1),
            (probs_t_ref, dot(k, q, (1, 1)), 0),
        ):
            scores = jnp.where(allowed, scores * scale, -jnp.inf)
            weights = jnp.exp(scores - jnp.max(scores, axis=axis, keepdims=True))
            out[head] = weights / jnp.sum(weights, axis=axis, keepdims=True)


def window_probs(queries, keys, ids):
    patches = queries.shape[0]
    shape = jax.ShapeDtypeStruct((HEADS, patches, patches), F32)
    return pl.pallas_call(
        probs_kernel,
        out_shape=[shape, shape],
        in_specs=vmem(3),
        out_specs=vmem(2),
        compiler_params=pltpu.CompilerParams(vmem_limit_bytes=VMEM_BYTES),
        cost_estimate=pl.CostEstimate(
            flops=8 * HEADS * patches * patches * LANES,
            bytes_accessed=8 * HEADS * patches * patches,
            transcendentals=2 * HEADS * patches * patches,
        ),
        name="probs",
    )(queries, keys, ids)


def norm_kernel(peers, carries, patches_ref, gain_ref, routed_ref, out_ref, share_ref):
    patches, width = patches_ref.shape
    slots = routed_ref.shape[0]
    per_token = routed_ref.shape[1] // width
    labels = routed_ref[:, per_token * width : per_token * width + LANES].astype(F32)[:, :1]
    columns = [routed_ref[:, c * width : (c + 1) * width].astype(F32) for c in range(per_token)]
    held = jnp.concatenate(columns, axis=0).astype(BF16)
    lanes = len(columns) * slots
    lane = iota((slots, lanes), 1)
    row_of_lane = jnp.sum(
        jnp.where(lane % slots == iota((slots, lanes), 0), labels, 0.0), axis=0, keepdims=True
    ).astype(jnp.int32)
    patch_of_lane = row_of_lane * len(columns) + iota((1, lanes), 1) // slots
    patch_of_lane = jnp.where(row_of_lane < 0, -1, patch_of_lane)
    chosen = patch_of_lane == iota((patches, lanes), 0)
    patch_grads = dot(chosen.astype(F32).astype(BF16), held, (1, 0))
    inputs = patches_ref[...].astype(F32)
    inverse_rms = lax.rsqrt(jnp.mean(inputs * inputs, axis=1, keepdims=True) + 1e-06)
    normed = inputs * inverse_rms
    gain_part = jnp.sum(patch_grads * normed, axis=0, keepdims=True)
    share_ref[:, :, :width] = jnp.broadcast_to(gain_part[None], (share_ref.shape[0], 1, width))
    if carries:
        carried = routed_ref[:, per_token * width + LANES :].astype(F32)
        capacity = slots // peers
        pieces = (share_ref.shape[2] - width) // LANES
        row = iota((slots, LANES), 0) % capacity
        for piece in range(pieces):
            kept = jnp.logical_and(row % pieces == piece, row < 3 * pieces)
            line = jnp.sum(jnp.where(kept, carried, 0.0), axis=0, keepdims=True)
            at = width + piece * LANES
            share_ref[:, :, at : at + LANES] = jnp.broadcast_to(
                line[None], (share_ref.shape[0], 1, LANES)
            )
    scaled = gain_ref[...] * patch_grads
    out_ref[...] = (
        inverse_rms * (scaled - normed * jnp.mean(scaled * normed, axis=1, keepdims=True))
    ).astype(BF16)


def norm_backward(routed, peers, patches, gain, share):
    count, width = patches.shape
    return pl.pallas_call(
        functools.partial(norm_kernel, peers, share[2] > width),
        out_shape=[jax.ShapeDtypeStruct((count, width), BF16), jax.ShapeDtypeStruct(share, F32)],
        in_specs=vmem(3),
        out_specs=vmem(2),
        compiler_params=pltpu.CompilerParams(vmem_limit_bytes=VMEM_BYTES),
        cost_estimate=pl.CostEstimate(
            flops=2 * count * routed.size,
            bytes_accessed=4 * count * width + 2 * routed.size,
            transcendentals=0,
        ),
        name="norm",
    )(patches, gain, routed)


def window_kernel(g_ref, q_ref, k_ref, v_ref, probs_ref, probs_t_ref, dq_ref, dk_ref, dv_ref):
    width = g_ref.shape[1]
    windows = head_windows()
    scores, scores_t, probs_t = [], [], []
    for head, (low, high, start, stop) in enumerate(windows):
        g = masked(g_ref[:, start:stop], low, high, start, stop)
        v = v_ref[:, start:stop]
        found = []
        for ref, grads, axis in (
            (probs_ref, dot(g, v, (1, 1)), 1),
            (probs_t_ref, dot(v, g, (1, 1)), 0),
        ):
            probs = ref[head]
            rounded = probs.astype(BF16)
            delta = jnp.sum(rounded.astype(F32) * grads, axis=axis, keepdims=True)
            found.append(((probs * (grads - delta)).astype(BF16), rounded))
        scores.append(found[0][0])
        scores_t.append(found[1][0])
        probs_t.append(found[1][1])
    scale = 1.0 / math.sqrt(HEAD_DIM)
    for start in range(0, width, LANES):
        stop = start + LANES
        heads = [h for h, (low, high, _, _) in enumerate(windows) if low < stop and high > start]
        for out, left, right_ref, factor in (
            (dq_ref, scores, k_ref, scale),
            (dk_ref, scores_t, q_ref, scale),
            (dv_ref, probs_t, g_ref, 1.0),
        ):
            right = right_ref[:, start:stop]
            rows = [masked(right, windows[h][0], windows[h][1], start, stop) for h in heads]
            product = dot(
                jnp.concatenate([left[h] for h in heads], axis=1),
                jnp.concatenate(rows, axis=0),
                (1, 0),
            )
            out[:, start:stop] = (product * factor).astype(BF16)


def window_backward(out_grads, queries, keys, values, probs, probs_t):
    patches, width = queries.shape
    shape = jax.ShapeDtypeStruct((patches, width), BF16)
    return pl.pallas_call(
        window_kernel,
        out_shape=[shape] * 3,
        in_specs=vmem(6),
        out_specs=vmem(3),
        compiler_params=pltpu.CompilerParams(vmem_limit_bytes=VMEM_BYTES),
        cost_estimate=pl.CostEstimate(
            flops=10 * HEADS * patches * patches * LANES,
            bytes_accessed=8 * HEADS * patches * patches + 14 * patches * width,
            transcendentals=0,
        ),
        name="window",
    )(out_grads, queries, keys, values, probs, probs_t)


def body(llm_grads, token_target, patches, gain, w_down, queries, keys, values, window_ids):
    grad_rows = llm_grads[0]
    rows = grad_rows.shape[0]
    images, peers = lax.axis_size("img"), lax.axis_size("seq")
    devices = images * peers
    capacity = max(1, 2 * rows // peers)
    block = w_down.shape[1]
    width = patches.shape[2]
    pieces = block // peers // LANES
    carries = pieces > 0 and 3 * pieces <= capacity

    order = [0]
    while len(order) < images:
        order = [2 * j for j in order] + [2 * j + 1 for j in order]
    image = lax.axis_index("img")

    def columns(j):
        return lax.dynamic_slice(grad_rows, (0, (image ^ j) * block), (rows, block))

    x_blocks = [columns(0)] + [swap(columns(j), "img", j) for j in range(1, images)]
    x_blocks = [x_blocks[j] for j in order]
    probs, probs_t = window_probs(queries[0], keys[0], window_ids[0])

    touched = touch(w_down)
    wide = w_down.shape[0] + (2 * LANES if carries else LANES)
    packed, first = None, 0
    for index, count in enumerate(CHUNKS):
        kept, sent, *sums = project(x_blocks, w_down, touched, first, count * width, index == 0)
        at, first = first, first + count * width
        if index == 0:
            bias_part = sums[0]
        mask = 1
        while 2 * mask < images:
            kept, sent = halve(kept, swap(sent, "img", mask))
            mask *= 2
        got = swap(sent, "img", mask)
        packed = pack(
            packed, kept, got, token_target, bias_part, peers, capacity, at, wide, carries
        )
    routed = exchange(packed, "seq", peers)

    share = (1, 1, width + pieces * LANES if carries else width)
    out_grads, shared = norm_backward(routed, peers, patches[0], gain[None], share)
    if carries:
        shared = jnp.broadcast_to(shared, (devices,) + shared.shape[1:])
        shared = exchange(shared, ("img", "seq"), devices)
        gain_total = jnp.sum(shared[:, 0, :width], axis=0)
        bias_total = shared[:, 0, width:].reshape(-1)
    else:
        gain_total = lax.psum(shared[0, 0], ("img", "seq"))
        bias_total = lax.all_gather(lax.psum(bias_part[0], "seq"), "img", tiled=True)
    grads = window_backward(out_grads, queries[0], keys[0], values[0], probs, probs_t)
    gain_grad = gain_total / math.sqrt(devices * patches.shape[1])
    bias_grad = bias_total / math.sqrt(devices * rows)
    return (grads[0][None], grads[1][None], grads[2][None], gain_grad, bias_grad)


def solution(mesh):
    return jax.shard_map(
        body,
        mesh=mesh,
        in_specs=(
            P("img", "seq", None),
            P("img", "seq"),
            P("img", "seq", None),
            P(),
            P(None, "img"),
            P("img", "seq", None),
            P("img", "seq", None),
            P("img", "seq", None),
            P("img", "seq", None),
        ),
        out_specs=(P("img", "seq", None), P("img", "seq", None), P("img", "seq", None), P(), P()),
        check_vma=False,
    )
```

```python
import functools
import math

import jax
import jax.numpy as jnp
from jax import lax
from jax.experimental import pallas as pl
from jax.experimental.pallas import tpu as pltpu
from jax.sharding import PartitionSpec as P

HEADS = 16
HEAD_DIM = 80
LANES = 128
CHUNKS = (2, 2)
DIRECT = 8
VMEM_BYTES = 16 * 1024 * 1024

F32 = jnp.float32
BF16 = jnp.bfloat16


def iota(shape, axis):
    return lax.broadcasted_iota(jnp.int32, shape, axis)


def dot(a, b, over):
    return lax.dot_general(a, b, ((over[:1], over[1:]), ((), ())), preferred_element_type=F32)


def vmem(count):
    return [pl.BlockSpec(memory_space=pltpu.VMEM)] * count


def head_windows():
    windows = []
    for head in range(HEADS):
        low, high = head * HEAD_DIM, (head + 1) * HEAD_DIM
        start = low // LANES * LANES
        windows.append((low, high, start, -(-high // LANES) * LANES))
    return windows


def lane_mask(low, high, start, stop):
    at = iota((1, stop - start), 1) + start
    return jnp.logical_and(at >= low, at < high)


def masked(x, low, high, start, stop):
    return jnp.where(lane_mask(low, high, start, stop), x, jnp.zeros_like(x))


def project_kernel(blocks, first, tile, with_sum, *refs):
    x_refs, w_ref = refs[:blocks], refs[blocks]
    keep_ref, send_ref = refs[blocks + 2 : blocks + 4]
    x = jnp.concatenate([ref[...] for ref in x_refs], axis=0)
    if with_sum:
        refs[blocks + 4][...] = dot(jnp.ones((16, x.shape[0]), BF16), x, (1, 0))[:1]
    x = x.T
    half = keep_ref.shape[0]
    for t in range(0, keep_ref.shape[1], tile):
        product = dot(w_ref[first + t : first + t + tile], x, (1, 0)).T.astype(BF16)
        keep_ref[:, t : t + tile] = product[:half]
        send_ref[:, t : t + tile] = product[half:]


def project(x_blocks, w_down, touched, first, width, with_sum):
    blocks, (rows, depth) = len(x_blocks), x_blocks[0].shape
    tile = 512
    while width % tile:
        tile //= 2
    out_shape = [jax.ShapeDtypeStruct((blocks * rows // 2, width), BF16)] * 2
    if with_sum:
        out_shape = out_shape + [jax.ShapeDtypeStruct((1, depth), F32)]
    return pl.pallas_call(
        functools.partial(project_kernel, blocks, first, tile, with_sum),
        out_shape=out_shape,
        in_specs=vmem(blocks + 1) + [pl.BlockSpec(memory_space=pl.ANY)],
        out_specs=vmem(len(out_shape)),
        compiler_params=pltpu.CompilerParams(vmem_limit_bytes=VMEM_BYTES),
        cost_estimate=pl.CostEstimate(
            flops=2 * blocks * rows * depth * width,
            bytes_accessed=2 * width * depth,
            transcendentals=0,
        ),
        name="project",
    )(*x_blocks, pltpu.with_memory_space_constraint(w_down, pltpu.VMEM), touched)


def touch_kernel(w_ref, out_ref):
    out_ref[...] = w_ref[: out_ref.shape[0], : out_ref.shape[1]]


def touch(w_down):
    return pl.pallas_call(
        touch_kernel,
        out_shape=jax.ShapeDtypeStruct((16, LANES), w_down.dtype),
        in_specs=vmem(1),
        out_specs=pl.BlockSpec(memory_space=pltpu.VMEM),
        compiler_params=pltpu.CompilerParams(vmem_limit_bytes=VMEM_BYTES),
        cost_estimate=pl.CostEstimate(
            flops=0, bytes_accessed=2 * w_down.size, transcendentals=0
        ),
        name="touch",
    )(pltpu.with_memory_space_constraint(w_down, pltpu.VMEM))


def halve_kernel(kept_ref, got_ref, keep_ref, send_ref):
    half = keep_ref.shape[0]
    keep_ref[...] = kept_ref[:half].astype(F32) + got_ref[:half].astype(F32)
    send_ref[...] = (kept_ref[half:].astype(F32) + got_ref[half:].astype(F32)).astype(BF16)


def halve(kept, got):
    rows, width = kept.shape
    return pl.pallas_call(
        halve_kernel,
        out_shape=[
            jax.ShapeDtypeStruct((rows // 2, width), F32),
            jax.ShapeDtypeStruct((rows // 2, width), BF16),
        ],
        in_specs=vmem(2),
        out_specs=vmem(2),
        compiler_params=pltpu.CompilerParams(vmem_limit_bytes=VMEM_BYTES),
        cost_estimate=pl.CostEstimate(
            flops=rows * width, bytes_accessed=7 * rows * width, transcendentals=0
        ),
        name="halve",
    )(kept, got)


def peer_masks(peers):
    return (0, 7, 2, 3, 1, 4, 6, 5) if peers == 8 else tuple(range(peers))


def block_peer(block, peers, me):
    peer = jnp.zeros_like(block)
    for place, mask in enumerate(peer_masks(peers)):
        peer = jnp.where(block == place, mask ^ me, peer)
    return peer


def pack_kernel(peers, capacity, chunks, direct, carries, me_ref, targets_ref, *refs):
    terms, refs = refs[: 2 * chunks], refs[2 * chunks :]
    outs = refs[1:] if carries else refs
    targets = targets_ref[...]
    rows = targets.shape[1]
    dest = targets // rows
    local = targets - dest * rows
    dest_column = jnp.sum(
        jnp.where(iota((rows, rows), 0) == iota((rows, rows), 1), dest, 0), axis=1, keepdims=True
    )
    same_before = jnp.logical_and(dest_column == dest, iota((rows, rows), 0) < iota((rows, rows), 1))
    rank = jnp.sum(same_before.astype(jnp.int32), axis=0, keepdims=True)
    slots = peers * capacity
    slot = iota((slots, rows), 0)
    holder = slot // capacity
    if direct:
        holder = block_peer(holder, peers, me_ref[0])
    chosen = jnp.logical_and(dest == holder, rank == slot % capacity)
    selector = chosen.astype(F32).astype(BF16)
    parts = []
    for chunk in range(chunks):
        kept, got = terms[2 * chunk : 2 * chunk + 2]
        total = (kept[...].astype(F32) + got[...].astype(F32)).astype(BF16)
        parts.append(dot(selector, total, (1, 0)))
    label = jnp.sum(jnp.where(chosen, local + 1, 0), axis=1, keepdims=True) - 1
    parts.append(jnp.broadcast_to(label.astype(F32), (slots, LANES)))
    if carries:
        sums = refs[0][...]
        high = sums.astype(BF16).astype(F32)
        middle = (sums - high).astype(BF16).astype(F32)
        low = (sums - high - middle).astype(BF16).astype(F32)
        extra = jnp.zeros((slots, LANES), F32)
        row = iota((slots, LANES), 0) % capacity
        peer = iota((slots, LANES), 0) // capacity
        if direct:
            peer = block_peer(peer, peers, me_ref[0])
        pieces = sums.shape[1] // peers // LANES
        for p in range(peers):
            for level, values in enumerate((high, middle, low)):
                for piece in range(pieces):
                    start = (p * pieces + piece) * LANES
                    line = jnp.broadcast_to(values[:, start : start + LANES], (slots, LANES))
                    here = jnp.logical_and(peer == p, row == level * pieces + piece)
                    extra = jnp.where(here, line, extra)
        parts.append(extra)
    at = 0
    for part in parts:
        end = at + part.shape[1]
        if direct:
            for m in range(peers):
                outs[m][:, at:end] = part[m * capacity : (m + 1) * capacity].astype(BF16)
        else:
            outs[0][:, at:end] = part.astype(BF16)
        at = end


def pack(terms, targets, me, sums, peers, capacity, direct, carries):
    rows = targets.shape[1]
    width = sum(kept.shape[1] for kept, _ in terms) + (2 * LANES if carries else LANES)
    operands = [me, targets] + [x for pair in terms for x in pair] + ([sums] if carries else [])
    if direct:
        out_shape = [jax.ShapeDtypeStruct((capacity, width), BF16)] * peers
    else:
        out_shape = [jax.ShapeDtypeStruct((peers * capacity, width), BF16)]
    return pl.pallas_call(
        functools.partial(pack_kernel, peers, capacity, len(terms), direct, carries),
        out_shape=out_shape,
        in_specs=[pl.BlockSpec(memory_space=pltpu.SMEM)] + vmem(len(operands) - 1),
        out_specs=vmem(len(out_shape)),
        compiler_params=pltpu.CompilerParams(vmem_limit_bytes=VMEM_BYTES),
        cost_estimate=pl.CostEstimate(
            flops=2 * rows * peers * capacity * width,
            bytes_accessed=(6 * rows + 2 * peers * capacity) * width,
            transcendentals=0,
        ),
        name="pack",
    )(*operands)


def route(packed, peers, direct):
    if not direct:
        return [exchange(packed[0], "seq", peers)]
    masks = peer_masks(peers)
    return [swap(block, "seq", mask) if mask else block for block, mask in zip(packed, masks)]


def swap(x, axis, mask):
    n = lax.axis_size(axis)
    return lax.ppermute(x, axis, [(i, i ^ mask) for i in range(n)])


def exchange(x, axis, pieces):
    shape = x.shape
    if x.ndim == 2:
        x = x.reshape(pieces, -1, shape[1])
    return lax.all_to_all(x, axis, split_axis=0, concat_axis=0, tiled=True).reshape(shape)


def probs_kernel(q_ref, k_ref, ids_ref, probs_ref, probs_t_ref):
    patches = q_ref.shape[0]
    ids = ids_ref[...]
    per_token = patches // ids.shape[1]
    token = iota((patches, ids.shape[1]), 0) // per_token
    column = jnp.sum(
        jnp.where(token == iota((patches, ids.shape[1]), 1), ids, 0), axis=1, keepdims=True
    )
    square = (patches, patches)
    row = jnp.sum(
        jnp.where(iota(square, 0) == iota(square, 1), column, 0), axis=0, keepdims=True
    )
    allowed = column == row
    scale = 1.0 / math.sqrt(HEAD_DIM)
    for head, (low, high, start, stop) in enumerate(head_windows()):
        q = masked(q_ref[:, start:stop], low, high, start, stop)
        k = k_ref[:, start:stop]
        for out, scores, axis in (
            (probs_ref, dot(q, k, (1, 1)), 1),
            (probs_t_ref, dot(k, q, (1, 1)), 0),
        ):
            scores = jnp.where(allowed, scores * scale, -jnp.inf)
            weights = jnp.exp(scores - jnp.max(scores, axis=axis, keepdims=True))
            out[head] = weights / jnp.sum(weights, axis=axis, keepdims=True)


def window_probs(queries, keys, ids):
    patches = queries.shape[0]
    shape = jax.ShapeDtypeStruct((HEADS, patches, patches), F32)
    return pl.pallas_call(
        probs_kernel,
        out_shape=[shape, shape],
        in_specs=vmem(3),
        out_specs=vmem(2),
        compiler_params=pltpu.CompilerParams(vmem_limit_bytes=VMEM_BYTES),
        cost_estimate=pl.CostEstimate(
            flops=8 * HEADS * patches * patches * LANES,
            bytes_accessed=8 * HEADS * patches * patches,
            transcendentals=2 * HEADS * patches * patches,
        ),
        name="probs",
    )(queries, keys, ids)


def norm_kernel(peers, carries, patches_ref, gain_ref, *refs):
    pieces, (out_ref, share_ref) = refs[:-2], refs[-2:]
    patches, width = patches_ref.shape
    pieces = [ref[...].astype(F32) for ref in pieces]
    routed = jnp.concatenate(pieces, axis=0) if len(pieces) > 1 else pieces[0]
    slots = routed.shape[0]
    per_token = routed.shape[1] // width
    labels = routed[:, per_token * width : per_token * width + 1]
    columns = [routed[:, c * width : (c + 1) * width] for c in range(per_token)]
    held = jnp.concatenate(columns, axis=0).astype(BF16)
    lanes = len(columns) * slots
    lane = iota((slots, lanes), 1)
    row_of_lane = jnp.sum(
        jnp.where(lane % slots == iota((slots, lanes), 0), labels, 0.0), axis=0, keepdims=True
    ).astype(jnp.int32)
    patch_of_lane = row_of_lane * len(columns) + iota((1, lanes), 1) // slots
    patch_of_lane = jnp.where(row_of_lane < 0, -1, patch_of_lane)
    chosen = patch_of_lane == iota((patches, lanes), 0)
    patch_grads = dot(chosen.astype(F32).astype(BF16), held, (1, 0))
    inputs = patches_ref[...].astype(F32)
    inverse_rms = lax.rsqrt(jnp.mean(inputs * inputs, axis=1, keepdims=True) + 1e-06)
    normed = inputs * inverse_rms
    gain_part = jnp.sum(patch_grads * normed, axis=0, keepdims=True)
    share_ref[:, :, :width] = jnp.broadcast_to(gain_part[None], (share_ref.shape[0], 1, width))
    if carries:
        carried = routed[:, per_token * width + LANES :]
        capacity = slots // peers
        pieces = (share_ref.shape[2] - width) // LANES
        row = iota((slots, LANES), 0) % capacity
        for piece in range(pieces):
            kept = jnp.logical_and(row % pieces == piece, row < 3 * pieces)
            line = jnp.sum(jnp.where(kept, carried, 0.0), axis=0, keepdims=True)
            at = width + piece * LANES
            share_ref[:, :, at : at + LANES] = jnp.broadcast_to(
                line[None], (share_ref.shape[0], 1, LANES)
            )
    scaled = gain_ref[...] * patch_grads
    out_ref[...] = (
        inverse_rms * (scaled - normed * jnp.mean(scaled * normed, axis=1, keepdims=True))
    ).astype(BF16)


def norm_backward(received, peers, patches, gain, share):
    count, width = patches.shape
    routed = sum(x.size for x in received)
    return pl.pallas_call(
        functools.partial(norm_kernel, peers, share[2] > width),
        out_shape=[jax.ShapeDtypeStruct((count, width), BF16), jax.ShapeDtypeStruct(share, F32)],
        in_specs=vmem(2 + len(received)),
        out_specs=vmem(2),
        compiler_params=pltpu.CompilerParams(vmem_limit_bytes=VMEM_BYTES),
        cost_estimate=pl.CostEstimate(
            flops=2 * count * routed,
            bytes_accessed=4 * count * width + 2 * routed,
            transcendentals=0,
        ),
        name="norm",
    )(patches, gain, *received)


def window_kernel(g_ref, q_ref, k_ref, v_ref, probs_ref, probs_t_ref, dq_ref, dk_ref, dv_ref):
    width = g_ref.shape[1]
    windows = head_windows()
    scores, scores_t, probs_t = [], [], []
    for head, (low, high, start, stop) in enumerate(windows):
        g = masked(g_ref[:, start:stop], low, high, start, stop)
        v = v_ref[:, start:stop]
        found = []
        for ref, grads, axis in (
            (probs_ref, dot(g, v, (1, 1)), 1),
            (probs_t_ref, dot(v, g, (1, 1)), 0),
        ):
            probs = ref[head]
            rounded = probs.astype(BF16)
            delta = jnp.sum(rounded.astype(F32) * grads, axis=axis, keepdims=True)
            found.append(((probs * (grads - delta)).astype(BF16), rounded))
        scores.append(found[0][0])
        scores_t.append(found[1][0])
        probs_t.append(found[1][1])
    scale = 1.0 / math.sqrt(HEAD_DIM)
    for start in range(0, width, LANES):
        stop = start + LANES
        heads = [h for h, (low, high, _, _) in enumerate(windows) if low < stop and high > start]
        for out, left, right_ref, factor in (
            (dq_ref, scores, k_ref, scale),
            (dk_ref, scores_t, q_ref, scale),
            (dv_ref, probs_t, g_ref, 1.0),
        ):
            right = right_ref[:, start:stop]
            rows = [masked(right, windows[h][0], windows[h][1], start, stop) for h in heads]
            product = dot(
                jnp.concatenate([left[h] for h in heads], axis=1),
                jnp.concatenate(rows, axis=0),
                (1, 0),
            )
            out[:, start:stop] = (product * factor).astype(BF16)


def window_backward(out_grads, queries, keys, values, probs, probs_t):
    patches, width = queries.shape
    shape = jax.ShapeDtypeStruct((patches, width), BF16)
    return pl.pallas_call(
        window_kernel,
        out_shape=[shape] * 3,
        in_specs=vmem(6),
        out_specs=vmem(3),
        compiler_params=pltpu.CompilerParams(vmem_limit_bytes=VMEM_BYTES),
        cost_estimate=pl.CostEstimate(
            flops=10 * HEADS * patches * patches * LANES,
            bytes_accessed=8 * HEADS * patches * patches + 14 * patches * width,
            transcendentals=0,
        ),
        name="window",
    )(out_grads, queries, keys, values, probs, probs_t)


def body(llm_grads, token_target, patches, gain, w_down, queries, keys, values, window_ids):
    grad_rows = llm_grads[0]
    rows = grad_rows.shape[0]
    images, peers = lax.axis_size("img"), lax.axis_size("seq")
    devices = images * peers
    capacity = max(1, 2 * rows // peers)
    direct = peers <= DIRECT
    block = w_down.shape[1]
    width = patches.shape[2]
    pieces = block // peers // LANES
    carries = pieces > 0 and 3 * pieces <= capacity

    order = [0]
    while len(order) < images:
        order = [2 * j for j in order] + [2 * j + 1 for j in order]
    image, me = lax.axis_index("img"), lax.axis_index("seq")

    def columns(j):
        return lax.dynamic_slice(grad_rows, (0, (image ^ j) * block), (rows, block))

    x_blocks = [columns(0)] + [swap(columns(j), "img", j) for j in range(1, images)]
    x_blocks = [x_blocks[j] for j in order]
    probs, probs_t = window_probs(queries[0], keys[0], window_ids[0])

    touched = touch(w_down)
    terms, first = [], 0
    for index, count in enumerate(CHUNKS):
        kept, sent, *sums = project(x_blocks, w_down, touched, first, count * width, index == 0)
        first += count * width
        if index == 0:
            bias_part = sums[0]
        mask = 1
        while 2 * mask < images:
            kept, sent = halve(kept, swap(sent, "img", mask))
            mask *= 2
        terms.append((kept, swap(sent, "img", mask)))
    packed = pack(terms, token_target, me.reshape(1), bias_part, peers, capacity, direct, carries)
    routed = route(packed, peers, direct)

    share = (1, 1, width + pieces * LANES if carries else width)
    out_grads, shared = norm_backward(routed, peers, patches[0], gain[None], share)
    if carries:
        shared = jnp.broadcast_to(shared, (devices,) + shared.shape[1:])
        shared = exchange(shared, ("img", "seq"), devices)
        gain_total = jnp.sum(shared[:, 0, :width], axis=0)
        bias_total = shared[:, 0, width:].reshape(-1)
    else:
        gain_total = lax.psum(shared[0, 0], ("img", "seq"))
        bias_total = lax.all_gather(lax.psum(bias_part[0], "seq"), "img", tiled=True)
    grads = window_backward(out_grads, queries[0], keys[0], values[0], probs, probs_t)
    gain_grad = gain_total / math.sqrt(devices * patches.shape[1])
    bias_grad = bias_total / math.sqrt(devices * rows)
    return (grads[0][None], grads[1][None], grads[2][None], gain_grad, bias_grad)


def solution(mesh):
    return jax.shard_map(
        body,
        mesh=mesh,
        in_specs=(
            P("img", "seq", None),
            P("img", "seq"),
            P("img", "seq", None),
            P(),
            P(None, "img"),
            P("img", "seq", None),
            P("img", "seq", None),
            P("img", "seq", None),
            P("img", "seq", None),
        ),
        out_specs=(P("img", "seq", None), P("img", "seq", None), P("img", "seq", None), P(), P()),
        check_vma=False,
    )
```

```python
import functools
import math

import jax
import jax.numpy as jnp
from jax import lax
from jax.experimental import pallas as pl
from jax.experimental.pallas import tpu as pltpu
from jax.sharding import PartitionSpec as P

HEADS = 16
HEAD_DIM = 80
LANES = 128
CHUNKS = (2, 2)
DIRECT = 8
VMEM_BYTES = 16 * 1024 * 1024

F32 = jnp.float32
BF16 = jnp.bfloat16


def iota(shape, axis):
    return lax.broadcasted_iota(jnp.int32, shape, axis)


def dot(a, b, over):
    return lax.dot_general(a, b, ((over[:1], over[1:]), ((), ())), preferred_element_type=F32)


def vmem(count):
    return [pl.BlockSpec(memory_space=pltpu.VMEM)] * count


def head_windows():
    windows = []
    for head in range(HEADS):
        low, high = head * HEAD_DIM, (head + 1) * HEAD_DIM
        start = low // LANES * LANES
        windows.append((low, high, start, -(-high // LANES) * LANES))
    return windows


def lane_mask(low, high, start, stop):
    at = iota((1, stop - start), 1) + start
    return jnp.logical_and(at >= low, at < high)


def masked(x, low, high, start, stop):
    return jnp.where(lane_mask(low, high, start, stop), x, jnp.zeros_like(x))


def project_kernel(blocks, first, tile, with_sum, *refs):
    x_refs, w_ref = refs[:blocks], refs[blocks]
    keep_ref, send_ref = refs[blocks + 2 : blocks + 4]
    x = jnp.concatenate([ref[...] for ref in x_refs], axis=0)
    if with_sum:
        refs[blocks + 4][...] = dot(jnp.ones((16, x.shape[0]), BF16), x, (1, 0))[:1]
    x = x.T
    half = keep_ref.shape[0]
    for t in range(0, keep_ref.shape[1], tile):
        product = dot(w_ref[first + t : first + t + tile], x, (1, 0)).T.astype(BF16)
        keep_ref[:, t : t + tile] = product[:half]
        send_ref[:, t : t + tile] = product[half:]


def project(x_blocks, w_down, touched, first, width, with_sum):
    blocks, (rows, depth) = len(x_blocks), x_blocks[0].shape
    tile = 1280
    while width % tile:
        tile //= 2
    out_shape = [jax.ShapeDtypeStruct((blocks * rows // 2, width), BF16)] * 2
    if with_sum:
        out_shape = out_shape + [jax.ShapeDtypeStruct((1, depth), F32)]
    return pl.pallas_call(
        functools.partial(project_kernel, blocks, first, tile, with_sum),
        out_shape=out_shape,
        in_specs=vmem(blocks + 1) + [pl.BlockSpec(memory_space=pl.ANY)],
        out_specs=vmem(len(out_shape)),
        compiler_params=pltpu.CompilerParams(vmem_limit_bytes=VMEM_BYTES),
        cost_estimate=pl.CostEstimate(
            flops=2 * blocks * rows * depth * width,
            bytes_accessed=2 * width * depth,
            transcendentals=0,
        ),
        name="project",
    )(*x_blocks, pltpu.with_memory_space_constraint(w_down, pltpu.VMEM), touched)


def touch_kernel(w_ref, out_ref):
    out_ref[...] = w_ref[: out_ref.shape[0], : out_ref.shape[1]]


def touch(w_down):
    return pl.pallas_call(
        touch_kernel,
        out_shape=jax.ShapeDtypeStruct((16, LANES), w_down.dtype),
        in_specs=vmem(1),
        out_specs=pl.BlockSpec(memory_space=pltpu.VMEM),
        compiler_params=pltpu.CompilerParams(vmem_limit_bytes=VMEM_BYTES),
        cost_estimate=pl.CostEstimate(
            flops=0, bytes_accessed=2 * w_down.size, transcendentals=0
        ),
        name="touch",
    )(pltpu.with_memory_space_constraint(w_down, pltpu.VMEM))


def halve_kernel(kept_ref, got_ref, keep_ref, send_ref):
    half = keep_ref.shape[0]
    keep_ref[...] = kept_ref[:half].astype(F32) + got_ref[:half].astype(F32)
    send_ref[...] = (kept_ref[half:].astype(F32) + got_ref[half:].astype(F32)).astype(BF16)


def halve(kept, got):
    rows, width = kept.shape
    return pl.pallas_call(
        halve_kernel,
        out_shape=[
            jax.ShapeDtypeStruct((rows // 2, width), F32),
            jax.ShapeDtypeStruct((rows // 2, width), BF16),
        ],
        in_specs=vmem(2),
        out_specs=vmem(2),
        compiler_params=pltpu.CompilerParams(vmem_limit_bytes=VMEM_BYTES),
        cost_estimate=pl.CostEstimate(
            flops=rows * width, bytes_accessed=7 * rows * width, transcendentals=0
        ),
        name="halve",
    )(kept, got)


def peer_masks(peers):
    return (0, 1, 4, 6, 5, 7, 2, 3) if peers == 8 else tuple(range(peers))


def block_peer(block, peers, me):
    peer = jnp.zeros_like(block)
    for place, mask in enumerate(peer_masks(peers)):
        peer = jnp.where(block == place, mask ^ me, peer)
    return peer


def pack_kernel(peers, capacity, chunks, direct, carries, me_ref, targets_ref, *refs):
    terms, refs = refs[: 2 * chunks], refs[2 * chunks :]
    outs = refs[1:] if carries else refs
    targets = targets_ref[...]
    rows = targets.shape[1]
    dest = targets // rows
    local = targets - dest * rows
    dest_column = jnp.sum(
        jnp.where(iota((rows, rows), 0) == iota((rows, rows), 1), dest, 0), axis=1, keepdims=True
    )
    same_before = jnp.logical_and(dest_column == dest, iota((rows, rows), 0) < iota((rows, rows), 1))
    rank = jnp.sum(same_before.astype(jnp.int32), axis=0, keepdims=True)
    slots = peers * capacity
    slot = iota((slots, rows), 0)
    holder = slot // capacity
    if direct:
        holder = block_peer(holder, peers, me_ref[0])
    chosen = jnp.logical_and(dest == holder, rank == slot % capacity)
    selector = chosen.astype(F32).astype(BF16)
    parts = []
    for chunk in range(chunks):
        kept, got = terms[2 * chunk : 2 * chunk + 2]
        total = (kept[...].astype(F32) + got[...].astype(F32)).astype(BF16)
        parts.append(dot(selector, total, (1, 0)))
    label = jnp.sum(jnp.where(chosen, local + 1, 0), axis=1, keepdims=True) - 1
    parts.append(jnp.broadcast_to(label.astype(F32), (slots, LANES)))
    if carries:
        sums = refs[0][...]
        high = sums.astype(BF16).astype(F32)
        middle = (sums - high).astype(BF16).astype(F32)
        low = (sums - high - middle).astype(BF16).astype(F32)
        extra = jnp.zeros((slots, LANES), F32)
        row = iota((slots, LANES), 0) % capacity
        peer = iota((slots, LANES), 0) // capacity
        if direct:
            peer = block_peer(peer, peers, me_ref[0])
        pieces = sums.shape[1] // peers // LANES
        for p in range(peers):
            for level, values in enumerate((high, middle, low)):
                for piece in range(pieces):
                    start = (p * pieces + piece) * LANES
                    line = jnp.broadcast_to(values[:, start : start + LANES], (slots, LANES))
                    here = jnp.logical_and(peer == p, row == level * pieces + piece)
                    extra = jnp.where(here, line, extra)
        parts.append(extra)
    at = 0
    for part in parts:
        end = at + part.shape[1]
        if direct:
            for m in range(peers):
                outs[m][:, at:end] = part[m * capacity : (m + 1) * capacity].astype(BF16)
        else:
            outs[0][:, at:end] = part.astype(BF16)
        at = end


def pack(terms, targets, me, sums, peers, capacity, direct, carries):
    rows = targets.shape[1]
    width = sum(kept.shape[1] for kept, _ in terms) + (2 * LANES if carries else LANES)
    operands = [me, targets] + [x for pair in terms for x in pair] + ([sums] if carries else [])
    if direct:
        out_shape = [jax.ShapeDtypeStruct((capacity, width), BF16)] * peers
    else:
        out_shape = [jax.ShapeDtypeStruct((peers * capacity, width), BF16)]
    return pl.pallas_call(
        functools.partial(pack_kernel, peers, capacity, len(terms), direct, carries),
        out_shape=out_shape,
        in_specs=[pl.BlockSpec(memory_space=pltpu.SMEM)] + vmem(len(operands) - 1),
        out_specs=vmem(len(out_shape)),
        compiler_params=pltpu.CompilerParams(vmem_limit_bytes=VMEM_BYTES),
        cost_estimate=pl.CostEstimate(
            flops=2 * rows * peers * capacity * width,
            bytes_accessed=(6 * rows + 2 * peers * capacity) * width,
            transcendentals=0,
        ),
        name="pack",
    )(*operands)


def route(packed, peers, direct):
    if not direct:
        return [exchange(packed[0], "seq", peers)]
    masks = peer_masks(peers)
    return [swap(block, "seq", mask) if mask else block for block, mask in zip(packed, masks)]


def swap(x, axis, mask):
    n = lax.axis_size(axis)
    return lax.ppermute(x, axis, [(i, i ^ mask) for i in range(n)])


def exchange(x, axis, pieces):
    shape = x.shape
    if x.ndim == 2:
        x = x.reshape(pieces, -1, shape[1])
    return lax.all_to_all(x, axis, split_axis=0, concat_axis=0, tiled=True).reshape(shape)


def probs_kernel(q_ref, k_ref, ids_ref, probs_ref, probs_t_ref):
    patches = q_ref.shape[0]
    ids = ids_ref[...]
    per_token = patches // ids.shape[1]
    token = iota((patches, ids.shape[1]), 0) // per_token
    column = jnp.sum(
        jnp.where(token == iota((patches, ids.shape[1]), 1), ids, 0), axis=1, keepdims=True
    )
    square = (patches, patches)
    row = jnp.sum(
        jnp.where(iota(square, 0) == iota(square, 1), column, 0), axis=0, keepdims=True
    )
    allowed = column == row
    scale = 1.0 / math.sqrt(HEAD_DIM)
    for head, (low, high, start, stop) in enumerate(head_windows()):
        q = masked(q_ref[:, start:stop], low, high, start, stop)
        k = k_ref[:, start:stop]
        for out, scores, axis in (
            (probs_ref, dot(q, k, (1, 1)), 1),
            (probs_t_ref, dot(k, q, (1, 1)), 0),
        ):
            scores = jnp.where(allowed, scores * scale, -jnp.inf)
            weights = jnp.exp(scores - jnp.max(scores, axis=axis, keepdims=True))
            out[head] = weights / jnp.sum(weights, axis=axis, keepdims=True)


def window_probs(queries, keys, ids):
    patches = queries.shape[0]
    shape = jax.ShapeDtypeStruct((HEADS, patches, patches), F32)
    return pl.pallas_call(
        probs_kernel,
        out_shape=[shape, shape],
        in_specs=vmem(3),
        out_specs=vmem(2),
        compiler_params=pltpu.CompilerParams(vmem_limit_bytes=VMEM_BYTES),
        cost_estimate=pl.CostEstimate(
            flops=8 * HEADS * patches * patches * LANES,
            bytes_accessed=8 * HEADS * patches * patches,
            transcendentals=2 * HEADS * patches * patches,
        ),
        name="probs",
    )(queries, keys, ids)


def norm_kernel(peers, carries, patches_ref, gain_ref, *refs):
    pieces, (out_ref, share_ref) = refs[:-2], refs[-2:]
    patches, width = patches_ref.shape
    pieces = [ref[...].astype(F32) for ref in pieces]
    routed = jnp.concatenate(pieces, axis=0) if len(pieces) > 1 else pieces[0]
    slots = routed.shape[0]
    per_token = routed.shape[1] // width
    labels = routed[:, per_token * width : per_token * width + 1]
    columns = [routed[:, c * width : (c + 1) * width] for c in range(per_token)]
    held = jnp.concatenate(columns, axis=0).astype(BF16)
    lanes = len(columns) * slots
    lane = iota((slots, lanes), 1)
    row_of_lane = jnp.sum(
        jnp.where(lane % slots == iota((slots, lanes), 0), labels, 0.0), axis=0, keepdims=True
    ).astype(jnp.int32)
    patch_of_lane = row_of_lane * len(columns) + iota((1, lanes), 1) // slots
    patch_of_lane = jnp.where(row_of_lane < 0, -1, patch_of_lane)
    chosen = patch_of_lane == iota((patches, lanes), 0)
    patch_grads = dot(chosen.astype(F32).astype(BF16), held, (1, 0))
    inputs = patches_ref[...].astype(F32)
    inverse_rms = lax.rsqrt(jnp.mean(inputs * inputs, axis=1, keepdims=True) + 1e-06)
    normed = inputs * inverse_rms
    row = jnp.sum(patch_grads * normed, axis=0, keepdims=True)
    if carries:
        carried = routed[:, per_token * width + LANES :]
        capacity = slots // peers
        copies, lines, line_width = share_ref.shape
        pieces = (lines * line_width - width) // LANES
        place = iota((slots, LANES), 0) % capacity
        parts = [row]
        for piece in range(pieces):
            kept = jnp.logical_and(place % pieces == piece, place < 3 * pieces)
            parts.append(jnp.sum(jnp.where(kept, carried, 0.0), axis=0, keepdims=True))
        row = jnp.concatenate(parts, axis=1)
        lines = [row[:, at : at + line_width] for at in range(0, row.shape[1], line_width)]
        row = jnp.broadcast_to(jnp.concatenate(lines, axis=0)[None], share_ref.shape)
    share_ref[...] = row.astype(share_ref.dtype)
    scaled = gain_ref[...] * patch_grads
    out_ref[...] = (
        inverse_rms * (scaled - normed * jnp.mean(scaled * normed, axis=1, keepdims=True))
    ).astype(BF16)


def norm_backward(received, peers, patches, gain, share):
    count, width = patches.shape
    routed = sum(x.size for x in received)
    return pl.pallas_call(
        functools.partial(norm_kernel, peers, len(share.shape) == 3),
        out_shape=[jax.ShapeDtypeStruct((count, width), BF16), share],
        in_specs=vmem(2 + len(received)),
        out_specs=vmem(2),
        compiler_params=pltpu.CompilerParams(vmem_limit_bytes=VMEM_BYTES),
        cost_estimate=pl.CostEstimate(
            flops=2 * count * routed,
            bytes_accessed=4 * count * width + 2 * routed,
            transcendentals=0,
        ),
        name="norm",
    )(patches, gain, *received)


def window_kernel(g_ref, q_ref, k_ref, v_ref, probs_ref, probs_t_ref, dq_ref, dk_ref, dv_ref):
    width = g_ref.shape[1]
    windows = head_windows()
    scores, scores_t, probs_t = [], [], []
    for head, (low, high, start, stop) in enumerate(windows):
        g = masked(g_ref[:, start:stop], low, high, start, stop)
        v = v_ref[:, start:stop]
        found = []
        for ref, grads, axis in (
            (probs_ref, dot(g, v, (1, 1)), 1),
            (probs_t_ref, dot(v, g, (1, 1)), 0),
        ):
            probs = ref[head]
            rounded = probs.astype(BF16)
            delta = jnp.sum(rounded.astype(F32) * grads, axis=axis, keepdims=True)
            found.append(((probs * (grads - delta)).astype(BF16), rounded))
        scores.append(found[0][0])
        scores_t.append(found[1][0])
        probs_t.append(found[1][1])
    scale = 1.0 / math.sqrt(HEAD_DIM)
    for start in range(0, width, LANES):
        stop = start + LANES
        heads = [h for h, (low, high, _, _) in enumerate(windows) if low < stop and high > start]
        for out, left, right_ref, factor in (
            (dq_ref, scores, k_ref, scale),
            (dk_ref, scores_t, q_ref, scale),
            (dv_ref, probs_t, g_ref, 1.0),
        ):
            right = right_ref[:, start:stop]
            rows = [masked(right, windows[h][0], windows[h][1], start, stop) for h in heads]
            product = dot(
                jnp.concatenate([left[h] for h in heads], axis=1),
                jnp.concatenate(rows, axis=0),
                (1, 0),
            )
            out[:, start:stop] = (product * factor).astype(BF16)


def window_backward(out_grads, queries, keys, values, probs, probs_t):
    patches, width = queries.shape
    shape = jax.ShapeDtypeStruct((patches, width), BF16)
    return pl.pallas_call(
        window_kernel,
        out_shape=[shape] * 3,
        in_specs=vmem(6),
        out_specs=vmem(3),
        compiler_params=pltpu.CompilerParams(vmem_limit_bytes=VMEM_BYTES),
        cost_estimate=pl.CostEstimate(
            flops=10 * HEADS * patches * patches * LANES,
            bytes_accessed=8 * HEADS * patches * patches + 14 * patches * width,
            transcendentals=0,
        ),
        name="window",
    )(out_grads, queries, keys, values, probs, probs_t)


def body(llm_grads, token_target, patches, gain, w_down, queries, keys, values, window_ids):
    grad_rows = llm_grads[0]
    rows = grad_rows.shape[0]
    images, peers = lax.axis_size("img"), lax.axis_size("seq")
    devices = images * peers
    capacity = max(1, 2 * rows // peers)
    direct = peers <= DIRECT
    block = w_down.shape[1]
    width = patches.shape[2]
    pieces = block // peers // LANES
    carries = pieces > 0 and 3 * pieces <= capacity and (width // LANES + pieces) % 2 == 0

    order = [0]
    while len(order) < images:
        order = [2 * j for j in order] + [2 * j + 1 for j in order]
    image, me = lax.axis_index("img"), lax.axis_index("seq")

    def columns(j):
        return lax.dynamic_slice(grad_rows, (0, (image ^ j) * block), (rows, block))

    x_blocks = [columns(0)] + [swap(columns(j), "img", j) for j in range(1, images)]
    x_blocks = [x_blocks[j] for j in order]
    probs, probs_t = window_probs(queries[0], keys[0], window_ids[0])

    touched = touch(w_down)
    terms, first = [], 0
    for index, count in enumerate(CHUNKS):
        kept, sent, *sums = project(x_blocks, w_down, touched, first, count * width, index == 0)
        first += count * width
        if index == 0:
            bias_part = sums[0]
        mask = 1
        while 2 * mask < images:
            kept, sent = halve(kept, swap(sent, "img", mask))
            mask *= 2
        terms.append((kept, swap(sent, "img", mask)))
    packed = pack(terms, token_target, me.reshape(1), bias_part, peers, capacity, direct, carries)
    routed = route(packed, peers, direct)

    if carries:
        share = jax.ShapeDtypeStruct((devices, 2, (width + pieces * LANES) // 2), BF16)
    else:
        share = jax.ShapeDtypeStruct((1, width), F32)
    out_grads, shared = norm_backward(routed, peers, patches[0], gain[None], share)
    if carries:
        shared = exchange(shared, ("img", "seq"), devices).astype(F32).reshape(devices, -1)
        gain_total = jnp.sum(shared[:, :width], axis=0)
        bias_total = shared[:, width:].reshape(-1)
    else:
        gain_total = lax.psum(shared[0], ("img", "seq"))
        bias_total = lax.all_gather(lax.psum(bias_part[0], "seq"), "img", tiled=True)
    gain_grad = gain_total / math.sqrt(devices * patches.shape[1])
    bias_grad = bias_total / math.sqrt(devices * rows)
    grads = window_backward(out_grads, queries[0], keys[0], values[0], probs, probs_t)
    gain_grad = gain_total / math.sqrt(devices * patches.shape[1])
    bias_grad = bias_total / math.sqrt(devices * rows)
    return (grads[0][None], grads[1][None], grads[2][None], gain_grad, bias_grad)


def solution(mesh):
    return jax.shard_map(
        body,
        mesh=mesh,
        in_specs=(
            P("img", "seq", None),
            P("img", "seq"),
            P("img", "seq", None),
            P(),
            P(None, "img"),
            P("img", "seq", None),
            P("img", "seq", None),
            P("img", "seq", None),
            P("img", "seq", None),
        ),
        out_specs=(P("img", "seq", None), P("img", "seq", None), P("img", "seq", None), P(), P()),
        check_vma=False,
    )
```

```python
import functools
import math

import jax
import jax.numpy as jnp
from jax import lax
from jax.experimental import pallas as pl
from jax.experimental.pallas import tpu as pltpu
from jax.sharding import PartitionSpec as P

HEADS = 16
HEAD_DIM = 80
LANES = 128
CHUNKS = (2, 2)
DIRECT = 8
VMEM_BYTES = 16 * 1024 * 1024

F32 = jnp.float32
BF16 = jnp.bfloat16


def iota(shape, axis):
    return lax.broadcasted_iota(jnp.int32, shape, axis)


def dot(a, b, over):
    return lax.dot_general(a, b, ((over[:1], over[1:]), ((), ())), preferred_element_type=F32)


def vmem(count):
    return [pl.BlockSpec(memory_space=pltpu.VMEM)] * count


def head_windows():
    windows = []
    for head in range(HEADS):
        low, high = head * HEAD_DIM, (head + 1) * HEAD_DIM
        start = low // LANES * LANES
        windows.append((low, high, start, -(-high // LANES) * LANES))
    return windows


def lane_mask(low, high, start, stop):
    at = iota((1, stop - start), 1) + start
    return jnp.logical_and(at >= low, at < high)


def masked(x, low, high, start, stop):
    return jnp.where(lane_mask(low, high, start, stop), x, jnp.zeros_like(x))


def project_kernel(blocks, first, tile, with_sum, *refs):
    x_refs, w_ref = refs[:blocks], refs[blocks]
    keep_ref, send_ref = refs[blocks + 2 : blocks + 4]
    x = jnp.concatenate([ref[...] for ref in x_refs], axis=0)
    if with_sum:
        refs[blocks + 4][...] = dot(jnp.ones((16, x.shape[0]), BF16), x, (1, 0))[:1]
    x = x.T
    half = keep_ref.shape[0]
    for t in range(0, keep_ref.shape[1], tile):
        product = dot(w_ref[first + t : first + t + tile], x, (1, 0)).T.astype(BF16)
        keep_ref[:, t : t + tile] = product[:half]
        send_ref[:, t : t + tile] = product[half:]


def project(x_blocks, w_down, touched, first, width, with_sum):
    blocks, (rows, depth) = len(x_blocks), x_blocks[0].shape
    tile = 1280
    while width % tile:
        tile //= 2
    out_shape = [jax.ShapeDtypeStruct((blocks * rows // 2, width), BF16)] * 2
    if with_sum:
        out_shape = out_shape + [jax.ShapeDtypeStruct((1, depth), F32)]
    return pl.pallas_call(
        functools.partial(project_kernel, blocks, first, tile, with_sum),
        out_shape=out_shape,
        in_specs=vmem(blocks + 1) + [pl.BlockSpec(memory_space=pl.ANY)],
        out_specs=vmem(len(out_shape)),
        compiler_params=pltpu.CompilerParams(vmem_limit_bytes=VMEM_BYTES),
        cost_estimate=pl.CostEstimate(
            flops=2 * blocks * rows * depth * width,
            bytes_accessed=2 * width * depth,
            transcendentals=0,
        ),
        name="project",
    )(*x_blocks, pltpu.with_memory_space_constraint(w_down, pltpu.VMEM), touched)


def touch_kernel(w_ref, out_ref):
    out_ref[...] = w_ref[: out_ref.shape[0], : out_ref.shape[1]]


def touch(w_down):
    return pl.pallas_call(
        touch_kernel,
        out_shape=jax.ShapeDtypeStruct((16, LANES), w_down.dtype),
        in_specs=vmem(1),
        out_specs=pl.BlockSpec(memory_space=pltpu.VMEM),
        compiler_params=pltpu.CompilerParams(vmem_limit_bytes=VMEM_BYTES),
        cost_estimate=pl.CostEstimate(
            flops=0, bytes_accessed=2 * w_down.size, transcendentals=0
        ),
        name="touch",
    )(pltpu.with_memory_space_constraint(w_down, pltpu.VMEM))


def halve_kernel(kept_ref, got_ref, keep_ref, send_ref):
    half = keep_ref.shape[0]
    keep_ref[...] = kept_ref[:half].astype(F32) + got_ref[:half].astype(F32)
    send_ref[...] = (kept_ref[half:].astype(F32) + got_ref[half:].astype(F32)).astype(BF16)


def halve(kept, got):
    rows, width = kept.shape
    return pl.pallas_call(
        halve_kernel,
        out_shape=[
            jax.ShapeDtypeStruct((rows // 2, width), F32),
            jax.ShapeDtypeStruct((rows // 2, width), BF16),
        ],
        in_specs=vmem(2),
        out_specs=vmem(2),
        compiler_params=pltpu.CompilerParams(vmem_limit_bytes=VMEM_BYTES),
        cost_estimate=pl.CostEstimate(
            flops=rows * width, bytes_accessed=7 * rows * width, transcendentals=0
        ),
        name="halve",
    )(kept, got)


def peer_masks(peers):
    return (0, 4, 6, 1, 5, 2, 7, 3) if peers == 8 else tuple(range(peers))


def block_peer(block, peers, me):
    peer = jnp.zeros_like(block)
    for place, mask in enumerate(peer_masks(peers)):
        peer = jnp.where(block == place, mask ^ me, peer)
    return peer


def pack_kernel(peers, capacity, chunks, direct, carries, me_ref, targets_ref, *refs):
    terms, refs = refs[: 2 * chunks], refs[2 * chunks :]
    outs = refs[1:] if carries else refs
    targets = targets_ref[...]
    rows = targets.shape[1]
    dest = targets // rows
    local = targets - dest * rows
    dest_column = jnp.sum(
        jnp.where(iota((rows, rows), 0) == iota((rows, rows), 1), dest, 0), axis=1, keepdims=True
    )
    same_before = jnp.logical_and(dest_column == dest, iota((rows, rows), 0) < iota((rows, rows), 1))
    rank = jnp.sum(same_before.astype(jnp.int32), axis=0, keepdims=True)
    slots = peers * capacity
    slot = iota((slots, rows), 0)
    holder = slot // capacity
    if direct:
        holder = block_peer(holder, peers, me_ref[0])
    chosen = jnp.logical_and(dest == holder, rank == slot % capacity)
    selector = chosen.astype(F32).astype(BF16)
    parts = []
    for chunk in range(chunks):
        kept, got = terms[2 * chunk : 2 * chunk + 2]
        total = (kept[...].astype(F32) + got[...].astype(F32)).astype(BF16)
        parts.append(dot(selector, total, (1, 0)))
    if carries:
        local = jnp.broadcast_to((local + 1).astype(F32), (16, rows)).astype(BF16)
        labels = dot(local, selector, (1, 1))[:1] - 1.0
        square = (slots, slots)
        own = iota(square, 0) // capacity == iota(square, 1) // capacity
        own = jnp.logical_and(own, iota(square, 0) % capacity == capacity - 1)
        turn = (iota((slots, LANES), 0) % capacity == iota((slots, LANES), 1)).astype(F32)
        extra = dot(jnp.where(own, labels, 0.0).astype(BF16), turn.astype(BF16), (1, 0))
        sums = refs[0][...]
        high = sums.astype(BF16).astype(F32)
        middle = (sums - high).astype(BF16).astype(F32)
        low = (sums - high - middle).astype(BF16).astype(F32)
        row = iota((slots, LANES), 0) % capacity
        peer = iota((slots, LANES), 0) // capacity
        if direct:
            peer = block_peer(peer, peers, me_ref[0])
        pieces = sums.shape[1] // peers // LANES
        for p in range(peers):
            for level, values in enumerate((high, middle, low)):
                for piece in range(pieces):
                    start = (p * pieces + piece) * LANES
                    line = jnp.broadcast_to(values[:, start : start + LANES], (slots, LANES))
                    here = jnp.logical_and(peer == p, row == level * pieces + piece)
                    extra = jnp.where(here, line, extra)
        parts.append(extra)
    else:
        label = jnp.sum(jnp.where(chosen, local + 1, 0), axis=1, keepdims=True) - 1
        parts.append(jnp.broadcast_to(label.astype(F32), (slots, LANES)))
    at = 0
    for part in parts:
        end = at + part.shape[1]
        if direct:
            for m in range(peers):
                outs[m][:, at:end] = part[m * capacity : (m + 1) * capacity].astype(BF16)
        else:
            outs[0][:, at:end] = part.astype(BF16)
        at = end


def pack(terms, targets, me, sums, peers, capacity, direct, carries):
    rows = targets.shape[1]
    width = sum(kept.shape[1] for kept, _ in terms) + LANES
    operands = [me, targets] + [x for pair in terms for x in pair] + ([sums] if carries else [])
    if direct:
        out_shape = [jax.ShapeDtypeStruct((capacity, width), BF16)] * peers
    else:
        out_shape = [jax.ShapeDtypeStruct((peers * capacity, width), BF16)]
    return pl.pallas_call(
        functools.partial(pack_kernel, peers, capacity, len(terms), direct, carries),
        out_shape=out_shape,
        in_specs=[pl.BlockSpec(memory_space=pltpu.SMEM)] + vmem(len(operands) - 1),
        out_specs=vmem(len(out_shape)),
        compiler_params=pltpu.CompilerParams(vmem_limit_bytes=VMEM_BYTES),
        cost_estimate=pl.CostEstimate(
            flops=2 * rows * peers * capacity * width,
            bytes_accessed=(6 * rows + 2 * peers * capacity) * width,
            transcendentals=0,
        ),
        name="pack",
    )(*operands)


def route(packed, peers, direct):
    if not direct:
        return [exchange(packed[0], "seq", peers)]
    masks = peer_masks(peers)
    return [swap(block, "seq", mask) if mask else block for block, mask in zip(packed, masks)]


def swap(x, axis, mask):
    n = lax.axis_size(axis)
    return lax.ppermute(x, axis, [(i, i ^ mask) for i in range(n)])


def exchange(x, axis, pieces):
    shape = x.shape
    if x.ndim == 2:
        x = x.reshape(pieces, -1, shape[1])
    return lax.all_to_all(x, axis, split_axis=0, concat_axis=0, tiled=True).reshape(shape)


def probs_kernel(q_ref, k_ref, ids_ref, probs_ref, probs_t_ref):
    patches = q_ref.shape[0]
    ids = ids_ref[...]
    per_token = patches // ids.shape[1]
    token = iota((patches, ids.shape[1]), 0) // per_token
    column = jnp.sum(
        jnp.where(token == iota((patches, ids.shape[1]), 1), ids, 0), axis=1, keepdims=True
    )
    square = (patches, patches)
    row = jnp.sum(
        jnp.where(iota(square, 0) == iota(square, 1), column, 0), axis=0, keepdims=True
    )
    allowed = column == row
    scale = 1.0 / math.sqrt(HEAD_DIM)
    for head, (low, high, start, stop) in enumerate(head_windows()):
        q = masked(q_ref[:, start:stop], low, high, start, stop)
        k = k_ref[:, start:stop]
        for out, scores, axis in (
            (probs_ref, dot(q, k, (1, 1)), 1),
            (probs_t_ref, dot(k, q, (1, 1)), 0),
        ):
            scores = jnp.where(allowed, scores * scale, -jnp.inf)
            weights = jnp.exp(scores - jnp.max(scores, axis=axis, keepdims=True))
            out[head] = weights / jnp.sum(weights, axis=axis, keepdims=True)


def window_probs(queries, keys, ids):
    patches = queries.shape[0]
    shape = jax.ShapeDtypeStruct((HEADS, patches, patches), F32)
    return pl.pallas_call(
        probs_kernel,
        out_shape=[shape, shape],
        in_specs=vmem(3),
        out_specs=vmem(2),
        compiler_params=pltpu.CompilerParams(vmem_limit_bytes=VMEM_BYTES),
        cost_estimate=pl.CostEstimate(
            flops=8 * HEADS * patches * patches * LANES,
            bytes_accessed=8 * HEADS * patches * patches,
            transcendentals=2 * HEADS * patches * patches,
        ),
        name="probs",
    )(queries, keys, ids)


def norm_kernel(peers, carries, patches_ref, gain_ref, *refs):
    pieces, (out_ref, share_ref) = refs[:-2], refs[-2:]
    patches, width = patches_ref.shape
    pieces = [ref[...].astype(F32) for ref in pieces]
    routed = jnp.concatenate(pieces, axis=0) if len(pieces) > 1 else pieces[0]
    slots = routed.shape[0]
    per_token = routed.shape[1] // width
    columns = [routed[:, c * width : (c + 1) * width] for c in range(per_token)]
    held = jnp.concatenate(columns, axis=0).astype(BF16)
    lanes = per_token * slots
    extra = routed[:, per_token * width :]
    capacity = slots // peers
    if carries:
        place = iota((slots, LANES), 0) % capacity
        labels = jnp.where(place == capacity - 1, extra, 0.0).astype(BF16)
        turn = (iota((LANES, lanes), 0) == iota((LANES, lanes), 1) % capacity).astype(F32)
        spread = dot(labels, turn.astype(BF16), (1, 0))
        own = iota((slots, lanes), 0) // capacity == iota((slots, lanes), 1) % slots // capacity
        row_of_lane = jnp.sum(jnp.where(own, spread, 0.0), axis=0, keepdims=True)
    else:
        own = iota((slots, lanes), 1) % slots == iota((slots, lanes), 0)
        row_of_lane = jnp.sum(jnp.where(own, extra[:, :1], 0.0), axis=0, keepdims=True)
    row_of_lane = row_of_lane.astype(jnp.int32)
    patch_of_lane = row_of_lane * len(columns) + iota((1, lanes), 1) // slots
    patch_of_lane = jnp.where(row_of_lane < 0, -1, patch_of_lane)
    chosen = patch_of_lane == iota((patches, lanes), 0)
    patch_grads = dot(chosen.astype(F32).astype(BF16), held, (1, 0))
    inputs = patches_ref[...].astype(F32)
    inverse_rms = lax.rsqrt(jnp.mean(inputs * inputs, axis=1, keepdims=True) + 1e-06)
    normed = inputs * inverse_rms
    row = jnp.sum(patch_grads * normed, axis=0, keepdims=True)
    if carries:
        copies, lines, line_width = share_ref.shape
        pieces = (lines * line_width - width) // LANES
        parts = [row]
        for piece in range(pieces):
            kept = jnp.logical_and(place % pieces == piece, place < 3 * pieces)
            parts.append(jnp.sum(jnp.where(kept, extra, 0.0), axis=0, keepdims=True))
        row = jnp.concatenate(parts, axis=1)
        lines = [row[:, at : at + line_width] for at in range(0, row.shape[1], line_width)]
        row = jnp.broadcast_to(jnp.concatenate(lines, axis=0)[None], share_ref.shape)
    share_ref[...] = row.astype(share_ref.dtype)
    scaled = gain_ref[...] * patch_grads
    out_ref[...] = (
        inverse_rms * (scaled - normed * jnp.mean(scaled * normed, axis=1, keepdims=True))
    ).astype(BF16)


def norm_backward(received, peers, patches, gain, share):
    count, width = patches.shape
    routed = sum(x.size for x in received)
    return pl.pallas_call(
        functools.partial(norm_kernel, peers, len(share.shape) == 3),
        out_shape=[jax.ShapeDtypeStruct((count, width), BF16), share],
        in_specs=vmem(2 + len(received)),
        out_specs=vmem(2),
        compiler_params=pltpu.CompilerParams(vmem_limit_bytes=VMEM_BYTES),
        cost_estimate=pl.CostEstimate(
            flops=2 * count * routed,
            bytes_accessed=4 * count * width + 2 * routed,
            transcendentals=0,
        ),
        name="norm",
    )(patches, gain, *received)


def window_kernel(g_ref, q_ref, k_ref, v_ref, probs_ref, probs_t_ref, dq_ref, dk_ref, dv_ref):
    width = g_ref.shape[1]
    windows = head_windows()
    scores, scores_t, probs_t = [], [], []
    for head, (low, high, start, stop) in enumerate(windows):
        g = masked(g_ref[:, start:stop], low, high, start, stop)
        v = v_ref[:, start:stop]
        found = []
        for ref, grads, axis in (
            (probs_ref, dot(g, v, (1, 1)), 1),
            (probs_t_ref, dot(v, g, (1, 1)), 0),
        ):
            probs = ref[head]
            rounded = probs.astype(BF16)
            delta = jnp.sum(rounded.astype(F32) * grads, axis=axis, keepdims=True)
            found.append(((probs * (grads - delta)).astype(BF16), rounded))
        scores.append(found[0][0])
        scores_t.append(found[1][0])
        probs_t.append(found[1][1])
    scale = 1.0 / math.sqrt(HEAD_DIM)
    for start in range(0, width, LANES):
        stop = start + LANES
        heads = [h for h, (low, high, _, _) in enumerate(windows) if low < stop and high > start]
        for out, left, right_ref, factor in (
            (dq_ref, scores, k_ref, scale),
            (dk_ref, scores_t, q_ref, scale),
            (dv_ref, probs_t, g_ref, 1.0),
        ):
            right = right_ref[:, start:stop]
            rows = [masked(right, windows[h][0], windows[h][1], start, stop) for h in heads]
            product = dot(
                jnp.concatenate([left[h] for h in heads], axis=1),
                jnp.concatenate(rows, axis=0),
                (1, 0),
            )
            out[:, start:stop] = (product * factor).astype(BF16)


def window_backward(out_grads, queries, keys, values, probs, probs_t):
    patches, width = queries.shape
    shape = jax.ShapeDtypeStruct((patches, width), BF16)
    return pl.pallas_call(
        window_kernel,
        out_shape=[shape] * 3,
        in_specs=vmem(6),
        out_specs=vmem(3),
        compiler_params=pltpu.CompilerParams(vmem_limit_bytes=VMEM_BYTES),
        cost_estimate=pl.CostEstimate(
            flops=10 * HEADS * patches * patches * LANES,
            bytes_accessed=8 * HEADS * patches * patches + 14 * patches * width,
            transcendentals=0,
        ),
        name="window",
    )(out_grads, queries, keys, values, probs, probs_t)


def body(llm_grads, token_target, patches, gain, w_down, queries, keys, values, window_ids):
    grad_rows = llm_grads[0]
    rows = grad_rows.shape[0]
    images, peers = lax.axis_size("img"), lax.axis_size("seq")
    devices = images * peers
    capacity = max(1, 2 * rows // peers)
    direct = peers <= DIRECT
    block = w_down.shape[1]
    width = patches.shape[2]
    pieces = block // peers // LANES
    carries = pieces > 0 and 3 * pieces < capacity and (width // LANES + pieces) % 2 == 0

    order = [0]
    while len(order) < images:
        order = [2 * j for j in order] + [2 * j + 1 for j in order]
    image, me = lax.axis_index("img"), lax.axis_index("seq")

    def columns(j):
        return lax.dynamic_slice(grad_rows, (0, (image ^ j) * block), (rows, block))

    x_blocks = [columns(0)] + [swap(columns(j), "img", j) for j in range(1, images)]
    x_blocks = [x_blocks[j] for j in order]
    probs, probs_t = window_probs(queries[0], keys[0], window_ids[0])

    touched = touch(w_down)
    terms, first = [], 0
    for index, count in enumerate(CHUNKS):
        kept, sent, *sums = project(x_blocks, w_down, touched, first, count * width, index == 0)
        first += count * width
        if index == 0:
            bias_part = sums[0]
        mask = 1
        while 2 * mask < images:
            kept, sent = halve(kept, swap(sent, "img", mask))
            mask *= 2
        terms.append((kept, swap(sent, "img", mask)))
    packed = pack(terms, token_target, me.reshape(1), bias_part, peers, capacity, direct, carries)
    routed = route(packed, peers, direct)

    if carries:
        share = jax.ShapeDtypeStruct((devices, 2, (width + pieces * LANES) // 2), BF16)
    else:
        share = jax.ShapeDtypeStruct((1, width), F32)
    out_grads, shared = norm_backward(routed, peers, patches[0], gain[None], share)
    if carries:
        shared = exchange(shared, ("img", "seq"), devices).astype(F32).reshape(devices, -1)
        gain_total = jnp.sum(shared[:, :width], axis=0)
        bias_total = shared[:, width:].reshape(-1)
    else:
        gain_total = lax.psum(shared[0], ("img", "seq"))
        bias_total = lax.all_gather(lax.psum(bias_part[0], "seq"), "img", tiled=True)
    gain_grad = gain_total / math.sqrt(devices * patches.shape[1])
    bias_grad = bias_total / math.sqrt(devices * rows)
    grads = window_backward(out_grads, queries[0], keys[0], values[0], probs, probs_t)
    gain_grad = gain_total / math.sqrt(devices * patches.shape[1])
    bias_grad = bias_total / math.sqrt(devices * rows)
    return (grads[0][None], grads[1][None], grads[2][None], gain_grad, bias_grad)


def solution(mesh):
    return jax.shard_map(
        body,
        mesh=mesh,
        in_specs=(
            P("img", "seq", None),
            P("img", "seq"),
            P("img", "seq", None),
            P(),
            P(None, "img"),
            P("img", "seq", None),
            P("img", "seq", None),
            P("img", "seq", None),
            P("img", "seq", None),
        ),
        out_specs=(P("img", "seq", None), P("img", "seq", None), P("img", "seq", None), P(), P()),
        check_vma=False,
    )
```

```python
import functools
import math

import jax
import jax.numpy as jnp
from jax import lax
from jax.experimental import pallas as pl
from jax.experimental.pallas import tpu as pltpu
from jax.sharding import PartitionSpec as P

HEADS = 16
HEAD_DIM = 80
LANES = 128
CHUNKS = (2, 2)
DIRECT = 8
VMEM_BYTES = 16 * 1024 * 1024

F32 = jnp.float32
BF16 = jnp.bfloat16


def iota(shape, axis):
    return lax.broadcasted_iota(jnp.int32, shape, axis)


def dot(a, b, over):
    return lax.dot_general(a, b, ((over[:1], over[1:]), ((), ())), preferred_element_type=F32)


def vmem(count):
    return [pl.BlockSpec(memory_space=pltpu.VMEM)] * count


def head_windows():
    windows = []
    for head in range(HEADS):
        low, high = head * HEAD_DIM, (head + 1) * HEAD_DIM
        start = low // LANES * LANES
        windows.append((low, high, start, -(-high // LANES) * LANES))
    return windows


def lane_mask(low, high, start, stop):
    at = iota((1, stop - start), 1) + start
    return jnp.logical_and(at >= low, at < high)


def masked(x, low, high, start, stop):
    return jnp.where(lane_mask(low, high, start, stop), x, jnp.zeros_like(x))


def project_kernel(blocks, first, tile, with_sum, *refs):
    x_refs, w_ref = refs[:blocks], refs[blocks]
    keep_ref, send_ref = refs[blocks + 2 : blocks + 4]
    x = jnp.concatenate([ref[...] for ref in x_refs], axis=0)
    if with_sum:
        refs[blocks + 4][...] = dot(jnp.ones((16, x.shape[0]), BF16), x, (1, 0))[:1]
    x = x.T
    half = keep_ref.shape[0]
    for t in range(0, keep_ref.shape[1], tile):
        product = dot(w_ref[first + t : first + t + tile], x, (1, 0)).T.astype(BF16)
        keep_ref[:, t : t + tile] = product[:half]
        send_ref[:, t : t + tile] = product[half:]


def project(x_blocks, w_down, touched, first, width, with_sum):
    blocks, (rows, depth) = len(x_blocks), x_blocks[0].shape
    tile = 1280
    while width % tile:
        tile //= 2
    out_shape = [jax.ShapeDtypeStruct((blocks * rows // 2, width), BF16)] * 2
    if with_sum:
        out_shape = out_shape + [jax.ShapeDtypeStruct((1, depth), F32)]
    return pl.pallas_call(
        functools.partial(project_kernel, blocks, first, tile, with_sum),
        out_shape=out_shape,
        in_specs=vmem(blocks + 1) + [pl.BlockSpec(memory_space=pl.ANY)],
        out_specs=vmem(len(out_shape)),
        compiler_params=pltpu.CompilerParams(vmem_limit_bytes=VMEM_BYTES),
        cost_estimate=pl.CostEstimate(
            flops=2 * blocks * rows * depth * width,
            bytes_accessed=2 * width * depth,
            transcendentals=0,
        ),
        name="project",
    )(*x_blocks, pltpu.with_memory_space_constraint(w_down, pltpu.VMEM), touched)


def touch_kernel(w_ref, out_ref):
    out_ref[...] = w_ref[: out_ref.shape[0], : out_ref.shape[1]]


def touch(w_down):
    return pl.pallas_call(
        touch_kernel,
        out_shape=jax.ShapeDtypeStruct((16, LANES), w_down.dtype),
        in_specs=vmem(1),
        out_specs=pl.BlockSpec(memory_space=pltpu.VMEM),
        compiler_params=pltpu.CompilerParams(vmem_limit_bytes=VMEM_BYTES),
        cost_estimate=pl.CostEstimate(
            flops=0, bytes_accessed=2 * w_down.size, transcendentals=0
        ),
        name="touch",
    )(pltpu.with_memory_space_constraint(w_down, pltpu.VMEM))


def halve_kernel(kept_ref, got_ref, keep_ref, send_ref):
    half = keep_ref.shape[0]
    keep_ref[...] = kept_ref[:half].astype(F32) + got_ref[:half].astype(F32)
    send_ref[...] = (kept_ref[half:].astype(F32) + got_ref[half:].astype(F32)).astype(BF16)


def halve(kept, got):
    rows, width = kept.shape
    return pl.pallas_call(
        halve_kernel,
        out_shape=[
            jax.ShapeDtypeStruct((rows // 2, width), F32),
            jax.ShapeDtypeStruct((rows // 2, width), BF16),
        ],
        in_specs=vmem(2),
        out_specs=vmem(2),
        compiler_params=pltpu.CompilerParams(vmem_limit_bytes=VMEM_BYTES),
        cost_estimate=pl.CostEstimate(
            flops=rows * width, bytes_accessed=7 * rows * width, transcendentals=0
        ),
        name="halve",
    )(kept, got)


def peer_masks(peers):
    return (0, 5, 7, 4, 6, 1, 2, 3) if peers == 8 else tuple(range(peers))


def early_masks(peers):
    return (4, 6) if peers == 8 else ()


def block_peer(block, masks, me):
    peer = jnp.zeros_like(block)
    for place, mask in enumerate(masks):
        peer = jnp.where(block == place, mask ^ me, peer)
    return peer


def pack_kernel(
    peers, capacity, chunks, masks, starts, direct, carries, after, me_ref, *refs
):
    targets_ref, terms, refs = refs[0], refs[1 : 2 * chunks + 1], refs[2 * chunks + 1 :]
    outs = refs[after + carries :]
    targets = targets_ref[...]
    rows = targets.shape[1]
    dest = targets // rows
    local = targets - dest * rows
    dest_column = jnp.sum(
        jnp.where(iota((rows, rows), 0) == iota((rows, rows), 1), dest, 0), axis=1, keepdims=True
    )
    same_before = jnp.logical_and(dest_column == dest, iota((rows, rows), 0) < iota((rows, rows), 1))
    rank = jnp.sum(same_before.astype(jnp.int32), axis=0, keepdims=True)
    slots = len(masks) * capacity
    slot = iota((slots, rows), 0)
    holder = slot // capacity
    if direct:
        holder = block_peer(holder, masks, me_ref[0])
    chosen = jnp.logical_and(dest == holder, rank == slot % capacity)
    selector = chosen.astype(F32).astype(BF16)
    parts = []
    if carries:
        local = jnp.broadcast_to((local + 1).astype(F32), (16, rows)).astype(BF16)
        labels = dot(local, selector, (1, 1))[:1] - 1.0
        square = (slots, slots)
        own = iota(square, 0) // capacity == iota(square, 1) // capacity
        own = jnp.logical_and(own, iota(square, 0) % capacity == capacity - 1)
        turn = (iota((slots, LANES), 0) % capacity == iota((slots, LANES), 1)).astype(F32)
        extra = dot(jnp.where(own, labels, 0.0).astype(BF16), turn.astype(BF16), (1, 0))
        sums = refs[0][...]
        high = sums.astype(BF16).astype(F32)
        middle = (sums - high).astype(BF16).astype(F32)
        low = (sums - high - middle).astype(BF16).astype(F32)
        row = iota((slots, LANES), 0) % capacity
        peer = iota((slots, LANES), 0) // capacity
        if direct:
            peer = block_peer(peer, masks, me_ref[0])
        pieces = sums.shape[1] // peers // LANES
        for p in range(peers):
            for level, values in enumerate((high, middle, low)):
                for piece in range(pieces):
                    start = (p * pieces + piece) * LANES
                    line = jnp.broadcast_to(values[:, start : start + LANES], (slots, LANES))
                    here = jnp.logical_and(peer == p, row == level * pieces + piece)
                    extra = jnp.where(here, line, extra)
        parts.append(extra)
    else:
        label = jnp.sum(jnp.where(chosen, local + 1, 0), axis=1, keepdims=True) - 1
        parts.append(jnp.broadcast_to(label.astype(F32), (slots, LANES)))
    for chunk in range(chunks):
        kept, got = terms[2 * chunk : 2 * chunk + 2]
        total = (kept[...].astype(F32) + got[...].astype(F32)).astype(BF16)
        parts.append(dot(selector, total, (1, 0)))
    if not direct:
        masks, starts, capacity = masks[:1], starts[:1], slots
    for block, start in enumerate(starts):
        at = 0
        for part in parts[start:]:
            end = at + part.shape[1]
            rows_of_block = part[block * capacity : (block + 1) * capacity]
            outs[block][:, at:end] = rows_of_block.astype(BF16)
            at = end


def pack(terms, targets, me, sums, after, peers, capacity, masks, starts, direct):
    rows = targets.shape[1]
    carries = sums is not None
    widths = [LANES] + [kept.shape[1] for kept, _ in terms]
    operands = [me, targets] + [x for pair in terms for x in pair] + ([sums] if carries else [])
    blocks = len(operands) - 1
    operands += after
    if direct:
        out_shape = [
            jax.ShapeDtypeStruct((capacity, sum(widths[start:])), BF16) for start in starts
        ]
    else:
        out_shape = [jax.ShapeDtypeStruct((peers * capacity, sum(widths)), BF16)]
    return pl.pallas_call(
        functools.partial(
            pack_kernel, peers, capacity, len(terms), masks, starts, direct, carries,
            len(after),
        ),
        out_shape=out_shape,
        in_specs=[pl.BlockSpec(memory_space=pltpu.SMEM)]
        + vmem(blocks)
        + [pl.BlockSpec(memory_space=pl.ANY)] * len(after),
        out_specs=vmem(len(out_shape)),
        compiler_params=pltpu.CompilerParams(vmem_limit_bytes=VMEM_BYTES),
        cost_estimate=pl.CostEstimate(
            flops=2 * rows * len(masks) * capacity * sum(widths),
            bytes_accessed=(6 * rows + 2 * len(masks) * capacity) * sum(widths),
            transcendentals=0,
        ),
        name="pack",
    )(*operands)


def swap(x, axis, mask):
    n = lax.axis_size(axis)
    return lax.ppermute(x, axis, [(i, i ^ mask) for i in range(n)])


def exchange(x, axis, pieces):
    shape = x.shape
    if x.ndim == 2:
        x = x.reshape(pieces, -1, shape[1])
    return lax.all_to_all(x, axis, split_axis=0, concat_axis=0, tiled=True).reshape(shape)


def probs_kernel(q_ref, k_ref, ids_ref, probs_ref, probs_t_ref):
    patches = q_ref.shape[0]
    ids = ids_ref[...]
    per_token = patches // ids.shape[1]
    token = iota((patches, ids.shape[1]), 0) // per_token
    column = jnp.sum(
        jnp.where(token == iota((patches, ids.shape[1]), 1), ids, 0), axis=1, keepdims=True
    )
    square = (patches, patches)
    row = jnp.sum(
        jnp.where(iota(square, 0) == iota(square, 1), column, 0), axis=0, keepdims=True
    )
    allowed = column == row
    scale = 1.0 / math.sqrt(HEAD_DIM)
    for head, (low, high, start, stop) in enumerate(head_windows()):
        q = masked(q_ref[:, start:stop], low, high, start, stop)
        k = k_ref[:, start:stop]
        for out, scores, axis in (
            (probs_ref, dot(q, k, (1, 1)), 1),
            (probs_t_ref, dot(k, q, (1, 1)), 0),
        ):
            scores = jnp.where(allowed, scores * scale, -jnp.inf)
            weights = jnp.exp(scores - jnp.max(scores, axis=axis, keepdims=True))
            out[head] = weights / jnp.sum(weights, axis=axis, keepdims=True)


def window_probs(queries, keys, ids):
    patches = queries.shape[0]
    shape = jax.ShapeDtypeStruct((HEADS, patches, patches), F32)
    return pl.pallas_call(
        probs_kernel,
        out_shape=[shape, shape],
        in_specs=vmem(3),
        out_specs=vmem(2),
        compiler_params=pltpu.CompilerParams(vmem_limit_bytes=VMEM_BYTES),
        cost_estimate=pl.CostEstimate(
            flops=8 * HEADS * patches * patches * LANES,
            bytes_accessed=8 * HEADS * patches * patches,
            transcendentals=2 * HEADS * patches * patches,
        ),
        name="probs",
    )(queries, keys, ids)


def norm_kernel(peers, early, carries, patches_ref, gain_ref, *refs):
    pieces, (out_ref, share_ref) = refs[:-2], refs[-2:]
    patches, width = patches_ref.shape
    pieces = [ref[...].astype(F32) for ref in pieces]
    pieces, begun = pieces[len(early) :], pieces[: len(early)]
    for place, begin in zip(early, begun):
        pieces[place] = jnp.concatenate([begin, pieces[place]], axis=1)
    routed = jnp.concatenate(pieces, axis=0) if len(pieces) > 1 else pieces[0]
    slots = routed.shape[0]
    per_token = routed.shape[1] // width
    columns = [routed[:, LANES + c * width : LANES + (c + 1) * width] for c in range(per_token)]
    held = jnp.concatenate(columns, axis=0).astype(BF16)
    lanes = per_token * slots
    extra = routed[:, :LANES]
    capacity = slots // peers
    if carries:
        place = iota((slots, LANES), 0) % capacity
        labels = jnp.where(place == capacity - 1, extra, 0.0).astype(BF16)
        turn = (iota((LANES, lanes), 0) == iota((LANES, lanes), 1) % capacity).astype(F32)
        spread = dot(labels, turn.astype(BF16), (1, 0))
        own = iota((slots, lanes), 0) // capacity == iota((slots, lanes), 1) % slots // capacity
        row_of_lane = jnp.sum(jnp.where(own, spread, 0.0), axis=0, keepdims=True)
    else:
        own = iota((slots, lanes), 1) % slots == iota((slots, lanes), 0)
        row_of_lane = jnp.sum(jnp.where(own, extra[:, :1], 0.0), axis=0, keepdims=True)
    row_of_lane = row_of_lane.astype(jnp.int32)
    patch_of_lane = row_of_lane * len(columns) + iota((1, lanes), 1) // slots
    patch_of_lane = jnp.where(row_of_lane < 0, -1, patch_of_lane)
    chosen = patch_of_lane == iota((patches, lanes), 0)
    patch_grads = dot(chosen.astype(F32).astype(BF16), held, (1, 0))
    inputs = patches_ref[...].astype(F32)
    inverse_rms = lax.rsqrt(jnp.mean(inputs * inputs, axis=1, keepdims=True) + 1e-06)
    normed = inputs * inverse_rms
    row = jnp.sum(patch_grads * normed, axis=0, keepdims=True)
    if carries:
        copies, lines, line_width = share_ref.shape
        pieces = (lines * line_width - width) // LANES
        parts = [row]
        for piece in range(pieces):
            kept = jnp.logical_and(place % pieces == piece, place < 3 * pieces)
            parts.append(jnp.sum(jnp.where(kept, extra, 0.0), axis=0, keepdims=True))
        row = jnp.concatenate(parts, axis=1)
        lines = [row[:, at : at + line_width] for at in range(0, row.shape[1], line_width)]
        row = jnp.broadcast_to(jnp.concatenate(lines, axis=0)[None], share_ref.shape)
    share_ref[...] = row.astype(share_ref.dtype)
    scaled = gain_ref[...] * patch_grads
    out_ref[...] = (
        inverse_rms * (scaled - normed * jnp.mean(scaled * normed, axis=1, keepdims=True))
    ).astype(BF16)


def norm_backward(received, peers, early, patches, gain, share):
    count, width = patches.shape
    routed = sum(x.size for x in received)
    return pl.pallas_call(
        functools.partial(norm_kernel, peers, early, len(share.shape) == 3),
        out_shape=[jax.ShapeDtypeStruct((count, width), BF16), share],
        in_specs=vmem(2 + len(received)),
        out_specs=vmem(2),
        compiler_params=pltpu.CompilerParams(vmem_limit_bytes=VMEM_BYTES),
        cost_estimate=pl.CostEstimate(
            flops=2 * count * routed,
            bytes_accessed=4 * count * width + 2 * routed,
            transcendentals=0,
        ),
        name="norm",
    )(patches, gain, *received)


def window_kernel(g_ref, q_ref, k_ref, v_ref, probs_ref, probs_t_ref, dq_ref, dk_ref, dv_ref):
    width = g_ref.shape[1]
    windows = head_windows()
    scores, scores_t, probs_t = [], [], []
    for head, (low, high, start, stop) in enumerate(windows):
        g = masked(g_ref[:, start:stop], low, high, start, stop)
        v = v_ref[:, start:stop]
        found = []
        for ref, grads, axis in (
            (probs_ref, dot(g, v, (1, 1)), 1),
            (probs_t_ref, dot(v, g, (1, 1)), 0),
        ):
            probs = ref[head]
            rounded = probs.astype(BF16)
            delta = jnp.sum(rounded.astype(F32) * grads, axis=axis, keepdims=True)
            found.append(((probs * (grads - delta)).astype(BF16), rounded))
        scores.append(found[0][0])
        scores_t.append(found[1][0])
        probs_t.append(found[1][1])
    scale = 1.0 / math.sqrt(HEAD_DIM)
    for start in range(0, width, LANES):
        stop = start + LANES
        heads = [h for h, (low, high, _, _) in enumerate(windows) if low < stop and high > start]
        for out, left, right_ref, factor in (
            (dq_ref, scores, k_ref, scale),
            (dk_ref, scores_t, q_ref, scale),
            (dv_ref, probs_t, g_ref, 1.0),
        ):
            right = right_ref[:, start:stop]
            rows = [masked(right, windows[h][0], windows[h][1], start, stop) for h in heads]
            product = dot(
                jnp.concatenate([left[h] for h in heads], axis=1),
                jnp.concatenate(rows, axis=0),
                (1, 0),
            )
            out[:, start:stop] = (product * factor).astype(BF16)


def window_backward(out_grads, queries, keys, values, probs, probs_t):
    patches, width = queries.shape
    shape = jax.ShapeDtypeStruct((patches, width), BF16)
    return pl.pallas_call(
        window_kernel,
        out_shape=[shape] * 3,
        in_specs=vmem(6),
        out_specs=vmem(3),
        compiler_params=pltpu.CompilerParams(vmem_limit_bytes=VMEM_BYTES),
        cost_estimate=pl.CostEstimate(
            flops=10 * HEADS * patches * patches * LANES,
            bytes_accessed=8 * HEADS * patches * patches + 14 * patches * width,
            transcendentals=0,
        ),
        name="window",
    )(out_grads, queries, keys, values, probs, probs_t)


def body(llm_grads, token_target, patches, gain, w_down, queries, keys, values, window_ids):
    grad_rows = llm_grads[0]
    rows = grad_rows.shape[0]
    images, peers = lax.axis_size("img"), lax.axis_size("seq")
    devices = images * peers
    capacity = max(1, 2 * rows // peers)
    direct = peers <= DIRECT
    block = w_down.shape[1]
    width = patches.shape[2]
    pieces = block // peers // LANES
    carries = pieces > 0 and 3 * pieces < capacity and (width // LANES + pieces) % 2 == 0

    order = [0]
    while len(order) < images:
        order = [2 * j for j in order] + [2 * j + 1 for j in order]
    image, me = lax.axis_index("img"), lax.axis_index("seq")

    def columns(j):
        return lax.dynamic_slice(grad_rows, (0, (image ^ j) * block), (rows, block))

    x_blocks = [columns(0)] + [swap(columns(j), "img", j) for j in range(1, images)]
    x_blocks = [x_blocks[j] for j in order]
    probs, probs_t = window_probs(queries[0], keys[0], window_ids[0])

    touched = touch(w_down)
    terms, first = [], 0
    for index, count in enumerate(CHUNKS):
        kept, sent, *sums = project(x_blocks, w_down, touched, first, count * width, index == 0)
        first += count * width
        if index == 0:
            bias_part = sums[0]
        mask = 1
        while 2 * mask < images:
            kept, sent = halve(kept, swap(sent, "img", mask))
            mask *= 2
        terms.append((kept, swap(sent, "img", mask)))
    masks = peer_masks(peers)
    early = early_masks(peers) if direct else ()
    places = tuple(masks.index(mask) for mask in early)
    place = me.reshape(1)
    sums = bias_part if carries else None
    begun = []
    if early:
        begun = list(
            pack(
                terms[:1], token_target, place, sums, [], peers, capacity, early,
                (0,) * len(early), direct,
            )
        )
    starts = tuple(2 if mask in early else 0 for mask in masks)
    packed = pack(
        terms, token_target, place, sums, begun, peers, capacity, masks, starts, direct
    )
    if direct:
        routed = [swap(x, "seq", mask) if mask else x for x, mask in zip(packed, masks)]
    else:
        routed = [exchange(packed[0], "seq", peers)]
    routed = [swap(block, "seq", mask) for block, mask in zip(begun, early)] + routed

    if carries:
        share = jax.ShapeDtypeStruct((devices, 2, (width + pieces * LANES) // 2), BF16)
    else:
        share = jax.ShapeDtypeStruct((1, width), F32)
    out_grads, shared = norm_backward(routed, peers, places, patches[0], gain[None], share)
    if carries:
        shared = exchange(shared, ("img", "seq"), devices).astype(F32).reshape(devices, -1)
        gain_total = jnp.sum(shared[:, :width], axis=0)
        bias_total = shared[:, width:].reshape(-1)
    else:
        gain_total = lax.psum(shared[0], ("img", "seq"))
        bias_total = lax.all_gather(lax.psum(bias_part[0], "seq"), "img", tiled=True)
    gain_grad = gain_total / math.sqrt(devices * patches.shape[1])
    bias_grad = bias_total / math.sqrt(devices * rows)
    grads = window_backward(out_grads, queries[0], keys[0], values[0], probs, probs_t)
    gain_grad = gain_total / math.sqrt(devices * patches.shape[1])
    bias_grad = bias_total / math.sqrt(devices * rows)
    return (grads[0][None], grads[1][None], grads[2][None], gain_grad, bias_grad)


def solution(mesh):
    return jax.shard_map(
        body,
        mesh=mesh,
        in_specs=(
            P("img", "seq", None),
            P("img", "seq"),
            P("img", "seq", None),
            P(),
            P(None, "img"),
            P("img", "seq", None),
            P("img", "seq", None),
            P("img", "seq", None),
            P("img", "seq", None),
        ),
        out_specs=(P("img", "seq", None), P("img", "seq", None), P("img", "seq", None), P(), P()),
        check_vma=False,
    )
```

```python
import functools
import math

import jax
import jax.numpy as jnp
from jax import lax
from jax.experimental import pallas as pl
from jax.experimental.pallas import tpu as pltpu
from jax.sharding import PartitionSpec as P

HEADS = 16
HEAD_DIM = 80
LANES = 128
CHUNKS = (2, 2)
DIRECT = 8
VMEM_BYTES = 16 * 1024 * 1024

F32 = jnp.float32
BF16 = jnp.bfloat16


def iota(shape, axis):
    return lax.broadcasted_iota(jnp.int32, shape, axis)


def dot(a, b, over):
    return lax.dot_general(a, b, ((over[:1], over[1:]), ((), ())), preferred_element_type=F32)


def vmem(count):
    return [pl.BlockSpec(memory_space=pltpu.VMEM)] * count


def head_windows():
    windows = []
    for head in range(HEADS):
        low, high = head * HEAD_DIM, (head + 1) * HEAD_DIM
        start = low // LANES * LANES
        windows.append((low, high, start, -(-high // LANES) * LANES))
    return windows


def lane_mask(low, high, start, stop):
    at = iota((1, stop - start), 1) + start
    return jnp.logical_and(at >= low, at < high)


def masked(x, low, high, start, stop):
    return jnp.where(lane_mask(low, high, start, stop), x, jnp.zeros_like(x))


def project_kernel(blocks, first, tile, with_sum, *refs):
    x_refs, w_ref = refs[:blocks], refs[blocks]
    keep_ref, send_ref = refs[blocks + 2 : blocks + 4]
    x = jnp.concatenate([ref[...] for ref in x_refs], axis=0)
    if with_sum:
        refs[blocks + 4][...] = dot(jnp.ones((16, x.shape[0]), BF16), x, (1, 0))[:1]
    x = x.T
    half = keep_ref.shape[0]
    for t in range(0, keep_ref.shape[1], tile):
        product = dot(w_ref[first + t : first + t + tile], x, (1, 0)).T.astype(BF16)
        keep_ref[:, t : t + tile] = product[:half]
        send_ref[:, t : t + tile] = product[half:]


def project(x_blocks, w_down, touched, first, width, with_sum):
    blocks, (rows, depth) = len(x_blocks), x_blocks[0].shape
    tile = 1280
    while width % tile:
        tile //= 2
    out_shape = [jax.ShapeDtypeStruct((blocks * rows // 2, width), BF16)] * 2
    if with_sum:
        out_shape = out_shape + [jax.ShapeDtypeStruct((1, depth), F32)]
    return pl.pallas_call(
        functools.partial(project_kernel, blocks, first, tile, with_sum),
        out_shape=out_shape,
        in_specs=vmem(blocks + 1) + [pl.BlockSpec(memory_space=pl.ANY)],
        out_specs=vmem(len(out_shape)),
        compiler_params=pltpu.CompilerParams(vmem_limit_bytes=VMEM_BYTES),
        cost_estimate=pl.CostEstimate(
            flops=2 * blocks * rows * depth * width,
            bytes_accessed=2 * width * depth,
            transcendentals=0,
        ),
        name="project",
    )(*x_blocks, pltpu.with_memory_space_constraint(w_down, pltpu.VMEM), touched)


def touch_kernel(w_ref, out_ref):
    out_ref[...] = w_ref[: out_ref.shape[0], : out_ref.shape[1]]


def touch(w_down):
    return pl.pallas_call(
        touch_kernel,
        out_shape=jax.ShapeDtypeStruct((16, LANES), w_down.dtype),
        in_specs=vmem(1),
        out_specs=pl.BlockSpec(memory_space=pltpu.VMEM),
        compiler_params=pltpu.CompilerParams(vmem_limit_bytes=VMEM_BYTES),
        cost_estimate=pl.CostEstimate(
            flops=0, bytes_accessed=2 * w_down.size, transcendentals=0
        ),
        name="touch",
    )(pltpu.with_memory_space_constraint(w_down, pltpu.VMEM))


def halve_kernel(kept_ref, got_ref, keep_ref, send_ref):
    half = keep_ref.shape[0]
    keep_ref[...] = kept_ref[:half].astype(F32) + got_ref[:half].astype(F32)
    send_ref[...] = (kept_ref[half:].astype(F32) + got_ref[half:].astype(F32)).astype(BF16)


def halve(kept, got):
    rows, width = kept.shape
    return pl.pallas_call(
        halve_kernel,
        out_shape=[
            jax.ShapeDtypeStruct((rows // 2, width), F32),
            jax.ShapeDtypeStruct((rows // 2, width), BF16),
        ],
        in_specs=vmem(2),
        out_specs=vmem(2),
        compiler_params=pltpu.CompilerParams(vmem_limit_bytes=VMEM_BYTES),
        cost_estimate=pl.CostEstimate(
            flops=rows * width, bytes_accessed=7 * rows * width, transcendentals=0
        ),
        name="halve",
    )(kept, got)


def peer_masks(peers):
    return (0, 5, 1, 7, 2, 3, 4, 6) if peers == 8 else tuple(range(peers))


def early_masks(peers):
    return (4, 6) if peers == 8 else ()


def block_peer(block, masks, me):
    peer = jnp.zeros_like(block)
    for place, mask in enumerate(masks):
        peer = jnp.where(block == place, mask ^ me, peer)
    return peer


def pack_kernel(
    peers, capacity, chunks, masks, starts, direct, carries, after, me_ref, *refs
):
    targets_ref, terms, refs = refs[0], refs[1 : 2 * chunks + 1], refs[2 * chunks + 1 :]
    outs = refs[after + carries :]
    targets = targets_ref[...]
    rows = targets.shape[1]
    dest = targets // rows
    local = targets - dest * rows
    dest_column = jnp.sum(
        jnp.where(iota((rows, rows), 0) == iota((rows, rows), 1), dest, 0), axis=1, keepdims=True
    )
    same_before = jnp.logical_and(dest_column == dest, iota((rows, rows), 0) < iota((rows, rows), 1))
    rank = jnp.sum(same_before.astype(jnp.int32), axis=0, keepdims=True)
    slots = len(masks) * capacity
    slot = iota((slots, rows), 0)
    holder = slot // capacity
    if direct:
        holder = block_peer(holder, masks, me_ref[0])
    chosen = jnp.logical_and(dest == holder, rank == slot % capacity)
    selector = chosen.astype(F32).astype(BF16)
    parts = []
    if carries:
        local = jnp.broadcast_to((local + 1).astype(F32), (16, rows)).astype(BF16)
        labels = dot(local, selector, (1, 1))[:1] - 1.0
        square = (slots, slots)
        own = iota(square, 0) // capacity == iota(square, 1) // capacity
        own = jnp.logical_and(own, iota(square, 0) % capacity == capacity - 1)
        turn = (iota((slots, LANES), 0) % capacity == iota((slots, LANES), 1)).astype(F32)
        extra = dot(jnp.where(own, labels, 0.0).astype(BF16), turn.astype(BF16), (1, 0))
        sums = refs[0][...]
        high = sums.astype(BF16).astype(F32)
        middle = (sums - high).astype(BF16).astype(F32)
        low = (sums - high - middle).astype(BF16).astype(F32)
        row = iota((slots, LANES), 0) % capacity
        peer = iota((slots, LANES), 0) // capacity
        if direct:
            peer = block_peer(peer, masks, me_ref[0])
        pieces = sums.shape[1] // peers // LANES
        for p in range(peers):
            for level, values in enumerate((high, middle, low)):
                for piece in range(pieces):
                    start = (p * pieces + piece) * LANES
                    line = jnp.broadcast_to(values[:, start : start + LANES], (slots, LANES))
                    here = jnp.logical_and(peer == p, row == level * pieces + piece)
                    extra = jnp.where(here, line, extra)
        parts.append(extra)
    else:
        label = jnp.sum(jnp.where(chosen, local + 1, 0), axis=1, keepdims=True) - 1
        parts.append(jnp.broadcast_to(label.astype(F32), (slots, LANES)))
    for chunk in range(chunks):
        kept, got = terms[2 * chunk : 2 * chunk + 2]
        total = (kept[...].astype(F32) + got[...].astype(F32)).astype(BF16)
        parts.append(dot(selector, total, (1, 0)))
    if not direct:
        masks, starts, capacity = masks[:1], starts[:1], slots
    for block, start in enumerate(starts):
        at = 0
        for part in parts[start:]:
            end = at + part.shape[1]
            rows_of_block = part[block * capacity : (block + 1) * capacity]
            outs[block][:, at:end] = rows_of_block.astype(BF16)
            at = end


def pack(terms, targets, me, sums, after, peers, capacity, masks, starts, direct):
    rows = targets.shape[1]
    carries = sums is not None
    widths = [LANES] + [kept.shape[1] for kept, _ in terms]
    operands = [me, targets] + [x for pair in terms for x in pair] + ([sums] if carries else [])
    blocks = len(operands) - 1
    operands += after
    if direct:
        out_shape = [
            jax.ShapeDtypeStruct((capacity, sum(widths[start:])), BF16) for start in starts
        ]
    else:
        out_shape = [jax.ShapeDtypeStruct((peers * capacity, sum(widths)), BF16)]
    return pl.pallas_call(
        functools.partial(
            pack_kernel, peers, capacity, len(terms), masks, starts, direct, carries,
            len(after),
        ),
        out_shape=out_shape,
        in_specs=[pl.BlockSpec(memory_space=pltpu.SMEM)]
        + vmem(blocks)
        + [pl.BlockSpec(memory_space=pl.ANY)] * len(after),
        out_specs=vmem(len(out_shape)),
        compiler_params=pltpu.CompilerParams(vmem_limit_bytes=VMEM_BYTES),
        cost_estimate=pl.CostEstimate(
            flops=2 * rows * len(masks) * capacity * sum(widths),
            bytes_accessed=(6 * rows + 2 * len(masks) * capacity) * sum(widths),
            transcendentals=0,
        ),
        name="pack",
    )(*operands)


def swap(x, axis, mask):
    n = lax.axis_size(axis)
    return lax.ppermute(x, axis, [(i, i ^ mask) for i in range(n)])


def exchange(x, axis, pieces):
    shape = x.shape
    if x.ndim == 2:
        x = x.reshape(pieces, -1, shape[1])
    return lax.all_to_all(x, axis, split_axis=0, concat_axis=0, tiled=True).reshape(shape)


def probs_kernel(q_ref, k_ref, ids_ref, probs_ref, probs_t_ref):
    patches = q_ref.shape[0]
    ids = ids_ref[...]
    per_token = patches // ids.shape[1]
    token = iota((patches, ids.shape[1]), 0) // per_token
    column = jnp.sum(
        jnp.where(token == iota((patches, ids.shape[1]), 1), ids, 0), axis=1, keepdims=True
    )
    square = (patches, patches)
    row = jnp.sum(
        jnp.where(iota(square, 0) == iota(square, 1), column, 0), axis=0, keepdims=True
    )
    allowed = column == row
    scale = 1.0 / math.sqrt(HEAD_DIM)
    for head, (low, high, start, stop) in enumerate(head_windows()):
        q = masked(q_ref[:, start:stop], low, high, start, stop)
        k = k_ref[:, start:stop]
        for out, scores, axis in (
            (probs_ref, dot(q, k, (1, 1)), 1),
            (probs_t_ref, dot(k, q, (1, 1)), 0),
        ):
            scores = jnp.where(allowed, scores * scale, -jnp.inf)
            weights = jnp.exp(scores - jnp.max(scores, axis=axis, keepdims=True))
            out[head] = weights / jnp.sum(weights, axis=axis, keepdims=True)


def window_probs(queries, keys, ids):
    patches = queries.shape[0]
    shape = jax.ShapeDtypeStruct((HEADS, patches, patches), F32)
    return pl.pallas_call(
        probs_kernel,
        out_shape=[shape, shape],
        in_specs=vmem(3),
        out_specs=vmem(2),
        compiler_params=pltpu.CompilerParams(vmem_limit_bytes=VMEM_BYTES),
        cost_estimate=pl.CostEstimate(
            flops=8 * HEADS * patches * patches * LANES,
            bytes_accessed=8 * HEADS * patches * patches,
            transcendentals=2 * HEADS * patches * patches,
        ),
        name="probs",
    )(queries, keys, ids)


def norm_kernel(peers, early, carries, patches_ref, gain_ref, *refs):
    pieces, (out_ref, share_ref) = refs[:-2], refs[-2:]
    patches, width = patches_ref.shape
    pieces = [ref[...].astype(F32) for ref in pieces]
    pieces, begun = pieces[len(early) :], pieces[: len(early)]
    for place, begin in zip(early, begun):
        pieces[place] = jnp.concatenate([begin, pieces[place]], axis=1)
    routed = jnp.concatenate(pieces, axis=0) if len(pieces) > 1 else pieces[0]
    slots = routed.shape[0]
    per_token = routed.shape[1] // width
    columns = [routed[:, LANES + c * width : LANES + (c + 1) * width] for c in range(per_token)]
    held = jnp.concatenate(columns, axis=0).astype(BF16)
    lanes = per_token * slots
    extra = routed[:, :LANES]
    capacity = slots // peers
    if carries:
        place = iota((slots, LANES), 0) % capacity
        labels = jnp.where(place == capacity - 1, extra, 0.0).astype(BF16)
        turn = (iota((LANES, lanes), 0) == iota((LANES, lanes), 1) % capacity).astype(F32)
        spread = dot(labels, turn.astype(BF16), (1, 0))
        own = iota((slots, lanes), 0) // capacity == iota((slots, lanes), 1) % slots // capacity
        row_of_lane = jnp.sum(jnp.where(own, spread, 0.0), axis=0, keepdims=True)
    else:
        own = iota((slots, lanes), 1) % slots == iota((slots, lanes), 0)
        row_of_lane = jnp.sum(jnp.where(own, extra[:, :1], 0.0), axis=0, keepdims=True)
    row_of_lane = row_of_lane.astype(jnp.int32)
    patch_of_lane = row_of_lane * len(columns) + iota((1, lanes), 1) // slots
    patch_of_lane = jnp.where(row_of_lane < 0, -1, patch_of_lane)
    chosen = patch_of_lane == iota((patches, lanes), 0)
    patch_grads = dot(chosen.astype(F32).astype(BF16), held, (1, 0))
    inputs = patches_ref[...].astype(F32)
    inverse_rms = lax.rsqrt(jnp.mean(inputs * inputs, axis=1, keepdims=True) + 1e-06)
    normed = inputs * inverse_rms
    row = jnp.sum(patch_grads * normed, axis=0, keepdims=True)
    if carries:
        copies, lines, line_width = share_ref.shape
        pieces = (lines * line_width - width) // LANES
        parts = [row]
        for piece in range(pieces):
            kept = jnp.logical_and(place % pieces == piece, place < 3 * pieces)
            parts.append(jnp.sum(jnp.where(kept, extra, 0.0), axis=0, keepdims=True))
        row = jnp.concatenate(parts, axis=1)
        lines = [row[:, at : at + line_width] for at in range(0, row.shape[1], line_width)]
        row = jnp.broadcast_to(jnp.concatenate(lines, axis=0)[None], share_ref.shape)
    share_ref[...] = row.astype(share_ref.dtype)
    scaled = gain_ref[...] * patch_grads
    out_ref[...] = (
        inverse_rms * (scaled - normed * jnp.mean(scaled * normed, axis=1, keepdims=True))
    ).astype(BF16)


def norm_backward(received, peers, early, patches, gain, share):
    count, width = patches.shape
    routed = sum(x.size for x in received)
    return pl.pallas_call(
        functools.partial(norm_kernel, peers, early, len(share.shape) == 3),
        out_shape=[jax.ShapeDtypeStruct((count, width), BF16), share],
        in_specs=vmem(2 + len(received)),
        out_specs=vmem(2),
        compiler_params=pltpu.CompilerParams(vmem_limit_bytes=VMEM_BYTES),
        cost_estimate=pl.CostEstimate(
            flops=2 * count * routed,
            bytes_accessed=4 * count * width + 2 * routed,
            transcendentals=0,
        ),
        name="norm",
    )(patches, gain, *received)


def window_kernel(g_ref, q_ref, k_ref, v_ref, probs_ref, probs_t_ref, dq_ref, dk_ref, dv_ref):
    width = g_ref.shape[1]
    windows = head_windows()
    scores, scores_t, probs_t = [], [], []
    for head, (low, high, start, stop) in enumerate(windows):
        g = masked(g_ref[:, start:stop], low, high, start, stop)
        v = v_ref[:, start:stop]
        found = []
        for ref, grads, axis in (
            (probs_ref, dot(g, v, (1, 1)), 1),
            (probs_t_ref, dot(v, g, (1, 1)), 0),
        ):
            probs = ref[head]
            rounded = probs.astype(BF16)
            delta = jnp.sum(rounded.astype(F32) * grads, axis=axis, keepdims=True)
            found.append(((probs * (grads - delta)).astype(BF16), rounded))
        scores.append(found[0][0])
        scores_t.append(found[1][0])
        probs_t.append(found[1][1])
    scale = 1.0 / math.sqrt(HEAD_DIM)
    for start in range(0, width, LANES):
        stop = start + LANES
        heads = [h for h, (low, high, _, _) in enumerate(windows) if low < stop and high > start]
        for out, left, right_ref, factor in (
            (dq_ref, scores, k_ref, scale),
            (dk_ref, scores_t, q_ref, scale),
            (dv_ref, probs_t, g_ref, 1.0),
        ):
            right = right_ref[:, start:stop]
            rows = [masked(right, windows[h][0], windows[h][1], start, stop) for h in heads]
            product = dot(
                jnp.concatenate([left[h] for h in heads], axis=1),
                jnp.concatenate(rows, axis=0),
                (1, 0),
            )
            out[:, start:stop] = (product * factor).astype(BF16)


def window_backward(out_grads, queries, keys, values, probs, probs_t):
    patches, width = queries.shape
    shape = jax.ShapeDtypeStruct((patches, width), BF16)
    return pl.pallas_call(
        window_kernel,
        out_shape=[shape] * 3,
        in_specs=vmem(6),
        out_specs=vmem(3),
        compiler_params=pltpu.CompilerParams(vmem_limit_bytes=VMEM_BYTES),
        cost_estimate=pl.CostEstimate(
            flops=10 * HEADS * patches * patches * LANES,
            bytes_accessed=8 * HEADS * patches * patches + 14 * patches * width,
            transcendentals=0,
        ),
        name="window",
    )(out_grads, queries, keys, values, probs, probs_t)


def body(llm_grads, token_target, patches, gain, w_down, queries, keys, values, window_ids):
    grad_rows = llm_grads[0]
    rows = grad_rows.shape[0]
    images, peers = lax.axis_size("img"), lax.axis_size("seq")
    devices = images * peers
    capacity = max(1, 2 * rows // peers)
    direct = peers <= DIRECT
    block = w_down.shape[1]
    width = patches.shape[2]
    pieces = block // peers // LANES
    carries = pieces > 0 and 3 * pieces < capacity and (width // LANES + pieces) % 2 == 0

    order = [0]
    while len(order) < images:
        order = [2 * j for j in order] + [2 * j + 1 for j in order]
    image, me = lax.axis_index("img"), lax.axis_index("seq")

    def columns(j):
        return lax.dynamic_slice(grad_rows, (0, (image ^ j) * block), (rows, block))

    x_blocks = [columns(0)] + [swap(columns(j), "img", j) for j in range(1, images)]
    x_blocks = [x_blocks[j] for j in order]
    probs, probs_t = window_probs(queries[0], keys[0], window_ids[0])

    touched = touch(w_down)
    terms, first = [], 0
    for index, count in enumerate(CHUNKS):
        kept, sent, *sums = project(x_blocks, w_down, touched, first, count * width, index == 0)
        first += count * width
        if index == 0:
            bias_part = sums[0]
        mask = 1
        while 2 * mask < images:
            kept, sent = halve(kept, swap(sent, "img", mask))
            mask *= 2
        terms.append((kept, swap(sent, "img", mask)))
    masks = peer_masks(peers)
    early = early_masks(peers) if direct else ()
    places = tuple(masks.index(mask) for mask in early)
    place = me.reshape(1)
    sums = bias_part if carries else None
    begun = []
    if early:
        begun = list(
            pack(
                terms[:1], token_target, place, sums, [], peers, capacity, early,
                (0,) * len(early), direct,
            )
        )
    starts = tuple(2 if mask in early else 0 for mask in masks)
    packed = pack(
        terms, token_target, place, sums, begun, peers, capacity, masks, starts, direct
    )
    if direct:
        routed = [swap(x, "seq", mask) if mask else x for x, mask in zip(packed, masks)]
    else:
        routed = [exchange(packed[0], "seq", peers)]
    routed = [swap(block, "seq", mask) for block, mask in zip(begun, early)] + routed

    if carries:
        share = jax.ShapeDtypeStruct((devices, 2, (width + pieces * LANES) // 2), BF16)
    else:
        share = jax.ShapeDtypeStruct((1, width), F32)
    out_grads, shared = norm_backward(routed, peers, places, patches[0], gain[None], share)
    if carries:
        shared = exchange(shared, ("img", "seq"), devices).astype(F32).reshape(devices, -1)
        gain_total = jnp.sum(shared[:, :width], axis=0)
        bias_total = shared[:, width:].reshape(-1)
    else:
        gain_total = lax.psum(shared[0], ("img", "seq"))
        bias_total = lax.all_gather(lax.psum(bias_part[0], "seq"), "img", tiled=True)
    gain_grad = gain_total / math.sqrt(devices * patches.shape[1])
    bias_grad = bias_total / math.sqrt(devices * rows)
    grads = window_backward(out_grads, queries[0], keys[0], values[0], probs, probs_t)
    gain_grad = gain_total / math.sqrt(devices * patches.shape[1])
    bias_grad = bias_total / math.sqrt(devices * rows)
    return (grads[0][None], grads[1][None], grads[2][None], gain_grad, bias_grad)


def solution(mesh):
    return jax.shard_map(
        body,
        mesh=mesh,
        in_specs=(
            P("img", "seq", None),
            P("img", "seq"),
            P("img", "seq", None),
            P(),
            P(None, "img"),
            P("img", "seq", None),
            P("img", "seq", None),
            P("img", "seq", None),
            P("img", "seq", None),
        ),
        out_specs=(P("img", "seq", None), P("img", "seq", None), P("img", "seq", None), P(), P()),
        check_vma=False,
    )
```

```python
import functools
import math

import jax
import jax.numpy as jnp
from jax import lax
from jax.experimental import pallas as pl
from jax.experimental.pallas import tpu as pltpu
from jax.sharding import PartitionSpec as P

HEADS = 16
HEAD_DIM = 80
LANES = 128
CHUNKS = (2, 2)
DIRECT = 8
VMEM_BYTES = 16 * 1024 * 1024

F32 = jnp.float32
BF16 = jnp.bfloat16


def iota(shape, axis):
    return lax.broadcasted_iota(jnp.int32, shape, axis)


def dot(a, b, over):
    return lax.dot_general(a, b, ((over[:1], over[1:]), ((), ())), preferred_element_type=F32)


def vmem(count):
    return [pl.BlockSpec(memory_space=pltpu.VMEM)] * count


def head_windows():
    windows = []
    for head in range(HEADS):
        low, high = head * HEAD_DIM, (head + 1) * HEAD_DIM
        start = low // LANES * LANES
        windows.append((low, high, start, -(-high // LANES) * LANES))
    return windows


def lane_mask(low, high, start, stop):
    at = iota((1, stop - start), 1) + start
    return jnp.logical_and(at >= low, at < high)


def masked(x, low, high, start, stop):
    return jnp.where(lane_mask(low, high, start, stop), x, jnp.zeros_like(x))


def project_kernel(blocks, first, tile, with_sum, *refs):
    x_refs, w_ref = refs[:blocks], refs[blocks]
    keep_ref, send_ref = refs[blocks + 2 : blocks + 4]
    x = jnp.concatenate([ref[...] for ref in x_refs], axis=0)
    if with_sum:
        refs[blocks + 4][...] = dot(jnp.ones((16, x.shape[0]), BF16), x, (1, 0))[:1]
    half = keep_ref.shape[0]
    for t in range(0, keep_ref.shape[1], tile):
        product = dot(x, w_ref[first + t : first + t + tile], (1, 1)).astype(BF16)
        keep_ref[:, t : t + tile] = product[:half]
        send_ref[:, t : t + tile] = product[half:]


def project(x_blocks, w_down, touched, first, width, with_sum):
    blocks, (rows, depth) = len(x_blocks), x_blocks[0].shape
    tile = 512
    while width % tile:
        tile //= 2
    out_shape = [jax.ShapeDtypeStruct((blocks * rows // 2, width), BF16)] * 2
    if with_sum:
        out_shape = out_shape + [jax.ShapeDtypeStruct((1, depth), F32)]
    return pl.pallas_call(
        functools.partial(project_kernel, blocks, first, tile, with_sum),
        out_shape=out_shape,
        in_specs=vmem(blocks + 1) + [pl.BlockSpec(memory_space=pl.ANY)],
        out_specs=vmem(len(out_shape)),
        compiler_params=pltpu.CompilerParams(vmem_limit_bytes=VMEM_BYTES),
        cost_estimate=pl.CostEstimate(
            flops=2 * blocks * rows * depth * width,
            bytes_accessed=2 * width * depth,
            transcendentals=0,
        ),
        name="project",
    )(*x_blocks, pltpu.with_memory_space_constraint(w_down, pltpu.VMEM), touched)


def touch_kernel(w_ref, out_ref):
    out_ref[...] = w_ref[: out_ref.shape[0], : out_ref.shape[1]]


def touch(w_down):
    return pl.pallas_call(
        touch_kernel,
        out_shape=jax.ShapeDtypeStruct((16, LANES), w_down.dtype),
        in_specs=vmem(1),
        out_specs=pl.BlockSpec(memory_space=pltpu.VMEM),
        compiler_params=pltpu.CompilerParams(vmem_limit_bytes=VMEM_BYTES),
        cost_estimate=pl.CostEstimate(
            flops=0, bytes_accessed=2 * w_down.size, transcendentals=0
        ),
        name="touch",
    )(pltpu.with_memory_space_constraint(w_down, pltpu.VMEM))


def halve_kernel(kept_ref, got_ref, keep_ref, send_ref):
    half = keep_ref.shape[0]
    keep_ref[...] = kept_ref[:half].astype(F32) + got_ref[:half].astype(F32)
    send_ref[...] = (kept_ref[half:].astype(F32) + got_ref[half:].astype(F32)).astype(BF16)


def halve(kept, got):
    rows, width = kept.shape
    return pl.pallas_call(
        halve_kernel,
        out_shape=[
            jax.ShapeDtypeStruct((rows // 2, width), F32),
            jax.ShapeDtypeStruct((rows // 2, width), BF16),
        ],
        in_specs=vmem(2),
        out_specs=vmem(2),
        compiler_params=pltpu.CompilerParams(vmem_limit_bytes=VMEM_BYTES),
        cost_estimate=pl.CostEstimate(
            flops=rows * width, bytes_accessed=7 * rows * width, transcendentals=0
        ),
        name="halve",
    )(kept, got)


def peer_masks(peers):
    return (0, 5, 1, 7, 2, 3, 4, 6) if peers == 8 else tuple(range(peers))


def early_masks(peers):
    return (4, 6) if peers == 8 else ()


def block_peer(block, masks, me):
    peer = jnp.zeros_like(block)
    for place, mask in enumerate(masks):
        peer = jnp.where(block == place, mask ^ me, peer)
    return peer


def pack_kernel(
    peers, capacity, chunks, masks, starts, direct, carries, after, me_ref, *refs
):
    targets_ref, terms, refs = refs[0], refs[1 : 2 * chunks + 1], refs[2 * chunks + 1 :]
    outs = refs[after + carries :]
    targets = targets_ref[...]
    rows = targets.shape[1]
    dest = targets // rows
    local = targets - dest * rows
    dest_column = jnp.sum(
        jnp.where(iota((rows, rows), 0) == iota((rows, rows), 1), dest, 0), axis=1, keepdims=True
    )
    same_before = jnp.logical_and(dest_column == dest, iota((rows, rows), 0) < iota((rows, rows), 1))
    rank = jnp.sum(same_before.astype(jnp.int32), axis=0, keepdims=True)
    slots = len(masks) * capacity
    slot = iota((slots, rows), 0)
    holder = slot // capacity
    if direct:
        holder = block_peer(holder, masks, me_ref[0])
    chosen = jnp.logical_and(dest == holder, rank == slot % capacity)
    selector = chosen.astype(F32).astype(BF16)
    parts = []
    if carries:
        local = jnp.broadcast_to((local + 1).astype(F32), (16, rows)).astype(BF16)
        labels = dot(local, selector, (1, 1))[:1] - 1.0
        square = (slots, slots)
        own = iota(square, 0) // capacity == iota(square, 1) // capacity
        own = jnp.logical_and(own, iota(square, 0) % capacity == capacity - 1)
        turn = (iota((slots, LANES), 0) % capacity == iota((slots, LANES), 1)).astype(F32)
        extra = dot(jnp.where(own, labels, 0.0).astype(BF16), turn.astype(BF16), (1, 0))
        sums = refs[0][...]
        high = sums.astype(BF16).astype(F32)
        middle = (sums - high).astype(BF16).astype(F32)
        low = (sums - high - middle).astype(BF16).astype(F32)
        row = iota((slots, LANES), 0) % capacity
        peer = iota((slots, LANES), 0) // capacity
        if direct:
            peer = block_peer(peer, masks, me_ref[0])
        pieces = sums.shape[1] // peers // LANES
        for p in range(peers):
            for level, values in enumerate((high, middle, low)):
                for piece in range(pieces):
                    start = (p * pieces + piece) * LANES
                    line = jnp.broadcast_to(values[:, start : start + LANES], (slots, LANES))
                    here = jnp.logical_and(peer == p, row == level * pieces + piece)
                    extra = jnp.where(here, line, extra)
        parts.append(extra)
    else:
        label = jnp.sum(jnp.where(chosen, local + 1, 0), axis=1, keepdims=True) - 1
        parts.append(jnp.broadcast_to(label.astype(F32), (slots, LANES)))
    for chunk in range(chunks):
        kept, got = terms[2 * chunk : 2 * chunk + 2]
        total = (kept[...].astype(F32) + got[...].astype(F32)).astype(BF16)
        parts.append(dot(selector, total, (1, 0)))
    if not direct:
        masks, starts, capacity = masks[:1], starts[:1], slots
    for block, start in enumerate(starts):
        at = 0
        for part in parts[start:]:
            end = at + part.shape[1]
            rows_of_block = part[block * capacity : (block + 1) * capacity]
            outs[block][:, at:end] = rows_of_block.astype(BF16)
            at = end


def pack(terms, targets, me, sums, after, peers, capacity, masks, starts, direct):
    rows = targets.shape[1]
    carries = sums is not None
    widths = [LANES] + [kept.shape[1] for kept, _ in terms]
    operands = [me, targets] + [x for pair in terms for x in pair] + ([sums] if carries else [])
    blocks = len(operands) - 1
    operands += after
    if direct:
        out_shape = [
            jax.ShapeDtypeStruct((capacity, sum(widths[start:])), BF16) for start in starts
        ]
    else:
        out_shape = [jax.ShapeDtypeStruct((peers * capacity, sum(widths)), BF16)]
    return pl.pallas_call(
        functools.partial(
            pack_kernel, peers, capacity, len(terms), masks, starts, direct, carries,
            len(after),
        ),
        out_shape=out_shape,
        in_specs=[pl.BlockSpec(memory_space=pltpu.SMEM)]
        + vmem(blocks)
        + [pl.BlockSpec(memory_space=pl.ANY)] * len(after),
        out_specs=vmem(len(out_shape)),
        compiler_params=pltpu.CompilerParams(vmem_limit_bytes=VMEM_BYTES),
        cost_estimate=pl.CostEstimate(
            flops=2 * rows * len(masks) * capacity * sum(widths),
            bytes_accessed=(6 * rows + 2 * len(masks) * capacity) * sum(widths),
            transcendentals=0,
        ),
        name="pack",
    )(*operands)


def swap(x, axis, mask):
    n = lax.axis_size(axis)
    return lax.ppermute(x, axis, [(i, i ^ mask) for i in range(n)])


def exchange(x, axis, pieces):
    shape = x.shape
    if x.ndim == 2:
        x = x.reshape(pieces, -1, shape[1])
    return lax.all_to_all(x, axis, split_axis=0, concat_axis=0, tiled=True).reshape(shape)


def probs_kernel(q_ref, k_ref, ids_ref, probs_ref, probs_t_ref):
    patches = q_ref.shape[0]
    ids = ids_ref[...]
    per_token = patches // ids.shape[1]
    token = iota((patches, ids.shape[1]), 0) // per_token
    column = jnp.sum(
        jnp.where(token == iota((patches, ids.shape[1]), 1), ids, 0), axis=1, keepdims=True
    )
    square = (patches, patches)
    row = jnp.sum(
        jnp.where(iota(square, 0) == iota(square, 1), column, 0), axis=0, keepdims=True
    )
    allowed = column == row
    scale = 1.0 / math.sqrt(HEAD_DIM)
    for head, (low, high, start, stop) in enumerate(head_windows()):
        q = masked(q_ref[:, start:stop], low, high, start, stop)
        k = k_ref[:, start:stop]
        for out, scores, axis in (
            (probs_ref, dot(q, k, (1, 1)), 1),
            (probs_t_ref, dot(k, q, (1, 1)), 0),
        ):
            scores = jnp.where(allowed, scores * scale, -jnp.inf)
            weights = jnp.exp(scores - jnp.max(scores, axis=axis, keepdims=True))
            out[head] = weights / jnp.sum(weights, axis=axis, keepdims=True)


def window_probs(queries, keys, ids):
    patches = queries.shape[0]
    shape = jax.ShapeDtypeStruct((HEADS, patches, patches), F32)
    return pl.pallas_call(
        probs_kernel,
        out_shape=[shape, shape],
        in_specs=vmem(3),
        out_specs=vmem(2),
        compiler_params=pltpu.CompilerParams(vmem_limit_bytes=VMEM_BYTES),
        cost_estimate=pl.CostEstimate(
            flops=8 * HEADS * patches * patches * LANES,
            bytes_accessed=8 * HEADS * patches * patches,
            transcendentals=2 * HEADS * patches * patches,
        ),
        name="probs",
    )(queries, keys, ids)


def norm_kernel(peers, early, carries, patches_ref, gain_ref, *refs):
    pieces, (out_ref, share_ref) = refs[:-2], refs[-2:]
    patches, width = patches_ref.shape
    pieces = [ref[...].astype(F32) for ref in pieces]
    pieces, begun = pieces[len(early) :], pieces[: len(early)]
    for place, begin in zip(early, begun):
        pieces[place] = jnp.concatenate([begin, pieces[place]], axis=1)
    routed = jnp.concatenate(pieces, axis=0) if len(pieces) > 1 else pieces[0]
    slots = routed.shape[0]
    per_token = routed.shape[1] // width
    columns = [routed[:, LANES + c * width : LANES + (c + 1) * width] for c in range(per_token)]
    held = jnp.concatenate(columns, axis=0).astype(BF16)
    lanes = per_token * slots
    extra = routed[:, :LANES]
    capacity = slots // peers
    if carries:
        place = iota((slots, LANES), 0) % capacity
        labels = jnp.where(place == capacity - 1, extra, 0.0).astype(BF16)
        turn = (iota((LANES, lanes), 0) == iota((LANES, lanes), 1) % capacity).astype(F32)
        spread = dot(labels, turn.astype(BF16), (1, 0))
        own = iota((slots, lanes), 0) // capacity == iota((slots, lanes), 1) % slots // capacity
        row_of_lane = jnp.sum(jnp.where(own, spread, 0.0), axis=0, keepdims=True)
    else:
        own = iota((slots, lanes), 1) % slots == iota((slots, lanes), 0)
        row_of_lane = jnp.sum(jnp.where(own, extra[:, :1], 0.0), axis=0, keepdims=True)
    row_of_lane = row_of_lane.astype(jnp.int32)
    patch_of_lane = row_of_lane * len(columns) + iota((1, lanes), 1) // slots
    patch_of_lane = jnp.where(row_of_lane < 0, -1, patch_of_lane)
    chosen = patch_of_lane == iota((patches, lanes), 0)
    patch_grads = dot(chosen.astype(F32).astype(BF16), held, (1, 0))
    inputs = patches_ref[...].astype(F32)
    inverse_rms = lax.rsqrt(jnp.mean(inputs * inputs, axis=1, keepdims=True) + 1e-06)
    normed = inputs * inverse_rms
    row = jnp.sum(patch_grads * normed, axis=0, keepdims=True)
    if carries:
        copies, lines, line_width = share_ref.shape
        pieces = (lines * line_width - width) // LANES
        parts = [row]
        for piece in range(pieces):
            kept = jnp.logical_and(place % pieces == piece, place < 3 * pieces)
            parts.append(jnp.sum(jnp.where(kept, extra, 0.0), axis=0, keepdims=True))
        row = jnp.concatenate(parts, axis=1)
        lines = [row[:, at : at + line_width] for at in range(0, row.shape[1], line_width)]
        row = jnp.broadcast_to(jnp.concatenate(lines, axis=0)[None], share_ref.shape)
    share_ref[...] = row.astype(share_ref.dtype)
    scaled = gain_ref[...] * patch_grads
    out_ref[...] = (
        inverse_rms * (scaled - normed * jnp.mean(scaled * normed, axis=1, keepdims=True))
    ).astype(BF16)


def norm_backward(received, peers, early, patches, gain, share):
    count, width = patches.shape
    routed = sum(x.size for x in received)
    return pl.pallas_call(
        functools.partial(norm_kernel, peers, early, len(share.shape) == 3),
        out_shape=[jax.ShapeDtypeStruct((count, width), BF16), share],
        in_specs=vmem(2 + len(received)),
        out_specs=vmem(2),
        compiler_params=pltpu.CompilerParams(vmem_limit_bytes=VMEM_BYTES),
        cost_estimate=pl.CostEstimate(
            flops=2 * count * routed,
            bytes_accessed=4 * count * width + 2 * routed,
            transcendentals=0,
        ),
        name="norm",
    )(patches, gain, *received)


def window_kernel(g_ref, q_ref, k_ref, v_ref, probs_ref, probs_t_ref, dq_ref, dk_ref, dv_ref):
    width = g_ref.shape[1]
    windows = head_windows()
    scores, scores_t, probs_t = [], [], []
    for head, (low, high, start, stop) in enumerate(windows):
        g = masked(g_ref[:, start:stop], low, high, start, stop)
        v = v_ref[:, start:stop]
        found = []
        for ref, grads, axis in (
            (probs_ref, dot(g, v, (1, 1)), 1),
            (probs_t_ref, dot(v, g, (1, 1)), 0),
        ):
            probs = ref[head]
            rounded = probs.astype(BF16)
            delta = jnp.sum(rounded.astype(F32) * grads, axis=axis, keepdims=True)
            found.append(((probs * (grads - delta)).astype(BF16), rounded))
        scores.append(found[0][0])
        scores_t.append(found[1][0])
        probs_t.append(found[1][1])
    scale = 1.0 / math.sqrt(HEAD_DIM)
    for start in range(0, width, LANES):
        stop = start + LANES
        heads = [h for h, (low, high, _, _) in enumerate(windows) if low < stop and high > start]
        for out, left, right_ref, factor in (
            (dq_ref, scores, k_ref, scale),
            (dk_ref, scores_t, q_ref, scale),
            (dv_ref, probs_t, g_ref, 1.0),
        ):
            right = right_ref[:, start:stop]
            rows = [masked(right, windows[h][0], windows[h][1], start, stop) for h in heads]
            product = dot(
                jnp.concatenate([left[h] for h in heads], axis=1),
                jnp.concatenate(rows, axis=0),
                (1, 0),
            )
            out[:, start:stop] = (product * factor).astype(BF16)


def window_backward(out_grads, queries, keys, values, probs, probs_t):
    patches, width = queries.shape
    shape = jax.ShapeDtypeStruct((patches, width), BF16)
    return pl.pallas_call(
        window_kernel,
        out_shape=[shape] * 3,
        in_specs=vmem(6),
        out_specs=vmem(3),
        compiler_params=pltpu.CompilerParams(vmem_limit_bytes=VMEM_BYTES),
        cost_estimate=pl.CostEstimate(
            flops=10 * HEADS * patches * patches * LANES,
            bytes_accessed=8 * HEADS * patches * patches + 14 * patches * width,
            transcendentals=0,
        ),
        name="window",
    )(out_grads, queries, keys, values, probs, probs_t)


def finish_kernel(width, gain_scale, bias_scale, shared_ref, gain_ref, bias_ref):
    devices, lines, line_width = shared_ref.shape
    total = jnp.sum(shared_ref[...].astype(F32), axis=0) * gain_scale
    for line in range(lines):
        at = line * line_width
        end = min(at + line_width, width)
        gain_ref[at:end] = total[line, : end - at]
    start = width - (lines - 1) * line_width
    for device in range(devices):
        piece = line_width - start
        own = shared_ref[device, lines - 1, start:].astype(F32) * bias_scale
        bias_ref[device * piece : (device + 1) * piece] = own


def finish(shared, width, gain_scale, bias_scale):
    devices, lines, line_width = shared.shape
    return pl.pallas_call(
        functools.partial(finish_kernel, width, gain_scale, bias_scale),
        out_shape=[
            jax.ShapeDtypeStruct((width,), F32),
            jax.ShapeDtypeStruct((devices * (lines * line_width - width),), F32),
        ],
        in_specs=vmem(1),
        out_specs=vmem(2),
        compiler_params=pltpu.CompilerParams(vmem_limit_bytes=VMEM_BYTES),
        name="finish",
    )(shared)


def body(llm_grads, token_target, patches, gain, w_down, queries, keys, values, window_ids):
    grad_rows = llm_grads[0]
    rows = grad_rows.shape[0]
    images, peers = lax.axis_size("img"), lax.axis_size("seq")
    devices = images * peers
    capacity = max(1, 2 * rows // peers)
    direct = peers <= DIRECT
    block = w_down.shape[1]
    width = patches.shape[2]
    pieces = block // peers // LANES
    carries = pieces > 0 and 3 * pieces < capacity and (width // LANES + pieces) % 2 == 0

    order = [0]
    while len(order) < images:
        order = [2 * j for j in order] + [2 * j + 1 for j in order]
    image, me = lax.axis_index("img"), lax.axis_index("seq")

    def columns(j):
        return lax.dynamic_slice(grad_rows, (0, (image ^ j) * block), (rows, block))

    x_blocks = [columns(0)] + [swap(columns(j), "img", j) for j in range(1, images)]
    x_blocks = [x_blocks[j] for j in order]
    probs, probs_t = window_probs(queries[0], keys[0], window_ids[0])

    touched = touch(w_down)
    terms, first = [], 0
    for index, count in enumerate(CHUNKS):
        kept, sent, *sums = project(x_blocks, w_down, touched, first, count * width, index == 0)
        first += count * width
        if index == 0:
            bias_part = sums[0]
        mask = 1
        while 2 * mask < images:
            kept, sent = halve(kept, swap(sent, "img", mask))
            mask *= 2
        terms.append((kept, swap(sent, "img", mask)))
    masks = peer_masks(peers)
    early = early_masks(peers) if direct else ()
    places = tuple(masks.index(mask) for mask in early)
    place = me.reshape(1)
    sums = bias_part if carries else None
    begun = []
    if early:
        begun = list(
            pack(
                terms[:1], token_target, place, sums, [], peers, capacity, early,
                (0,) * len(early), direct,
            )
        )
    starts = tuple(2 if mask in early else 0 for mask in masks)
    packed = pack(
        terms, token_target, place, sums, begun, peers, capacity, masks, starts, direct
    )
    if direct:
        routed = [swap(x, "seq", mask) if mask else x for x, mask in zip(packed, masks)]
    else:
        routed = [exchange(packed[0], "seq", peers)]
    routed = [swap(block, "seq", mask) for block, mask in zip(begun, early)] + routed

    if carries:
        share = jax.ShapeDtypeStruct((devices, 2, (width + pieces * LANES) // 2), BF16)
    else:
        share = jax.ShapeDtypeStruct((1, width), F32)
    out_grads, shared = norm_backward(routed, peers, places, patches[0], gain[None], share)
    gain_scale = 1.0 / math.sqrt(devices * patches.shape[1])
    bias_scale = 1.0 / math.sqrt(devices * rows)
    if carries:
        shared = exchange(shared, ("img", "seq"), devices)
        gain_grad, bias_grad = finish(shared, width, gain_scale, bias_scale)
    else:
        gain_grad = lax.psum(shared[0], ("img", "seq")) * gain_scale
        bias_grad = lax.all_gather(lax.psum(bias_part[0], "seq"), "img", tiled=True) * bias_scale
    grads = window_backward(out_grads, queries[0], keys[0], values[0], probs, probs_t)
    return (grads[0][None], grads[1][None], grads[2][None], gain_grad, bias_grad)


def solution(mesh):
    return jax.shard_map(
        body,
        mesh=mesh,
        in_specs=(
            P("img", "seq", None),
            P("img", "seq"),
            P("img", "seq", None),
            P(),
            P(None, "img"),
            P("img", "seq", None),
            P("img", "seq", None),
            P("img", "seq", None),
            P("img", "seq", None),
        ),
        out_specs=(P("img", "seq", None), P("img", "seq", None), P("img", "seq", None), P(), P()),
        check_vma=False,
    )
```

```python
import functools
import math

import jax
import jax.numpy as jnp
from jax import lax
from jax.experimental import pallas as pl
from jax.experimental.pallas import tpu as pltpu
from jax.sharding import PartitionSpec as P

HEADS = 16
HEAD_DIM = 80
LANES = 128
CHUNKS = (2, 2)
DIRECT = 8
VMEM_BYTES = 16 * 1024 * 1024

F32 = jnp.float32
BF16 = jnp.bfloat16


def iota(shape, axis):
    return lax.broadcasted_iota(jnp.int32, shape, axis)


def dot(a, b, over):
    return lax.dot_general(a, b, ((over[:1], over[1:]), ((), ())), preferred_element_type=F32)


def vmem(count):
    return [pl.BlockSpec(memory_space=pltpu.VMEM)] * count


def head_windows():
    windows = []
    for head in range(HEADS):
        low, high = head * HEAD_DIM, (head + 1) * HEAD_DIM
        start = low // LANES * LANES
        windows.append((low, high, start, -(-high // LANES) * LANES))
    return windows


def lane_mask(low, high, start, stop):
    at = iota((1, stop - start), 1) + start
    return jnp.logical_and(at >= low, at < high)


def masked(x, low, high, start, stop):
    return jnp.where(lane_mask(low, high, start, stop), x, jnp.zeros_like(x))


def project_kernel(blocks, first, tile, with_sum, *refs):
    x_refs, w_ref = refs[:blocks], refs[blocks]
    keep_ref, send_ref = refs[blocks + 2 : blocks + 4]
    x = jnp.concatenate([ref[...] for ref in x_refs], axis=0)
    if with_sum:
        refs[blocks + 4][...] = dot(jnp.ones((16, x.shape[0]), BF16), x, (1, 0))[:1]
    x = x.T
    half = keep_ref.shape[0]
    for t in range(0, keep_ref.shape[1], tile):
        product = dot(w_ref[first + t : first + t + tile], x, (1, 0)).T.astype(BF16)
        keep_ref[:, t : t + tile] = product[:half]
        send_ref[:, t : t + tile] = product[half:]


def project(x_blocks, w_down, touched, first, width, with_sum):
    blocks, (rows, depth) = len(x_blocks), x_blocks[0].shape
    tile = 512
    while width % tile:
        tile //= 2
    out_shape = [jax.ShapeDtypeStruct((blocks * rows // 2, width), BF16)] * 2
    if with_sum:
        out_shape = out_shape + [jax.ShapeDtypeStruct((1, depth), F32)]
    return pl.pallas_call(
        functools.partial(project_kernel, blocks, first, tile, with_sum),
        out_shape=out_shape,
        in_specs=vmem(blocks + 1) + [pl.BlockSpec(memory_space=pl.ANY)],
        out_specs=vmem(len(out_shape)),
        compiler_params=pltpu.CompilerParams(vmem_limit_bytes=VMEM_BYTES),
        cost_estimate=pl.CostEstimate(
            flops=2 * blocks * rows * depth * width,
            bytes_accessed=2 * width * depth,
            transcendentals=0,
        ),
        name="project",
    )(*x_blocks, pltpu.with_memory_space_constraint(w_down, pltpu.VMEM), touched)


def touch_kernel(w_ref, out_ref):
    out_ref[...] = w_ref[: out_ref.shape[0], : out_ref.shape[1]]


def touch(w_down):
    return pl.pallas_call(
        touch_kernel,
        out_shape=jax.ShapeDtypeStruct((16, LANES), w_down.dtype),
        in_specs=vmem(1),
        out_specs=pl.BlockSpec(memory_space=pltpu.VMEM),
        compiler_params=pltpu.CompilerParams(vmem_limit_bytes=VMEM_BYTES),
        cost_estimate=pl.CostEstimate(
            flops=0, bytes_accessed=2 * w_down.size, transcendentals=0
        ),
        name="touch",
    )(pltpu.with_memory_space_constraint(w_down, pltpu.VMEM))


def halve_kernel(kept_ref, got_ref, keep_ref, send_ref):
    half = keep_ref.shape[0]
    keep_ref[...] = kept_ref[:half].astype(F32) + got_ref[:half].astype(F32)
    send_ref[...] = (kept_ref[half:].astype(F32) + got_ref[half:].astype(F32)).astype(BF16)


def halve(kept, got):
    rows, width = kept.shape
    return pl.pallas_call(
        halve_kernel,
        out_shape=[
            jax.ShapeDtypeStruct((rows // 2, width), F32),
            jax.ShapeDtypeStruct((rows // 2, width), BF16),
        ],
        in_specs=vmem(2),
        out_specs=vmem(2),
        compiler_params=pltpu.CompilerParams(vmem_limit_bytes=VMEM_BYTES),
        cost_estimate=pl.CostEstimate(
            flops=rows * width, bytes_accessed=7 * rows * width, transcendentals=0
        ),
        name="halve",
    )(kept, got)


def peer_masks(peers):
    return (0, 5, 1, 7, 2, 3, 4, 6) if peers == 8 else tuple(range(peers))


def early_masks(peers):
    return (4, 6) if peers == 8 else ()


def block_peer(block, masks, me):
    peer = jnp.zeros_like(block)
    for place, mask in enumerate(masks):
        peer = jnp.where(block == place, mask ^ me, peer)
    return peer


def pack_kernel(
    peers, capacity, chunks, masks, starts, direct, carries, after, me_ref, *refs
):
    targets_ref, terms, refs = refs[0], refs[1 : 2 * chunks + 1], refs[2 * chunks + 1 :]
    outs = refs[after + carries :]
    targets = targets_ref[...]
    rows = targets.shape[1]
    dest = targets // rows
    local = targets - dest * rows
    dest_column = jnp.sum(
        jnp.where(iota((rows, rows), 0) == iota((rows, rows), 1), dest, 0), axis=1, keepdims=True
    )
    same_before = jnp.logical_and(dest_column == dest, iota((rows, rows), 0) < iota((rows, rows), 1))
    rank = jnp.sum(same_before.astype(jnp.int32), axis=0, keepdims=True)
    slots = len(masks) * capacity
    slot = iota((slots, rows), 0)
    holder = slot // capacity
    if direct:
        holder = block_peer(holder, masks, me_ref[0])
    chosen = jnp.logical_and(dest == holder, rank == slot % capacity)
    selector = chosen.astype(F32).astype(BF16)
    parts = []
    if carries:
        local = jnp.broadcast_to((local + 1).astype(F32), (16, rows)).astype(BF16)
        labels = dot(local, selector, (1, 1))[:1] - 1.0
        square = (slots, slots)
        own = iota(square, 0) // capacity == iota(square, 1) // capacity
        own = jnp.logical_and(own, iota(square, 0) % capacity == capacity - 1)
        turn = (iota((slots, LANES), 0) % capacity == iota((slots, LANES), 1)).astype(F32)
        extra = dot(jnp.where(own, labels, 0.0).astype(BF16), turn.astype(BF16), (1, 0))
        sums = refs[0][...]
        high = sums.astype(BF16).astype(F32)
        middle = (sums - high).astype(BF16).astype(F32)
        low = (sums - high - middle).astype(BF16).astype(F32)
        row = iota((slots, LANES), 0) % capacity
        peer = iota((slots, LANES), 0) // capacity
        if direct:
            peer = block_peer(peer, masks, me_ref[0])
        pieces = sums.shape[1] // peers // LANES
        for p in range(peers):
            for level, values in enumerate((high, middle, low)):
                for piece in range(pieces):
                    start = (p * pieces + piece) * LANES
                    line = jnp.broadcast_to(values[:, start : start + LANES], (slots, LANES))
                    here = jnp.logical_and(peer == p, row == level * pieces + piece)
                    extra = jnp.where(here, line, extra)
        parts.append(extra)
    else:
        label = jnp.sum(jnp.where(chosen, local + 1, 0), axis=1, keepdims=True) - 1
        parts.append(jnp.broadcast_to(label.astype(F32), (slots, LANES)))
    for chunk in range(chunks):
        kept, got = terms[2 * chunk : 2 * chunk + 2]
        total = (kept[...].astype(F32) + got[...].astype(F32)).astype(BF16)
        parts.append(dot(selector, total, (1, 0)))
    if not direct:
        masks, starts, capacity = masks[:1], starts[:1], slots
    for block, start in enumerate(starts):
        at = 0
        for part in parts[start:]:
            end = at + part.shape[1]
            rows_of_block = part[block * capacity : (block + 1) * capacity]
            outs[block][:, at:end] = rows_of_block.astype(BF16)
            at = end


def pack(terms, targets, me, sums, after, peers, capacity, masks, starts, direct):
    rows = targets.shape[1]
    carries = sums is not None
    widths = [LANES] + [kept.shape[1] for kept, _ in terms]
    operands = [me, targets] + [x for pair in terms for x in pair] + ([sums] if carries else [])
    blocks = len(operands) - 1
    operands += after
    if direct:
        out_shape = [
            jax.ShapeDtypeStruct((capacity, sum(widths[start:])), BF16) for start in starts
        ]
    else:
        out_shape = [jax.ShapeDtypeStruct((peers * capacity, sum(widths)), BF16)]
    return pl.pallas_call(
        functools.partial(
            pack_kernel, peers, capacity, len(terms), masks, starts, direct, carries,
            len(after),
        ),
        out_shape=out_shape,
        in_specs=[pl.BlockSpec(memory_space=pltpu.SMEM)]
        + vmem(blocks)
        + [pl.BlockSpec(memory_space=pl.ANY)] * len(after),
        out_specs=vmem(len(out_shape)),
        compiler_params=pltpu.CompilerParams(vmem_limit_bytes=VMEM_BYTES),
        cost_estimate=pl.CostEstimate(
            flops=2 * rows * len(masks) * capacity * sum(widths),
            bytes_accessed=(6 * rows + 2 * len(masks) * capacity) * sum(widths),
            transcendentals=0,
        ),
        name="pack",
    )(*operands)


def swap(x, axis, mask):
    n = lax.axis_size(axis)
    return lax.ppermute(x, axis, [(i, i ^ mask) for i in range(n)])


def exchange(x, axis, pieces):
    shape = x.shape
    if x.ndim == 2:
        x = x.reshape(pieces, -1, shape[1])
    return lax.all_to_all(x, axis, split_axis=0, concat_axis=0, tiled=True).reshape(shape)


def probs_kernel(q_ref, k_ref, ids_ref, probs_ref, probs_t_ref):
    patches = q_ref.shape[0]
    ids = ids_ref[...]
    per_token = patches // ids.shape[1]
    token = iota((patches, ids.shape[1]), 0) // per_token
    column = jnp.sum(
        jnp.where(token == iota((patches, ids.shape[1]), 1), ids, 0), axis=1, keepdims=True
    )
    square = (patches, patches)
    row = jnp.sum(
        jnp.where(iota(square, 0) == iota(square, 1), column, 0), axis=0, keepdims=True
    )
    allowed = column == row
    scale = 1.0 / math.sqrt(HEAD_DIM)
    for head, (low, high, start, stop) in enumerate(head_windows()):
        q = masked(q_ref[:, start:stop], low, high, start, stop)
        k = k_ref[:, start:stop]
        for out, scores, axis in (
            (probs_ref, dot(q, k, (1, 1)), 1),
            (probs_t_ref, dot(k, q, (1, 1)), 0),
        ):
            scores = jnp.where(allowed, scores * scale, -jnp.inf)
            weights = jnp.exp(scores - jnp.max(scores, axis=axis, keepdims=True))
            out[head] = weights / jnp.sum(weights, axis=axis, keepdims=True)


def window_probs(queries, keys, ids):
    patches = queries.shape[0]
    shape = jax.ShapeDtypeStruct((HEADS, patches, patches), F32)
    return pl.pallas_call(
        probs_kernel,
        out_shape=[shape, shape],
        in_specs=vmem(3),
        out_specs=vmem(2),
        compiler_params=pltpu.CompilerParams(vmem_limit_bytes=VMEM_BYTES),
        cost_estimate=pl.CostEstimate(
            flops=8 * HEADS * patches * patches * LANES,
            bytes_accessed=8 * HEADS * patches * patches,
            transcendentals=2 * HEADS * patches * patches,
        ),
        name="probs",
    )(queries, keys, ids)


def norm_kernel(peers, early, carries, patches_ref, gain_ref, *refs):
    pieces, (out_ref, share_ref) = refs[:-2], refs[-2:]
    patches, width = patches_ref.shape
    pieces = [ref[...].astype(F32) for ref in pieces]
    pieces, begun = pieces[len(early) :], pieces[: len(early)]
    for place, begin in zip(early, begun):
        pieces[place] = jnp.concatenate([begin, pieces[place]], axis=1)
    routed = jnp.concatenate(pieces, axis=0) if len(pieces) > 1 else pieces[0]
    slots = routed.shape[0]
    per_token = routed.shape[1] // width
    columns = [routed[:, LANES + c * width : LANES + (c + 1) * width] for c in range(per_token)]
    held = jnp.concatenate(columns, axis=0).astype(BF16)
    lanes = per_token * slots
    extra = routed[:, :LANES]
    capacity = slots // peers
    if carries:
        place = iota((slots, LANES), 0) % capacity
        labels = jnp.where(place == capacity - 1, extra, 0.0).astype(BF16)
        turn = (iota((LANES, lanes), 0) == iota((LANES, lanes), 1) % capacity).astype(F32)
        spread = dot(labels, turn.astype(BF16), (1, 0))
        own = iota((slots, lanes), 0) // capacity == iota((slots, lanes), 1) % slots // capacity
        row_of_lane = jnp.sum(jnp.where(own, spread, 0.0), axis=0, keepdims=True)
    else:
        own = iota((slots, lanes), 1) % slots == iota((slots, lanes), 0)
        row_of_lane = jnp.sum(jnp.where(own, extra[:, :1], 0.0), axis=0, keepdims=True)
    row_of_lane = row_of_lane.astype(jnp.int32)
    patch_of_lane = row_of_lane * len(columns) + iota((1, lanes), 1) // slots
    patch_of_lane = jnp.where(row_of_lane < 0, -1, patch_of_lane)
    chosen = patch_of_lane == iota((patches, lanes), 0)
    patch_grads = dot(chosen.astype(F32).astype(BF16), held, (1, 0))
    inputs = patches_ref[...].astype(F32)
    inverse_rms = lax.rsqrt(jnp.mean(inputs * inputs, axis=1, keepdims=True) + 1e-06)
    normed = inputs * inverse_rms
    row = jnp.sum(patch_grads * normed, axis=0, keepdims=True)
    if carries:
        copies, lines, line_width = share_ref.shape
        pieces = (lines * line_width - width) // LANES
        parts = [row]
        for piece in range(pieces):
            kept = jnp.logical_and(place % pieces == piece, place < 3 * pieces)
            parts.append(jnp.sum(jnp.where(kept, extra, 0.0), axis=0, keepdims=True))
        row = jnp.concatenate(parts, axis=1)
        lines = [row[:, at : at + line_width] for at in range(0, row.shape[1], line_width)]
        row = jnp.broadcast_to(jnp.concatenate(lines, axis=0)[None], share_ref.shape)
    share_ref[...] = row.astype(share_ref.dtype)
    scaled = gain_ref[...] * patch_grads
    out_ref[...] = (
        inverse_rms * (scaled - normed * jnp.mean(scaled * normed, axis=1, keepdims=True))
    ).astype(BF16)


def norm_backward(received, peers, early, patches, gain, share):
    count, width = patches.shape
    routed = sum(x.size for x in received)
    return pl.pallas_call(
        functools.partial(norm_kernel, peers, early, len(share.shape) == 3),
        out_shape=[jax.ShapeDtypeStruct((count, width), BF16), share],
        in_specs=vmem(2 + len(received)),
        out_specs=vmem(2),
        compiler_params=pltpu.CompilerParams(vmem_limit_bytes=VMEM_BYTES),
        cost_estimate=pl.CostEstimate(
            flops=2 * count * routed,
            bytes_accessed=4 * count * width + 2 * routed,
            transcendentals=0,
        ),
        name="norm",
    )(patches, gain, *received)


def window_kernel(g_ref, q_ref, k_ref, v_ref, probs_ref, probs_t_ref, dq_ref, dk_ref, dv_ref):
    width = g_ref.shape[1]
    windows = head_windows()
    scores, scores_t, probs_t = [], [], []
    for head, (low, high, start, stop) in enumerate(windows):
        g = masked(g_ref[:, start:stop], low, high, start, stop)
        v = v_ref[:, start:stop]
        found = []
        for ref, grads, axis in (
            (probs_ref, dot(g, v, (1, 1)), 1),
            (probs_t_ref, dot(v, g, (1, 1)), 0),
        ):
            probs = ref[head]
            rounded = probs.astype(BF16)
            delta = jnp.sum(rounded.astype(F32) * grads, axis=axis, keepdims=True)
            found.append(((probs * (grads - delta)).astype(BF16), rounded))
        scores.append(found[0][0])
        scores_t.append(found[1][0])
        probs_t.append(found[1][1])
    scale = 1.0 / math.sqrt(HEAD_DIM)
    for start in range(0, width, LANES):
        stop = start + LANES
        heads = [h for h, (low, high, _, _) in enumerate(windows) if low < stop and high > start]
        for out, left, right_ref, factor in (
            (dq_ref, scores, k_ref, scale),
            (dk_ref, scores_t, q_ref, scale),
            (dv_ref, probs_t, g_ref, 1.0),
        ):
            right = right_ref[:, start:stop]
            rows = [masked(right, windows[h][0], windows[h][1], start, stop) for h in heads]
            product = dot(
                jnp.concatenate([left[h] for h in heads], axis=1),
                jnp.concatenate(rows, axis=0),
                (1, 0),
            )
            out[:, start:stop] = (product * factor).astype(BF16)


def window_backward(out_grads, queries, keys, values, probs, probs_t):
    patches, width = queries.shape
    shape = jax.ShapeDtypeStruct((patches, width), BF16)
    return pl.pallas_call(
        window_kernel,
        out_shape=[shape] * 3,
        in_specs=vmem(6),
        out_specs=vmem(3),
        compiler_params=pltpu.CompilerParams(vmem_limit_bytes=VMEM_BYTES),
        cost_estimate=pl.CostEstimate(
            flops=10 * HEADS * patches * patches * LANES,
            bytes_accessed=8 * HEADS * patches * patches + 14 * patches * width,
            transcendentals=0,
        ),
        name="window",
    )(out_grads, queries, keys, values, probs, probs_t)


def finish_kernel(width, images, gain_scale, bias_scale, shared_ref, gain_ref, bias_ref):
    devices, lines, line_width = shared_ref.shape
    total = jnp.sum(shared_ref[...].astype(F32), axis=0) * gain_scale
    for line in range(lines):
        at = line * line_width
        end = min(at + line_width, width)
        gain_ref[at:end] = total[line, : end - at]
    start = width - (lines - 1) * line_width
    for device in range(devices):
        piece = line_width - start
        own = shared_ref[device, lines - 1, start:].astype(F32) * bias_scale
        place = device % images * (devices // images) + device // images
        bias_ref[place * piece : (place + 1) * piece] = own


def finish(shared, width, images, gain_scale, bias_scale):
    devices, lines, line_width = shared.shape
    return pl.pallas_call(
        functools.partial(finish_kernel, width, images, gain_scale, bias_scale),
        out_shape=[
            jax.ShapeDtypeStruct((width,), F32),
            jax.ShapeDtypeStruct((devices * (lines * line_width - width),), F32),
        ],
        in_specs=vmem(1),
        out_specs=vmem(2),
        compiler_params=pltpu.CompilerParams(vmem_limit_bytes=VMEM_BYTES),
        name="finish",
    )(shared)


def body(llm_grads, token_target, patches, gain, w_down, queries, keys, values, window_ids):
    grad_rows = llm_grads[0]
    rows = grad_rows.shape[0]
    images, peers = lax.axis_size("img"), lax.axis_size("seq")
    devices = images * peers
    capacity = max(1, 2 * rows // peers)
    direct = peers <= DIRECT
    block = w_down.shape[1]
    width = patches.shape[2]
    pieces = block // peers // LANES
    carries = pieces > 0 and 3 * pieces < capacity and (width // LANES + pieces) % 2 == 0

    order = [0]
    while len(order) < images:
        order = [2 * j for j in order] + [2 * j + 1 for j in order]
    image, me = lax.axis_index("img"), lax.axis_index("seq")

    def columns(j):
        return lax.dynamic_slice(grad_rows, (0, (image ^ j) * block), (rows, block))

    x_blocks = [columns(0)] + [swap(columns(j), "img", j) for j in range(1, images)]
    x_blocks = [x_blocks[j] for j in order]
    probs, probs_t = window_probs(queries[0], keys[0], window_ids[0])

    touched = touch(w_down)
    terms, first = [], 0
    for index, count in enumerate(CHUNKS):
        kept, sent, *sums = project(x_blocks, w_down, touched, first, count * width, index == 0)
        first += count * width
        if index == 0:
            bias_part = sums[0]
        mask = 1
        while 2 * mask < images:
            kept, sent = halve(kept, swap(sent, "img", mask))
            mask *= 2
        terms.append((kept, swap(sent, "img", mask)))
    masks = peer_masks(peers)
    early = early_masks(peers) if direct else ()
    places = tuple(masks.index(mask) for mask in early)
    place = me.reshape(1)
    sums = bias_part if carries else None
    begun = []
    if early:
        begun = list(
            pack(
                terms[:1], token_target, place, sums, [], peers, capacity, early,
                (0,) * len(early), direct,
            )
        )
    starts = tuple(2 if mask in early else 0 for mask in masks)
    packed = pack(
        terms, token_target, place, sums, begun, peers, capacity, masks, starts, direct
    )
    if direct:
        routed = [swap(x, "seq", mask) if mask else x for x, mask in zip(packed, masks)]
    else:
        routed = [exchange(packed[0], "seq", peers)]
    routed = [swap(block, "seq", mask) for block, mask in zip(begun, early)] + routed

    if carries:
        share = jax.ShapeDtypeStruct((devices, 2, (width + pieces * LANES) // 2), BF16)
    else:
        share = jax.ShapeDtypeStruct((1, width), F32)
    out_grads, shared = norm_backward(routed, peers, places, patches[0], gain[None], share)
    gain_scale = 1.0 / math.sqrt(devices * patches.shape[1])
    bias_scale = 1.0 / math.sqrt(devices * rows)
    if carries:
        shared = exchange(shared, ("seq", "img"), devices)
        gain_grad, bias_grad = finish(shared, width, images, gain_scale, bias_scale)
    else:
        gain_grad = lax.psum(shared[0], ("img", "seq")) * gain_scale
        bias_grad = lax.all_gather(lax.psum(bias_part[0], "seq"), "img", tiled=True) * bias_scale
    grads = window_backward(out_grads, queries[0], keys[0], values[0], probs, probs_t)
    return (grads[0][None], grads[1][None], grads[2][None], gain_grad, bias_grad)


def solution(mesh):
    return jax.shard_map(
        body,
        mesh=mesh,
        in_specs=(
            P("img", "seq", None),
            P("img", "seq"),
            P("img", "seq", None),
            P(),
            P(None, "img"),
            P("img", "seq", None),
            P("img", "seq", None),
            P("img", "seq", None),
            P("img", "seq", None),
        ),
        out_specs=(P("img", "seq", None), P("img", "seq", None), P("img", "seq", None), P(), P()),
        check_vma=False,
    )
```

```python
import functools
import math

import jax
import jax.numpy as jnp
from jax import lax
from jax.experimental import pallas as pl
from jax.experimental.pallas import tpu as pltpu
from jax.sharding import PartitionSpec as P

HEADS = 16
HEAD_DIM = 80
LANES = 128
CHUNKS = (2, 2)
DIRECT = 8
VMEM_BYTES = 16 * 1024 * 1024

F32 = jnp.float32
BF16 = jnp.bfloat16


def iota(shape, axis):
    return lax.broadcasted_iota(jnp.int32, shape, axis)


def dot(a, b, over):
    return lax.dot_general(a, b, ((over[:1], over[1:]), ((), ())), preferred_element_type=F32)


def vmem(count):
    return [pl.BlockSpec(memory_space=pltpu.VMEM)] * count


def head_windows():
    windows = []
    for head in range(HEADS):
        low, high = head * HEAD_DIM, (head + 1) * HEAD_DIM
        start = low // LANES * LANES
        windows.append((low, high, start, -(-high // LANES) * LANES))
    return windows


def lane_mask(low, high, start, stop):
    at = iota((1, stop - start), 1) + start
    return jnp.logical_and(at >= low, at < high)


def masked(x, low, high, start, stop):
    return jnp.where(lane_mask(low, high, start, stop), x, jnp.zeros_like(x))


def project_kernel(blocks, first, tile, with_sum, *refs):
    x_refs, w_ref = refs[:blocks], refs[blocks]
    keep_ref, send_ref = refs[blocks + 2 : blocks + 4]
    x = jnp.concatenate([ref[...] for ref in x_refs], axis=0)
    if with_sum:
        refs[blocks + 4][...] = dot(jnp.ones((16, x.shape[0]), BF16), x, (1, 0))[:1]
    x = x.T
    half = keep_ref.shape[0]
    for t in range(0, keep_ref.shape[1], tile):
        product = dot(w_ref[first + t : first + t + tile], x, (1, 0)).T.astype(BF16)
        keep_ref[:, t : t + tile] = product[:half]
        send_ref[:, t : t + tile] = product[half:]


def project(x_blocks, w_down, touched, first, width, with_sum):
    blocks, (rows, depth) = len(x_blocks), x_blocks[0].shape
    tile = 512
    while width % tile:
        tile //= 2
    out_shape = [jax.ShapeDtypeStruct((blocks * rows // 2, width), BF16)] * 2
    if with_sum:
        out_shape = out_shape + [jax.ShapeDtypeStruct((1, depth), F32)]
    return pl.pallas_call(
        functools.partial(project_kernel, blocks, first, tile, with_sum),
        out_shape=out_shape,
        in_specs=vmem(blocks + 1) + [pl.BlockSpec(memory_space=pl.ANY)],
        out_specs=vmem(len(out_shape)),
        compiler_params=pltpu.CompilerParams(vmem_limit_bytes=VMEM_BYTES),
        cost_estimate=pl.CostEstimate(
            flops=2 * blocks * rows * depth * width,
            bytes_accessed=2 * width * depth,
            transcendentals=0,
        ),
        name="project",
    )(*x_blocks, pltpu.with_memory_space_constraint(w_down, pltpu.VMEM), touched)


def touch_kernel(w_ref, out_ref):
    out_ref[...] = w_ref[: out_ref.shape[0], : out_ref.shape[1]]


def touch(w_down):
    return pl.pallas_call(
        touch_kernel,
        out_shape=jax.ShapeDtypeStruct((16, LANES), w_down.dtype),
        in_specs=vmem(1),
        out_specs=pl.BlockSpec(memory_space=pltpu.VMEM),
        compiler_params=pltpu.CompilerParams(vmem_limit_bytes=VMEM_BYTES),
        cost_estimate=pl.CostEstimate(
            flops=0, bytes_accessed=2 * w_down.size, transcendentals=0
        ),
        name="touch",
    )(pltpu.with_memory_space_constraint(w_down, pltpu.VMEM))


def halve_kernel(kept_ref, got_ref, keep_ref, send_ref):
    half = keep_ref.shape[0]
    keep_ref[...] = kept_ref[:half].astype(F32) + got_ref[:half].astype(F32)
    send_ref[...] = (kept_ref[half:].astype(F32) + got_ref[half:].astype(F32)).astype(BF16)


def halve(kept, got):
    rows, width = kept.shape
    return pl.pallas_call(
        halve_kernel,
        out_shape=[
            jax.ShapeDtypeStruct((rows // 2, width), F32),
            jax.ShapeDtypeStruct((rows // 2, width), BF16),
        ],
        in_specs=vmem(2),
        out_specs=vmem(2),
        compiler_params=pltpu.CompilerParams(vmem_limit_bytes=VMEM_BYTES),
        cost_estimate=pl.CostEstimate(
            flops=rows * width, bytes_accessed=7 * rows * width, transcendentals=0
        ),
        name="halve",
    )(kept, got)


def peer_masks(peers):
    return (0, 4, 6, 1, 5, 2, 7, 3) if peers == 8 else tuple(range(peers))


def block_peer(block, masks, me):
    peer = jnp.zeros_like(block)
    for place, mask in enumerate(masks):
        peer = jnp.where(block == place, mask ^ me, peer)
    return peer


def pack_kernel(peers, capacity, masks, direct, labelled, carries, me_ref, *refs):
    targets_ref, kept_ref, got_ref, refs = refs[0], refs[1], refs[2], refs[3:]
    outs = refs[carries:]
    targets = targets_ref[...]
    rows = targets.shape[1]
    dest = targets // rows
    local = targets - dest * rows
    dest_column = jnp.sum(
        jnp.where(iota((rows, rows), 0) == iota((rows, rows), 1), dest, 0), axis=1, keepdims=True
    )
    same_before = jnp.logical_and(dest_column == dest, iota((rows, rows), 0) < iota((rows, rows), 1))
    rank = jnp.sum(same_before.astype(jnp.int32), axis=0, keepdims=True)
    slots = len(masks) * capacity
    slot = iota((slots, rows), 0)
    holder = slot // capacity
    if direct:
        holder = block_peer(holder, masks, me_ref[0])
    chosen = jnp.logical_and(dest == holder, rank == slot % capacity)
    selector = chosen.astype(F32).astype(BF16)
    parts = []
    if labelled and carries:
        local = jnp.broadcast_to((local + 1).astype(F32), (16, rows)).astype(BF16)
        labels = dot(local, selector, (1, 1))[:1] - 1.0
        square = (slots, slots)
        own = iota(square, 0) // capacity == iota(square, 1) // capacity
        own = jnp.logical_and(own, iota(square, 0) % capacity == capacity - 1)
        turn = (iota((slots, LANES), 0) % capacity == iota((slots, LANES), 1)).astype(F32)
        extra = dot(jnp.where(own, labels, 0.0).astype(BF16), turn.astype(BF16), (1, 0))
        sums = refs[0][...]
        high = sums.astype(BF16).astype(F32)
        middle = (sums - high).astype(BF16).astype(F32)
        low = (sums - high - middle).astype(BF16).astype(F32)
        row = iota((slots, LANES), 0) % capacity
        peer = iota((slots, LANES), 0) // capacity
        if direct:
            peer = block_peer(peer, masks, me_ref[0])
        pieces = sums.shape[1] // peers // LANES
        for p in range(peers):
            for level, values in enumerate((high, middle, low)):
                for piece in range(pieces):
                    start = (p * pieces + piece) * LANES
                    line = jnp.broadcast_to(values[:, start : start + LANES], (slots, LANES))
                    here = jnp.logical_and(peer == p, row == level * pieces + piece)
                    extra = jnp.where(here, line, extra)
        parts.append(extra)
    elif labelled:
        label = jnp.sum(jnp.where(chosen, local + 1, 0), axis=1, keepdims=True) - 1
        parts.append(jnp.broadcast_to(label.astype(F32), (slots, LANES)))
    total = (kept_ref[...].astype(F32) + got_ref[...].astype(F32)).astype(BF16)
    parts.append(dot(selector, total, (1, 0)))
    if not direct:
        capacity = slots
    at = 0
    for part in parts:
        end = at + part.shape[1]
        for block, out_ref in enumerate(outs):
            rows_of_block = part[block * capacity : (block + 1) * capacity]
            out_ref[:, at:end] = rows_of_block.astype(BF16)
        at = end


def pack(kept, got, targets, me, sums, peers, capacity, direct, labelled):
    rows, width = kept.shape
    carries = sums is not None
    width = width + (LANES if labelled else 0)
    operands = [me, targets, kept, got] + ([sums] if carries else [])
    if direct:
        out_shape = [jax.ShapeDtypeStruct((capacity, width), BF16)] * peers
    else:
        out_shape = [jax.ShapeDtypeStruct((peers * capacity, width), BF16)]
    return pl.pallas_call(
        functools.partial(
            pack_kernel, peers, capacity, peer_masks(peers), direct, labelled, carries
        ),
        out_shape=out_shape,
        in_specs=[pl.BlockSpec(memory_space=pltpu.SMEM)] + vmem(len(operands) - 1),
        out_specs=vmem(len(out_shape)),
        compiler_params=pltpu.CompilerParams(vmem_limit_bytes=VMEM_BYTES),
        cost_estimate=pl.CostEstimate(
            flops=2 * rows * peers * capacity * width,
            bytes_accessed=(6 * rows + 2 * peers * capacity) * width,
            transcendentals=0,
        ),
        name="pack",
    )(*operands)


def swap(x, axis, mask):
    n = lax.axis_size(axis)
    return lax.ppermute(x, axis, [(i, i ^ mask) for i in range(n)])


def exchange(x, axis, pieces):
    shape = x.shape
    if x.ndim == 2:
        x = x.reshape(pieces, -1, shape[1])
    return lax.all_to_all(x, axis, split_axis=0, concat_axis=0, tiled=True).reshape(shape)


def probs_kernel(q_ref, k_ref, ids_ref, probs_ref, probs_t_ref):
    patches = q_ref.shape[0]
    ids = ids_ref[...]
    per_token = patches // ids.shape[1]
    token = iota((patches, ids.shape[1]), 0) // per_token
    column = jnp.sum(
        jnp.where(token == iota((patches, ids.shape[1]), 1), ids, 0), axis=1, keepdims=True
    )
    square = (patches, patches)
    row = jnp.sum(
        jnp.where(iota(square, 0) == iota(square, 1), column, 0), axis=0, keepdims=True
    )
    allowed = column == row
    scale = 1.0 / math.sqrt(HEAD_DIM)
    for head, (low, high, start, stop) in enumerate(head_windows()):
        q = masked(q_ref[:, start:stop], low, high, start, stop)
        k = k_ref[:, start:stop]
        for out, scores, axis in (
            (probs_ref, dot(q, k, (1, 1)), 1),
            (probs_t_ref, dot(k, q, (1, 1)), 0),
        ):
            scores = jnp.where(allowed, scores * scale, -jnp.inf)
            weights = jnp.exp(scores - jnp.max(scores, axis=axis, keepdims=True))
            out[head] = weights / jnp.sum(weights, axis=axis, keepdims=True)


def window_probs(queries, keys, ids):
    patches = queries.shape[0]
    shape = jax.ShapeDtypeStruct((HEADS, patches, patches), F32)
    return pl.pallas_call(
        probs_kernel,
        out_shape=[shape, shape],
        in_specs=vmem(3),
        out_specs=vmem(2),
        compiler_params=pltpu.CompilerParams(vmem_limit_bytes=VMEM_BYTES),
        cost_estimate=pl.CostEstimate(
            flops=8 * HEADS * patches * patches * LANES,
            bytes_accessed=8 * HEADS * patches * patches,
            transcendentals=2 * HEADS * patches * patches,
        ),
        name="probs",
    )(queries, keys, ids)


def norm_kernel(peers, carries, me_ref, patches_ref, gain_ref, *refs):
    pieces, (out_ref, share_ref, blocks_ref) = refs[:-3], refs[-3:]
    patches, width = patches_ref.shape
    blocks, rest = pieces[:-1], pieces[-1]
    capacity = rest.shape[0] // peers
    if len(blocks) > 1:
        for mask, ref in zip(peer_masks(peers), blocks):
            start = pl.multiple_of((me_ref[0] ^ mask) * capacity, capacity)
            blocks_ref[pl.ds(start, capacity), :] = ref[...].astype(F32)
    else:
        blocks_ref[...] = blocks[0][...].astype(F32)
    routed = jnp.concatenate([blocks_ref[...], rest[...].astype(F32)], axis=1)
    slots = routed.shape[0]
    per_token = routed.shape[1] // width
    columns = [routed[:, LANES + c * width : LANES + (c + 1) * width] for c in range(per_token)]
    held = jnp.concatenate(columns, axis=0).astype(BF16)
    lanes = per_token * slots
    extra = routed[:, :LANES]
    if carries:
        place = iota((slots, LANES), 0) % capacity
        labels = jnp.where(place == capacity - 1, extra, 0.0).astype(BF16)
        turn = (iota((LANES, lanes), 0) == iota((LANES, lanes), 1) % capacity).astype(F32)
        spread = dot(labels, turn.astype(BF16), (1, 0))
        own = iota((slots, lanes), 0) // capacity == iota((slots, lanes), 1) % slots // capacity
        row_of_lane = jnp.sum(jnp.where(own, spread, 0.0), axis=0, keepdims=True)
    else:
        own = iota((slots, lanes), 1) % slots == iota((slots, lanes), 0)
        row_of_lane = jnp.sum(jnp.where(own, extra[:, :1], 0.0), axis=0, keepdims=True)
    row_of_lane = row_of_lane.astype(jnp.int32)
    patch_of_lane = row_of_lane * len(columns) + iota((1, lanes), 1) // slots
    patch_of_lane = jnp.where(row_of_lane < 0, -1, patch_of_lane)
    chosen = patch_of_lane == iota((patches, lanes), 0)
    patch_grads = dot(chosen.astype(F32).astype(BF16), held, (1, 0))
    inputs = patches_ref[...].astype(F32)
    inverse_rms = lax.rsqrt(jnp.mean(inputs * inputs, axis=1, keepdims=True) + 1e-06)
    normed = inputs * inverse_rms
    row = jnp.sum(patch_grads * normed, axis=0, keepdims=True)
    if carries:
        copies, lines, line_width = share_ref.shape
        pieces = (lines * line_width - width) // LANES
        parts = [row]
        for piece in range(pieces):
            kept = jnp.logical_and(place % pieces == piece, place < 3 * pieces)
            parts.append(jnp.sum(jnp.where(kept, extra, 0.0), axis=0, keepdims=True))
        row = jnp.concatenate(parts, axis=1)
        lines = [row[:, at : at + line_width] for at in range(0, row.shape[1], line_width)]
        row = jnp.broadcast_to(jnp.concatenate(lines, axis=0)[None], share_ref.shape)
    share_ref[...] = row.astype(share_ref.dtype)
    scaled = gain_ref[...] * patch_grads
    out_ref[...] = (
        inverse_rms * (scaled - normed * jnp.mean(scaled * normed, axis=1, keepdims=True))
    ).astype(BF16)


def norm_backward(received, me, peers, patches, gain, share):
    count, width = patches.shape
    routed = sum(x.size for x in received)
    return pl.pallas_call(
        functools.partial(norm_kernel, peers, len(share.shape) == 3),
        out_shape=[jax.ShapeDtypeStruct((count, width), BF16), share],
        in_specs=[pl.BlockSpec(memory_space=pltpu.SMEM)] + vmem(2 + len(received)),
        out_specs=vmem(2),
        scratch_shapes=[pltpu.VMEM((received[-1].shape[0], received[0].shape[1]), F32)],
        compiler_params=pltpu.CompilerParams(vmem_limit_bytes=VMEM_BYTES),
        cost_estimate=pl.CostEstimate(
            flops=2 * count * routed,
            bytes_accessed=4 * count * width + 2 * routed,
            transcendentals=0,
        ),
        name="norm",
    )(me, patches, gain, *received)


def window_kernel(g_ref, q_ref, k_ref, v_ref, probs_ref, probs_t_ref, dq_ref, dk_ref, dv_ref):
    width = g_ref.shape[1]
    windows = head_windows()
    scores, scores_t, probs_t = [], [], []
    for head, (low, high, start, stop) in enumerate(windows):
        g = masked(g_ref[:, start:stop], low, high, start, stop)
        v = v_ref[:, start:stop]
        found = []
        for ref, grads, axis in (
            (probs_ref, dot(g, v, (1, 1)), 1),
            (probs_t_ref, dot(v, g, (1, 1)), 0),
        ):
            probs = ref[head]
            rounded = probs.astype(BF16)
            delta = jnp.sum(rounded.astype(F32) * grads, axis=axis, keepdims=True)
            found.append(((probs * (grads - delta)).astype(BF16), rounded))
        scores.append(found[0][0])
        scores_t.append(found[1][0])
        probs_t.append(found[1][1])
    scale = 1.0 / math.sqrt(HEAD_DIM)
    for start in range(0, width, LANES):
        stop = start + LANES
        heads = [h for h, (low, high, _, _) in enumerate(windows) if low < stop and high > start]
        for out, left, right_ref, factor in (
            (dq_ref, scores, k_ref, scale),
            (dk_ref, scores_t, q_ref, scale),
            (dv_ref, probs_t, g_ref, 1.0),
        ):
            right = right_ref[:, start:stop]
            rows = [masked(right, windows[h][0], windows[h][1], start, stop) for h in heads]
            product = dot(
                jnp.concatenate([left[h] for h in heads], axis=1),
                jnp.concatenate(rows, axis=0),
                (1, 0),
            )
            out[:, start:stop] = (product * factor).astype(BF16)


def window_backward(out_grads, queries, keys, values, probs, probs_t):
    patches, width = queries.shape
    shape = jax.ShapeDtypeStruct((patches, width), BF16)
    return pl.pallas_call(
        window_kernel,
        out_shape=[shape] * 3,
        in_specs=vmem(6),
        out_specs=vmem(3),
        compiler_params=pltpu.CompilerParams(vmem_limit_bytes=VMEM_BYTES),
        cost_estimate=pl.CostEstimate(
            flops=10 * HEADS * patches * patches * LANES,
            bytes_accessed=8 * HEADS * patches * patches + 14 * patches * width,
            transcendentals=0,
        ),
        name="window",
    )(out_grads, queries, keys, values, probs, probs_t)


def finish_kernel(width, images, gain_scale, bias_scale, shared_ref, gain_ref, bias_ref):
    devices, lines, line_width = shared_ref.shape
    total = jnp.sum(shared_ref[...].astype(F32), axis=0) * gain_scale
    for line in range(lines):
        at = line * line_width
        end = min(at + line_width, width)
        gain_ref[at:end] = total[line, : end - at]
    start = width - (lines - 1) * line_width
    for device in range(devices):
        piece = line_width - start
        own = shared_ref[device, lines - 1, start:].astype(F32) * bias_scale
        place = device % images * (devices // images) + device // images
        bias_ref[place * piece : (place + 1) * piece] = own


def finish(shared, width, images, gain_scale, bias_scale):
    devices, lines, line_width = shared.shape
    return pl.pallas_call(
        functools.partial(finish_kernel, width, images, gain_scale, bias_scale),
        out_shape=[
            jax.ShapeDtypeStruct((width,), F32),
            jax.ShapeDtypeStruct((devices * (lines * line_width - width),), F32),
        ],
        in_specs=vmem(1),
        out_specs=vmem(2),
        compiler_params=pltpu.CompilerParams(vmem_limit_bytes=VMEM_BYTES),
        name="finish",
    )(shared)


def body(llm_grads, token_target, patches, gain, w_down, queries, keys, values, window_ids):
    grad_rows = llm_grads[0]
    rows = grad_rows.shape[0]
    images, peers = lax.axis_size("img"), lax.axis_size("seq")
    devices = images * peers
    capacity = max(1, 2 * rows // peers)
    direct = peers <= DIRECT
    block = w_down.shape[1]
    width = patches.shape[2]
    pieces = block // peers // LANES
    carries = pieces > 0 and 3 * pieces < capacity and (width // LANES + pieces) % 2 == 0

    order = [0]
    while len(order) < images:
        order = [2 * j for j in order] + [2 * j + 1 for j in order]
    image, me = lax.axis_index("img"), lax.axis_index("seq")

    def columns(j):
        return lax.dynamic_slice(grad_rows, (0, (image ^ j) * block), (rows, block))

    x_blocks = [columns(0)] + [swap(columns(j), "img", j) for j in range(1, images)]
    x_blocks = [x_blocks[j] for j in order]
    probs, probs_t = window_probs(queries[0], keys[0], window_ids[0])

    touched = touch(w_down)
    terms, first = [], 0
    for index, count in enumerate(CHUNKS):
        kept, sent, *sums = project(x_blocks, w_down, touched, first, count * width, index == 0)
        first += count * width
        if index == 0:
            bias_part = sums[0]
        mask = 1
        while 2 * mask < images:
            kept, sent = halve(kept, swap(sent, "img", mask))
            mask *= 2
        terms.append((kept, swap(sent, "img", mask)))
    place = me.reshape(1)
    (kept, got), (last_kept, last_got) = terms
    sums = bias_part if carries else None
    blocks = pack(kept, got, token_target, place, sums, peers, capacity, direct, True)
    rest = pack(last_kept, last_got, token_target, place, None, peers, capacity, False, False)[0]
    if direct:
        masks = peer_masks(peers)
        routed = [swap(x, "seq", mask) if mask else x for x, mask in zip(blocks, masks)]
    else:
        routed = [exchange(blocks[0], "seq", peers)]
    routed = routed + [exchange(rest, "seq", peers)]

    if carries:
        share = jax.ShapeDtypeStruct((devices, 2, (width + pieces * LANES) // 2), BF16)
    else:
        share = jax.ShapeDtypeStruct((1, width), F32)
    out_grads, shared = norm_backward(routed, place, peers, patches[0], gain[None], share)
    gain_scale = 1.0 / math.sqrt(devices * patches.shape[1])
    bias_scale = 1.0 / math.sqrt(devices * rows)
    if carries:
        shared = exchange(shared, ("seq", "img"), devices)
        gain_grad, bias_grad = finish(shared, width, images, gain_scale, bias_scale)
    else:
        gain_grad = lax.psum(shared[0], ("img", "seq")) * gain_scale
        bias_grad = lax.all_gather(lax.psum(bias_part[0], "seq"), "img", tiled=True) * bias_scale
    grads = window_backward(out_grads, queries[0], keys[0], values[0], probs, probs_t)
    return (grads[0][None], grads[1][None], grads[2][None], gain_grad, bias_grad)


def solution(mesh):
    return jax.shard_map(
        body,
        mesh=mesh,
        in_specs=(
            P("img", "seq", None),
            P("img", "seq"),
            P("img", "seq", None),
            P(),
            P(None, "img"),
            P("img", "seq", None),
            P("img", "seq", None),
            P("img", "seq", None),
            P("img", "seq", None),
        ),
        out_specs=(P("img", "seq", None), P("img", "seq", None), P("img", "seq", None), P(), P()),
        check_vma=False,
    )
```

```python
import functools
import math

import jax
import jax.numpy as jnp
from jax import lax
from jax.experimental import pallas as pl
from jax.experimental.pallas import tpu as pltpu
from jax.sharding import PartitionSpec as P

HEADS = 16
HEAD_DIM = 80
LANES = 128
CHUNKS = (2, 2)
DIRECT = 8
VMEM_BYTES = 16 * 1024 * 1024

F32 = jnp.float32
BF16 = jnp.bfloat16


def iota(shape, axis):
    return lax.broadcasted_iota(jnp.int32, shape, axis)


def dot(a, b, over):
    return lax.dot_general(a, b, ((over[:1], over[1:]), ((), ())), preferred_element_type=F32)


def vmem(count):
    return [pl.BlockSpec(memory_space=pltpu.VMEM)] * count


def head_windows():
    windows = []
    for head in range(HEADS):
        low, high = head * HEAD_DIM, (head + 1) * HEAD_DIM
        start = low // LANES * LANES
        windows.append((low, high, start, -(-high // LANES) * LANES))
    return windows


def lane_mask(low, high, start, stop):
    at = iota((1, stop - start), 1) + start
    return jnp.logical_and(at >= low, at < high)


def masked(x, low, high, start, stop):
    return jnp.where(lane_mask(low, high, start, stop), x, jnp.zeros_like(x))


def project_kernel(blocks, first, tile, with_sum, *refs):
    x_refs, w_ref = refs[:blocks], refs[blocks]
    keep_ref, send_ref = refs[blocks + 2 : blocks + 4]
    x = jnp.concatenate([ref[...] for ref in x_refs], axis=0)
    if with_sum:
        refs[blocks + 4][...] = dot(jnp.ones((16, x.shape[0]), BF16), x, (1, 0))[:1]
    x = x.T
    half = keep_ref.shape[0]
    for t in range(0, keep_ref.shape[1], tile):
        product = dot(w_ref[first + t : first + t + tile], x, (1, 0)).T.astype(BF16)
        keep_ref[:, t : t + tile] = product[:half]
        send_ref[:, t : t + tile] = product[half:]


def project(x_blocks, w_down, touched, first, width, with_sum):
    blocks, (rows, depth) = len(x_blocks), x_blocks[0].shape
    tile = 512
    while width % tile:
        tile //= 2
    out_shape = [jax.ShapeDtypeStruct((blocks * rows // 2, width), BF16)] * 2
    if with_sum:
        out_shape = out_shape + [jax.ShapeDtypeStruct((1, depth), F32)]
    return pl.pallas_call(
        functools.partial(project_kernel, blocks, first, tile, with_sum),
        out_shape=out_shape,
        in_specs=vmem(blocks + 1) + [pl.BlockSpec(memory_space=pl.ANY)],
        out_specs=vmem(len(out_shape)),
        compiler_params=pltpu.CompilerParams(vmem_limit_bytes=VMEM_BYTES),
        cost_estimate=pl.CostEstimate(
            flops=2 * blocks * rows * depth * width,
            bytes_accessed=2 * width * depth,
            transcendentals=0,
        ),
        name="project",
    )(*x_blocks, pltpu.with_memory_space_constraint(w_down, pltpu.VMEM), touched)


def touch_kernel(w_ref, out_ref):
    out_ref[...] = w_ref[: out_ref.shape[0], : out_ref.shape[1]]


def touch(w_down):
    return pl.pallas_call(
        touch_kernel,
        out_shape=jax.ShapeDtypeStruct((16, LANES), w_down.dtype),
        in_specs=vmem(1),
        out_specs=pl.BlockSpec(memory_space=pltpu.VMEM),
        compiler_params=pltpu.CompilerParams(vmem_limit_bytes=VMEM_BYTES),
        cost_estimate=pl.CostEstimate(
            flops=0, bytes_accessed=2 * w_down.size, transcendentals=0
        ),
        name="touch",
    )(pltpu.with_memory_space_constraint(w_down, pltpu.VMEM))


def halve_kernel(kept_ref, got_ref, keep_ref, send_ref):
    half = keep_ref.shape[0]
    keep_ref[...] = kept_ref[:half].astype(F32) + got_ref[:half].astype(F32)
    send_ref[...] = (kept_ref[half:].astype(F32) + got_ref[half:].astype(F32)).astype(BF16)


def halve(kept, got):
    rows, width = kept.shape
    return pl.pallas_call(
        halve_kernel,
        out_shape=[
            jax.ShapeDtypeStruct((rows // 2, width), F32),
            jax.ShapeDtypeStruct((rows // 2, width), BF16),
        ],
        in_specs=vmem(2),
        out_specs=vmem(2),
        compiler_params=pltpu.CompilerParams(vmem_limit_bytes=VMEM_BYTES),
        cost_estimate=pl.CostEstimate(
            flops=rows * width, bytes_accessed=7 * rows * width, transcendentals=0
        ),
        name="halve",
    )(kept, got)


def peer_masks(peers):
    return (0, 4, 1, 6, 2, 5, 3, 7) if peers == 8 else tuple(range(peers))


def early_masks(peers):
    return ()


def block_peer(block, masks, me):
    peer = jnp.zeros_like(block)
    for place, mask in enumerate(masks):
        peer = jnp.where(block == place, mask ^ me, peer)
    return peer


def pack_kernel(
    peers, capacity, chunks, masks, starts, direct, carries, after, me_ref, *refs
):
    targets_ref, terms, refs = refs[0], refs[1 : 2 * chunks + 1], refs[2 * chunks + 1 :]
    outs = refs[after + carries :]
    targets = targets_ref[...]
    rows = targets.shape[1]
    dest = targets // rows
    local = targets - dest * rows
    dest_column = jnp.sum(
        jnp.where(iota((rows, rows), 0) == iota((rows, rows), 1), dest, 0), axis=1, keepdims=True
    )
    same_before = jnp.logical_and(dest_column == dest, iota((rows, rows), 0) < iota((rows, rows), 1))
    rank = jnp.sum(same_before.astype(jnp.int32), axis=0, keepdims=True)
    slots = len(masks) * capacity
    slot = iota((slots, rows), 0)
    holder = slot // capacity
    if direct:
        holder = block_peer(holder, masks, me_ref[0])
    chosen = jnp.logical_and(dest == holder, rank == slot % capacity)
    selector = chosen.astype(F32).astype(BF16)
    parts = []
    if carries:
        local = jnp.broadcast_to((local + 1).astype(F32), (16, rows)).astype(BF16)
        labels = dot(local, selector, (1, 1))[:1] - 1.0
        square = (slots, slots)
        own = iota(square, 0) // capacity == iota(square, 1) // capacity
        own = jnp.logical_and(own, iota(square, 0) % capacity == capacity - 1)
        turn = (iota((slots, LANES), 0) % capacity == iota((slots, LANES), 1)).astype(F32)
        extra = dot(jnp.where(own, labels, 0.0).astype(BF16), turn.astype(BF16), (1, 0))
        sums = refs[0][...]
        high = sums.astype(BF16).astype(F32)
        middle = (sums - high).astype(BF16).astype(F32)
        low = (sums - high - middle).astype(BF16).astype(F32)
        row = iota((slots, LANES), 0) % capacity
        peer = iota((slots, LANES), 0) // capacity
        if direct:
            peer = block_peer(peer, masks, me_ref[0])
        pieces = sums.shape[1] // peers // LANES
        for p in range(peers):
            for level, values in enumerate((high, middle, low)):
                for piece in range(pieces):
                    start = (p * pieces + piece) * LANES
                    line = jnp.broadcast_to(values[:, start : start + LANES], (slots, LANES))
                    here = jnp.logical_and(peer == p, row == level * pieces + piece)
                    extra = jnp.where(here, line, extra)
        parts.append(extra)
    else:
        label = jnp.sum(jnp.where(chosen, local + 1, 0), axis=1, keepdims=True) - 1
        parts.append(jnp.broadcast_to(label.astype(F32), (slots, LANES)))
    for chunk in range(chunks):
        kept, got = terms[2 * chunk : 2 * chunk + 2]
        total = (kept[...].astype(F32) + got[...].astype(F32)).astype(BF16)
        parts.append(dot(selector, total, (1, 0)))
    if not direct:
        masks, starts, capacity = masks[:1], starts[:1], slots
    for block, start in enumerate(starts):
        at = 0
        for part in parts[start:]:
            end = at + part.shape[1]
            rows_of_block = part[block * capacity : (block + 1) * capacity]
            outs[block][:, at:end] = rows_of_block.astype(BF16)
            at = end


def pack(terms, targets, me, sums, after, peers, capacity, masks, starts, direct):
    rows = targets.shape[1]
    carries = sums is not None
    widths = [LANES] + [kept.shape[1] for kept, _ in terms]
    operands = [me, targets] + [x for pair in terms for x in pair] + ([sums] if carries else [])
    blocks = len(operands) - 1
    operands += after
    if direct:
        out_shape = [
            jax.ShapeDtypeStruct((capacity, sum(widths[start:])), BF16) for start in starts
        ]
    else:
        out_shape = [jax.ShapeDtypeStruct((peers * capacity, sum(widths)), BF16)]
    return pl.pallas_call(
        functools.partial(
            pack_kernel, peers, capacity, len(terms), masks, starts, direct, carries,
            len(after),
        ),
        out_shape=out_shape,
        in_specs=[pl.BlockSpec(memory_space=pltpu.SMEM)]
        + vmem(blocks)
        + [pl.BlockSpec(memory_space=pl.ANY)] * len(after),
        out_specs=vmem(len(out_shape)),
        compiler_params=pltpu.CompilerParams(vmem_limit_bytes=VMEM_BYTES),
        cost_estimate=pl.CostEstimate(
            flops=2 * rows * len(masks) * capacity * sum(widths),
            bytes_accessed=(6 * rows + 2 * len(masks) * capacity) * sum(widths),
            transcendentals=0,
        ),
        name="pack",
    )(*operands)


def swap(x, axis, mask):
    n = lax.axis_size(axis)
    return lax.ppermute(x, axis, [(i, i ^ mask) for i in range(n)])


def exchange(x, axis, pieces):
    shape = x.shape
    if x.ndim == 2:
        x = x.reshape(pieces, -1, shape[1])
    return lax.all_to_all(x, axis, split_axis=0, concat_axis=0, tiled=True).reshape(shape)


def probs_kernel(q_ref, k_ref, ids_ref, probs_ref, probs_t_ref):
    patches = q_ref.shape[0]
    ids = ids_ref[...]
    per_token = patches // ids.shape[1]
    token = iota((patches, ids.shape[1]), 0) // per_token
    column = jnp.sum(
        jnp.where(token == iota((patches, ids.shape[1]), 1), ids, 0), axis=1, keepdims=True
    )
    square = (patches, patches)
    row = jnp.sum(
        jnp.where(iota(square, 0) == iota(square, 1), column, 0), axis=0, keepdims=True
    )
    allowed = column == row
    scale = 1.0 / math.sqrt(HEAD_DIM)
    for head, (low, high, start, stop) in enumerate(head_windows()):
        q = masked(q_ref[:, start:stop], low, high, start, stop)
        k = k_ref[:, start:stop]
        for out, scores, axis in (
            (probs_ref, dot(q, k, (1, 1)), 1),
            (probs_t_ref, dot(k, q, (1, 1)), 0),
        ):
            scores = jnp.where(allowed, scores * scale, -jnp.inf)
            weights = jnp.exp(scores - jnp.max(scores, axis=axis, keepdims=True))
            out[head] = weights / jnp.sum(weights, axis=axis, keepdims=True)


def window_probs(queries, keys, ids):
    patches = queries.shape[0]
    shape = jax.ShapeDtypeStruct((HEADS, patches, patches), F32)
    return pl.pallas_call(
        probs_kernel,
        out_shape=[shape, shape],
        in_specs=vmem(3),
        out_specs=vmem(2),
        compiler_params=pltpu.CompilerParams(vmem_limit_bytes=VMEM_BYTES),
        cost_estimate=pl.CostEstimate(
            flops=8 * HEADS * patches * patches * LANES,
            bytes_accessed=8 * HEADS * patches * patches,
            transcendentals=2 * HEADS * patches * patches,
        ),
        name="probs",
    )(queries, keys, ids)


def norm_kernel(peers, early, carries, patches_ref, gain_ref, *refs):
    pieces, (out_ref, share_ref) = refs[:-2], refs[-2:]
    patches, width = patches_ref.shape
    pieces = [ref[...].astype(F32) for ref in pieces]
    pieces, begun = pieces[len(early) :], pieces[: len(early)]
    for place, begin in zip(early, begun):
        pieces[place] = jnp.concatenate([begin, pieces[place]], axis=1)
    routed = jnp.concatenate(pieces, axis=0) if len(pieces) > 1 else pieces[0]
    slots = routed.shape[0]
    per_token = routed.shape[1] // width
    columns = [routed[:, LANES + c * width : LANES + (c + 1) * width] for c in range(per_token)]
    held = jnp.concatenate(columns, axis=0).astype(BF16)
    lanes = per_token * slots
    extra = routed[:, :LANES]
    capacity = slots // peers
    if carries:
        place = iota((slots, LANES), 0) % capacity
        labels = jnp.where(place == capacity - 1, extra, 0.0).astype(BF16)
        turn = (iota((LANES, lanes), 0) == iota((LANES, lanes), 1) % capacity).astype(F32)
        spread = dot(labels, turn.astype(BF16), (1, 0))
        own = iota((slots, lanes), 0) // capacity == iota((slots, lanes), 1) % slots // capacity
        row_of_lane = jnp.sum(jnp.where(own, spread, 0.0), axis=0, keepdims=True)
    else:
        own = iota((slots, lanes), 1) % slots == iota((slots, lanes), 0)
        row_of_lane = jnp.sum(jnp.where(own, extra[:, :1], 0.0), axis=0, keepdims=True)
    row_of_lane = row_of_lane.astype(jnp.int32)
    patch_of_lane = row_of_lane * len(columns) + iota((1, lanes), 1) // slots
    patch_of_lane = jnp.where(row_of_lane < 0, -1, patch_of_lane)
    chosen = patch_of_lane == iota((patches, lanes), 0)
    patch_grads = dot(chosen.astype(F32).astype(BF16), held, (1, 0))
    inputs = patches_ref[...].astype(F32)
    inverse_rms = lax.rsqrt(jnp.mean(inputs * inputs, axis=1, keepdims=True) + 1e-06)
    normed = inputs * inverse_rms
    row = jnp.sum(patch_grads * normed, axis=0, keepdims=True)
    if carries:
        copies, lines, line_width = share_ref.shape
        pieces = (lines * line_width - width) // LANES
        parts = [row]
        for piece in range(pieces):
            kept = jnp.logical_and(place % pieces == piece, place < 3 * pieces)
            parts.append(jnp.sum(jnp.where(kept, extra, 0.0), axis=0, keepdims=True))
        row = jnp.concatenate(parts, axis=1)
        lines = [row[:, at : at + line_width] for at in range(0, row.shape[1], line_width)]
        row = jnp.broadcast_to(jnp.concatenate(lines, axis=0)[None], share_ref.shape)
    share_ref[...] = row.astype(share_ref.dtype)
    scaled = gain_ref[...] * patch_grads
    out_ref[...] = (
        inverse_rms * (scaled - normed * jnp.mean(scaled * normed, axis=1, keepdims=True))
    ).astype(BF16)


def norm_backward(received, peers, early, patches, gain, share):
    count, width = patches.shape
    routed = sum(x.size for x in received)
    return pl.pallas_call(
        functools.partial(norm_kernel, peers, early, len(share.shape) == 3),
        out_shape=[jax.ShapeDtypeStruct((count, width), BF16), share],
        in_specs=vmem(2 + len(received)),
        out_specs=vmem(2),
        compiler_params=pltpu.CompilerParams(vmem_limit_bytes=VMEM_BYTES),
        cost_estimate=pl.CostEstimate(
            flops=2 * count * routed,
            bytes_accessed=4 * count * width + 2 * routed,
            transcendentals=0,
        ),
        name="norm",
    )(patches, gain, *received)


def window_kernel(g_ref, q_ref, k_ref, v_ref, probs_ref, probs_t_ref, dq_ref, dk_ref, dv_ref):
    width = g_ref.shape[1]
    windows = head_windows()
    scores, scores_t, probs_t = [], [], []
    for head, (low, high, start, stop) in enumerate(windows):
        g = masked(g_ref[:, start:stop], low, high, start, stop)
        v = v_ref[:, start:stop]
        found = []
        for ref, grads, axis in (
            (probs_ref, dot(g, v, (1, 1)), 1),
            (probs_t_ref, dot(v, g, (1, 1)), 0),
        ):
            probs = ref[head]
            rounded = probs.astype(BF16)
            delta = jnp.sum(rounded.astype(F32) * grads, axis=axis, keepdims=True)
            found.append(((probs * (grads - delta)).astype(BF16), rounded))
        scores.append(found[0][0])
        scores_t.append(found[1][0])
        probs_t.append(found[1][1])
    scale = 1.0 / math.sqrt(HEAD_DIM)
    for start in range(0, width, LANES):
        stop = start + LANES
        heads = [h for h, (low, high, _, _) in enumerate(windows) if low < stop and high > start]
        for out, left, right_ref, factor in (
            (dq_ref, scores, k_ref, scale),
            (dk_ref, scores_t, q_ref, scale),
            (dv_ref, probs_t, g_ref, 1.0),
        ):
            right = right_ref[:, start:stop]
            rows = [masked(right, windows[h][0], windows[h][1], start, stop) for h in heads]
            product = dot(
                jnp.concatenate([left[h] for h in heads], axis=1),
                jnp.concatenate(rows, axis=0),
                (1, 0),
            )
            out[:, start:stop] = (product * factor).astype(BF16)


def window_backward(out_grads, queries, keys, values, probs, probs_t):
    patches, width = queries.shape
    shape = jax.ShapeDtypeStruct((patches, width), BF16)
    return pl.pallas_call(
        window_kernel,
        out_shape=[shape] * 3,
        in_specs=vmem(6),
        out_specs=vmem(3),
        compiler_params=pltpu.CompilerParams(vmem_limit_bytes=VMEM_BYTES),
        cost_estimate=pl.CostEstimate(
            flops=10 * HEADS * patches * patches * LANES,
            bytes_accessed=8 * HEADS * patches * patches + 14 * patches * width,
            transcendentals=0,
        ),
        name="window",
    )(out_grads, queries, keys, values, probs, probs_t)


def finish_kernel(width, images, gain_scale, bias_scale, shared_ref, gain_ref, bias_ref):
    devices, lines, line_width = shared_ref.shape
    total = jnp.sum(shared_ref[...].astype(F32), axis=0) * gain_scale
    for line in range(lines):
        at = line * line_width
        end = min(at + line_width, width)
        gain_ref[at:end] = total[line, : end - at]
    start = width - (lines - 1) * line_width
    for device in range(devices):
        piece = line_width - start
        own = shared_ref[device, lines - 1, start:].astype(F32) * bias_scale
        place = device % images * (devices // images) + device // images
        bias_ref[place * piece : (place + 1) * piece] = own


def finish(shared, width, images, gain_scale, bias_scale):
    devices, lines, line_width = shared.shape
    return pl.pallas_call(
        functools.partial(finish_kernel, width, images, gain_scale, bias_scale),
        out_shape=[
            jax.ShapeDtypeStruct((width,), F32),
            jax.ShapeDtypeStruct((devices * (lines * line_width - width),), F32),
        ],
        in_specs=vmem(1),
        out_specs=vmem(2),
        compiler_params=pltpu.CompilerParams(vmem_limit_bytes=VMEM_BYTES),
        name="finish",
    )(shared)


def body(llm_grads, token_target, patches, gain, w_down, queries, keys, values, window_ids):
    grad_rows = llm_grads[0]
    rows = grad_rows.shape[0]
    images, peers = lax.axis_size("img"), lax.axis_size("seq")
    devices = images * peers
    capacity = max(1, 2 * rows // peers)
    direct = peers <= DIRECT
    block = w_down.shape[1]
    width = patches.shape[2]
    pieces = block // peers // LANES
    carries = pieces > 0 and 3 * pieces < capacity and (width // LANES + pieces) % 2 == 0

    order = [0]
    while len(order) < images:
        order = [2 * j for j in order] + [2 * j + 1 for j in order]
    image, me = lax.axis_index("img"), lax.axis_index("seq")

    def columns(j):
        return lax.dynamic_slice(grad_rows, (0, (image ^ j) * block), (rows, block))

    x_blocks = [columns(0)] + [swap(columns(j), "img", j) for j in range(1, images)]
    x_blocks = [x_blocks[j] for j in order]
    probs, probs_t = window_probs(queries[0], keys[0], window_ids[0])

    touched = touch(w_down)
    terms, first = [], 0
    for index, count in enumerate(CHUNKS):
        kept, sent, *sums = project(x_blocks, w_down, touched, first, count * width, index == 0)
        first += count * width
        if index == 0:
            bias_part = sums[0]
        mask = 1
        while 2 * mask < images:
            kept, sent = halve(kept, swap(sent, "img", mask))
            mask *= 2
        terms.append((kept, swap(sent, "img", mask)))
    masks = peer_masks(peers)
    early = early_masks(peers) if direct else ()
    places = tuple(masks.index(mask) for mask in early)
    place = me.reshape(1)
    sums = bias_part if carries else None
    begun = []
    if early:
        begun = list(
            pack(
                terms[:1], token_target, place, sums, [], peers, capacity, early,
                (0,) * len(early), direct,
            )
        )
    starts = tuple(2 if mask in early else 0 for mask in masks)
    packed = pack(
        terms, token_target, place, sums, begun, peers, capacity, masks, starts, direct
    )
    if direct:
        routed = [swap(x, "seq", mask) if mask else x for x, mask in zip(packed, masks)]
    else:
        routed = [exchange(packed[0], "seq", peers)]
    routed = [swap(block, "seq", mask) for block, mask in zip(begun, early)] + routed

    if carries:
        share = jax.ShapeDtypeStruct((devices, 2, (width + pieces * LANES) // 2), BF16)
    else:
        share = jax.ShapeDtypeStruct((1, width), F32)
    out_grads, shared = norm_backward(routed, peers, places, patches[0], gain[None], share)
    gain_scale = 1.0 / math.sqrt(devices * patches.shape[1])
    bias_scale = 1.0 / math.sqrt(devices * rows)
    if carries:
        shared = exchange(shared, ("seq", "img"), devices)
        gain_grad, bias_grad = finish(shared, width, images, gain_scale, bias_scale)
    else:
        gain_grad = lax.psum(shared[0], ("img", "seq")) * gain_scale
        bias_grad = lax.all_gather(lax.psum(bias_part[0], "seq"), "img", tiled=True) * bias_scale
    grads = window_backward(out_grads, queries[0], keys[0], values[0], probs, probs_t)
    return (grads[0][None], grads[1][None], grads[2][None], gain_grad, bias_grad)


def solution(mesh):
    return jax.shard_map(
        body,
        mesh=mesh,
        in_specs=(
            P("img", "seq", None),
            P("img", "seq"),
            P("img", "seq", None),
            P(),
            P(None, "img"),
            P("img", "seq", None),
            P("img", "seq", None),
            P("img", "seq", None),
            P("img", "seq", None),
        ),
        out_specs=(P("img", "seq", None), P("img", "seq", None), P("img", "seq", None), P(), P()),
        check_vma=False,
    )
```

```python
import functools
import math

import jax
import jax.numpy as jnp
from jax import lax
from jax.experimental import pallas as pl
from jax.experimental.pallas import tpu as pltpu
from jax.sharding import PartitionSpec as P

HEADS = 16
HEAD_DIM = 80
LANES = 128
CHUNKS = (2, 2)
DIRECT = 8
VMEM_BYTES = 16 * 1024 * 1024

F32 = jnp.float32
BF16 = jnp.bfloat16


def iota(shape, axis):
    return lax.broadcasted_iota(jnp.int32, shape, axis)


def dot(a, b, over):
    return lax.dot_general(a, b, ((over[:1], over[1:]), ((), ())), preferred_element_type=F32)


def vmem(count):
    return [pl.BlockSpec(memory_space=pltpu.VMEM)] * count


def head_windows():
    windows = []
    for head in range(HEADS):
        low, high = head * HEAD_DIM, (head + 1) * HEAD_DIM
        start = low // LANES * LANES
        windows.append((low, high, start, -(-high // LANES) * LANES))
    return windows


def lane_mask(low, high, start, stop):
    at = iota((1, stop - start), 1) + start
    return jnp.logical_and(at >= low, at < high)


def masked(x, low, high, start, stop):
    return jnp.where(lane_mask(low, high, start, stop), x, jnp.zeros_like(x))


def project_kernel(blocks, first, tile, with_sum, *refs):
    x_refs, w_ref = refs[:blocks], refs[blocks]
    keep_ref, send_ref = refs[blocks + 2 : blocks + 4]
    x = jnp.concatenate([ref[...] for ref in x_refs], axis=0)
    if with_sum:
        refs[blocks + 4][...] = dot(jnp.ones((16, x.shape[0]), BF16), x, (1, 0))[:1]
    x = x.T
    half = keep_ref.shape[0]
    for t in range(0, keep_ref.shape[1], tile):
        product = dot(w_ref[first + t : first + t + tile], x, (1, 0)).T.astype(BF16)
        keep_ref[:, t : t + tile] = product[:half]
        send_ref[:, t : t + tile] = product[half:]


def project(x_blocks, w_down, touched, first, width, with_sum):
    blocks, (rows, depth) = len(x_blocks), x_blocks[0].shape
    tile = 512
    while width % tile:
        tile //= 2
    out_shape = [jax.ShapeDtypeStruct((blocks * rows // 2, width), BF16)] * 2
    if with_sum:
        out_shape = out_shape + [jax.ShapeDtypeStruct((1, depth), F32)]
    return pl.pallas_call(
        functools.partial(project_kernel, blocks, first, tile, with_sum),
        out_shape=out_shape,
        in_specs=vmem(blocks + 1) + [pl.BlockSpec(memory_space=pl.ANY)],
        out_specs=vmem(len(out_shape)),
        compiler_params=pltpu.CompilerParams(vmem_limit_bytes=VMEM_BYTES),
        cost_estimate=pl.CostEstimate(
            flops=2 * blocks * rows * depth * width,
            bytes_accessed=2 * width * depth,
            transcendentals=0,
        ),
        name="project",
    )(*x_blocks, pltpu.with_memory_space_constraint(w_down, pltpu.VMEM), touched)


def touch_kernel(w_ref, out_ref):
    out_ref[...] = w_ref[: out_ref.shape[0], : out_ref.shape[1]]


def touch(w_down):
    return pl.pallas_call(
        touch_kernel,
        out_shape=jax.ShapeDtypeStruct((16, LANES), w_down.dtype),
        in_specs=vmem(1),
        out_specs=pl.BlockSpec(memory_space=pltpu.VMEM),
        compiler_params=pltpu.CompilerParams(vmem_limit_bytes=VMEM_BYTES),
        cost_estimate=pl.CostEstimate(
            flops=0, bytes_accessed=2 * w_down.size, transcendentals=0
        ),
        name="touch",
    )(pltpu.with_memory_space_constraint(w_down, pltpu.VMEM))


def halve_kernel(kept_ref, got_ref, keep_ref, send_ref):
    half = keep_ref.shape[0]
    keep_ref[...] = kept_ref[:half].astype(F32) + got_ref[:half].astype(F32)
    send_ref[...] = (kept_ref[half:].astype(F32) + got_ref[half:].astype(F32)).astype(BF16)


def halve(kept, got):
    rows, width = kept.shape
    return pl.pallas_call(
        halve_kernel,
        out_shape=[
            jax.ShapeDtypeStruct((rows // 2, width), F32),
            jax.ShapeDtypeStruct((rows // 2, width), BF16),
        ],
        in_specs=vmem(2),
        out_specs=vmem(2),
        compiler_params=pltpu.CompilerParams(vmem_limit_bytes=VMEM_BYTES),
        cost_estimate=pl.CostEstimate(
            flops=rows * width, bytes_accessed=7 * rows * width, transcendentals=0
        ),
        name="halve",
    )(kept, got)


def peer_masks(peers):
    return (0, 4, 1, 6, 2, 5, 3, 7) if peers == 8 else tuple(range(peers))


def early_masks(peers):
    return ()


def block_peer(block, masks, me):
    peer = jnp.zeros_like(block)
    for place, mask in enumerate(masks):
        peer = jnp.where(block == place, mask ^ me, peer)
    return peer


def pack_kernel(
    peers, capacity, chunks, masks, starts, direct, carries, after, me_ref, *refs
):
    targets_ref, terms, refs = refs[0], refs[1 : 2 * chunks + 1], refs[2 * chunks + 1 :]
    outs = refs[after + carries :]
    targets = targets_ref[...]
    rows = targets.shape[1]
    dest = targets // rows
    local = targets - dest * rows
    dest_column = jnp.sum(
        jnp.where(iota((rows, rows), 0) == iota((rows, rows), 1), dest, 0), axis=1, keepdims=True
    )
    same_before = jnp.logical_and(dest_column == dest, iota((rows, rows), 0) < iota((rows, rows), 1))
    rank = jnp.sum(same_before.astype(jnp.int32), axis=0, keepdims=True)
    slots = len(masks) * capacity
    slot = iota((slots, rows), 0)
    holder = slot // capacity
    if direct:
        holder = block_peer(holder, masks, me_ref[0])
    chosen = jnp.logical_and(dest == holder, rank == slot % capacity)
    selector = chosen.astype(F32).astype(BF16)
    parts = []
    if carries:
        local = jnp.broadcast_to((local + 1).astype(F32), (16, rows)).astype(BF16)
        labels = dot(local, selector, (1, 1))[:1] - 1.0
        square = (slots, slots)
        own = iota(square, 0) // capacity == iota(square, 1) // capacity
        own = jnp.logical_and(own, iota(square, 0) % capacity == capacity - 1)
        turn = (iota((slots, LANES), 0) % capacity == iota((slots, LANES), 1)).astype(F32)
        extra = dot(jnp.where(own, labels, 0.0).astype(BF16), turn.astype(BF16), (1, 0))
        sums = refs[0][...]
        high = sums.astype(BF16).astype(F32)
        middle = (sums - high).astype(BF16).astype(F32)
        low = (sums - high - middle).astype(BF16).astype(F32)
        row = iota((slots, LANES), 0) % capacity
        peer = iota((slots, LANES), 0) // capacity
        if direct:
            peer = block_peer(peer, masks, me_ref[0])
        pieces = sums.shape[1] // peers // LANES
        for p in range(peers):
            for level, values in enumerate((high, middle, low)):
                for piece in range(pieces):
                    start = (p * pieces + piece) * LANES
                    line = jnp.broadcast_to(values[:, start : start + LANES], (slots, LANES))
                    here = jnp.logical_and(peer == p, row == level * pieces + piece)
                    extra = jnp.where(here, line, extra)
        parts.append(extra)
    else:
        label = jnp.sum(jnp.where(chosen, local + 1, 0), axis=1, keepdims=True) - 1
        parts.append(jnp.broadcast_to(label.astype(F32), (slots, LANES)))
    for chunk in range(chunks):
        kept, got = terms[2 * chunk : 2 * chunk + 2]
        total = (kept[...].astype(F32) + got[...].astype(F32)).astype(BF16)
        parts.append(dot(selector, total, (1, 0)))
    if not direct:
        masks, starts, capacity = masks[:1], starts[:1], slots
    for block, start in enumerate(starts):
        at = 0
        for part in parts[start:]:
            end = at + part.shape[1]
            rows_of_block = part[block * capacity : (block + 1) * capacity]
            outs[block][:, at:end] = rows_of_block.astype(BF16)
            at = end


def pack(terms, targets, me, sums, after, peers, capacity, masks, starts, direct):
    rows = targets.shape[1]
    carries = sums is not None
    widths = [LANES] + [kept.shape[1] for kept, _ in terms]
    operands = [me, targets] + [x for pair in terms for x in pair] + ([sums] if carries else [])
    blocks = len(operands) - 1
    operands += after
    if direct:
        out_shape = [
            jax.ShapeDtypeStruct((capacity, sum(widths[start:])), BF16) for start in starts
        ]
    else:
        out_shape = [jax.ShapeDtypeStruct((peers * capacity, sum(widths)), BF16)]
    return pl.pallas_call(
        functools.partial(
            pack_kernel, peers, capacity, len(terms), masks, starts, direct, carries,
            len(after),
        ),
        out_shape=out_shape,
        in_specs=[pl.BlockSpec(memory_space=pltpu.SMEM)]
        + vmem(blocks)
        + [pl.BlockSpec(memory_space=pl.ANY)] * len(after),
        out_specs=vmem(len(out_shape)),
        compiler_params=pltpu.CompilerParams(vmem_limit_bytes=VMEM_BYTES),
        cost_estimate=pl.CostEstimate(
            flops=2 * rows * len(masks) * capacity * sum(widths),
            bytes_accessed=(6 * rows + 2 * len(masks) * capacity) * sum(widths),
            transcendentals=0,
        ),
        name="pack",
    )(*operands)


def swap(x, axis, mask):
    n = lax.axis_size(axis)
    return lax.ppermute(x, axis, [(i, i ^ mask) for i in range(n)])


def exchange(x, axis, pieces):
    shape = x.shape
    if x.ndim == 2:
        x = x.reshape(pieces, -1, shape[1])
    return lax.all_to_all(x, axis, split_axis=0, concat_axis=0, tiled=True).reshape(shape)


def probs_kernel(q_ref, k_ref, ids_ref, probs_ref, probs_t_ref):
    patches = q_ref.shape[0]
    ids = ids_ref[...]
    per_token = patches // ids.shape[1]
    token = iota((patches, ids.shape[1]), 0) // per_token
    column = jnp.sum(
        jnp.where(token == iota((patches, ids.shape[1]), 1), ids, 0), axis=1, keepdims=True
    )
    square = (patches, patches)
    row = jnp.sum(
        jnp.where(iota(square, 0) == iota(square, 1), column, 0), axis=0, keepdims=True
    )
    allowed = column == row
    scale = 1.0 / math.sqrt(HEAD_DIM)
    for head, (low, high, start, stop) in enumerate(head_windows()):
        q = masked(q_ref[:, start:stop], low, high, start, stop)
        k = k_ref[:, start:stop]
        for out, scores, axis in (
            (probs_ref, dot(q, k, (1, 1)), 1),
            (probs_t_ref, dot(k, q, (1, 1)), 0),
        ):
            scores = jnp.where(allowed, scores * scale, -jnp.inf)
            weights = jnp.exp(scores - jnp.max(scores, axis=axis, keepdims=True))
            out[head] = weights / jnp.sum(weights, axis=axis, keepdims=True)


def window_probs(queries, keys, ids):
    patches = queries.shape[0]
    shape = jax.ShapeDtypeStruct((HEADS, patches, patches), F32)
    return pl.pallas_call(
        probs_kernel,
        out_shape=[shape, shape],
        in_specs=vmem(3),
        out_specs=vmem(2),
        compiler_params=pltpu.CompilerParams(vmem_limit_bytes=VMEM_BYTES),
        cost_estimate=pl.CostEstimate(
            flops=8 * HEADS * patches * patches * LANES,
            bytes_accessed=8 * HEADS * patches * patches,
            transcendentals=2 * HEADS * patches * patches,
        ),
        name="probs",
    )(queries, keys, ids)


def norm_kernel(peers, early, carries, patches_ref, gain_ref, *refs):
    pieces, (out_ref, share_ref) = refs[:-2], refs[-2:]
    patches, width = patches_ref.shape
    pieces = [ref[...].astype(F32) for ref in pieces]
    pieces, begun = pieces[len(early) :], pieces[: len(early)]
    for place, begin in zip(early, begun):
        pieces[place] = jnp.concatenate([begin, pieces[place]], axis=1)
    routed = jnp.concatenate(pieces, axis=0) if len(pieces) > 1 else pieces[0]
    slots = routed.shape[0]
    per_token = routed.shape[1] // width
    columns = [routed[:, LANES + c * width : LANES + (c + 1) * width] for c in range(per_token)]
    held = jnp.concatenate(columns, axis=0).astype(BF16)
    lanes = per_token * slots
    extra = routed[:, :LANES]
    capacity = slots // peers
    if carries:
        place = iota((slots, LANES), 0) % capacity
        labels = jnp.where(place == capacity - 1, extra, 0.0).astype(BF16)
        turn = (iota((LANES, lanes), 0) == iota((LANES, lanes), 1) % capacity).astype(F32)
        spread = dot(labels, turn.astype(BF16), (1, 0))
        own = iota((slots, lanes), 0) // capacity == iota((slots, lanes), 1) % slots // capacity
        row_of_lane = jnp.sum(jnp.where(own, spread, 0.0), axis=0, keepdims=True)
    else:
        own = iota((slots, lanes), 1) % slots == iota((slots, lanes), 0)
        row_of_lane = jnp.sum(jnp.where(own, extra[:, :1], 0.0), axis=0, keepdims=True)
    row_of_lane = row_of_lane.astype(jnp.int32)
    patch_of_lane = row_of_lane * len(columns) + iota((1, lanes), 1) // slots
    patch_of_lane = jnp.where(row_of_lane < 0, -1, patch_of_lane)
    chosen = patch_of_lane == iota((patches, lanes), 0)
    patch_grads = dot(chosen.astype(F32).astype(BF16), held, (1, 0))
    inputs = patches_ref[...].astype(F32)
    inverse_rms = lax.rsqrt(jnp.mean(inputs * inputs, axis=1, keepdims=True) + 1e-06)
    normed = inputs * inverse_rms
    row = jnp.sum(patch_grads * normed, axis=0, keepdims=True)
    if carries:
        copies, lines, line_width = share_ref.shape
        pieces = (lines * line_width - width) // LANES
        parts = [row]
        for piece in range(pieces):
            kept = jnp.logical_and(place % pieces == piece, place < 3 * pieces)
            parts.append(jnp.sum(jnp.where(kept, extra, 0.0), axis=0, keepdims=True))
        row = jnp.concatenate(parts, axis=1)
        lines = [row[:, at : at + line_width] for at in range(0, row.shape[1], line_width)]
        row = jnp.broadcast_to(jnp.concatenate(lines, axis=0)[None], share_ref.shape)
    share_ref[...] = row.astype(share_ref.dtype)
    scaled = gain_ref[...] * patch_grads
    out_ref[...] = (
        inverse_rms * (scaled - normed * jnp.mean(scaled * normed, axis=1, keepdims=True))
    ).astype(BF16)


def norm_backward(received, peers, early, patches, gain, share):
    count, width = patches.shape
    routed = sum(x.size for x in received)
    return pl.pallas_call(
        functools.partial(norm_kernel, peers, early, len(share.shape) == 3),
        out_shape=[jax.ShapeDtypeStruct((count, width), BF16), share],
        in_specs=vmem(2 + len(received)),
        out_specs=vmem(2),
        compiler_params=pltpu.CompilerParams(vmem_limit_bytes=VMEM_BYTES),
        cost_estimate=pl.CostEstimate(
            flops=2 * count * routed,
            bytes_accessed=4 * count * width + 2 * routed,
            transcendentals=0,
        ),
        name="norm",
    )(patches, gain, *received)


def window_kernel(g_ref, q_ref, k_ref, v_ref, probs_ref, probs_t_ref, dq_ref, dk_ref, dv_ref):
    width = g_ref.shape[1]
    windows = head_windows()
    scores, scores_t, probs_t = [], [], []
    for head, (low, high, start, stop) in enumerate(windows):
        g = masked(g_ref[:, start:stop], low, high, start, stop)
        v = v_ref[:, start:stop]
        found = []
        for ref, grads, axis in (
            (probs_ref, dot(g, v, (1, 1)), 1),
            (probs_t_ref, dot(v, g, (1, 1)), 0),
        ):
            probs = ref[head]
            rounded = probs.astype(BF16)
            delta = jnp.sum(rounded.astype(F32) * grads, axis=axis, keepdims=True)
            found.append(((probs * (grads - delta)).astype(BF16), rounded))
        scores.append(found[0][0])
        scores_t.append(found[1][0])
        probs_t.append(found[1][1])
    scale = 1.0 / math.sqrt(HEAD_DIM)
    for start in range(0, width, LANES):
        stop = start + LANES
        heads = [h for h, (low, high, _, _) in enumerate(windows) if low < stop and high > start]
        for out, left, right_ref, factor in (
            (dq_ref, scores, k_ref, scale),
            (dk_ref, scores_t, q_ref, scale),
            (dv_ref, probs_t, g_ref, 1.0),
        ):
            right = right_ref[:, start:stop]
            rows = [masked(right, windows[h][0], windows[h][1], start, stop) for h in heads]
            product = dot(
                jnp.concatenate([left[h] for h in heads], axis=1),
                jnp.concatenate(rows, axis=0),
                (1, 0),
            )
            out[:, start:stop] = (product * factor).astype(BF16)


def window_backward(out_grads, queries, keys, values, probs, probs_t):
    patches, width = queries.shape
    shape = jax.ShapeDtypeStruct((patches, width), BF16)
    return pl.pallas_call(
        window_kernel,
        out_shape=[shape] * 3,
        in_specs=vmem(6),
        out_specs=vmem(3),
        compiler_params=pltpu.CompilerParams(vmem_limit_bytes=VMEM_BYTES),
        cost_estimate=pl.CostEstimate(
            flops=10 * HEADS * patches * patches * LANES,
            bytes_accessed=8 * HEADS * patches * patches + 14 * patches * width,
            transcendentals=0,
        ),
        name="window",
    )(out_grads, queries, keys, values, probs, probs_t)


def finish_kernel(width, images, gain_scale, bias_scale, shared_ref, gain_ref, bias_ref):
    devices, lines, line_width = shared_ref.shape
    shared = shared_ref[...].astype(F32)
    total = jnp.sum(shared, axis=0) * gain_scale
    for line in range(lines):
        at = line * line_width
        end = min(at + line_width, width)
        gain_ref[at:end] = total[line, : end - at]
    start = width - (lines - 1) * line_width
    for device in range(devices):
        piece = line_width - start
        own = shared[device, lines - 1, start:] * bias_scale
        place = device % images * (devices // images) + device // images
        bias_ref[place * piece : (place + 1) * piece] = own


def finish(shared, width, images, gain_scale, bias_scale):
    devices, lines, line_width = shared.shape
    return pl.pallas_call(
        functools.partial(finish_kernel, width, images, gain_scale, bias_scale),
        out_shape=[
            jax.ShapeDtypeStruct((width,), F32),
            jax.ShapeDtypeStruct((devices * (lines * line_width - width),), F32),
        ],
        in_specs=vmem(1),
        out_specs=vmem(2),
        compiler_params=pltpu.CompilerParams(vmem_limit_bytes=VMEM_BYTES),
        name="finish",
    )(shared)


def body(llm_grads, token_target, patches, gain, w_down, queries, keys, values, window_ids):
    grad_rows = llm_grads[0]
    rows = grad_rows.shape[0]
    images, peers = lax.axis_size("img"), lax.axis_size("seq")
    devices = images * peers
    capacity = max(1, 2 * rows // peers)
    direct = peers <= DIRECT
    block = w_down.shape[1]
    width = patches.shape[2]
    pieces = block // peers // LANES
    carries = pieces > 0 and 3 * pieces < capacity and (width // LANES + pieces) % 2 == 0

    order = [0]
    while len(order) < images:
        order = [2 * j for j in order] + [2 * j + 1 for j in order]
    image, me = lax.axis_index("img"), lax.axis_index("seq")

    def columns(j):
        return lax.dynamic_slice(grad_rows, (0, (image ^ j) * block), (rows, block))

    x_blocks = [columns(0)] + [swap(columns(j), "img", j) for j in range(1, images)]
    x_blocks = [x_blocks[j] for j in order]
    probs, probs_t = window_probs(queries[0], keys[0], window_ids[0])

    touched = touch(w_down)
    terms, first = [], 0
    for index, count in enumerate(CHUNKS):
        kept, sent, *sums = project(x_blocks, w_down, touched, first, count * width, index == 0)
        first += count * width
        if index == 0:
            bias_part = sums[0]
        mask = 1
        while 2 * mask < images:
            kept, sent = halve(kept, swap(sent, "img", mask))
            mask *= 2
        terms.append((kept, swap(sent, "img", mask)))
    masks = peer_masks(peers)
    early = early_masks(peers) if direct else ()
    places = tuple(masks.index(mask) for mask in early)
    place = me.reshape(1)
    sums = bias_part if carries else None
    begun = []
    if early:
        begun = list(
            pack(
                terms[:1], token_target, place, sums, [], peers, capacity, early,
                (0,) * len(early), direct,
            )
        )
    starts = tuple(2 if mask in early else 0 for mask in masks)
    packed = pack(
        terms, token_target, place, sums, begun, peers, capacity, masks, starts, direct
    )
    if direct:
        routed = [swap(x, "seq", mask) if mask else x for x, mask in zip(packed, masks)]
    else:
        routed = [exchange(packed[0], "seq", peers)]
    routed = [swap(block, "seq", mask) for block, mask in zip(begun, early)] + routed

    if carries:
        share = jax.ShapeDtypeStruct((devices, 2, (width + pieces * LANES) // 2), BF16)
    else:
        share = jax.ShapeDtypeStruct((1, width), F32)
    out_grads, shared = norm_backward(routed, peers, places, patches[0], gain[None], share)
    gain_scale = 1.0 / math.sqrt(devices * patches.shape[1])
    bias_scale = 1.0 / math.sqrt(devices * rows)
    if carries:
        shared = exchange(shared, ("seq", "img"), devices)
        gain_grad, bias_grad = finish(shared, width, images, gain_scale, bias_scale)
    else:
        gain_grad = lax.psum(shared[0], ("img", "seq")) * gain_scale
        bias_grad = lax.all_gather(lax.psum(bias_part[0], "seq"), "img", tiled=True) * bias_scale
    grads = window_backward(out_grads, queries[0], keys[0], values[0], probs, probs_t)
    return (grads[0][None], grads[1][None], grads[2][None], gain_grad, bias_grad)


def solution(mesh):
    return jax.shard_map(
        body,
        mesh=mesh,
        in_specs=(
            P("img", "seq", None),
            P("img", "seq"),
            P("img", "seq", None),
            P(),
            P(None, "img"),
            P("img", "seq", None),
            P("img", "seq", None),
            P("img", "seq", None),
            P("img", "seq", None),
        ),
        out_specs=(P("img", "seq", None), P("img", "seq", None), P("img", "seq", None), P(), P()),
        check_vma=False,
    )
```

```python
import functools
import math

import jax
import jax.numpy as jnp
from jax import lax
from jax.experimental import pallas as pl
from jax.experimental.pallas import tpu as pltpu
from jax.sharding import PartitionSpec as P

HEADS = 16
HEAD_DIM = 80
LANES = 128
CHUNKS = (2, 2)
DIRECT = 8
VMEM_BYTES = 16 * 1024 * 1024

F32 = jnp.float32
BF16 = jnp.bfloat16


def iota(shape, axis):
    return lax.broadcasted_iota(jnp.int32, shape, axis)


def dot(a, b, over):
    return lax.dot_general(a, b, ((over[:1], over[1:]), ((), ())), preferred_element_type=F32)


def vmem(count):
    return [pl.BlockSpec(memory_space=pltpu.VMEM)] * count


def head_windows():
    windows = []
    for head in range(HEADS):
        low, high = head * HEAD_DIM, (head + 1) * HEAD_DIM
        start = low // LANES * LANES
        windows.append((low, high, start, -(-high // LANES) * LANES))
    return windows


def lane_mask(low, high, start, stop):
    at = iota((1, stop - start), 1) + start
    return jnp.logical_and(at >= low, at < high)


def masked(x, low, high, start, stop):
    return jnp.where(lane_mask(low, high, start, stop), x, jnp.zeros_like(x))


def project_kernel(blocks, first, tile, with_sum, *refs):
    x_refs, w_ref = refs[:blocks], refs[blocks]
    keep_ref, send_ref = refs[blocks + 2 : blocks + 4]
    x = jnp.concatenate([ref[...] for ref in x_refs], axis=0)
    if with_sum:
        refs[blocks + 4][...] = dot(jnp.ones((16, x.shape[0]), BF16), x, (1, 0))[:1]
    x = x.T
    half = keep_ref.shape[0]
    for t in range(0, keep_ref.shape[1], tile):
        product = dot(w_ref[first + t : first + t + tile], x, (1, 0)).T.astype(BF16)
        keep_ref[:, t : t + tile] = product[:half]
        send_ref[:, t : t + tile] = product[half:]


def project(x_blocks, w_down, touched, first, width, with_sum):
    blocks, (rows, depth) = len(x_blocks), x_blocks[0].shape
    tile = 512
    while width % tile:
        tile //= 2
    out_shape = [jax.ShapeDtypeStruct((blocks * rows // 2, width), BF16)] * 2
    if with_sum:
        out_shape = out_shape + [jax.ShapeDtypeStruct((1, depth), F32)]
    return pl.pallas_call(
        functools.partial(project_kernel, blocks, first, tile, with_sum),
        out_shape=out_shape,
        in_specs=vmem(blocks + 1) + [pl.BlockSpec(memory_space=pl.ANY)],
        out_specs=vmem(len(out_shape)),
        compiler_params=pltpu.CompilerParams(vmem_limit_bytes=VMEM_BYTES),
        cost_estimate=pl.CostEstimate(
            flops=2 * blocks * rows * depth * width,
            bytes_accessed=2 * width * depth,
            transcendentals=0,
        ),
        name="project",
    )(*x_blocks, pltpu.with_memory_space_constraint(w_down, pltpu.VMEM), touched)


def touch_kernel(w_ref, out_ref):
    out_ref[...] = w_ref[: out_ref.shape[0], : out_ref.shape[1]]


def touch(w_down):
    return pl.pallas_call(
        touch_kernel,
        out_shape=jax.ShapeDtypeStruct((16, LANES), w_down.dtype),
        in_specs=vmem(1),
        out_specs=pl.BlockSpec(memory_space=pltpu.VMEM),
        compiler_params=pltpu.CompilerParams(vmem_limit_bytes=VMEM_BYTES),
        cost_estimate=pl.CostEstimate(
            flops=0, bytes_accessed=2 * w_down.size, transcendentals=0
        ),
        name="touch",
    )(pltpu.with_memory_space_constraint(w_down, pltpu.VMEM))


def halve_kernel(kept_ref, got_ref, keep_ref, send_ref):
    half = keep_ref.shape[0]
    keep_ref[...] = kept_ref[:half].astype(F32) + got_ref[:half].astype(F32)
    send_ref[...] = (kept_ref[half:].astype(F32) + got_ref[half:].astype(F32)).astype(BF16)


def halve(kept, got):
    rows, width = kept.shape
    return pl.pallas_call(
        halve_kernel,
        out_shape=[
            jax.ShapeDtypeStruct((rows // 2, width), F32),
            jax.ShapeDtypeStruct((rows // 2, width), BF16),
        ],
        in_specs=vmem(2),
        out_specs=vmem(2),
        compiler_params=pltpu.CompilerParams(vmem_limit_bytes=VMEM_BYTES),
        cost_estimate=pl.CostEstimate(
            flops=rows * width, bytes_accessed=7 * rows * width, transcendentals=0
        ),
        name="halve",
    )(kept, got)


def peer_masks(peers):
    return (0, 7, 1, 6, 2, 5, 3, 4) if peers == 8 else tuple(range(peers))


def early_masks(peers):
    return ()


def block_peer(block, masks, me):
    peer = jnp.zeros_like(block)
    for place, mask in enumerate(masks):
        peer = jnp.where(block == place, mask ^ me, peer)
    return peer


def pack_kernel(
    peers, capacity, chunks, masks, starts, direct, carries, after, me_ref, *refs
):
    targets_ref, terms, refs = refs[0], refs[1 : 2 * chunks + 1], refs[2 * chunks + 1 :]
    outs = refs[after + carries :]
    targets = targets_ref[...]
    rows = targets.shape[1]
    dest = targets // rows
    local = targets - dest * rows
    dest_column = jnp.sum(
        jnp.where(iota((rows, rows), 0) == iota((rows, rows), 1), dest, 0), axis=1, keepdims=True
    )
    same_before = jnp.logical_and(dest_column == dest, iota((rows, rows), 0) < iota((rows, rows), 1))
    rank = jnp.sum(same_before.astype(jnp.int32), axis=0, keepdims=True)
    slots = len(masks) * capacity
    slot = iota((slots, rows), 0)
    holder = slot // capacity
    if direct:
        holder = block_peer(holder, masks, me_ref[0])
    chosen = jnp.logical_and(dest == holder, rank == slot % capacity)
    selector = chosen.astype(F32).astype(BF16)
    parts = []
    if carries:
        local = jnp.broadcast_to((local + 1).astype(F32), (16, rows)).astype(BF16)
        labels = dot(local, selector, (1, 1))[:1] - 1.0
        square = (slots, slots)
        own = iota(square, 0) // capacity == iota(square, 1) // capacity
        own = jnp.logical_and(own, iota(square, 0) % capacity == capacity - 1)
        turn = (iota((slots, LANES), 0) % capacity == iota((slots, LANES), 1)).astype(F32)
        extra = dot(jnp.where(own, labels, 0.0).astype(BF16), turn.astype(BF16), (1, 0))
        sums = refs[0][...]
        high = sums.astype(BF16).astype(F32)
        middle = (sums - high).astype(BF16).astype(F32)
        low = (sums - high - middle).astype(BF16).astype(F32)
        row = iota((slots, LANES), 0) % capacity
        peer = iota((slots, LANES), 0) // capacity
        if direct:
            peer = block_peer(peer, masks, me_ref[0])
        pieces = sums.shape[1] // peers // LANES
        for p in range(peers):
            for level, values in enumerate((high, middle, low)):
                for piece in range(pieces):
                    start = (p * pieces + piece) * LANES
                    line = jnp.broadcast_to(values[:, start : start + LANES], (slots, LANES))
                    here = jnp.logical_and(peer == p, row == level * pieces + piece)
                    extra = jnp.where(here, line, extra)
        parts.append(extra)
    else:
        label = jnp.sum(jnp.where(chosen, local + 1, 0), axis=1, keepdims=True) - 1
        parts.append(jnp.broadcast_to(label.astype(F32), (slots, LANES)))
    for chunk in range(chunks):
        kept, got = terms[2 * chunk : 2 * chunk + 2]
        total = (kept[...].astype(F32) + got[...].astype(F32)).astype(BF16)
        parts.append(dot(selector, total, (1, 0)))
    if not direct:
        masks, starts, capacity = masks[:1], starts[:1], slots
    for block, start in enumerate(starts):
        at = 0
        for part in parts[start:]:
            end = at + part.shape[1]
            rows_of_block = part[block * capacity : (block + 1) * capacity]
            outs[block][:, at:end] = rows_of_block.astype(BF16)
            at = end


def pack(terms, targets, me, sums, after, peers, capacity, masks, starts, direct):
    rows = targets.shape[1]
    carries = sums is not None
    widths = [LANES] + [kept.shape[1] for kept, _ in terms]
    operands = [me, targets] + [x for pair in terms for x in pair] + ([sums] if carries else [])
    blocks = len(operands) - 1
    operands += after
    if direct:
        out_shape = [
            jax.ShapeDtypeStruct((capacity, sum(widths[start:])), BF16) for start in starts
        ]
    else:
        out_shape = [jax.ShapeDtypeStruct((peers * capacity, sum(widths)), BF16)]
    return pl.pallas_call(
        functools.partial(
            pack_kernel, peers, capacity, len(terms), masks, starts, direct, carries,
            len(after),
        ),
        out_shape=out_shape,
        in_specs=[pl.BlockSpec(memory_space=pltpu.SMEM)]
        + vmem(blocks)
        + [pl.BlockSpec(memory_space=pl.ANY)] * len(after),
        out_specs=vmem(len(out_shape)),
        compiler_params=pltpu.CompilerParams(vmem_limit_bytes=VMEM_BYTES),
        cost_estimate=pl.CostEstimate(
            flops=2 * rows * len(masks) * capacity * sum(widths),
            bytes_accessed=(6 * rows + 2 * len(masks) * capacity) * sum(widths),
            transcendentals=0,
        ),
        name="pack",
    )(*operands)


def swap(x, axis, mask):
    n = lax.axis_size(axis)
    return lax.ppermute(x, axis, [(i, i ^ mask) for i in range(n)])


def exchange(x, axis, pieces):
    shape = x.shape
    if x.ndim == 2:
        x = x.reshape(pieces, -1, shape[1])
    return lax.all_to_all(x, axis, split_axis=0, concat_axis=0, tiled=True).reshape(shape)


def probs_kernel(q_ref, k_ref, ids_ref, probs_ref, probs_t_ref):
    patches = q_ref.shape[0]
    ids = ids_ref[...]
    per_token = patches // ids.shape[1]
    token = iota((patches, ids.shape[1]), 0) // per_token
    column = jnp.sum(
        jnp.where(token == iota((patches, ids.shape[1]), 1), ids, 0), axis=1, keepdims=True
    )
    square = (patches, patches)
    row = jnp.sum(
        jnp.where(iota(square, 0) == iota(square, 1), column, 0), axis=0, keepdims=True
    )
    allowed = column == row
    scale = 1.0 / math.sqrt(HEAD_DIM)
    for head, (low, high, start, stop) in enumerate(head_windows()):
        q = masked(q_ref[:, start:stop], low, high, start, stop)
        k = k_ref[:, start:stop]
        for out, scores, axis in (
            (probs_ref, dot(q, k, (1, 1)), 1),
            (probs_t_ref, dot(k, q, (1, 1)), 0),
        ):
            scores = jnp.where(allowed, scores * scale, -jnp.inf)
            weights = jnp.exp(scores - jnp.max(scores, axis=axis, keepdims=True))
            out[head] = weights / jnp.sum(weights, axis=axis, keepdims=True)


def window_probs(queries, keys, ids):
    patches = queries.shape[0]
    shape = jax.ShapeDtypeStruct((HEADS, patches, patches), F32)
    return pl.pallas_call(
        probs_kernel,
        out_shape=[shape, shape],
        in_specs=vmem(3),
        out_specs=vmem(2),
        compiler_params=pltpu.CompilerParams(vmem_limit_bytes=VMEM_BYTES),
        cost_estimate=pl.CostEstimate(
            flops=8 * HEADS * patches * patches * LANES,
            bytes_accessed=8 * HEADS * patches * patches,
            transcendentals=2 * HEADS * patches * patches,
        ),
        name="probs",
    )(queries, keys, ids)


def norm_kernel(peers, early, carries, patches_ref, gain_ref, *refs):
    pieces, (out_ref, share_ref) = refs[:-2], refs[-2:]
    patches, width = patches_ref.shape
    pieces = [ref[...].astype(F32) for ref in pieces]
    pieces, begun = pieces[len(early) :], pieces[: len(early)]
    for place, begin in zip(early, begun):
        pieces[place] = jnp.concatenate([begin, pieces[place]], axis=1)
    routed = jnp.concatenate(pieces, axis=0) if len(pieces) > 1 else pieces[0]
    slots = routed.shape[0]
    per_token = routed.shape[1] // width
    columns = [routed[:, LANES + c * width : LANES + (c + 1) * width] for c in range(per_token)]
    held = jnp.concatenate(columns, axis=0).astype(BF16)
    lanes = per_token * slots
    extra = routed[:, :LANES]
    capacity = slots // peers
    if carries:
        place = iota((slots, LANES), 0) % capacity
        labels = jnp.where(place == capacity - 1, extra, 0.0).astype(BF16)
        turn = (iota((LANES, lanes), 0) == iota((LANES, lanes), 1) % capacity).astype(F32)
        spread = dot(labels, turn.astype(BF16), (1, 0))
        own = iota((slots, lanes), 0) // capacity == iota((slots, lanes), 1) % slots // capacity
        row_of_lane = jnp.sum(jnp.where(own, spread, 0.0), axis=0, keepdims=True)
    else:
        own = iota((slots, lanes), 1) % slots == iota((slots, lanes), 0)
        row_of_lane = jnp.sum(jnp.where(own, extra[:, :1], 0.0), axis=0, keepdims=True)
    row_of_lane = row_of_lane.astype(jnp.int32)
    patch_of_lane = row_of_lane * len(columns) + iota((1, lanes), 1) // slots
    patch_of_lane = jnp.where(row_of_lane < 0, -1, patch_of_lane)
    chosen = patch_of_lane == iota((patches, lanes), 0)
    patch_grads = dot(chosen.astype(F32).astype(BF16), held, (1, 0))
    inputs = patches_ref[...].astype(F32)
    inverse_rms = lax.rsqrt(jnp.mean(inputs * inputs, axis=1, keepdims=True) + 1e-06)
    normed = inputs * inverse_rms
    row = jnp.sum(patch_grads * normed, axis=0, keepdims=True)
    if carries:
        copies, lines, line_width = share_ref.shape
        pieces = (lines * line_width - width) // LANES
        parts = [row]
        for piece in range(pieces):
            kept = jnp.logical_and(place % pieces == piece, place < 3 * pieces)
            parts.append(jnp.sum(jnp.where(kept, extra, 0.0), axis=0, keepdims=True))
        row = jnp.concatenate(parts, axis=1)
        lines = [row[:, at : at + line_width] for at in range(0, row.shape[1], line_width)]
        row = jnp.broadcast_to(jnp.concatenate(lines, axis=0)[None], share_ref.shape)
    share_ref[...] = row.astype(share_ref.dtype)
    scaled = gain_ref[...] * patch_grads
    out_ref[...] = (
        inverse_rms * (scaled - normed * jnp.mean(scaled * normed, axis=1, keepdims=True))
    ).astype(BF16)


def norm_backward(received, peers, early, patches, gain, share):
    count, width = patches.shape
    routed = sum(x.size for x in received)
    return pl.pallas_call(
        functools.partial(norm_kernel, peers, early, len(share.shape) == 3),
        out_shape=[jax.ShapeDtypeStruct((count, width), BF16), share],
        in_specs=vmem(2 + len(received)),
        out_specs=vmem(2),
        compiler_params=pltpu.CompilerParams(vmem_limit_bytes=VMEM_BYTES),
        cost_estimate=pl.CostEstimate(
            flops=2 * count * routed,
            bytes_accessed=4 * count * width + 2 * routed,
            transcendentals=0,
        ),
        name="norm",
    )(patches, gain, *received)


def window_kernel(g_ref, q_ref, k_ref, v_ref, probs_ref, probs_t_ref, dq_ref, dk_ref, dv_ref):
    width = g_ref.shape[1]
    windows = head_windows()
    scores, scores_t, probs_t = [], [], []
    for head, (low, high, start, stop) in enumerate(windows):
        g = masked(g_ref[:, start:stop], low, high, start, stop)
        v = v_ref[:, start:stop]
        found = []
        for ref, grads, axis in (
            (probs_ref, dot(g, v, (1, 1)), 1),
            (probs_t_ref, dot(v, g, (1, 1)), 0),
        ):
            probs = ref[head]
            rounded = probs.astype(BF16)
            delta = jnp.sum(rounded.astype(F32) * grads, axis=axis, keepdims=True)
            found.append(((probs * (grads - delta)).astype(BF16), rounded))
        scores.append(found[0][0])
        scores_t.append(found[1][0])
        probs_t.append(found[1][1])
    scale = 1.0 / math.sqrt(HEAD_DIM)
    for start in range(0, width, LANES):
        stop = start + LANES
        heads = [h for h, (low, high, _, _) in enumerate(windows) if low < stop and high > start]
        for out, left, right_ref, factor in (
            (dq_ref, scores, k_ref, scale),
            (dk_ref, scores_t, q_ref, scale),
            (dv_ref, probs_t, g_ref, 1.0),
        ):
            right = right_ref[:, start:stop]
            rows = [masked(right, windows[h][0], windows[h][1], start, stop) for h in heads]
            product = dot(
                jnp.concatenate([left[h] for h in heads], axis=1),
                jnp.concatenate(rows, axis=0),
                (1, 0),
            )
            out[:, start:stop] = (product * factor).astype(BF16)


def window_backward(out_grads, queries, keys, values, probs, probs_t):
    patches, width = queries.shape
    shape = jax.ShapeDtypeStruct((patches, width), BF16)
    return pl.pallas_call(
        window_kernel,
        out_shape=[shape] * 3,
        in_specs=vmem(6),
        out_specs=vmem(3),
        compiler_params=pltpu.CompilerParams(vmem_limit_bytes=VMEM_BYTES),
        cost_estimate=pl.CostEstimate(
            flops=10 * HEADS * patches * patches * LANES,
            bytes_accessed=8 * HEADS * patches * patches + 14 * patches * width,
            transcendentals=0,
        ),
        name="window",
    )(out_grads, queries, keys, values, probs, probs_t)


def finish_kernel(width, images, gain_scale, bias_scale, shared_ref, gain_ref, bias_ref):
    devices, lines, line_width = shared_ref.shape
    shared = shared_ref[...].astype(F32)
    total = jnp.sum(shared, axis=0) * gain_scale
    for line in range(lines):
        at = line * line_width
        end = min(at + line_width, width)
        gain_ref[at:end] = total[line, : end - at]
    start = width - (lines - 1) * line_width
    for device in range(devices):
        piece = line_width - start
        own = shared[device, lines - 1, start:] * bias_scale
        place = device % images * (devices // images) + device // images
        bias_ref[place * piece : (place + 1) * piece] = own


def finish(shared, width, images, gain_scale, bias_scale):
    devices, lines, line_width = shared.shape
    return pl.pallas_call(
        functools.partial(finish_kernel, width, images, gain_scale, bias_scale),
        out_shape=[
            jax.ShapeDtypeStruct((width,), F32),
            jax.ShapeDtypeStruct((devices * (lines * line_width - width),), F32),
        ],
        in_specs=vmem(1),
        out_specs=vmem(2),
        compiler_params=pltpu.CompilerParams(vmem_limit_bytes=VMEM_BYTES),
        name="finish",
    )(shared)


def body(llm_grads, token_target, patches, gain, w_down, queries, keys, values, window_ids):
    grad_rows = llm_grads[0]
    rows = grad_rows.shape[0]
    images, peers = lax.axis_size("img"), lax.axis_size("seq")
    devices = images * peers
    capacity = max(1, 2 * rows // peers)
    direct = peers <= DIRECT
    block = w_down.shape[1]
    width = patches.shape[2]
    pieces = block // peers // LANES
    carries = pieces > 0 and 3 * pieces < capacity and (width // LANES + pieces) % 2 == 0

    order = [0]
    while len(order) < images:
        order = [2 * j for j in order] + [2 * j + 1 for j in order]
    image, me = lax.axis_index("img"), lax.axis_index("seq")

    def columns(j):
        return lax.dynamic_slice(grad_rows, (0, (image ^ j) * block), (rows, block))

    x_blocks = [columns(0)] + [swap(columns(j), "img", j) for j in range(1, images)]
    x_blocks = [x_blocks[j] for j in order]
    probs, probs_t = window_probs(queries[0], keys[0], window_ids[0])

    touched = touch(w_down)
    terms, first = [], 0
    for index, count in enumerate(CHUNKS):
        kept, sent, *sums = project(x_blocks, w_down, touched, first, count * width, index == 0)
        first += count * width
        if index == 0:
            bias_part = sums[0]
        mask = 1
        while 2 * mask < images:
            kept, sent = halve(kept, swap(sent, "img", mask))
            mask *= 2
        terms.append((kept, swap(sent, "img", mask)))
    masks = peer_masks(peers)
    early = early_masks(peers) if direct else ()
    places = tuple(masks.index(mask) for mask in early)
    place = me.reshape(1)
    sums = bias_part if carries else None
    begun = []
    if early:
        begun = list(
            pack(
                terms[:1], token_target, place, sums, [], peers, capacity, early,
                (0,) * len(early), direct,
            )
        )
    starts = tuple(2 if mask in early else 0 for mask in masks)
    packed = pack(
        terms, token_target, place, sums, begun, peers, capacity, masks, starts, direct
    )
    if direct:
        routed = [swap(x, "seq", mask) if mask else x for x, mask in zip(packed, masks)]
    else:
        routed = [exchange(packed[0], "seq", peers)]
    routed = [swap(block, "seq", mask) for block, mask in zip(begun, early)] + routed

    if carries:
        share = jax.ShapeDtypeStruct((devices, 2, (width + pieces * LANES) // 2), BF16)
    else:
        share = jax.ShapeDtypeStruct((1, width), F32)
    out_grads, shared = norm_backward(routed, peers, places, patches[0], gain[None], share)
    gain_scale = 1.0 / math.sqrt(devices * patches.shape[1])
    bias_scale = 1.0 / math.sqrt(devices * rows)
    if carries:
        shared = exchange(shared, ("seq", "img"), devices)
        gain_grad, bias_grad = finish(shared, width, images, gain_scale, bias_scale)
    else:
        gain_grad = lax.psum(shared[0], ("img", "seq")) * gain_scale
        bias_grad = lax.all_gather(lax.psum(bias_part[0], "seq"), "img", tiled=True) * bias_scale
    grads = window_backward(out_grads, queries[0], keys[0], values[0], probs, probs_t)
    return (grads[0][None], grads[1][None], grads[2][None], gain_grad, bias_grad)


def solution(mesh):
    return jax.shard_map(
        body,
        mesh=mesh,
        in_specs=(
            P("img", "seq", None),
            P("img", "seq"),
            P("img", "seq", None),
            P(),
            P(None, "img"),
            P("img", "seq", None),
            P("img", "seq", None),
            P("img", "seq", None),
            P("img", "seq", None),
        ),
        out_specs=(P("img", "seq", None), P("img", "seq", None), P("img", "seq", None), P(), P()),
        check_vma=False,
    )
```

```python
import functools
import math

import jax
import jax.numpy as jnp
from jax import lax
from jax.experimental import pallas as pl
from jax.experimental.pallas import tpu as pltpu
from jax.sharding import PartitionSpec as P

HEADS = 16
HEAD_DIM = 80
LANES = 128
CHUNKS = (3, 1)
DIRECT = 8
VMEM_BYTES = 16 * 1024 * 1024

F32 = jnp.float32
BF16 = jnp.bfloat16


def iota(shape, axis):
    return lax.broadcasted_iota(jnp.int32, shape, axis)


def dot(a, b, over):
    return lax.dot_general(a, b, ((over[:1], over[1:]), ((), ())), preferred_element_type=F32)


def vmem(count):
    return [pl.BlockSpec(memory_space=pltpu.VMEM)] * count


def head_windows():
    windows = []
    for head in range(HEADS):
        low, high = head * HEAD_DIM, (head + 1) * HEAD_DIM
        start = low // LANES * LANES
        windows.append((low, high, start, -(-high // LANES) * LANES))
    return windows


def lane_mask(low, high, start, stop):
    at = iota((1, stop - start), 1) + start
    return jnp.logical_and(at >= low, at < high)


def masked(x, low, high, start, stop):
    return jnp.where(lane_mask(low, high, start, stop), x, jnp.zeros_like(x))


def project_kernel(blocks, first, tile, with_sum, *refs):
    x_refs, w_ref = refs[:blocks], refs[blocks]
    keep_ref, send_ref = refs[blocks + 2 : blocks + 4]
    x = jnp.concatenate([ref[...] for ref in x_refs], axis=0)
    if with_sum:
        refs[blocks + 4][...] = dot(jnp.ones((16, x.shape[0]), BF16), x, (1, 0))[:1]
    x = x.T
    half = keep_ref.shape[0]
    for t in range(0, keep_ref.shape[1], tile):
        product = dot(w_ref[first + t : first + t + tile], x, (1, 0)).T.astype(BF16)
        keep_ref[:, t : t + tile] = product[:half]
        send_ref[:, t : t + tile] = product[half:]


def project(x_blocks, w_down, touched, first, width, with_sum):
    blocks, (rows, depth) = len(x_blocks), x_blocks[0].shape
    tile = 512
    while width % tile:
        tile //= 2
    out_shape = [jax.ShapeDtypeStruct((blocks * rows // 2, width), BF16)] * 2
    if with_sum:
        out_shape = out_shape + [jax.ShapeDtypeStruct((1, depth), F32)]
    return pl.pallas_call(
        functools.partial(project_kernel, blocks, first, tile, with_sum),
        out_shape=out_shape,
        in_specs=vmem(blocks + 1) + [pl.BlockSpec(memory_space=pl.ANY)],
        out_specs=vmem(len(out_shape)),
        compiler_params=pltpu.CompilerParams(vmem_limit_bytes=VMEM_BYTES),
        cost_estimate=pl.CostEstimate(
            flops=2 * blocks * rows * depth * width,
            bytes_accessed=2 * width * depth,
            transcendentals=0,
        ),
        name="project",
    )(*x_blocks, pltpu.with_memory_space_constraint(w_down, pltpu.VMEM), touched)


def touch_kernel(w_ref, out_ref):
    out_ref[...] = w_ref[: out_ref.shape[0], : out_ref.shape[1]]


def touch(w_down):
    return pl.pallas_call(
        touch_kernel,
        out_shape=jax.ShapeDtypeStruct((16, LANES), w_down.dtype),
        in_specs=vmem(1),
        out_specs=pl.BlockSpec(memory_space=pltpu.VMEM),
        compiler_params=pltpu.CompilerParams(vmem_limit_bytes=VMEM_BYTES),
        cost_estimate=pl.CostEstimate(
            flops=0, bytes_accessed=2 * w_down.size, transcendentals=0
        ),
        name="touch",
    )(pltpu.with_memory_space_constraint(w_down, pltpu.VMEM))


def halve_kernel(kept_ref, got_ref, keep_ref, send_ref):
    half = keep_ref.shape[0]
    keep_ref[...] = kept_ref[:half].astype(F32) + got_ref[:half].astype(F32)
    send_ref[...] = (kept_ref[half:].astype(F32) + got_ref[half:].astype(F32)).astype(BF16)


def halve(kept, got):
    rows, width = kept.shape
    return pl.pallas_call(
        halve_kernel,
        out_shape=[
            jax.ShapeDtypeStruct((rows // 2, width), F32),
            jax.ShapeDtypeStruct((rows // 2, width), BF16),
        ],
        in_specs=vmem(2),
        out_specs=vmem(2),
        compiler_params=pltpu.CompilerParams(vmem_limit_bytes=VMEM_BYTES),
        cost_estimate=pl.CostEstimate(
            flops=rows * width, bytes_accessed=7 * rows * width, transcendentals=0
        ),
        name="halve",
    )(kept, got)


def peer_masks(peers):
    return (0, 7, 1, 6, 2, 5, 3, 4) if peers == 8 else tuple(range(peers))


def early_masks(peers):
    return ()


def block_peer(block, masks, me):
    peer = jnp.zeros_like(block)
    for place, mask in enumerate(masks):
        peer = jnp.where(block == place, mask ^ me, peer)
    return peer


def pack_kernel(
    peers, capacity, chunks, masks, starts, direct, carries, after, me_ref, *refs
):
    targets_ref, terms, refs = refs[0], refs[1 : 2 * chunks + 1], refs[2 * chunks + 1 :]
    outs = refs[after + carries :]
    targets = targets_ref[...]
    rows = targets.shape[1]
    dest = targets // rows
    local = targets - dest * rows
    dest_column = jnp.sum(
        jnp.where(iota((rows, rows), 0) == iota((rows, rows), 1), dest, 0), axis=1, keepdims=True
    )
    same_before = jnp.logical_and(dest_column == dest, iota((rows, rows), 0) < iota((rows, rows), 1))
    rank = jnp.sum(same_before.astype(jnp.int32), axis=0, keepdims=True)
    slots = len(masks) * capacity
    slot = iota((slots, rows), 0)
    holder = slot // capacity
    if direct:
        holder = block_peer(holder, masks, me_ref[0])
    chosen = jnp.logical_and(dest == holder, rank == slot % capacity)
    selector = chosen.astype(F32).astype(BF16)
    parts = []
    if carries:
        local = jnp.broadcast_to((local + 1).astype(F32), (16, rows)).astype(BF16)
        labels = dot(local, selector, (1, 1))[:1] - 1.0
        square = (slots, slots)
        own = iota(square, 0) // capacity == iota(square, 1) // capacity
        own = jnp.logical_and(own, iota(square, 0) % capacity == capacity - 1)
        turn = (iota((slots, LANES), 0) % capacity == iota((slots, LANES), 1)).astype(F32)
        extra = dot(jnp.where(own, labels, 0.0).astype(BF16), turn.astype(BF16), (1, 0))
        sums = refs[0][...]
        high = sums.astype(BF16).astype(F32)
        middle = (sums - high).astype(BF16).astype(F32)
        low = (sums - high - middle).astype(BF16).astype(F32)
        row = iota((slots, LANES), 0) % capacity
        peer = iota((slots, LANES), 0) // capacity
        if direct:
            peer = block_peer(peer, masks, me_ref[0])
        pieces = sums.shape[1] // peers // LANES
        for p in range(peers):
            for level, values in enumerate((high, middle, low)):
                for piece in range(pieces):
                    start = (p * pieces + piece) * LANES
                    line = jnp.broadcast_to(values[:, start : start + LANES], (slots, LANES))
                    here = jnp.logical_and(peer == p, row == level * pieces + piece)
                    extra = jnp.where(here, line, extra)
        parts.append(extra)
    else:
        label = jnp.sum(jnp.where(chosen, local + 1, 0), axis=1, keepdims=True) - 1
        parts.append(jnp.broadcast_to(label.astype(F32), (slots, LANES)))
    for chunk in range(chunks):
        kept, got = terms[2 * chunk : 2 * chunk + 2]
        total = (kept[...].astype(F32) + got[...].astype(F32)).astype(BF16)
        parts.append(dot(selector, total, (1, 0)))
    if not direct:
        masks, starts, capacity = masks[:1], starts[:1], slots
    for block, start in enumerate(starts):
        at = 0
        for part in parts[start:]:
            end = at + part.shape[1]
            rows_of_block = part[block * capacity : (block + 1) * capacity]
            outs[block][:, at:end] = rows_of_block.astype(BF16)
            at = end


def pack(terms, targets, me, sums, after, peers, capacity, masks, starts, direct):
    rows = targets.shape[1]
    carries = sums is not None
    widths = [LANES] + [kept.shape[1] for kept, _ in terms]
    operands = [me, targets] + [x for pair in terms for x in pair] + ([sums] if carries else [])
    blocks = len(operands) - 1
    operands += after
    if direct:
        out_shape = [
            jax.ShapeDtypeStruct((capacity, sum(widths[start:])), BF16) for start in starts
        ]
    else:
        out_shape = [jax.ShapeDtypeStruct((peers * capacity, sum(widths)), BF16)]
    return pl.pallas_call(
        functools.partial(
            pack_kernel, peers, capacity, len(terms), masks, starts, direct, carries,
            len(after),
        ),
        out_shape=out_shape,
        in_specs=[pl.BlockSpec(memory_space=pltpu.SMEM)]
        + vmem(blocks)
        + [pl.BlockSpec(memory_space=pl.ANY)] * len(after),
        out_specs=vmem(len(out_shape)),
        compiler_params=pltpu.CompilerParams(vmem_limit_bytes=VMEM_BYTES),
        cost_estimate=pl.CostEstimate(
            flops=2 * rows * len(masks) * capacity * sum(widths),
            bytes_accessed=(6 * rows + 2 * len(masks) * capacity) * sum(widths),
            transcendentals=0,
        ),
        name="pack",
    )(*operands)


def swap(x, axis, mask):
    n = lax.axis_size(axis)
    return lax.ppermute(x, axis, [(i, i ^ mask) for i in range(n)])


def exchange(x, axis, pieces):
    shape = x.shape
    if x.ndim == 2:
        x = x.reshape(pieces, -1, shape[1])
    return lax.all_to_all(x, axis, split_axis=0, concat_axis=0, tiled=True).reshape(shape)


def probs_kernel(q_ref, k_ref, ids_ref, probs_ref, probs_t_ref):
    patches = q_ref.shape[0]
    ids = ids_ref[...]
    per_token = patches // ids.shape[1]
    token = iota((patches, ids.shape[1]), 0) // per_token
    column = jnp.sum(
        jnp.where(token == iota((patches, ids.shape[1]), 1), ids, 0), axis=1, keepdims=True
    )
    square = (patches, patches)
    row = jnp.sum(
        jnp.where(iota(square, 0) == iota(square, 1), column, 0), axis=0, keepdims=True
    )
    allowed = column == row
    scale = 1.0 / math.sqrt(HEAD_DIM)
    for head, (low, high, start, stop) in enumerate(head_windows()):
        q = masked(q_ref[:, start:stop], low, high, start, stop)
        k = k_ref[:, start:stop]
        for out, scores, axis in (
            (probs_ref, dot(q, k, (1, 1)), 1),
            (probs_t_ref, dot(k, q, (1, 1)), 0),
        ):
            scores = jnp.where(allowed, scores * scale, -jnp.inf)
            weights = jnp.exp(scores - jnp.max(scores, axis=axis, keepdims=True))
            out[head] = weights / jnp.sum(weights, axis=axis, keepdims=True)


def window_probs(queries, keys, ids):
    patches = queries.shape[0]
    shape = jax.ShapeDtypeStruct((HEADS, patches, patches), F32)
    return pl.pallas_call(
        probs_kernel,
        out_shape=[shape, shape],
        in_specs=vmem(3),
        out_specs=vmem(2),
        compiler_params=pltpu.CompilerParams(vmem_limit_bytes=VMEM_BYTES),
        cost_estimate=pl.CostEstimate(
            flops=8 * HEADS * patches * patches * LANES,
            bytes_accessed=8 * HEADS * patches * patches,
            transcendentals=2 * HEADS * patches * patches,
        ),
        name="probs",
    )(queries, keys, ids)


def norm_kernel(peers, early, carries, patches_ref, gain_ref, *refs):
    pieces, (out_ref, share_ref) = refs[:-2], refs[-2:]
    patches, width = patches_ref.shape
    pieces = [ref[...].astype(F32) for ref in pieces]
    pieces, begun = pieces[len(early) :], pieces[: len(early)]
    for place, begin in zip(early, begun):
        pieces[place] = jnp.concatenate([begin, pieces[place]], axis=1)
    routed = jnp.concatenate(pieces, axis=0) if len(pieces) > 1 else pieces[0]
    slots = routed.shape[0]
    per_token = routed.shape[1] // width
    columns = [routed[:, LANES + c * width : LANES + (c + 1) * width] for c in range(per_token)]
    held = jnp.concatenate(columns, axis=0).astype(BF16)
    lanes = per_token * slots
    extra = routed[:, :LANES]
    capacity = slots // peers
    if carries:
        place = iota((slots, LANES), 0) % capacity
        labels = jnp.where(place == capacity - 1, extra, 0.0).astype(BF16)
        turn = (iota((LANES, lanes), 0) == iota((LANES, lanes), 1) % capacity).astype(F32)
        spread = dot(labels, turn.astype(BF16), (1, 0))
        own = iota((slots, lanes), 0) // capacity == iota((slots, lanes), 1) % slots // capacity
        row_of_lane = jnp.sum(jnp.where(own, spread, 0.0), axis=0, keepdims=True)
    else:
        own = iota((slots, lanes), 1) % slots == iota((slots, lanes), 0)
        row_of_lane = jnp.sum(jnp.where(own, extra[:, :1], 0.0), axis=0, keepdims=True)
    row_of_lane = row_of_lane.astype(jnp.int32)
    patch_of_lane = row_of_lane * len(columns) + iota((1, lanes), 1) // slots
    patch_of_lane = jnp.where(row_of_lane < 0, -1, patch_of_lane)
    chosen = patch_of_lane == iota((patches, lanes), 0)
    patch_grads = dot(chosen.astype(F32).astype(BF16), held, (1, 0))
    inputs = patches_ref[...].astype(F32)
    inverse_rms = lax.rsqrt(jnp.mean(inputs * inputs, axis=1, keepdims=True) + 1e-06)
    normed = inputs * inverse_rms
    row = jnp.sum(patch_grads * normed, axis=0, keepdims=True)
    if carries:
        copies, lines, line_width = share_ref.shape
        pieces = (lines * line_width - width) // LANES
        parts = [row]
        for piece in range(pieces):
            kept = jnp.logical_and(place % pieces == piece, place < 3 * pieces)
            parts.append(jnp.sum(jnp.where(kept, extra, 0.0), axis=0, keepdims=True))
        row = jnp.concatenate(parts, axis=1)
        lines = [row[:, at : at + line_width] for at in range(0, row.shape[1], line_width)]
        row = jnp.broadcast_to(jnp.concatenate(lines, axis=0)[None], share_ref.shape)
    share_ref[...] = row.astype(share_ref.dtype)
    scaled = gain_ref[...] * patch_grads
    out_ref[...] = (
        inverse_rms * (scaled - normed * jnp.mean(scaled * normed, axis=1, keepdims=True))
    ).astype(BF16)


def norm_backward(received, peers, early, patches, gain, share):
    count, width = patches.shape
    routed = sum(x.size for x in received)
    return pl.pallas_call(
        functools.partial(norm_kernel, peers, early, len(share.shape) == 3),
        out_shape=[jax.ShapeDtypeStruct((count, width), BF16), share],
        in_specs=vmem(2 + len(received)),
        out_specs=vmem(2),
        compiler_params=pltpu.CompilerParams(vmem_limit_bytes=VMEM_BYTES),
        cost_estimate=pl.CostEstimate(
            flops=2 * count * routed,
            bytes_accessed=4 * count * width + 2 * routed,
            transcendentals=0,
        ),
        name="norm",
    )(patches, gain, *received)


def window_kernel(g_ref, q_ref, k_ref, v_ref, probs_ref, probs_t_ref, dq_ref, dk_ref, dv_ref):
    width = g_ref.shape[1]
    windows = head_windows()
    scores, scores_t, probs_t = [], [], []
    for head, (low, high, start, stop) in enumerate(windows):
        g = masked(g_ref[:, start:stop], low, high, start, stop)
        v = v_ref[:, start:stop]
        found = []
        for ref, grads, axis in (
            (probs_ref, dot(g, v, (1, 1)), 1),
            (probs_t_ref, dot(v, g, (1, 1)), 0),
        ):
            probs = ref[head]
            rounded = probs.astype(BF16)
            delta = jnp.sum(rounded.astype(F32) * grads, axis=axis, keepdims=True)
            found.append(((probs * (grads - delta)).astype(BF16), rounded))
        scores.append(found[0][0])
        scores_t.append(found[1][0])
        probs_t.append(found[1][1])
    scale = 1.0 / math.sqrt(HEAD_DIM)
    for start in range(0, width, LANES):
        stop = start + LANES
        heads = [h for h, (low, high, _, _) in enumerate(windows) if low < stop and high > start]
        for out, left, right_ref, factor in (
            (dq_ref, scores, k_ref, scale),
            (dk_ref, scores_t, q_ref, scale),
            (dv_ref, probs_t, g_ref, 1.0),
        ):
            right = right_ref[:, start:stop]
            rows = [masked(right, windows[h][0], windows[h][1], start, stop) for h in heads]
            product = dot(
                jnp.concatenate([left[h] for h in heads], axis=1),
                jnp.concatenate(rows, axis=0),
                (1, 0),
            )
            out[:, start:stop] = (product * factor).astype(BF16)


def window_backward(out_grads, queries, keys, values, probs, probs_t):
    patches, width = queries.shape
    shape = jax.ShapeDtypeStruct((patches, width), BF16)
    return pl.pallas_call(
        window_kernel,
        out_shape=[shape] * 3,
        in_specs=vmem(6),
        out_specs=vmem(3),
        compiler_params=pltpu.CompilerParams(vmem_limit_bytes=VMEM_BYTES),
        cost_estimate=pl.CostEstimate(
            flops=10 * HEADS * patches * patches * LANES,
            bytes_accessed=8 * HEADS * patches * patches + 14 * patches * width,
            transcendentals=0,
        ),
        name="window",
    )(out_grads, queries, keys, values, probs, probs_t)


def finish_kernel(width, images, gain_scale, bias_scale, shared_ref, gain_ref, bias_ref):
    devices, lines, line_width = shared_ref.shape
    shared = shared_ref[...].astype(F32)
    total = jnp.sum(shared, axis=0) * gain_scale
    for line in range(lines):
        at = line * line_width
        end = min(at + line_width, width)
        gain_ref[at:end] = total[line, : end - at]
    start = width - (lines - 1) * line_width
    for device in range(devices):
        piece = line_width - start
        own = shared[device, lines - 1, start:] * bias_scale
        place = device % images * (devices // images) + device // images
        bias_ref[place * piece : (place + 1) * piece] = own


def finish(shared, width, images, gain_scale, bias_scale):
    devices, lines, line_width = shared.shape
    return pl.pallas_call(
        functools.partial(finish_kernel, width, images, gain_scale, bias_scale),
        out_shape=[
            jax.ShapeDtypeStruct((width,), F32),
            jax.ShapeDtypeStruct((devices * (lines * line_width - width),), F32),
        ],
        in_specs=vmem(1),
        out_specs=vmem(2),
        compiler_params=pltpu.CompilerParams(vmem_limit_bytes=VMEM_BYTES),
        name="finish",
    )(shared)


def body(llm_grads, token_target, patches, gain, w_down, queries, keys, values, window_ids):
    grad_rows = llm_grads[0]
    rows = grad_rows.shape[0]
    images, peers = lax.axis_size("img"), lax.axis_size("seq")
    devices = images * peers
    capacity = max(1, 2 * rows // peers)
    direct = peers <= DIRECT
    block = w_down.shape[1]
    width = patches.shape[2]
    pieces = block // peers // LANES
    carries = pieces > 0 and 3 * pieces < capacity and (width // LANES + pieces) % 2 == 0

    order = [0]
    while len(order) < images:
        order = [2 * j for j in order] + [2 * j + 1 for j in order]
    image, me = lax.axis_index("img"), lax.axis_index("seq")

    def columns(j):
        return lax.dynamic_slice(grad_rows, (0, (image ^ j) * block), (rows, block))

    x_blocks = [columns(0)] + [swap(columns(j), "img", j) for j in range(1, images)]
    x_blocks = [x_blocks[j] for j in order]
    probs, probs_t = window_probs(queries[0], keys[0], window_ids[0])

    touched = touch(w_down)
    terms, first = [], 0
    for index, count in enumerate(CHUNKS):
        kept, sent, *sums = project(x_blocks, w_down, touched, first, count * width, index == 0)
        first += count * width
        if index == 0:
            bias_part = sums[0]
        mask = 1
        while 2 * mask < images:
            kept, sent = halve(kept, swap(sent, "img", mask))
            mask *= 2
        terms.append((kept, swap(sent, "img", mask)))
    masks = peer_masks(peers)
    early = early_masks(peers) if direct else ()
    places = tuple(masks.index(mask) for mask in early)
    place = me.reshape(1)
    sums = bias_part if carries else None
    begun = []
    if early:
        begun = list(
            pack(
                terms[:1], token_target, place, sums, [], peers, capacity, early,
                (0,) * len(early), direct,
            )
        )
    starts = tuple(2 if mask in early else 0 for mask in masks)
    packed = pack(
        terms, token_target, place, sums, begun, peers, capacity, masks, starts, direct
    )
    if direct:
        routed = [swap(x, "seq", mask) if mask else x for x, mask in zip(packed, masks)]
    else:
        routed = [exchange(packed[0], "seq", peers)]
    routed = [swap(block, "seq", mask) for block, mask in zip(begun, early)] + routed

    if carries:
        share = jax.ShapeDtypeStruct((devices, 2, (width + pieces * LANES) // 2), BF16)
    else:
        share = jax.ShapeDtypeStruct((1, width), F32)
    out_grads, shared = norm_backward(routed, peers, places, patches[0], gain[None], share)
    gain_scale = 1.0 / math.sqrt(devices * patches.shape[1])
    bias_scale = 1.0 / math.sqrt(devices * rows)
    if carries:
        shared = exchange(shared, ("seq", "img"), devices)
        gain_grad, bias_grad = finish(shared, width, images, gain_scale, bias_scale)
    else:
        gain_grad = lax.psum(shared[0], ("img", "seq")) * gain_scale
        bias_grad = lax.all_gather(lax.psum(bias_part[0], "seq"), "img", tiled=True) * bias_scale
    grads = window_backward(out_grads, queries[0], keys[0], values[0], probs, probs_t)
    return (grads[0][None], grads[1][None], grads[2][None], gain_grad, bias_grad)


def solution(mesh):
    return jax.shard_map(
        body,
        mesh=mesh,
        in_specs=(
            P("img", "seq", None),
            P("img", "seq"),
            P("img", "seq", None),
            P(),
            P(None, "img"),
            P("img", "seq", None),
            P("img", "seq", None),
            P("img", "seq", None),
            P("img", "seq", None),
        ),
        out_specs=(P("img", "seq", None), P("img", "seq", None), P("img", "seq", None), P(), P()),
        check_vma=False,
    )
```

```python
import functools
import math

import jax
import jax.numpy as jnp
from jax import lax
from jax.experimental import pallas as pl
from jax.experimental.pallas import tpu as pltpu
from jax.sharding import PartitionSpec as P

HEADS = 16
HEAD_DIM = 80
LANES = 128
CHUNKS = (3, 1)
DIRECT = 8
VMEM_BYTES = 16 * 1024 * 1024

F32 = jnp.float32
BF16 = jnp.bfloat16


def iota(shape, axis):
    return lax.broadcasted_iota(jnp.int32, shape, axis)


def dot(a, b, over):
    return lax.dot_general(a, b, ((over[:1], over[1:]), ((), ())), preferred_element_type=F32)


def vmem(count):
    return [pl.BlockSpec(memory_space=pltpu.VMEM)] * count


def head_windows():
    windows = []
    for head in range(HEADS):
        low, high = head * HEAD_DIM, (head + 1) * HEAD_DIM
        start = low // LANES * LANES
        windows.append((low, high, start, -(-high // LANES) * LANES))
    return windows


def lane_mask(low, high, start, stop):
    at = iota((1, stop - start), 1) + start
    return jnp.logical_and(at >= low, at < high)


def masked(x, low, high, start, stop):
    return jnp.where(lane_mask(low, high, start, stop), x, jnp.zeros_like(x))


def project_kernel(blocks, first, tile, with_sum, *refs):
    x_refs, w_ref = refs[:blocks], refs[blocks]
    keep_ref, send_ref = refs[blocks + 2 : blocks + 4]
    x = jnp.concatenate([ref[...] for ref in x_refs], axis=0)
    if with_sum:
        refs[blocks + 4][...] = dot(jnp.ones((16, x.shape[0]), BF16), x, (1, 0))[:1]
    x = x.T
    half = keep_ref.shape[0]
    for t in range(0, keep_ref.shape[1], tile):
        product = dot(w_ref[first + t : first + t + tile], x, (1, 0)).T.astype(BF16)
        keep_ref[:, t : t + tile] = product[:half]
        send_ref[:, t : t + tile] = product[half:]


def project(x_blocks, w_down, touched, first, width, with_sum):
    blocks, (rows, depth) = len(x_blocks), x_blocks[0].shape
    tile = 512
    while width % tile:
        tile //= 2
    out_shape = [jax.ShapeDtypeStruct((blocks * rows // 2, width), BF16)] * 2
    if with_sum:
        out_shape = out_shape + [jax.ShapeDtypeStruct((1, depth), F32)]
    return pl.pallas_call(
        functools.partial(project_kernel, blocks, first, tile, with_sum),
        out_shape=out_shape,
        in_specs=vmem(blocks + 1) + [pl.BlockSpec(memory_space=pl.ANY)],
        out_specs=vmem(len(out_shape)),
        compiler_params=pltpu.CompilerParams(vmem_limit_bytes=VMEM_BYTES),
        cost_estimate=pl.CostEstimate(
            flops=2 * blocks * rows * depth * width,
            bytes_accessed=2 * width * depth,
            transcendentals=0,
        ),
        name="project",
    )(*x_blocks, pltpu.with_memory_space_constraint(w_down, pltpu.VMEM), touched)


def touch_kernel(w_ref, out_ref):
    out_ref[...] = w_ref[: out_ref.shape[0], : out_ref.shape[1]]


def touch(w_down):
    return pl.pallas_call(
        touch_kernel,
        out_shape=jax.ShapeDtypeStruct((16, LANES), w_down.dtype),
        in_specs=vmem(1),
        out_specs=pl.BlockSpec(memory_space=pltpu.VMEM),
        compiler_params=pltpu.CompilerParams(vmem_limit_bytes=VMEM_BYTES),
        cost_estimate=pl.CostEstimate(
            flops=0, bytes_accessed=2 * w_down.size, transcendentals=0
        ),
        name="touch",
    )(pltpu.with_memory_space_constraint(w_down, pltpu.VMEM))


def halve_kernel(kept_ref, got_ref, keep_ref, send_ref):
    half = keep_ref.shape[0]
    keep_ref[...] = kept_ref[:half].astype(F32) + got_ref[:half].astype(F32)
    send_ref[...] = (kept_ref[half:].astype(F32) + got_ref[half:].astype(F32)).astype(BF16)


def halve(kept, got):
    rows, width = kept.shape
    return pl.pallas_call(
        halve_kernel,
        out_shape=[
            jax.ShapeDtypeStruct((rows // 2, width), F32),
            jax.ShapeDtypeStruct((rows // 2, width), BF16),
        ],
        in_specs=vmem(2),
        out_specs=vmem(2),
        compiler_params=pltpu.CompilerParams(vmem_limit_bytes=VMEM_BYTES),
        cost_estimate=pl.CostEstimate(
            flops=rows * width, bytes_accessed=7 * rows * width, transcendentals=0
        ),
        name="halve",
    )(kept, got)


def peer_masks(peers):
    return (0, 5, 1, 7, 2, 3, 4, 6) if peers == 8 else tuple(range(peers))


def early_masks(peers):
    return ()


def block_peer(block, masks, me):
    peer = jnp.zeros_like(block)
    for place, mask in enumerate(masks):
        peer = jnp.where(block == place, mask ^ me, peer)
    return peer


def pack_kernel(
    peers, capacity, chunks, masks, starts, direct, carries, after, me_ref, *refs
):
    targets_ref, terms, refs = refs[0], refs[1 : 2 * chunks + 1], refs[2 * chunks + 1 :]
    outs = refs[after + carries :]
    targets = targets_ref[...]
    rows = targets.shape[1]
    dest = targets // rows
    local = targets - dest * rows
    dest_column = jnp.sum(
        jnp.where(iota((rows, rows), 0) == iota((rows, rows), 1), dest, 0), axis=1, keepdims=True
    )
    same_before = jnp.logical_and(dest_column == dest, iota((rows, rows), 0) < iota((rows, rows), 1))
    rank = jnp.sum(same_before.astype(jnp.int32), axis=0, keepdims=True)
    slots = len(masks) * capacity
    slot = iota((slots, rows), 0)
    holder = slot // capacity
    if direct:
        holder = block_peer(holder, masks, me_ref[0])
    chosen = jnp.logical_and(dest == holder, rank == slot % capacity)
    selector = chosen.astype(F32).astype(BF16)
    parts = []
    if carries:
        local = jnp.broadcast_to((local + 1).astype(F32), (16, rows)).astype(BF16)
        labels = dot(local, selector, (1, 1))[:1] - 1.0
        square = (slots, slots)
        own = iota(square, 0) // capacity == iota(square, 1) // capacity
        own = jnp.logical_and(own, iota(square, 0) % capacity == capacity - 1)
        turn = (iota((slots, LANES), 0) % capacity == iota((slots, LANES), 1)).astype(F32)
        extra = dot(jnp.where(own, labels, 0.0).astype(BF16), turn.astype(BF16), (1, 0))
        sums = refs[0][...]
        high = sums.astype(BF16).astype(F32)
        middle = (sums - high).astype(BF16).astype(F32)
        low = (sums - high - middle).astype(BF16).astype(F32)
        row = iota((slots, LANES), 0) % capacity
        peer = iota((slots, LANES), 0) // capacity
        if direct:
            peer = block_peer(peer, masks, me_ref[0])
        pieces = sums.shape[1] // peers // LANES
        for p in range(peers):
            for level, values in enumerate((high, middle, low)):
                for piece in range(pieces):
                    start = (p * pieces + piece) * LANES
                    line = jnp.broadcast_to(values[:, start : start + LANES], (slots, LANES))
                    here = jnp.logical_and(peer == p, row == level * pieces + piece)
                    extra = jnp.where(here, line, extra)
        parts.append(extra)
    else:
        label = jnp.sum(jnp.where(chosen, local + 1, 0), axis=1, keepdims=True) - 1
        parts.append(jnp.broadcast_to(label.astype(F32), (slots, LANES)))
    for chunk in range(chunks):
        kept, got = terms[2 * chunk : 2 * chunk + 2]
        total = (kept[...].astype(F32) + got[...].astype(F32)).astype(BF16)
        parts.append(dot(selector, total, (1, 0)))
    if not direct:
        masks, starts, capacity = masks[:1], starts[:1], slots
    for block, start in enumerate(starts):
        at = 0
        for part in parts[start:]:
            end = at + part.shape[1]
            rows_of_block = part[block * capacity : (block + 1) * capacity]
            outs[block][:, at:end] = rows_of_block.astype(BF16)
            at = end


def pack(terms, targets, me, sums, after, peers, capacity, masks, starts, direct):
    rows = targets.shape[1]
    carries = sums is not None
    widths = [LANES] + [kept.shape[1] for kept, _ in terms]
    operands = [me, targets] + [x for pair in terms for x in pair] + ([sums] if carries else [])
    blocks = len(operands) - 1
    operands += after
    if direct:
        out_shape = [
            jax.ShapeDtypeStruct((capacity, sum(widths[start:])), BF16) for start in starts
        ]
    else:
        out_shape = [jax.ShapeDtypeStruct((peers * capacity, sum(widths)), BF16)]
    return pl.pallas_call(
        functools.partial(
            pack_kernel, peers, capacity, len(terms), masks, starts, direct, carries,
            len(after),
        ),
        out_shape=out_shape,
        in_specs=[pl.BlockSpec(memory_space=pltpu.SMEM)]
        + vmem(blocks)
        + [pl.BlockSpec(memory_space=pl.ANY)] * len(after),
        out_specs=vmem(len(out_shape)),
        compiler_params=pltpu.CompilerParams(vmem_limit_bytes=VMEM_BYTES),
        cost_estimate=pl.CostEstimate(
            flops=2 * rows * len(masks) * capacity * sum(widths),
            bytes_accessed=(6 * rows + 2 * len(masks) * capacity) * sum(widths),
            transcendentals=0,
        ),
        name="pack",
    )(*operands)


def swap(x, axis, mask):
    n = lax.axis_size(axis)
    return lax.ppermute(x, axis, [(i, i ^ mask) for i in range(n)])


def exchange(x, axis, pieces):
    shape = x.shape
    if x.ndim == 2:
        x = x.reshape(pieces, -1, shape[1])
    return lax.all_to_all(x, axis, split_axis=0, concat_axis=0, tiled=True).reshape(shape)


def probs_kernel(q_ref, k_ref, ids_ref, probs_ref, probs_t_ref):
    patches = q_ref.shape[0]
    ids = ids_ref[...]
    per_token = patches // ids.shape[1]
    token = iota((patches, ids.shape[1]), 0) // per_token
    column = jnp.sum(
        jnp.where(token == iota((patches, ids.shape[1]), 1), ids, 0), axis=1, keepdims=True
    )
    square = (patches, patches)
    row = jnp.sum(
        jnp.where(iota(square, 0) == iota(square, 1), column, 0), axis=0, keepdims=True
    )
    allowed = column == row
    scale = 1.0 / math.sqrt(HEAD_DIM)
    for head, (low, high, start, stop) in enumerate(head_windows()):
        q = masked(q_ref[:, start:stop], low, high, start, stop)
        k = k_ref[:, start:stop]
        for out, scores, axis in (
            (probs_ref, dot(q, k, (1, 1)), 1),
            (probs_t_ref, dot(k, q, (1, 1)), 0),
        ):
            scores = jnp.where(allowed, scores * scale, -jnp.inf)
            weights = jnp.exp(scores - jnp.max(scores, axis=axis, keepdims=True))
            out[head] = weights / jnp.sum(weights, axis=axis, keepdims=True)


def window_probs(queries, keys, ids):
    patches = queries.shape[0]
    shape = jax.ShapeDtypeStruct((HEADS, patches, patches), F32)
    return pl.pallas_call(
        probs_kernel,
        out_shape=[shape, shape],
        in_specs=vmem(3),
        out_specs=vmem(2),
        compiler_params=pltpu.CompilerParams(vmem_limit_bytes=VMEM_BYTES),
        cost_estimate=pl.CostEstimate(
            flops=8 * HEADS * patches * patches * LANES,
            bytes_accessed=8 * HEADS * patches * patches,
            transcendentals=2 * HEADS * patches * patches,
        ),
        name="probs",
    )(queries, keys, ids)


def norm_kernel(peers, early, carries, patches_ref, gain_ref, *refs):
    pieces, (out_ref, share_ref) = refs[:-2], refs[-2:]
    patches, width = patches_ref.shape
    pieces = [ref[...].astype(F32) for ref in pieces]
    pieces, begun = pieces[len(early) :], pieces[: len(early)]
    for place, begin in zip(early, begun):
        pieces[place] = jnp.concatenate([begin, pieces[place]], axis=1)
    routed = jnp.concatenate(pieces, axis=0) if len(pieces) > 1 else pieces[0]
    slots = routed.shape[0]
    per_token = routed.shape[1] // width
    columns = [routed[:, LANES + c * width : LANES + (c + 1) * width] for c in range(per_token)]
    held = jnp.concatenate(columns, axis=0).astype(BF16)
    lanes = per_token * slots
    extra = routed[:, :LANES]
    capacity = slots // peers
    if carries:
        place = iota((slots, LANES), 0) % capacity
        labels = jnp.where(place == capacity - 1, extra, 0.0).astype(BF16)
        turn = (iota((LANES, lanes), 0) == iota((LANES, lanes), 1) % capacity).astype(F32)
        spread = dot(labels, turn.astype(BF16), (1, 0))
        own = iota((slots, lanes), 0) // capacity == iota((slots, lanes), 1) % slots // capacity
        row_of_lane = jnp.sum(jnp.where(own, spread, 0.0), axis=0, keepdims=True)
    else:
        own = iota((slots, lanes), 1) % slots == iota((slots, lanes), 0)
        row_of_lane = jnp.sum(jnp.where(own, extra[:, :1], 0.0), axis=0, keepdims=True)
    row_of_lane = row_of_lane.astype(jnp.int32)
    patch_of_lane = row_of_lane * len(columns) + iota((1, lanes), 1) // slots
    patch_of_lane = jnp.where(row_of_lane < 0, -1, patch_of_lane)
    chosen = patch_of_lane == iota((patches, lanes), 0)
    patch_grads = dot(chosen.astype(F32).astype(BF16), held, (1, 0))
    inputs = patches_ref[...].astype(F32)
    inverse_rms = lax.rsqrt(jnp.mean(inputs * inputs, axis=1, keepdims=True) + 1e-06)
    normed = inputs * inverse_rms
    row = jnp.sum(patch_grads * normed, axis=0, keepdims=True)
    if carries:
        copies, lines, line_width = share_ref.shape
        pieces = (lines * line_width - width) // LANES
        parts = [row]
        for piece in range(pieces):
            kept = jnp.logical_and(place % pieces == piece, place < 3 * pieces)
            parts.append(jnp.sum(jnp.where(kept, extra, 0.0), axis=0, keepdims=True))
        row = jnp.concatenate(parts, axis=1)
        lines = [row[:, at : at + line_width] for at in range(0, row.shape[1], line_width)]
        row = jnp.broadcast_to(jnp.concatenate(lines, axis=0)[None], share_ref.shape)
    share_ref[...] = row.astype(share_ref.dtype)
    scaled = gain_ref[...] * patch_grads
    out_ref[...] = (
        inverse_rms * (scaled - normed * jnp.mean(scaled * normed, axis=1, keepdims=True))
    ).astype(BF16)


def norm_backward(received, peers, early, patches, gain, share):
    count, width = patches.shape
    routed = sum(x.size for x in received)
    return pl.pallas_call(
        functools.partial(norm_kernel, peers, early, len(share.shape) == 3),
        out_shape=[jax.ShapeDtypeStruct((count, width), BF16), share],
        in_specs=vmem(2 + len(received)),
        out_specs=vmem(2),
        compiler_params=pltpu.CompilerParams(vmem_limit_bytes=VMEM_BYTES),
        cost_estimate=pl.CostEstimate(
            flops=2 * count * routed,
            bytes_accessed=4 * count * width + 2 * routed,
            transcendentals=0,
        ),
        name="norm",
    )(patches, gain, *received)


def window_kernel(g_ref, q_ref, k_ref, v_ref, probs_ref, probs_t_ref, dq_ref, dk_ref, dv_ref):
    width = g_ref.shape[1]
    windows = head_windows()
    scores, scores_t, probs_t = [], [], []
    for head, (low, high, start, stop) in enumerate(windows):
        g = masked(g_ref[:, start:stop], low, high, start, stop)
        v = v_ref[:, start:stop]
        found = []
        for ref, grads, axis in (
            (probs_ref, dot(g, v, (1, 1)), 1),
            (probs_t_ref, dot(v, g, (1, 1)), 0),
        ):
            probs = ref[head]
            rounded = probs.astype(BF16)
            delta = jnp.sum(rounded.astype(F32) * grads, axis=axis, keepdims=True)
            found.append(((probs * (grads - delta)).astype(BF16), rounded))
        scores.append(found[0][0])
        scores_t.append(found[1][0])
        probs_t.append(found[1][1])
    scale = 1.0 / math.sqrt(HEAD_DIM)
    for start in range(0, width, LANES):
        stop = start + LANES
        heads = [h for h, (low, high, _, _) in enumerate(windows) if low < stop and high > start]
        for out, left, right_ref, factor in (
            (dq_ref, scores, k_ref, scale),
            (dk_ref, scores_t, q_ref, scale),
            (dv_ref, probs_t, g_ref, 1.0),
        ):
            right = right_ref[:, start:stop]
            rows = [masked(right, windows[h][0], windows[h][1], start, stop) for h in heads]
            product = dot(
                jnp.concatenate([left[h] for h in heads], axis=1),
                jnp.concatenate(rows, axis=0),
                (1, 0),
            )
            out[:, start:stop] = (product * factor).astype(BF16)


def window_backward(out_grads, queries, keys, values, probs, probs_t):
    patches, width = queries.shape
    shape = jax.ShapeDtypeStruct((patches, width), BF16)
    return pl.pallas_call(
        window_kernel,
        out_shape=[shape] * 3,
        in_specs=vmem(6),
        out_specs=vmem(3),
        compiler_params=pltpu.CompilerParams(vmem_limit_bytes=VMEM_BYTES),
        cost_estimate=pl.CostEstimate(
            flops=10 * HEADS * patches * patches * LANES,
            bytes_accessed=8 * HEADS * patches * patches + 14 * patches * width,
            transcendentals=0,
        ),
        name="window",
    )(out_grads, queries, keys, values, probs, probs_t)


def finish_kernel(width, images, gain_scale, bias_scale, shared_ref, gain_ref, bias_ref):
    devices, lines, line_width = shared_ref.shape
    shared = shared_ref[...].astype(F32)
    total = jnp.sum(shared, axis=0) * gain_scale
    for line in range(lines):
        at = line * line_width
        end = min(at + line_width, width)
        gain_ref[at:end] = total[line, : end - at]
    start = width - (lines - 1) * line_width
    for device in range(devices):
        piece = line_width - start
        own = shared[device, lines - 1, start:] * bias_scale
        place = device % images * (devices // images) + device // images
        bias_ref[place * piece : (place + 1) * piece] = own


def finish(shared, width, images, gain_scale, bias_scale):
    devices, lines, line_width = shared.shape
    return pl.pallas_call(
        functools.partial(finish_kernel, width, images, gain_scale, bias_scale),
        out_shape=[
            jax.ShapeDtypeStruct((width,), F32),
            jax.ShapeDtypeStruct((devices * (lines * line_width - width),), F32),
        ],
        in_specs=vmem(1),
        out_specs=vmem(2),
        compiler_params=pltpu.CompilerParams(vmem_limit_bytes=VMEM_BYTES),
        name="finish",
    )(shared)


def body(llm_grads, token_target, patches, gain, w_down, queries, keys, values, window_ids):
    grad_rows = llm_grads[0]
    rows = grad_rows.shape[0]
    images, peers = lax.axis_size("img"), lax.axis_size("seq")
    devices = images * peers
    capacity = max(1, 2 * rows // peers)
    direct = peers <= DIRECT
    block = w_down.shape[1]
    width = patches.shape[2]
    pieces = block // peers // LANES
    carries = pieces > 0 and 3 * pieces < capacity and (width // LANES + pieces) % 2 == 0

    order = [0]
    while len(order) < images:
        order = [2 * j for j in order] + [2 * j + 1 for j in order]
    image, me = lax.axis_index("img"), lax.axis_index("seq")

    def columns(j):
        return lax.dynamic_slice(grad_rows, (0, (image ^ j) * block), (rows, block))

    x_blocks = [columns(0)] + [swap(columns(j), "img", j) for j in range(1, images)]
    x_blocks = [x_blocks[j] for j in order]
    probs, probs_t = window_probs(queries[0], keys[0], window_ids[0])

    touched = touch(w_down)
    terms, first = [], 0
    for index, count in enumerate(CHUNKS):
        kept, sent, *sums = project(x_blocks, w_down, touched, first, count * width, index == 0)
        first += count * width
        if index == 0:
            bias_part = sums[0]
        mask = 1
        while 2 * mask < images:
            kept, sent = halve(kept, swap(sent, "img", mask))
            mask *= 2
        terms.append((kept, swap(sent, "img", mask)))
    masks = peer_masks(peers)
    early = early_masks(peers) if direct else ()
    places = tuple(masks.index(mask) for mask in early)
    place = me.reshape(1)
    sums = bias_part if carries else None
    begun = []
    if early:
        begun = list(
            pack(
                terms[:1], token_target, place, sums, [], peers, capacity, early,
                (0,) * len(early), direct,
            )
        )
    starts = tuple(2 if mask in early else 0 for mask in masks)
    packed = pack(
        terms, token_target, place, sums, begun, peers, capacity, masks, starts, direct
    )
    if direct:
        routed = [swap(x, "seq", mask) if mask else x for x, mask in zip(packed, masks)]
    else:
        routed = [exchange(packed[0], "seq", peers)]
    routed = [swap(block, "seq", mask) for block, mask in zip(begun, early)] + routed

    if carries:
        share = jax.ShapeDtypeStruct((devices, 2, (width + pieces * LANES) // 2), BF16)
    else:
        share = jax.ShapeDtypeStruct((1, width), F32)
    out_grads, shared = norm_backward(routed, peers, places, patches[0], gain[None], share)
    gain_scale = 1.0 / math.sqrt(devices * patches.shape[1])
    bias_scale = 1.0 / math.sqrt(devices * rows)
    if carries:
        shared = exchange(shared, ("seq", "img"), devices)
        gain_grad, bias_grad = finish(shared, width, images, gain_scale, bias_scale)
    else:
        gain_grad = lax.psum(shared[0], ("img", "seq")) * gain_scale
        bias_grad = lax.all_gather(lax.psum(bias_part[0], "seq"), "img", tiled=True) * bias_scale
    grads = window_backward(out_grads, queries[0], keys[0], values[0], probs, probs_t)
    return (grads[0][None], grads[1][None], grads[2][None], gain_grad, bias_grad)


def solution(mesh):
    return jax.shard_map(
        body,
        mesh=mesh,
        in_specs=(
            P("img", "seq", None),
            P("img", "seq"),
            P("img", "seq", None),
            P(),
            P(None, "img"),
            P("img", "seq", None),
            P("img", "seq", None),
            P("img", "seq", None),
            P("img", "seq", None),
        ),
        out_specs=(P("img", "seq", None), P("img", "seq", None), P("img", "seq", None), P(), P()),
        check_vma=False,
    )
```
